32 devices in a mesh: group: 2 (over y), row: 8 (over z, x), epoch: 2 (over core).
Axes of the slice: x: 2, y: 2, z: 4, core: 2. Of those that a mesh axis runs over, the one named last changes fastest.
Arguments:
- images: bfloat16 [8, 2048, 2048], P(('group', 'epoch'), 'row'), parts along dimension 0, may hold values from -6 to 6
- rate_vectors: int32 [2, 2], replicated, may hold values from -192 to 192
- epoch_times: int32 [4], replicated, may hold values from 0 to 127
Outputs:
- rate_images: float32 [4, 2048, 2048], P(('group', 'epoch'), 'row'), parts along dimension 0
The draws below stay inside these ranges and needn't reach their ends.
There are 2 independent parts, one for each index of `group`. The reference program is written for one: setup_inputs(seed, part) draws one part's arguments, and reference() takes and returns one part's arrays. A program takes and returns all parts, laid end to end along the dimension named above; an argument that names none is the same for every part. Nothing has to cross between parts.
All inputs are finite; a program needn't handle non-finite values.
Results may differ from the reference program's by a relative error of at most 0.011.
Values may be sent and summed in bfloat16 or wider, within the bound.
No kernel may reach another device: no remote copies, remote signals or barrier semaphores. Data moves between devices by JAX's collectives and lax.ppermute only.
A program may use at most 128 MiB of HBM per device.

```python
import math
import jax
import jax.numpy as jnp

N = 2048
SUBPIX = 16
EPOCHS = 4
RATES = 2


def plant(values, own_key, smallest, high):
    dims = values.shape
    spot = [jax.random.randint(jax.random.fold_in(own_key, axis), (), 0, dims[axis]) for axis in range(len(dims))]
    values = values.at[tuple(spot)].set(smallest)
    longest = dims.index(max(dims))
    spot[longest] = (spot[longest] + 1) % dims[longest]
    return values.at[tuple(spot)].set(high)


def levels(rng, extent, pieces, smallest, top_value):
    loudness, own = 1.0, jax.random.fold_in(rng, 6)
    for position, parts in pieces:
        heights = jnp.exp(jax.random.uniform(jax.random.fold_in(own, position), (parts,), jnp.float32, smallest / len(pieces), top_value / len(pieces)))
        loudness = loudness * jnp.repeat(heights, extent[position] // parts).reshape([-1 if axis == position else 1 for axis in range(len(extent))])
    return loudness


def bell_draw(rng, dims, deviation, bound, split=(), held_as=jnp.bfloat16):
    array = jax.random.normal(rng, dims, jnp.float32) * deviation
    if len(split) > 0:
        array = levels(rng, dims, split, -0.22, 0.18) * array
    return jnp.clip(array, min=-bound, max=bound).astype(held_as)


def setup_inputs(seed: int = 0, part: int = 0) -> dict:
    splits = jax.random.split(jax.random.key(seed), 4)
    part_splits = jax.random.split(jax.random.fold_in(splits[3], part), 4)
    images = bell_draw(part_splits[0], (EPOCHS, N, N), 1.0, 6.0, ((0, 2), (1, 8)))
    rate_vectors = plant(jax.random.randint(splits[1], (RATES, 2), -192, 193), jax.random.fold_in(splits[1], 1), -192, 192).astype(jnp.int32)
    epoch_times = plant(jax.random.randint(splits[2], (EPOCHS,), 0, 128), jax.random.fold_in(splits[2], 1), 0, 127).astype(jnp.int32)
    return dict(images=images, rate_vectors=rate_vectors, epoch_times=epoch_times)


def dft_tables(length):
    positions = jnp.arange(length, dtype=jnp.int32)
    turn_count = positions[:, None] * positions[None, :] % length
    angles = turn_count.astype(jnp.float32) * (2.0 * math.pi / length)
    factor = 1.0 / math.sqrt(length)
    return ((jnp.cos(angles) * factor).astype(jnp.bfloat16), (jnp.sin(angles) * factor).astype(jnp.bfloat16))

def reference(images, rate_vectors, epoch_times):
    cosine, sine = dft_tables(N)
    flattened = images.reshape(EPOCHS * N, N)
    row_re = jnp.dot(flattened, cosine, preferred_element_type=jnp.float32).astype(jnp.bfloat16).reshape(EPOCHS, N, N)
    row_im = (-jnp.dot(flattened, sine, preferred_element_type=jnp.float32)).astype(jnp.bfloat16).reshape(EPOCHS, N, N)
    spec_re_list = []
    spec_im_list = []
    for epoch_pos in range(EPOCHS):
        part_re = jnp.dot(cosine, row_re[epoch_pos], preferred_element_type=jnp.float32) + jnp.dot(sine, row_im[epoch_pos], preferred_element_type=jnp.float32)
        part_im = jnp.dot(cosine, row_im[epoch_pos], preferred_element_type=jnp.float32) - jnp.dot(sine, row_re[epoch_pos], preferred_element_type=jnp.float32)
        spec_re_list.append(part_re.astype(jnp.bfloat16).astype(jnp.float32))
        spec_im_list.append(part_im.astype(jnp.bfloat16).astype(jnp.float32))
    period = SUBPIX * N
    freq_index = jnp.arange(N, dtype=jnp.int32)
    shift_y = rate_vectors[:, 0:1] * epoch_times[None, :] % period
    shift_x = rate_vectors[:, 1:2] * epoch_times[None, :] % period
    stack_scale = 1.0 / math.sqrt(EPOCHS)
    outputs = []
    for rate_pos in range(RATES):
        summed_re = jnp.zeros((N, N), jnp.float32)
        summed_im = jnp.zeros((N, N), jnp.float32)
        for epoch_pos in range(EPOCHS):
            row_turns = freq_index * shift_y[rate_pos, epoch_pos] % period
            col_turns = freq_index * shift_x[rate_pos, epoch_pos] % period
            row_angles = row_turns.astype(jnp.float32) * (2.0 * math.pi / period)
            col_angles = col_turns.astype(jnp.float32) * (2.0 * math.pi / period)
            row_cos = jnp.cos(row_angles)[:, None]
            row_sin = jnp.sin(row_angles)[:, None]
            col_cos = jnp.cos(col_angles)[None, :]
            col_sin = jnp.sin(col_angles)[None, :]
            ramp_re = col_cos * row_cos - col_sin * row_sin
            ramp_im = col_sin * row_cos + col_cos * row_sin
            summed_re = summed_re + (spec_re_list[epoch_pos] * ramp_re - spec_im_list[epoch_pos] * ramp_im)
            summed_im = summed_im + (spec_re_list[epoch_pos] * ramp_im + spec_im_list[epoch_pos] * ramp_re)
        rate_re = (summed_re * stack_scale).astype(jnp.bfloat16)
        rate_im = (summed_im * stack_scale).astype(jnp.bfloat16)
        back_re = (jnp.dot(cosine, rate_re, preferred_element_type=jnp.float32) - jnp.dot(sine, rate_im, preferred_element_type=jnp.float32)).astype(jnp.bfloat16)
        back_im = (jnp.dot(cosine, rate_im, preferred_element_type=jnp.float32) + jnp.dot(sine, rate_re, preferred_element_type=jnp.float32)).astype(jnp.bfloat16)
        picture = jnp.dot(back_re, cosine, preferred_element_type=jnp.float32) - jnp.dot(back_im, sine, preferred_element_type=jnp.float32)
        outputs.append(picture)
    return jnp.stack(outputs)
```

```python
import functools
import math

import jax
import jax.numpy as jnp
import ml_dtypes
import numpy as np
from jax import lax
from jax.experimental import pallas as pl
from jax.experimental.pallas import tpu as pltpu
from jax.sharding import PartitionSpec as P

SUBPIX = 16
BLOCK = 256
VMEM_LIMIT = 56 * 1024 * 1024


def packed_table(length, cols):
    half = length // 2
    freqs = np.arange(half, dtype=np.int32)
    positions = np.arange(length, dtype=np.int32)
    turns = freqs[:, None] * positions[None, :] % length
    angles = turns.astype(np.float32) * np.float32(2.0 * math.pi / length)
    factor = np.float32(1.0 / math.sqrt(length))
    cosine = np.cos(angles) * factor
    sine = np.sin(angles) * factor
    sine[0] = np.where(positions % 2 == 0, factor, -factor)
    blocks = np.stack([cosine.reshape(-1, cols, length), sine.reshape(-1, cols, length)], axis=1)
    return blocks.reshape(length, length).astype(ml_dtypes.bfloat16)


def row_kernel(images_ref, table_ref, out_ref):
    loc_epochs, loc_rows, length = images_ref.shape
    dests, _, _, width = out_ref.shape
    pixels = images_ref[...].reshape(loc_epochs * loc_rows, length)
    terms = jnp.dot(pixels, table_ref[...], preferred_element_type=jnp.float32)
    terms = terms.astype(jnp.bfloat16)
    for dest in range(dests):
        part = terms[:, dest * width : (dest + 1) * width]
        out_ref[dest] = part.reshape(loc_epochs, loc_rows, width)


def row_transform(images, table_t, devices, width):
    loc_epochs, loc_rows, length = images.shape
    dests = BLOCK // width
    return pl.pallas_call(
        row_kernel,
        grid=(length // BLOCK,),
        in_specs=[
            pl.BlockSpec((loc_epochs, loc_rows, length), lambda i: (0, 0, 0)),
            pl.BlockSpec((length, BLOCK), lambda i: (0, i)),
        ],
        out_specs=pl.BlockSpec((dests, loc_epochs, loc_rows, width), lambda i: (i, 0, 0, 0)),
        out_shape=jax.ShapeDtypeStruct((devices, loc_epochs, loc_rows, width), jnp.bfloat16),
        compiler_params=pltpu.CompilerParams(vmem_limit_bytes=VMEM_LIMIT),
        cost_estimate=pl.CostEstimate(
            flops=2 * loc_epochs * loc_rows * length * length,
            bytes_accessed=2 * length * length + 4 * loc_epochs * loc_rows * length,
            transcendentals=0,
        ),
        name="row_transform",
    )(images, table_t)


def swap_halves(values):
    width = values.shape[1]
    if width % 128 == 0:
        return pltpu.roll(values, width // 2, axis=1)
    return jnp.concatenate([values[:, width // 2 :], values[:, : width // 2]], axis=1)


def column_kernel(
    epoch_count, rates, z_ref, table_ref, table_t_ref, coef_ref, lane_ref, out_ref, z_all, sums
):
    devices, loc_epochs, loc_rows, width = z_ref.shape
    row_count = devices // epoch_count
    epochs = epoch_count * loc_epochs
    cols = width // 2
    half_steps = pl.num_programs(0) // 2
    step = pl.program_id(0)
    pairs = rates * epochs

    @pl.when(step == 0)
    def _():
        for row in range(row_count):
            parts = [
                z_ref[row * epoch_count + core, loc]
                for core in range(epoch_count)
                for loc in range(loc_epochs)
            ]
            z_all[row * loc_rows : (row + 1) * loc_rows, :] = jnp.concatenate(parts, axis=1)

    @pl.when(step < half_steps)
    def _():
        products = jnp.dot(table_ref[...], z_all[...], preferred_element_type=jnp.float32)
        groups = BLOCK // width
        products = products.reshape(groups, 2, cols, epochs * width)
        even = products[:, 0].reshape(groups * cols, epochs * width)
        odd = products[:, 1].reshape(groups * cols, epochs * width)
        first = (step == 0) & (lax.broadcasted_iota(jnp.int32, (groups * cols, width), 0) == 0)
        results = []
        for rate in range(rates):
            straight = [0.0, 0.0]
            crossed = [0.0, 0.0]
            lead = [0.0, 0.0]
            for epoch in range(epochs):
                pair = rate * epochs + epoch
                even_part = even[:, epoch * width : (epoch + 1) * width]
                odd_part = odd[:, epoch * width : (epoch + 1) * width]
                cos_row = coef_ref[:, pair : pair + 1]
                sin_row = coef_ref[:, pairs + pair : pairs + pair + 1]
                turned = (
                    cos_row * even_part + sin_row * odd_part,
                    cos_row * odd_part - sin_row * even_part,
                )
                for which in range(2):
                    straight[which] += turned[which] * lane_ref[pair : pair + 1, :]
                    crossed[which] += turned[which] * lane_ref[pairs + pair : pairs + pair + 1, :]
                lead[0] += even_part[:8] * lane_ref[2 * pairs + pair : 2 * pairs + pair + 1, :]
                lead[1] += even_part[:8] * lane_ref[3 * pairs + pair : 3 * pairs + pair + 1, :]
            even_sum = straight[0] + swap_halves(crossed[0])
            odd_sum = straight[1] + swap_halves(crossed[1])
            lead_sum = lead[0] + swap_halves(lead[1])
            even_sum = jnp.where(first, lead_sum[0:1], even_sum)
            both = jnp.stack(
                [even_sum.reshape(groups, cols, width), odd_sum.reshape(groups, cols, width)], axis=1
            )
            results.append(both.reshape(BLOCK, width))
        start = pl.multiple_of(step * BLOCK, BLOCK)
        sums[pl.ds(start, BLOCK), :] = jnp.concatenate(results, axis=1).astype(jnp.bfloat16)

    @pl.when(step >= half_steps)
    def _():
        back = jnp.dot(table_t_ref[...], sums[...], preferred_element_type=jnp.float32)
        back = back.astype(jnp.bfloat16)
        dests, loc_rates = out_ref.shape[:2]
        for row in range(dests // epoch_count):
            for rate in range(rates):
                part = back[row * loc_rows : (row + 1) * loc_rows, rate * width : (rate + 1) * width]
                out_ref[row * epoch_count + rate // loc_rates, rate % loc_rates] = part


def column_stage(spectra, table, table_t, coefs, lanes, epoch_count, rates):
    devices, loc_epochs, loc_rows, width = spectra.shape
    length = table.shape[0]
    epochs = epoch_count * loc_epochs
    steps = length // BLOCK
    dests = BLOCK // loc_rows * epoch_count
    loc_rates = rates // epoch_count
    half_block = BLOCK // 2
    return pl.pallas_call(
        functools.partial(column_kernel, epoch_count, rates),
        grid=(2 * steps,),
        in_specs=[
            pl.BlockSpec(spectra.shape, lambda i: (0, 0, 0, 0)),
            pl.BlockSpec((BLOCK, length), lambda i: (jnp.minimum(i, steps - 1), 0)),
            pl.BlockSpec((BLOCK, length), lambda i: (jnp.maximum(i - steps, 0), 0)),
            pl.BlockSpec((half_block, coefs.shape[1]), lambda i: (jnp.minimum(i, steps - 1), 0)),
            pl.BlockSpec(lanes.shape, lambda i: (0, 0)),
        ],
        out_specs=pl.BlockSpec(
            (dests, loc_rates, loc_rows, width), lambda i: (jnp.maximum(i - steps, 0), 0, 0, 0)
        ),
        out_shape=jax.ShapeDtypeStruct((devices, loc_rates, loc_rows, width), jnp.bfloat16),
        scratch_shapes=[
            pltpu.VMEM((length, epochs * width), jnp.bfloat16),
            pltpu.VMEM((length, rates * width), jnp.bfloat16),
        ],
        compiler_params=pltpu.CompilerParams(vmem_limit_bytes=VMEM_LIMIT),
        cost_estimate=pl.CostEstimate(
            flops=2 * length * length * (epochs + rates) * width,
            bytes_accessed=4 * length * length,
            transcendentals=0,
        ),
        name="column_stage",
    )(spectra, table, table_t, coefs, lanes)


def image_kernel(back_ref, table_ref, out_ref, left):
    devices, loc_rates, loc_rows, width = back_ref.shape
    length = devices * width

    @pl.when(pl.program_id(0) == 0)
    def _():
        per_tile = 128 // width
        for rate in range(loc_rates):
            for tile in range(length // 128):
                parts = [back_ref[tile * per_tile + part, rate] for part in range(per_tile)]
                whole = parts[0] if per_tile == 1 else jnp.concatenate(parts, axis=1)
                left[rate * loc_rows : (rate + 1) * loc_rows, tile * 128 : (tile + 1) * 128] = whole

    pixels = jnp.dot(left[...], table_ref[...], preferred_element_type=jnp.float32)
    out_ref[...] = pixels.reshape(out_ref.shape)


def image_rows(back, table):
    devices, loc_rates, loc_rows, width = back.shape
    length = table.shape[0]
    return pl.pallas_call(
        image_kernel,
        grid=(length // BLOCK,),
        in_specs=[
            pl.BlockSpec(back.shape, lambda i: (0, 0, 0, 0)),
            pl.BlockSpec((length, BLOCK), lambda i: (0, i)),
        ],
        out_specs=pl.BlockSpec((loc_rates, loc_rows, BLOCK), lambda i: (0, 0, i)),
        out_shape=jax.ShapeDtypeStruct((loc_rates, loc_rows, length), jnp.float32),
        scratch_shapes=[pltpu.VMEM((loc_rates * loc_rows, length), jnp.bfloat16)],
        compiler_params=pltpu.CompilerParams(vmem_limit_bytes=VMEM_LIMIT),
        cost_estimate=pl.CostEstimate(
            flops=2 * loc_rates * loc_rows * length * length,
            bytes_accessed=2 * length * length + 6 * loc_rates * loc_rows * length,
            transcendentals=0,
        ),
        name="image_rows",
    )(back, table)


def ramp_factors(rate_vectors, epoch_times, device, cols, length):
    period = SUBPIX * length
    half = length // 2
    rates, epochs = rate_vectors.shape[0], epoch_times.shape[0]
    shift_y = (rate_vectors[:, 0:1] * epoch_times[None, :] % period).reshape(-1, 1)
    shift_x = (rate_vectors[:, 1:2] * epoch_times[None, :] % period).reshape(-1, 1)

    def angle(turns, whole):
        return (turns % whole).astype(jnp.float32) * (2.0 * math.pi / whole)

    freq_rows = jnp.arange(half, dtype=jnp.int32)[None, :]
    row_angle = angle(shift_y * (freq_rows - half), period)
    coefs = jnp.concatenate(
        [
            jnp.where(freq_rows == 0, 1.0, 2.0 * jnp.cos(row_angle)),
            jnp.where(freq_rows == 0, 0.0, 2.0 * jnp.sin(row_angle)),
        ]
    ).T
    lane = jnp.arange(2 * cols, dtype=jnp.int32)[None, :]
    freq_cols = device * cols + lane % cols
    is_sine = lane >= cols
    zero_col = (freq_cols == 0) & ~is_sine
    paired = freq_cols == 0
    col_angle = angle(shift_x * (freq_cols - half), period)
    scale = 1.0 / math.sqrt(epochs)
    ramp_cos = jnp.where(paired, scale, 2.0 * scale * jnp.cos(col_angle))
    ramp_sin = jnp.where(paired, 0.0, 2.0 * scale * jnp.sin(col_angle))
    ramp_sin = jnp.where(is_sine, ramp_sin, -ramp_sin)
    cos_x = jnp.cos(angle(shift_x, 2 * SUBPIX))
    cos_y = jnp.cos(angle(shift_y, 2 * SUBPIX))
    cos_xy = jnp.cos(angle(shift_x + shift_y, 2 * SUBPIX))
    main = jnp.where(zero_col, cos_y, cos_xy)
    lead = jnp.where(zero_col, 1.0, cos_x)
    lanes = jnp.concatenate([main * ramp_cos, main * ramp_sin, lead * ramp_cos, lead * ramp_sin])
    return coefs, lanes


def local(images, rate_vectors, epoch_times):
    loc_epochs, loc_rows, length = images.shape
    epoch_count = lax.axis_size("epoch")
    devices = lax.axis_size("row") * epoch_count
    device = lax.axis_index("row") * epoch_count + lax.axis_index("epoch")
    cols = length // 2 // devices
    table = packed_table(length, cols)
    table_t = jnp.asarray(np.ascontiguousarray(table.T))
    table = jnp.asarray(table)
    coefs, lanes = ramp_factors(rate_vectors, epoch_times, device, cols, length)
    rates = rate_vectors.shape[0]
    row_spectra = row_transform(images, table_t, devices, 2 * cols)
    spectra = lax.all_to_all(row_spectra, ("row", "epoch"), 0, 0, tiled=True)
    columns_back = column_stage(spectra, table, table_t, coefs, lanes, epoch_count, rates)
    back = lax.all_to_all(columns_back, ("row", "epoch"), 0, 0, tiled=True)
    return image_rows(back, table)


def solution(mesh):
    in_specs = (P(("group", "epoch"), "row", None), P(), P())
    out_specs = P(("group", "epoch"), "row", None)
    return jax.shard_map(local, mesh=mesh, in_specs=in_specs, out_specs=out_specs, check_vma=False)
```

```python
import functools
import math

import jax
import jax.numpy as jnp
import ml_dtypes
import numpy as np
from jax import lax
from jax.experimental import pallas as pl
from jax.experimental.pallas import tpu as pltpu
from jax.sharding import PartitionSpec as P

SUBPIX = 16
CHUNKS = 2
MIN_COLS = 32
ROW_BLOCK = 512
COLUMN_BLOCK = 512
IMAGE_BLOCK = 512
VMEM_LIMIT = 44 * 1024 * 1024


def packed_table(length, cols):
    half = length // 2
    freqs = np.arange(half, dtype=np.int32)
    positions = np.arange(length, dtype=np.int32)
    turns = freqs[:, None] * positions[None, :] % length
    angles = turns.astype(np.float32) * np.float32(2.0 * math.pi / length)
    factor = np.float32(1.0 / math.sqrt(length))
    cosine = np.cos(angles) * factor
    sine = np.sin(angles) * factor
    sine[0] = np.where(positions % 2 == 0, factor, -factor)
    blocks = np.stack([cosine.reshape(-1, cols, length), sine.reshape(-1, cols, length)], axis=1)
    return blocks.reshape(length, length).astype(ml_dtypes.bfloat16)


def cost(flops, bytes_accessed):
    return pl.CostEstimate(flops=flops, bytes_accessed=bytes_accessed, transcendentals=0)


def is_low(shape, group):
    return lax.broadcasted_iota(jnp.int32, shape, 1) % (2 * group) < group


def pair_lanes(upper, lower, width):
    count = upper.shape[1] // width
    if 2 * width == 128:
        parts = []
        low = is_low((upper.shape[0], 128), width)
        for tile in range(count // 2):
            first = upper[:, tile * 128 : (tile + 1) * 128]
            second = lower[:, tile * 128 : (tile + 1) * 128]
            parts.append(jnp.where(low, first, pltpu.roll(second, width, axis=1)))
            parts.append(jnp.where(low, pltpu.roll(first, width, axis=1), second))
        return parts
    groups = [slice(group * width, (group + 1) * width) for group in range(count)]
    return [jnp.concatenate([upper[:, group], lower[:, group]], axis=1) for group in groups]


def row_kernel(images_ref, table_ref, out_ref):
    loc_epochs, loc_rows, length = images_ref.shape
    dests, _, width = out_ref.shape
    pixels = images_ref[...].reshape(loc_epochs * loc_rows, length)
    terms = jnp.dot(pixels, table_ref[...], preferred_element_type=jnp.float32)
    if loc_epochs == 2:
        parts = pair_lanes(terms[:loc_rows], terms[loc_rows:], width // 2)
    else:
        by_epoch = terms.reshape(loc_epochs, loc_rows, terms.shape[1])
        one = width // loc_epochs
        parts = [
            jnp.concatenate(
                [by_epoch[loc][:, dest * one : (dest + 1) * one] for loc in range(loc_epochs)],
                axis=1,
            )
            for dest in range(dests)
        ]
    for dest in range(dests):
        out_ref[dest] = parts[dest].astype(jnp.bfloat16)


def row_transform(images, table_t, chunk, chunks, devices):
    loc_epochs, loc_rows, length = images.shape
    columns = length // chunks
    width = columns // devices * loc_epochs
    block = min(ROW_BLOCK, columns)
    steps = columns // block
    dests = devices // steps
    return pl.pallas_call(
        row_kernel,
        grid=(steps,),
        in_specs=[
            pl.BlockSpec((loc_epochs, loc_rows, length), lambda i: (0, 0, 0)),
            pl.BlockSpec((length, block), lambda i: (0, chunk * steps + i)),
        ],
        out_specs=pl.BlockSpec((dests, loc_rows, width), lambda i: (i, 0, 0)),
        out_shape=jax.ShapeDtypeStruct((devices, loc_rows, width), jnp.bfloat16),
        compiler_params=pltpu.CompilerParams(vmem_limit_bytes=VMEM_LIMIT),
        cost_estimate=cost(
            2 * loc_epochs * loc_rows * length * columns,
            2 * length * columns + 4 * loc_epochs * loc_rows * length,
        ),
        name=f"row_transform_{chunk}",
    )(images, table_t)


def fold_epochs(sums, epochs, width):
    if len(sums) == 2 and epochs == 4 and width == 64:
        halves = [part[:, :128] + part[:, 128:] for part in sums]
        low = is_low(halves[0].shape, 64)
        kept = jnp.where(low, halves[0], halves[1])
        return kept + pltpu.roll(jnp.where(low, halves[1], halves[0]), 64, axis=1)
    folded = [
        sum(part[:, epoch * width : (epoch + 1) * width] for epoch in range(epochs))
        for part in sums
    ]
    return jnp.concatenate(folded, axis=1)


def swap_halves(values, cols):
    total = values.shape[1]
    if total == 128:
        low = is_low(values.shape, cols)
        ahead = pltpu.roll(values, 128 - cols, axis=1)
        return jnp.where(low, ahead, pltpu.roll(values, cols, axis=1))
    parts = [values[:, start : start + cols] for start in range(0, total, cols)]
    return jnp.concatenate([parts[index ^ 1] for index in range(len(parts))], axis=1)


def column_kernel(
    epoch_count, epochs, rates, z_ref, table_ref, table_t_ref, coef_ref, lane_ref, out_ref, z_all, sums
):
    devices, loc_rows, core_lanes = z_ref.shape
    row_count = devices // epoch_count
    lanes = core_lanes * epoch_count
    width = lanes // epochs
    cols = width // 2
    block = table_ref.shape[0]
    half_steps = pl.num_programs(0) // 2
    step = pl.program_id(0)

    @pl.when(step == 0)
    def _():
        for row in range(row_count):
            parts = [z_ref[row * epoch_count + core] for core in range(epoch_count)]
            z_all[row * loc_rows : (row + 1) * loc_rows, :] = jnp.concatenate(parts, axis=1)

    @pl.when(step < half_steps)
    def _():
        products = jnp.dot(table_ref[...], z_all[...], preferred_element_type=jnp.float32)
        groups = block // width
        products = products.reshape(groups, 2, cols, lanes)
        even = products[:, 0].reshape(groups * cols, lanes)
        odd = products[:, 1].reshape(groups * cols, lanes)
        straight, crossed, lead = ([], []), ([], []), ([], [])
        for rate in range(rates):
            cos_row = coef_ref[:, rate * lanes : (rate + 1) * lanes]
            sin_row = coef_ref[:, (rates + rate) * lanes : (rates + rate + 1) * lanes]
            turned = (cos_row * even + sin_row * odd, cos_row * odd - sin_row * even)
            for which in range(2):
                straight[which].append(turned[which] * lane_ref[rate : rate + 1, :])
                crossed[which].append(turned[which] * lane_ref[rates + rate : rates + rate + 1, :])
                at = (2 + which) * rates + rate
                lead[which].append(even[:8] * lane_ref[at : at + 1, :])

        def collect(plain, turned):
            summed = fold_epochs(plain, epochs, width)
            return summed + swap_halves(fold_epochs(turned, epochs, width), cols)

        even_sum = collect(straight[0], crossed[0])
        odd_sum = collect(straight[1], crossed[1])
        lead_sum = collect(lead[0], lead[1])
        first = lax.broadcasted_iota(jnp.int32, even_sum.shape, 0) == 0
        even_sum = jnp.where(first & (step == 0), lead_sum[0:1], even_sum)
        both = jnp.stack(
            [part.reshape(groups, cols, rates * width) for part in (even_sum, odd_sum)], axis=1
        )
        start = pl.multiple_of(step * block, block)
        sums[pl.ds(start, block), :] = both.reshape(block, rates * width).astype(jnp.bfloat16)

    @pl.when(step >= half_steps)
    def _():
        back = jnp.dot(table_t_ref[...], sums[...], preferred_element_type=jnp.float32)
        half_rows = loc_rows // 2
        for row in range(block // loc_rows):
            part = back[row * loc_rows : (row + 1) * loc_rows]
            pairs = pair_lanes(part[:half_rows], part[half_rows:], width)
            for rate in range(rates):
                out_ref[row * rates + rate] = pairs[rate].astype(jnp.bfloat16)


def column_stage(spectra, table, table_t, coefs, lane_factors, epoch_count, epochs, rates, chunk):
    devices, loc_rows, core_lanes = spectra.shape
    length = table.shape[0]
    lanes = core_lanes * epoch_count
    width = lanes // epochs
    block = COLUMN_BLOCK
    steps = length // block
    return pl.pallas_call(
        functools.partial(column_kernel, epoch_count, epochs, rates),
        grid=(2 * steps,),
        in_specs=[
            pl.BlockSpec(spectra.shape, lambda i: (0, 0, 0)),
            pl.BlockSpec((block, length), lambda i: (jnp.minimum(i, steps - 1), 0)),
            pl.BlockSpec((block, length), lambda i: (jnp.maximum(i - steps, 0), 0)),
            pl.BlockSpec((block // 2, coefs.shape[1]), lambda i: (jnp.minimum(i, steps - 1), 0)),
            pl.BlockSpec(lane_factors.shape, lambda i: (0, 0)),
        ],
        out_specs=pl.BlockSpec(
            (devices // steps, loc_rows // 2, 2 * width), lambda i: (jnp.maximum(i - steps, 0), 0, 0)
        ),
        out_shape=jax.ShapeDtypeStruct((devices, loc_rows // 2, 2 * width), jnp.bfloat16),
        scratch_shapes=[
            pltpu.VMEM((length, lanes), jnp.bfloat16),
            pltpu.VMEM((length, rates * width), jnp.bfloat16),
        ],
        compiler_params=pltpu.CompilerParams(vmem_limit_bytes=VMEM_LIMIT),
        cost_estimate=cost(
            2 * length * length * (epochs + rates) * width,
            4 * length * length + 4 * coefs.size + 4 * spectra.size,
        ),
        name=f"column_stage_{chunk}",
    )(spectra, table, table_t, coefs, lane_factors)


def image_kernel(has_partial, back_ref, table_ref, *refs):
    out_ref, left = refs[-2:]
    devices, half_rows, two_widths = back_ref.shape
    width = two_widths // 2

    @pl.when(pl.program_id(0) == 0)
    def _():
        per_tile = 128 // width
        for tile in range(devices * width // 128):
            blocks = [back_ref[tile * per_tile + part] for part in range(per_tile)]
            if per_tile == 2:
                blocks = [block.astype(jnp.float32) for block in blocks]
                sides = pair_lanes(blocks[0], blocks[1], width)
            else:
                sides = [
                    jnp.concatenate([block[:, :width] for block in blocks], axis=1),
                    jnp.concatenate([block[:, width:] for block in blocks], axis=1),
                ]
            for side in range(2):
                at = slice(side * half_rows, (side + 1) * half_rows)
                left[at, tile * 128 : (tile + 1) * 128] = sides[side].astype(jnp.bfloat16)

    pixels = jnp.dot(left[...], table_ref[...], preferred_element_type=jnp.float32)
    if has_partial:
        pixels = pixels + refs[0][...].reshape(pixels.shape)
    out_ref[...] = pixels.reshape(out_ref.shape)


def image_rows(back, table, partial, chunk, chunks):
    devices, half_rows, two_widths = back.shape
    length = table.shape[0]
    depth = devices * two_widths // 2
    rows = 2 * half_rows
    block = IMAGE_BLOCK
    image_spec = pl.BlockSpec((1, rows, block), lambda i: (0, 0, i))
    return pl.pallas_call(
        functools.partial(image_kernel, partial is not None),
        grid=(length // block,),
        in_specs=[
            pl.BlockSpec(back.shape, lambda i: (0, 0, 0)),
            pl.BlockSpec((depth, block), lambda i: (chunk, i)),
        ]
        + ([] if partial is None else [image_spec]),
        out_specs=image_spec,
        out_shape=jax.ShapeDtypeStruct((1, rows, length), jnp.float32),
        scratch_shapes=[pltpu.VMEM((rows, depth), jnp.bfloat16)],
        compiler_params=pltpu.CompilerParams(vmem_limit_bytes=VMEM_LIMIT),
        cost_estimate=cost(
            2 * rows * depth * length, 2 * depth * length + 8 * rows * length
        ),
        name=f"image_rows_{chunk}",
    )(back, table, *([] if partial is None else [partial]))


def turn_angle(turns, whole):
    return (turns % whole).astype(jnp.float32) * (2.0 * math.pi / whole)


def row_factors(shift_y, rates, width, length):
    half = length // 2
    freqs = jnp.arange(half, dtype=jnp.int32)[None, :]
    angles = turn_angle(shift_y * (freqs - half), SUBPIX * length)
    coefs = jnp.concatenate(
        [
            jnp.where(freqs == 0, 1.0, 2.0 * jnp.cos(angles)),
            jnp.where(freqs == 0, 0.0, 2.0 * jnp.sin(angles)),
        ]
    )
    spread = jnp.broadcast_to(coefs.T[:, :, None], (half, coefs.shape[0], width))
    return spread.reshape(half, coefs.shape[0] * width)


def column_factors(shift_y, shift_x, rates, epochs, first_freq, cols, length):
    half = length // 2
    lane = jnp.arange(2 * cols, dtype=jnp.int32)[None, :]
    freqs = first_freq + lane % cols
    is_sine = lane >= cols
    paired = freqs == 0
    zero_col = paired & ~is_sine
    angles = turn_angle(shift_x * (freqs - half), SUBPIX * length)
    scale = 1.0 / math.sqrt(epochs)
    ramp_cos = jnp.where(paired, scale, 2.0 * scale * jnp.cos(angles))
    ramp_sin = jnp.where(paired, 0.0, 2.0 * scale * jnp.sin(angles))
    ramp_sin = jnp.where(is_sine, ramp_sin, -ramp_sin)
    cos_x = jnp.cos(turn_angle(shift_x, 2 * SUBPIX))
    cos_y = jnp.cos(turn_angle(shift_y, 2 * SUBPIX))
    cos_xy = jnp.cos(turn_angle(shift_x + shift_y, 2 * SUBPIX))
    main = jnp.where(zero_col, cos_y, cos_xy)
    lead = jnp.where(zero_col, 1.0, cos_x)
    factors = jnp.stack([main * ramp_cos, main * ramp_sin, lead * ramp_cos, lead * ramp_sin])
    return factors.reshape(4 * rates, epochs * 2 * cols)


def local(images, rate_vectors, epoch_times):
    loc_epochs, loc_rows, length = images.shape
    epoch_count = lax.axis_size("epoch")
    devices = lax.axis_size("row") * epoch_count
    device = lax.axis_index("row") * epoch_count + lax.axis_index("epoch")
    rates, epochs = rate_vectors.shape[0], epoch_times.shape[0]
    chunks = max(1, min(CHUNKS, length // 2 // devices // MIN_COLS))
    cols = length // 2 // devices // chunks
    table = packed_table(length, cols)
    table_t = jnp.asarray(np.ascontiguousarray(table.T))
    table = jnp.asarray(table)
    period = SUBPIX * length
    shift_y = (rate_vectors[:, 0:1] * epoch_times[None, :] % period).reshape(-1, 1)
    shift_x = (rate_vectors[:, 1:2] * epoch_times[None, :] % period).reshape(-1, 1)
    coefs = row_factors(shift_y, rates, 2 * cols, length)

    def exchange(values):
        return lax.all_to_all(values, ("row", "epoch"), 0, 0, tiled=True)

    spectra = [
        exchange(row_transform(images, table_t, chunk, chunks, devices)) for chunk in range(chunks)
    ]
    backs = []
    for chunk in range(chunks):
        first_freq = (chunk * devices + device) * cols
        factors = column_factors(shift_y, shift_x, rates, epochs, first_freq, cols, length)
        backs.append(
            exchange(
                column_stage(
                    spectra[chunk], table, table_t, coefs, factors, epoch_count, epochs, rates, chunk
                )
            )
        )
    result = None
    for chunk in range(chunks):
        result = image_rows(backs[chunk], table, result, chunk, chunks)
    return result


def solution(mesh):
    in_specs = (P(("group", "epoch"), "row", None), P(), P())
    out_specs = P(("group", "epoch"), "row", None)
    return jax.shard_map(local, mesh=mesh, in_specs=in_specs, out_specs=out_specs, check_vma=False)
```

```python
import functools
import math

import jax
import jax.numpy as jnp
import ml_dtypes
import numpy as np
from jax import lax
from jax.experimental import pallas as pl
from jax.experimental.pallas import tpu as pltpu
from jax.sharding import PartitionSpec as P

SUBPIX = 16
CHUNKS = 2
MIN_COLS = 32
PAIRWISE_LIMIT = 16
ROW_BLOCK = 512
COLUMN_BLOCK = 512
IMAGE_BLOCK = 512
VMEM_LIMIT = 44 * 1024 * 1024


def packed_table(length, cols):
    half = length // 2
    freqs = np.arange(half, dtype=np.int32)
    positions = np.arange(length, dtype=np.int32)
    turns = freqs[:, None] * positions[None, :] % length
    angles = turns.astype(np.float32) * np.float32(2.0 * math.pi / length)
    factor = np.float32(1.0 / math.sqrt(length))
    cosine = np.cos(angles) * factor
    sine = np.sin(angles) * factor
    sine[0] = np.where(positions % 2 == 0, factor, -factor)
    blocks = np.stack([cosine.reshape(-1, cols, length), sine.reshape(-1, cols, length)], axis=1)
    return blocks.reshape(length, length).astype(ml_dtypes.bfloat16)


def cost(flops, bytes_accessed):
    return pl.CostEstimate(flops=flops, bytes_accessed=bytes_accessed, transcendentals=0)


def is_low(shape, group):
    return lax.broadcasted_iota(jnp.int32, shape, 1) % (2 * group) < group


def pair_lanes(upper, lower, width):
    count = upper.shape[1] // width
    if 2 * width == 128:
        parts = []
        low = is_low((upper.shape[0], 128), width)
        for tile in range(count // 2):
            first = upper[:, tile * 128 : (tile + 1) * 128]
            second = lower[:, tile * 128 : (tile + 1) * 128]
            parts.append(jnp.where(low, first, pltpu.roll(second, width, axis=1)))
            parts.append(jnp.where(low, pltpu.roll(first, width, axis=1), second))
        return parts
    groups = [slice(group * width, (group + 1) * width) for group in range(count)]
    return [jnp.concatenate([upper[:, group], lower[:, group]], axis=1) for group in groups]


def row_kernel(images_ref, table_ref, out_ref):
    loc_epochs, loc_rows, length = images_ref.shape
    dests, _, width = out_ref.shape
    pixels = images_ref[...].reshape(loc_epochs * loc_rows, length)
    terms = jnp.dot(pixels, table_ref[...], preferred_element_type=jnp.float32)
    if loc_epochs == 2:
        parts = pair_lanes(terms[:loc_rows], terms[loc_rows:], width // 2)
    else:
        by_epoch = terms.reshape(loc_epochs, loc_rows, terms.shape[1])
        one = width // loc_epochs
        parts = [
            jnp.concatenate(
                [by_epoch[loc][:, dest * one : (dest + 1) * one] for loc in range(loc_epochs)],
                axis=1,
            )
            for dest in range(dests)
        ]
    for dest in range(dests):
        out_ref[dest] = parts[dest].astype(jnp.bfloat16)


def row_transform(images, table_t, chunk, chunks, devices):
    loc_epochs, loc_rows, length = images.shape
    columns = length // chunks
    width = columns // devices * loc_epochs
    block = min(ROW_BLOCK, columns)
    steps = columns // block
    dests = devices // steps
    return pl.pallas_call(
        row_kernel,
        grid=(steps,),
        in_specs=[
            pl.BlockSpec((loc_epochs, loc_rows, length), lambda i: (0, 0, 0)),
            pl.BlockSpec((length, block), lambda i: (0, chunk * steps + i)),
        ],
        out_specs=pl.BlockSpec((dests, loc_rows, width), lambda i: (i, 0, 0)),
        out_shape=jax.ShapeDtypeStruct((devices, loc_rows, width), jnp.bfloat16),
        compiler_params=pltpu.CompilerParams(vmem_limit_bytes=VMEM_LIMIT),
        cost_estimate=cost(
            2 * loc_epochs * loc_rows * length * columns,
            2 * length * columns + 4 * loc_epochs * loc_rows * length,
        ),
        name=f"row_transform_{chunk}",
    )(images, table_t)


def fold_epochs(sums, epochs, width):
    if len(sums) == 2 and epochs == 4 and width == 64:
        halves = [part[:, :128] + part[:, 128:] for part in sums]
        low = is_low(halves[0].shape, 64)
        kept = jnp.where(low, halves[0], halves[1])
        return kept + pltpu.roll(jnp.where(low, halves[1], halves[0]), 64, axis=1)
    folded = [
        sum(part[:, epoch * width : (epoch + 1) * width] for epoch in range(epochs))
        for part in sums
    ]
    return jnp.concatenate(folded, axis=1)


def swap_halves(values, cols):
    total = values.shape[1]
    if total == 128:
        low = is_low(values.shape, cols)
        ahead = pltpu.roll(values, 128 - cols, axis=1)
        return jnp.where(low, ahead, pltpu.roll(values, cols, axis=1))
    parts = [values[:, start : start + cols] for start in range(0, total, cols)]
    return jnp.concatenate([parts[index ^ 1] for index in range(len(parts))], axis=1)


def column_kernel(
    epoch_count, epochs, rates, z_ref, table_ref, table_t_ref, coef_ref, lane_ref, out_ref, z_all, sums
):
    devices, loc_rows, core_lanes = z_ref.shape
    row_count = devices // epoch_count
    lanes = core_lanes * epoch_count
    width = lanes // epochs
    cols = width // 2
    block = table_ref.shape[0]
    half_steps = pl.num_programs(0) // 2
    step = pl.program_id(0)

    @pl.when(step == 0)
    def _():
        for row in range(row_count):
            parts = [z_ref[row * epoch_count + core] for core in range(epoch_count)]
            z_all[row * loc_rows : (row + 1) * loc_rows, :] = jnp.concatenate(parts, axis=1)

    @pl.when(step < half_steps)
    def _():
        products = jnp.dot(table_ref[...], z_all[...], preferred_element_type=jnp.float32)
        groups = block // width
        products = products.reshape(groups, 2, cols, lanes)
        even = products[:, 0].reshape(groups * cols, lanes)
        odd = products[:, 1].reshape(groups * cols, lanes)
        straight, crossed, lead = ([], []), ([], []), ([], [])
        for rate in range(rates):
            cos_row = coef_ref[:, rate * lanes : (rate + 1) * lanes]
            sin_row = coef_ref[:, (rates + rate) * lanes : (rates + rate + 1) * lanes]
            turned = (cos_row * even + sin_row * odd, cos_row * odd - sin_row * even)
            for which in range(2):
                straight[which].append(turned[which] * lane_ref[rate : rate + 1, :])
                crossed[which].append(turned[which] * lane_ref[rates + rate : rates + rate + 1, :])
                at = (2 + which) * rates + rate
                lead[which].append(even[:8] * lane_ref[at : at + 1, :])

        def collect(plain, turned):
            summed = fold_epochs(plain, epochs, width)
            return summed + swap_halves(fold_epochs(turned, epochs, width), cols)

        even_sum = collect(straight[0], crossed[0])
        odd_sum = collect(straight[1], crossed[1])
        lead_sum = collect(lead[0], lead[1])
        first = lax.broadcasted_iota(jnp.int32, even_sum.shape, 0) == 0
        even_sum = jnp.where(first & (step == 0), lead_sum[0:1], even_sum)
        both = jnp.stack(
            [part.reshape(groups, cols, rates * width) for part in (even_sum, odd_sum)], axis=1
        )
        start = pl.multiple_of(step * block, block)
        sums[pl.ds(start, block), :] = both.reshape(block, rates * width).astype(jnp.bfloat16)

    @pl.when(step >= half_steps)
    def _():
        back = jnp.dot(table_t_ref[...], sums[...], preferred_element_type=jnp.float32)
        half_rows = loc_rows // 2
        for row in range(block // loc_rows):
            part = back[row * loc_rows : (row + 1) * loc_rows]
            pairs = pair_lanes(part[:half_rows], part[half_rows:], width)
            for rate in range(rates):
                out_ref[row * rates + rate] = pairs[rate].astype(jnp.bfloat16)


def column_stage(spectra, table, table_t, coefs, lane_factors, epoch_count, epochs, rates, chunk):
    devices, loc_rows, core_lanes = spectra.shape
    length = table.shape[0]
    lanes = core_lanes * epoch_count
    width = lanes // epochs
    block = COLUMN_BLOCK
    steps = length // block
    return pl.pallas_call(
        functools.partial(column_kernel, epoch_count, epochs, rates),
        grid=(2 * steps,),
        in_specs=[
            pl.BlockSpec(spectra.shape, lambda i: (0, 0, 0)),
            pl.BlockSpec((block, length), lambda i: (jnp.minimum(i, steps - 1), 0)),
            pl.BlockSpec((block, length), lambda i: (jnp.maximum(i - steps, 0), 0)),
            pl.BlockSpec((block // 2, coefs.shape[1]), lambda i: (jnp.minimum(i, steps - 1), 0)),
            pl.BlockSpec(lane_factors.shape, lambda i: (0, 0)),
        ],
        out_specs=pl.BlockSpec(
            (devices // steps, loc_rows // 2, 2 * width), lambda i: (jnp.maximum(i - steps, 0), 0, 0)
        ),
        out_shape=jax.ShapeDtypeStruct((devices, loc_rows // 2, 2 * width), jnp.bfloat16),
        scratch_shapes=[
            pltpu.VMEM((length, lanes), jnp.bfloat16),
            pltpu.VMEM((length, rates * width), jnp.bfloat16),
        ],
        compiler_params=pltpu.CompilerParams(vmem_limit_bytes=VMEM_LIMIT),
        cost_estimate=cost(
            2 * length * length * (epochs + rates) * width,
            4 * length * length + 4 * coefs.size + 4 * spectra.size,
        ),
        name=f"column_stage_{chunk}",
    )(spectra, table, table_t, coefs, lane_factors)


def image_kernel(has_partial, back_ref, table_ref, *refs):
    out_ref, left = refs[-2:]
    devices, half_rows, two_widths = back_ref.shape
    width = two_widths // 2

    @pl.when(pl.program_id(0) == 0)
    def _():
        per_tile = 128 // width
        for tile in range(devices * width // 128):
            blocks = [back_ref[tile * per_tile + part] for part in range(per_tile)]
            if per_tile == 2:
                blocks = [block.astype(jnp.float32) for block in blocks]
                sides = pair_lanes(blocks[0], blocks[1], width)
            else:
                sides = [
                    jnp.concatenate([block[:, :width] for block in blocks], axis=1),
                    jnp.concatenate([block[:, width:] for block in blocks], axis=1),
                ]
            for side in range(2):
                at = slice(side * half_rows, (side + 1) * half_rows)
                left[at, tile * 128 : (tile + 1) * 128] = sides[side].astype(jnp.bfloat16)

    pixels = jnp.dot(left[...], table_ref[...], preferred_element_type=jnp.float32)
    if has_partial:
        pixels = pixels + refs[0][...].reshape(pixels.shape)
    out_ref[...] = pixels.reshape(out_ref.shape)


def image_rows(back, table, partial, chunk, chunks):
    devices, half_rows, two_widths = back.shape
    length = table.shape[0]
    depth = devices * two_widths // 2
    rows = 2 * half_rows
    block = IMAGE_BLOCK
    image_spec = pl.BlockSpec((1, rows, block), lambda i: (0, 0, i))
    return pl.pallas_call(
        functools.partial(image_kernel, partial is not None),
        grid=(length // block,),
        in_specs=[
            pl.BlockSpec(back.shape, lambda i: (0, 0, 0)),
            pl.BlockSpec((depth, block), lambda i: (chunk, i)),
        ]
        + ([] if partial is None else [image_spec]),
        out_specs=image_spec,
        out_shape=jax.ShapeDtypeStruct((1, rows, length), jnp.float32),
        scratch_shapes=[pltpu.VMEM((rows, depth), jnp.bfloat16)],
        compiler_params=pltpu.CompilerParams(vmem_limit_bytes=VMEM_LIMIT),
        cost_estimate=cost(
            2 * rows * depth * length, 2 * depth * length + 8 * rows * length
        ),
        name=f"image_rows_{chunk}",
    )(back, table, *([] if partial is None else [partial]))


def turn_angle(turns, whole):
    return (turns % whole).astype(jnp.float32) * (2.0 * math.pi / whole)


def row_factors(shift_y, rates, width, length):
    half = length // 2
    freqs = jnp.arange(half, dtype=jnp.int32)[None, :]
    angles = turn_angle(shift_y * (freqs - half), SUBPIX * length)
    coefs = jnp.concatenate(
        [
            jnp.where(freqs == 0, 1.0, 2.0 * jnp.cos(angles)),
            jnp.where(freqs == 0, 0.0, 2.0 * jnp.sin(angles)),
        ]
    )
    spread = jnp.broadcast_to(coefs.T[:, :, None], (half, coefs.shape[0], width))
    return spread.reshape(half, coefs.shape[0] * width)


def column_factors(shift_y, shift_x, rates, epochs, first_freq, cols, length):
    half = length // 2
    lane = jnp.arange(2 * cols, dtype=jnp.int32)[None, :]
    freqs = first_freq + lane % cols
    is_sine = lane >= cols
    paired = freqs == 0
    zero_col = paired & ~is_sine
    angles = turn_angle(shift_x * (freqs - half), SUBPIX * length)
    scale = 1.0 / math.sqrt(epochs)
    ramp_cos = jnp.where(paired, scale, 2.0 * scale * jnp.cos(angles))
    ramp_sin = jnp.where(paired, 0.0, 2.0 * scale * jnp.sin(angles))
    ramp_sin = jnp.where(is_sine, ramp_sin, -ramp_sin)
    cos_x = jnp.cos(turn_angle(shift_x, 2 * SUBPIX))
    cos_y = jnp.cos(turn_angle(shift_y, 2 * SUBPIX))
    cos_xy = jnp.cos(turn_angle(shift_x + shift_y, 2 * SUBPIX))
    main = jnp.where(zero_col, cos_y, cos_xy)
    lead = jnp.where(zero_col, 1.0, cos_x)
    factors = jnp.stack([main * ramp_cos, main * ramp_sin, lead * ramp_cos, lead * ramp_sin])
    return factors.reshape(4 * rates, epochs * 2 * cols)


def local(images, rate_vectors, epoch_times):
    loc_epochs, loc_rows, length = images.shape
    epoch_count = lax.axis_size("epoch")
    devices = lax.axis_size("row") * epoch_count
    device = lax.axis_index("row") * epoch_count + lax.axis_index("epoch")
    rates, epochs = rate_vectors.shape[0], epoch_times.shape[0]
    chunks = max(1, min(CHUNKS, length // 2 // devices // MIN_COLS))
    cols = length // 2 // devices // chunks
    table = packed_table(length, cols)
    table_t = jnp.asarray(np.ascontiguousarray(table.T))
    table = jnp.asarray(table)
    period = SUBPIX * length
    shift_y = (rate_vectors[:, 0:1] * epoch_times[None, :] % period).reshape(-1, 1)
    shift_x = (rate_vectors[:, 1:2] * epoch_times[None, :] % period).reshape(-1, 1)
    coefs = row_factors(shift_y, rates, 2 * cols, length)

    def exchange(values):
        if devices > PAIRWISE_LIMIT:
            return lax.all_to_all(values, ("row", "epoch"), 0, 0, tiled=True)
        received = values
        for offset in range(1, devices):
            sent = lax.dynamic_index_in_dim(values, device ^ offset, 0, keepdims=True)
            pairs = [(index, index ^ offset) for index in range(devices)]
            arrived = lax.ppermute(sent, ("row", "epoch"), pairs)
            received = lax.dynamic_update_slice_in_dim(received, arrived, device ^ offset, 0)
        return received

    spectra = [
        exchange(row_transform(images, table_t, chunk, chunks, devices)) for chunk in range(chunks)
    ]
    backs = []
    for chunk in range(chunks):
        first_freq = (chunk * devices + device) * cols
        factors = column_factors(shift_y, shift_x, rates, epochs, first_freq, cols, length)
        backs.append(
            exchange(
                column_stage(
                    spectra[chunk], table, table_t, coefs, factors, epoch_count, epochs, rates, chunk
                )
            )
        )
    result = None
    for chunk in range(chunks):
        result = image_rows(backs[chunk], table, result, chunk, chunks)
    return result


def solution(mesh):
    in_specs = (P(("group", "epoch"), "row", None), P(), P())
    out_specs = P(("group", "epoch"), "row", None)
    return jax.shard_map(local, mesh=mesh, in_specs=in_specs, out_specs=out_specs, check_vma=False)
```

```python
import functools
import math

import jax
import jax.numpy as jnp
import ml_dtypes
import numpy as np
from jax import lax
from jax.experimental import pallas as pl
from jax.experimental.pallas import tpu as pltpu
from jax.sharding import PartitionSpec as P

SUBPIX = 16
CHUNKS = 2
MIN_COLS = 64
BLOCK = 512
VMEM_LIMIT = 40 * 1024 * 1024


def packed_table(length, cols):
    half = length // 2
    freqs = np.arange(half, dtype=np.int32)
    positions = np.arange(length, dtype=np.int32)
    turns = freqs[:, None] * positions[None, :] % length
    angles = turns.astype(np.float32) * np.float32(2.0 * math.pi / length)
    factor = np.float32(1.0 / math.sqrt(length))
    cosine = np.cos(angles) * factor
    sine = np.sin(angles) * factor
    sine[0] = np.where(positions % 2 == 0, factor, -factor)
    blocks = np.stack([cosine.reshape(-1, cols, length), sine.reshape(-1, cols, length)], axis=1)
    return blocks.reshape(length, length).astype(ml_dtypes.bfloat16)


def cost(flops, bytes_accessed):
    return pl.CostEstimate(flops=flops, bytes_accessed=bytes_accessed, transcendentals=0)


def row_kernel(images_ref, table_ref, out_ref, total):
    loc_epochs, loc_rows, depth = images_ref.shape
    dests, _, lanes = out_ref.shape
    width = lanes // loc_epochs
    step = pl.program_id(0)
    pixels = images_ref[...].reshape(loc_epochs * loc_rows, depth)
    terms = jnp.dot(pixels, table_ref[...], preferred_element_type=jnp.float32)

    @pl.when(step == 0)
    def _():
        total[...] = terms

    @pl.when(step > 0)
    def _():
        total[...] += terms

    @pl.when(step == pl.num_programs(0) - 1)
    def _():
        for dest in range(dests):
            for loc in range(loc_epochs):
                part = total[loc * loc_rows : (loc + 1) * loc_rows, dest * width : (dest + 1) * width]
                out_ref[dest, :, loc * width : (loc + 1) * width] = part.astype(jnp.bfloat16)


def row_transform(images, table_t, chunk, chunks, row_count):
    loc_epochs, loc_rows, length = images.shape
    columns = length // chunks
    lanes = columns // row_count * loc_epochs
    steps = length // BLOCK
    rows = loc_epochs * loc_rows
    return pl.pallas_call(
        row_kernel,
        grid=(steps,),
        in_specs=[
            pl.BlockSpec((loc_epochs, loc_rows, BLOCK), lambda i: (0, 0, i)),
            pl.BlockSpec((BLOCK, columns), lambda i: (i, chunk)),
        ],
        out_specs=pl.BlockSpec((row_count, loc_rows, lanes), lambda i: (0, 0, 0)),
        out_shape=jax.ShapeDtypeStruct((row_count, loc_rows, lanes), jnp.bfloat16),
        scratch_shapes=[pltpu.VMEM((rows, columns), jnp.float32)],
        compiler_params=pltpu.CompilerParams(vmem_limit_bytes=VMEM_LIMIT),
        cost_estimate=cost(2 * rows * length * columns, 2 * length * columns + 4 * rows * length),
        name=f"row_transform_{chunk}",
    )(images, table_t)


def swap_halves(values):
    width = values.shape[1]
    if width % 128 == 0:
        return pltpu.roll(values, width // 2, axis=1)
    return jnp.concatenate([values[:, width // 2 :], values[:, : width // 2]], axis=1)


def stack_kernel(rates, loc_epochs, z_ref, table_ref, coef_ref, lane_ref, *out_refs):
    width = z_ref.shape[1] // loc_epochs
    cols = width // 2
    block = table_ref.shape[0]
    groups = block // width
    pairs = rates * loc_epochs
    step = pl.program_id(0)
    products = jnp.dot(table_ref[...], z_ref[...], preferred_element_type=jnp.float32)
    products = products.reshape(groups, 2, cols, loc_epochs * width)
    even = products[:, 0].reshape(groups * cols, loc_epochs * width)
    odd = products[:, 1].reshape(groups * cols, loc_epochs * width)
    first = lax.broadcasted_iota(jnp.int32, (groups * cols, width), 0) == 0
    for rate in range(rates):
        straight, crossed, lead = [0.0, 0.0], [0.0, 0.0], [0.0, 0.0]
        for epoch in range(loc_epochs):
            pair = rate * loc_epochs + epoch
            even_part = even[:, epoch * width : (epoch + 1) * width]
            odd_part = odd[:, epoch * width : (epoch + 1) * width]
            cos_row = coef_ref[:, pair : pair + 1]
            sin_row = coef_ref[:, pairs + pair : pairs + pair + 1]
            turned = (
                cos_row * even_part + sin_row * odd_part,
                cos_row * odd_part - sin_row * even_part,
            )
            factors = [lane_ref[kind * pairs + pair : kind * pairs + pair + 1, :] for kind in range(4)]
            for which in range(2):
                straight[which] += turned[which] * factors[0]
                crossed[which] += turned[which] * factors[1]
                lead[which] += even_part[:8] * factors[2 + which]
        even_sum = straight[0] + swap_halves(crossed[0])
        odd_sum = straight[1] + swap_halves(crossed[1])
        lead_sum = lead[0] + swap_halves(lead[1])
        even_sum = jnp.where(first & (step == 0), lead_sum[0:1], even_sum)
        both = jnp.stack(
            [part.reshape(groups, cols, width) for part in (even_sum, odd_sum)], axis=1
        )
        out_refs[rate][...] = both.reshape(block, width).astype(jnp.bfloat16)


def stack_rates(spectra, table, coefs, lane_factors, rates, loc_epochs, chunk):
    length, lanes = spectra.shape
    width = lanes // loc_epochs
    return pl.pallas_call(
        functools.partial(stack_kernel, rates, loc_epochs),
        grid=(length // BLOCK,),
        in_specs=[
            pl.BlockSpec(spectra.shape, lambda i: (0, 0)),
            pl.BlockSpec((BLOCK, length), lambda i: (i, 0)),
            pl.BlockSpec((BLOCK // 2, coefs.shape[1]), lambda i: (i, 0)),
            pl.BlockSpec(lane_factors.shape, lambda i: (0, 0)),
        ],
        out_specs=[pl.BlockSpec((BLOCK, width), lambda i: (i, 0))] * rates,
        out_shape=[jax.ShapeDtypeStruct((length, width), jnp.bfloat16)] * rates,
        compiler_params=pltpu.CompilerParams(vmem_limit_bytes=VMEM_LIMIT),
        cost_estimate=cost(2 * length * length * lanes, 2 * length * length + 4 * length * lanes),
        name=f"stack_rates_{chunk}",
    )(spectra, table, coefs, lane_factors)


CONTRACT_FIRST = (((0,), (0,)), ((), ()))


def inverse_kernel(own_ref, other_ref, table_ref, out_ref, sums):
    dests, _, loc_rows = out_ref.shape

    @pl.when(pl.program_id(0) == 0)
    def _():
        total = own_ref[...].astype(jnp.float32) + other_ref[...].astype(jnp.float32)
        sums[...] = total.T.astype(jnp.bfloat16)

    back = jnp.dot(sums[...], table_ref[...], preferred_element_type=jnp.float32)
    back = back.astype(jnp.bfloat16)
    for dest in range(dests):
        out_ref[dest] = back[:, dest * loc_rows : (dest + 1) * loc_rows]


def inverse_columns(own, other, table, row_count, chunk):
    length, width = own.shape
    loc_rows = length // row_count
    dests = BLOCK // loc_rows
    return pl.pallas_call(
        inverse_kernel,
        grid=(length // BLOCK,),
        in_specs=[
            pl.BlockSpec(own.shape, lambda i: (0, 0)),
            pl.BlockSpec(own.shape, lambda i: (0, 0)),
            pl.BlockSpec((length, BLOCK), lambda i: (0, i)),
        ],
        out_specs=pl.BlockSpec((dests, width, loc_rows), lambda i: (i, 0, 0)),
        out_shape=jax.ShapeDtypeStruct((row_count, width, loc_rows), jnp.bfloat16),
        scratch_shapes=[pltpu.VMEM((width, length), jnp.bfloat16)],
        compiler_params=pltpu.CompilerParams(vmem_limit_bytes=VMEM_LIMIT),
        cost_estimate=cost(2 * length * length * width, 2 * length * length + 6 * length * width),
        name=f"inverse_columns_{chunk}",
    )(own, other, table)


def image_kernel(has_partial, back_ref, table_ref, *refs):
    out_ref, left = refs[-2:]

    @pl.when(pl.program_id(0) == 0)
    def _():
        left[...] = back_ref[...].T

    pixels = jnp.dot(left[...], table_ref[...], preferred_element_type=jnp.float32)
    if has_partial:
        pixels = pixels + refs[0][0]
    out_ref[0] = pixels


def image_rows(back, table, partial, chunk):
    depth, rows = back.shape
    length = table.shape[0]
    image_spec = pl.BlockSpec((1, rows, BLOCK), lambda i: (0, 0, i))
    partials = [] if partial is None else [partial]
    return pl.pallas_call(
        functools.partial(image_kernel, partial is not None),
        grid=(length // BLOCK,),
        in_specs=[
            pl.BlockSpec(back.shape, lambda i: (0, 0)),
            pl.BlockSpec((depth, BLOCK), lambda i: (chunk, i)),
        ]
        + [image_spec] * len(partials),
        out_specs=image_spec,
        out_shape=jax.ShapeDtypeStruct((1, rows, length), jnp.float32),
        scratch_shapes=[pltpu.VMEM((rows, depth), jnp.bfloat16)],
        compiler_params=pltpu.CompilerParams(vmem_limit_bytes=VMEM_LIMIT),
        cost_estimate=cost(2 * rows * depth * length, 2 * depth * length + 8 * rows * length),
        name=f"image_rows_{chunk}",
    )(back, table, *partials)


def turn_angle(turns, whole):
    return (turns % whole).astype(jnp.float32) * (2.0 * math.pi / whole)


def row_factors(shift_y, length):
    half = length // 2
    freqs = jnp.arange(half, dtype=jnp.int32)[:, None]
    angles = turn_angle((freqs - half) * shift_y[None, :], SUBPIX * length)
    return jnp.concatenate(
        [
            jnp.where(freqs == 0, 1.0, 2.0 * jnp.cos(angles)),
            jnp.where(freqs == 0, 0.0, 2.0 * jnp.sin(angles)),
        ],
        axis=1,
    )


def column_factors(shift_y, shift_x, scale, first_freq, cols, length):
    half = length // 2
    shift_y, shift_x = shift_y[:, None], shift_x[:, None]
    lane = jnp.arange(2 * cols, dtype=jnp.int32)[None, :]
    freqs = first_freq + lane % cols
    is_sine = lane >= cols
    paired = freqs == 0
    zero_col = paired & ~is_sine
    angles = turn_angle(shift_x * (freqs - half), SUBPIX * length)
    ramp_cos = jnp.where(paired, scale, 2.0 * scale * jnp.cos(angles))
    ramp_sin = jnp.where(paired, 0.0, 2.0 * scale * jnp.sin(angles))
    ramp_sin = jnp.where(is_sine, ramp_sin, -ramp_sin)
    cos_x = jnp.cos(turn_angle(shift_x, 2 * SUBPIX))
    cos_y = jnp.cos(turn_angle(shift_y, 2 * SUBPIX))
    cos_xy = jnp.cos(turn_angle(shift_x + shift_y, 2 * SUBPIX))
    main = jnp.where(zero_col, cos_y, cos_xy)
    lead = jnp.where(zero_col, 1.0, cos_x)
    return jnp.concatenate([main * ramp_cos, main * ramp_sin, lead * ramp_cos, lead * ramp_sin])


def local(images, rate_vectors, epoch_times):
    loc_epochs, loc_rows, length = images.shape
    row_count = lax.axis_size("row")
    row_pos, core = lax.axis_index("row"), lax.axis_index("epoch")
    rates, epochs = rate_vectors.shape[0], epoch_times.shape[0]
    chunks = max(1, min(CHUNKS, length // 2 // row_count // MIN_COLS))
    cols = length // 2 // row_count // chunks
    table = packed_table(length, cols)
    table_t = jnp.asarray(np.ascontiguousarray(table.T))
    table = jnp.asarray(table)
    period = SUBPIX * length
    own_times = lax.dynamic_slice_in_dim(epoch_times, core * loc_epochs, loc_epochs)
    own_first = jnp.where(core == 0, rate_vectors, rate_vectors[::-1])
    shift_y = (own_first[:, 0:1] * own_times[None, :] % period).reshape(-1)
    shift_x = (own_first[:, 1:2] * own_times[None, :] % period).reshape(-1)
    coefs = row_factors(shift_y, length)
    scale = 1.0 / math.sqrt(epochs)

    def exchange(values):
        return lax.all_to_all(values, "row", 0, 0, tiled=True)

    spectra = [
        exchange(row_transform(images, table_t, chunk, chunks, row_count))
        for chunk in range(chunks)
    ]
    backs = []
    for chunk in range(chunks):
        first_freq = (chunk * row_count + row_pos) * cols
        factors = column_factors(shift_y, shift_x, scale, first_freq, cols, length)
        own, other = stack_rates(
            spectra[chunk].reshape(length, -1), table, coefs, factors, rates, loc_epochs, chunk
        )
        other = lax.ppermute(other, "epoch", [(0, 1), (1, 0)])
        backs.append(exchange(inverse_columns(own, other, table, row_count, chunk)))
    result = None
    for chunk in range(chunks):
        result = image_rows(backs[chunk].reshape(-1, loc_rows), table, result, chunk)
    return result


def solution(mesh):
    in_specs = (P(("group", "epoch"), "row", None), P(), P())
    out_specs = P(("group", "epoch"), "row", None)
    return jax.shard_map(local, mesh=mesh, in_specs=in_specs, out_specs=out_specs, check_vma=False)
```

```python
import functools
import math

import jax
import jax.numpy as jnp
import ml_dtypes
import numpy as np
from jax import lax
from jax.experimental import pallas as pl
from jax.experimental.pallas import tpu as pltpu
from jax.sharding import PartitionSpec as P

SUBPIX = 16
CHUNKS = 2
MIN_COLS = 64
BLOCK = 512
VMEM_LIMIT = 58 * 1024 * 1024


def packed_table(length, cols):
    half = length // 2
    freqs = np.arange(half, dtype=np.int32)
    positions = np.arange(length, dtype=np.int32)
    turns = freqs[:, None] * positions[None, :] % length
    angles = turns.astype(np.float32) * np.float32(2.0 * math.pi / length)
    factor = np.float32(1.0 / math.sqrt(length))
    cosine = np.cos(angles) * factor
    sine = np.sin(angles) * factor
    sine[0] = np.where(positions % 2 == 0, factor, -factor)
    blocks = np.stack([cosine.reshape(-1, cols, length), sine.reshape(-1, cols, length)], axis=1)
    return blocks.reshape(length, length).astype(ml_dtypes.bfloat16)


def cost(flops, bytes_accessed):
    return pl.CostEstimate(flops=flops, bytes_accessed=bytes_accessed, transcendentals=0)


def row_kernel(images_ref, table_ref, out_ref, total):
    loc_epochs, loc_rows, depth = images_ref.shape
    dests, _, lanes = out_ref.shape
    width = lanes // loc_epochs
    step = pl.program_id(0)
    pixels = images_ref[...].reshape(loc_epochs * loc_rows, depth)
    terms = jnp.dot(pixels, table_ref[...], preferred_element_type=jnp.float32)

    @pl.when(step == 0)
    def _():
        total[...] = terms

    @pl.when(step > 0)
    def _():
        total[...] += terms

    @pl.when(step == pl.num_programs(0) - 1)
    def _():
        for dest in range(dests):
            for loc in range(loc_epochs):
                part = total[loc * loc_rows : (loc + 1) * loc_rows, dest * width : (dest + 1) * width]
                out_ref[dest, :, loc * width : (loc + 1) * width] = part.astype(jnp.bfloat16)


def row_transform(images, table_t, chunk, chunks, row_count):
    loc_epochs, loc_rows, length = images.shape
    columns = length // chunks
    lanes = columns // row_count * loc_epochs
    steps = length // BLOCK
    rows = loc_epochs * loc_rows
    return pl.pallas_call(
        row_kernel,
        grid=(steps,),
        in_specs=[
            pl.BlockSpec((loc_epochs, loc_rows, BLOCK), lambda i: (0, 0, i)),
            pl.BlockSpec((BLOCK, columns), lambda i: (i, chunk)),
        ],
        out_specs=pl.BlockSpec((row_count, loc_rows, lanes), lambda i: (0, 0, 0)),
        out_shape=jax.ShapeDtypeStruct((row_count, loc_rows, lanes), jnp.bfloat16),
        scratch_shapes=[pltpu.VMEM((rows, columns), jnp.float32)],
        compiler_params=pltpu.CompilerParams(vmem_limit_bytes=VMEM_LIMIT),
        cost_estimate=cost(2 * rows * length * columns, 2 * length * columns + 4 * rows * length),
        name=f"row_transform_{chunk}",
    )(images, table_t)


def swap_halves(values):
    width = values.shape[1]
    if width % 128 == 0:
        return pltpu.roll(values, width // 2, axis=1)
    return jnp.concatenate([values[:, width // 2 :], values[:, : width // 2]], axis=1)


def stack_kernel(rates, loc_epochs, z_ref, table_ref, coef_ref, lane_ref, *out_refs):
    width = z_ref.shape[1] // loc_epochs
    cols = width // 2
    block = table_ref.shape[0]
    groups = block // width
    pairs = rates * loc_epochs
    step = pl.program_id(0)
    products = jnp.dot(table_ref[...], z_ref[...], preferred_element_type=jnp.float32)
    products = products.reshape(groups, 2, cols, loc_epochs * width)
    even = products[:, 0].reshape(groups * cols, loc_epochs * width)
    odd = products[:, 1].reshape(groups * cols, loc_epochs * width)
    first = lax.broadcasted_iota(jnp.int32, (groups * cols, width), 0) == 0
    for rate in range(rates):
        straight, crossed, lead = [0.0, 0.0], [0.0, 0.0], [0.0, 0.0]
        for epoch in range(loc_epochs):
            pair = rate * loc_epochs + epoch
            even_part = even[:, epoch * width : (epoch + 1) * width]
            odd_part = odd[:, epoch * width : (epoch + 1) * width]
            cos_row = coef_ref[:, pair : pair + 1]
            sin_row = coef_ref[:, pairs + pair : pairs + pair + 1]
            turned = (
                cos_row * even_part + sin_row * odd_part,
                cos_row * odd_part - sin_row * even_part,
            )
            factors = [lane_ref[kind * pairs + pair : kind * pairs + pair + 1, :] for kind in range(4)]
            for which in range(2):
                straight[which] += turned[which] * factors[0]
                crossed[which] += turned[which] * factors[1]
                lead[which] += even_part[:8] * factors[2 + which]
        even_sum = straight[0] + swap_halves(crossed[0])
        odd_sum = straight[1] + swap_halves(crossed[1])
        lead_sum = lead[0] + swap_halves(lead[1])
        even_sum = jnp.where(first & (step == 0), lead_sum[0:1], even_sum)
        both = jnp.stack(
            [part.reshape(groups, cols, width) for part in (even_sum, odd_sum)], axis=1
        )
        out_refs[rate][...] = both.reshape(block, width).astype(jnp.bfloat16)


def stack_rates(spectra, table, coefs, lane_factors, rates, loc_epochs, chunk):
    length, lanes = spectra.shape
    width = lanes // loc_epochs
    return pl.pallas_call(
        functools.partial(stack_kernel, rates, loc_epochs),
        grid=(length // BLOCK,),
        in_specs=[
            pl.BlockSpec(spectra.shape, lambda i: (0, 0)),
            pl.BlockSpec((BLOCK, length), lambda i: (i, 0)),
            pl.BlockSpec((BLOCK // 2, coefs.shape[1]), lambda i: (i, 0)),
            pl.BlockSpec(lane_factors.shape, lambda i: (0, 0)),
        ],
        out_specs=[pl.BlockSpec((BLOCK, width), lambda i: (i, 0))] * rates,
        out_shape=[jax.ShapeDtypeStruct((length, width), jnp.bfloat16)] * rates,
        compiler_params=pltpu.CompilerParams(vmem_limit_bytes=VMEM_LIMIT),
        cost_estimate=cost(2 * length * length * lanes, 2 * length * length + 4 * length * lanes),
        name=f"stack_rates_{chunk}",
    )(spectra, table, coefs, lane_factors)


CONTRACT_FIRST = (((0,), (0,)), ((), ()))


def inverse_kernel(own_ref, other_ref, table_ref, out_ref, sums):
    dests, _, loc_rows = out_ref.shape

    @pl.when(pl.program_id(0) == 0)
    def _():
        total = own_ref[...].astype(jnp.float32) + other_ref[...].astype(jnp.float32)
        sums[...] = total.T.astype(jnp.bfloat16)

    back = jnp.dot(sums[...], table_ref[...], preferred_element_type=jnp.float32)
    back = back.astype(jnp.bfloat16)
    for dest in range(dests):
        out_ref[dest] = back[:, dest * loc_rows : (dest + 1) * loc_rows]


def inverse_columns(own, other, table, row_count, chunk):
    length, width = own.shape
    loc_rows = length // row_count
    dests = BLOCK // loc_rows
    return pl.pallas_call(
        inverse_kernel,
        grid=(length // BLOCK,),
        in_specs=[
            pl.BlockSpec(own.shape, lambda i: (0, 0)),
            pl.BlockSpec(own.shape, lambda i: (0, 0)),
            pl.BlockSpec((length, BLOCK), lambda i: (0, i)),
        ],
        out_specs=pl.BlockSpec((dests, width, loc_rows), lambda i: (i, 0, 0)),
        out_shape=jax.ShapeDtypeStruct((row_count, width, loc_rows), jnp.bfloat16),
        scratch_shapes=[pltpu.VMEM((width, length), jnp.bfloat16)],
        compiler_params=pltpu.CompilerParams(vmem_limit_bytes=VMEM_LIMIT),
        cost_estimate=cost(2 * length * length * width, 2 * length * length + 6 * length * width),
        name=f"inverse_columns_{chunk}",
    )(own, other, table)


def image_kernel(has_partial, back_ref, table_ref, *refs):
    out_ref, left = refs[-2:]

    @pl.when(pl.program_id(0) == 0)
    def _():
        left[...] = back_ref[...].T

    pixels = jnp.dot(left[...], table_ref[...], preferred_element_type=jnp.float32)
    if has_partial:
        pixels = pixels + refs[0][0]
    out_ref[0] = pixels


def image_rows(back, table, partial, chunk):
    depth, rows = back.shape
    length = table.shape[0]
    image_spec = pl.BlockSpec((1, rows, BLOCK), lambda i: (0, 0, i))
    partials = [] if partial is None else [partial]
    return pl.pallas_call(
        functools.partial(image_kernel, partial is not None),
        grid=(length // BLOCK,),
        in_specs=[
            pl.BlockSpec(back.shape, lambda i: (0, 0)),
            pl.BlockSpec((depth, BLOCK), lambda i: (chunk, i)),
        ]
        + [image_spec] * len(partials),
        out_specs=image_spec,
        out_shape=jax.ShapeDtypeStruct((1, rows, length), jnp.float32),
        scratch_shapes=[pltpu.VMEM((rows, depth), jnp.bfloat16)],
        compiler_params=pltpu.CompilerParams(vmem_limit_bytes=VMEM_LIMIT),
        cost_estimate=cost(2 * rows * depth * length, 2 * depth * length + 8 * rows * length),
        name=f"image_rows_{chunk}",
    )(back, table, *partials)


def turn_angle(turns, whole):
    return (turns % whole).astype(jnp.float32) * (2.0 * math.pi / whole)


def row_factors(shift_y, length):
    half = length // 2
    freqs = jnp.arange(half, dtype=jnp.int32)[:, None]
    angles = turn_angle((freqs - half) * shift_y[None, :], SUBPIX * length)
    return jnp.concatenate(
        [
            jnp.where(freqs == 0, 1.0, 2.0 * jnp.cos(angles)),
            jnp.where(freqs == 0, 0.0, 2.0 * jnp.sin(angles)),
        ],
        axis=1,
    )


def column_factors(shift_y, shift_x, scale, first_freq, cols, length):
    half = length // 2
    shift_y, shift_x = shift_y[:, None], shift_x[:, None]
    lane = jnp.arange(2 * cols, dtype=jnp.int32)[None, :]
    freqs = first_freq + lane % cols
    is_sine = lane >= cols
    paired = freqs == 0
    zero_col = paired & ~is_sine
    angles = turn_angle(shift_x * (freqs - half), SUBPIX * length)
    ramp_cos = jnp.where(paired, scale, 2.0 * scale * jnp.cos(angles))
    ramp_sin = jnp.where(paired, 0.0, 2.0 * scale * jnp.sin(angles))
    ramp_sin = jnp.where(is_sine, ramp_sin, -ramp_sin)
    cos_x = jnp.cos(turn_angle(shift_x, 2 * SUBPIX))
    cos_y = jnp.cos(turn_angle(shift_y, 2 * SUBPIX))
    cos_xy = jnp.cos(turn_angle(shift_x + shift_y, 2 * SUBPIX))
    main = jnp.where(zero_col, cos_y, cos_xy)
    lead = jnp.where(zero_col, 1.0, cos_x)
    return jnp.concatenate([main * ramp_cos, main * ramp_sin, lead * ramp_cos, lead * ramp_sin])


def local(images, rate_vectors, epoch_times):
    loc_epochs, loc_rows, length = images.shape
    row_count = lax.axis_size("row")
    row_pos, core = lax.axis_index("row"), lax.axis_index("epoch")
    rates, epochs = rate_vectors.shape[0], epoch_times.shape[0]
    chunks = max(1, min(CHUNKS, length // 2 // row_count // MIN_COLS))
    cols = length // 2 // row_count // chunks
    table = packed_table(length, cols)
    table_t = jnp.asarray(np.ascontiguousarray(table.T))
    table = jnp.asarray(table)
    period = SUBPIX * length
    own_times = lax.dynamic_slice_in_dim(epoch_times, core * loc_epochs, loc_epochs)
    own_first = jnp.where(core == 0, rate_vectors, rate_vectors[::-1])
    shift_y = (own_first[:, 0:1] * own_times[None, :] % period).reshape(-1)
    shift_x = (own_first[:, 1:2] * own_times[None, :] % period).reshape(-1)
    coefs = row_factors(shift_y, length)
    scale = 1.0 / math.sqrt(epochs)

    def exchange(values):
        return lax.all_to_all(values, "row", 0, 0, tiled=True)

    spectra = [
        exchange(row_transform(images, table_t, chunk, chunks, row_count))
        for chunk in range(chunks)
    ]
    backs = []
    for chunk in range(chunks):
        first_freq = (chunk * row_count + row_pos) * cols
        factors = column_factors(shift_y, shift_x, scale, first_freq, cols, length)
        own, other = stack_rates(
            spectra[chunk].reshape(length, -1), table, coefs, factors, rates, loc_epochs, chunk
        )
        other = lax.ppermute(other, "epoch", [(0, 1), (1, 0)])
        backs.append(exchange(inverse_columns(own, other, table, row_count, chunk)))
    result = None
    for chunk in range(chunks):
        result = image_rows(backs[chunk].reshape(-1, loc_rows), table, result, chunk)
    return result


def solution(mesh):
    in_specs = (P(("group", "epoch"), "row", None), P(), P())
    out_specs = P(("group", "epoch"), "row", None)
    return jax.shard_map(local, mesh=mesh, in_specs=in_specs, out_specs=out_specs, check_vma=False)
```

```python
import functools
import math

import jax
import jax.numpy as jnp
import ml_dtypes
import numpy as np
from jax import lax
from jax.experimental import pallas as pl
from jax.experimental.pallas import tpu as pltpu
from jax.sharding import PartitionSpec as P

SUBPIX = 16
CHUNKS = 2
MIN_COLS = 64
PAIRWISE_LIMIT = 8
PAIR_ORDER = (7, 4, 1, 6, 5, 2, 3)
BLOCK = 512
VMEM_LIMIT = 58 * 1024 * 1024


def packed_table(length, cols):
    half = length // 2
    freqs = np.arange(half, dtype=np.int32)
    positions = np.arange(length, dtype=np.int32)
    turns = freqs[:, None] * positions[None, :] % length
    angles = turns.astype(np.float32) * np.float32(2.0 * math.pi / length)
    factor = np.float32(1.0 / math.sqrt(length))
    cosine = np.cos(angles) * factor
    sine = np.sin(angles) * factor
    sine[0] = np.where(positions % 2 == 0, factor, -factor)
    blocks = np.stack([cosine.reshape(-1, cols, length), sine.reshape(-1, cols, length)], axis=1)
    return blocks.reshape(length, length).astype(ml_dtypes.bfloat16)


def cost(flops, bytes_accessed):
    return pl.CostEstimate(flops=flops, bytes_accessed=bytes_accessed, transcendentals=0)


def row_kernel(images_ref, table_ref, out_ref, total):
    loc_epochs, loc_rows, depth = images_ref.shape
    dests, _, lanes = out_ref.shape
    width = lanes // loc_epochs
    step = pl.program_id(0)
    pixels = images_ref[...].reshape(loc_epochs * loc_rows, depth)
    terms = jnp.dot(pixels, table_ref[...], preferred_element_type=jnp.float32)

    @pl.when(step == 0)
    def _():
        total[...] = terms

    @pl.when(step > 0)
    def _():
        total[...] += terms

    @pl.when(step == pl.num_programs(0) - 1)
    def _():
        for dest in range(dests):
            for loc in range(loc_epochs):
                part = total[loc * loc_rows : (loc + 1) * loc_rows, dest * width : (dest + 1) * width]
                out_ref[dest, :, loc * width : (loc + 1) * width] = part.astype(jnp.bfloat16)


def row_transform(images, table_t, chunk, chunks, row_count):
    loc_epochs, loc_rows, length = images.shape
    columns = length // chunks
    lanes = columns // row_count * loc_epochs
    steps = length // BLOCK
    rows = loc_epochs * loc_rows
    return pl.pallas_call(
        row_kernel,
        grid=(steps,),
        in_specs=[
            pl.BlockSpec((loc_epochs, loc_rows, BLOCK), lambda i: (0, 0, i)),
            pl.BlockSpec((BLOCK, columns), lambda i: (i, chunk)),
        ],
        out_specs=pl.BlockSpec((row_count, loc_rows, lanes), lambda i: (0, 0, 0)),
        out_shape=jax.ShapeDtypeStruct((row_count, loc_rows, lanes), jnp.bfloat16),
        scratch_shapes=[pltpu.VMEM((rows, columns), jnp.float32)],
        compiler_params=pltpu.CompilerParams(vmem_limit_bytes=VMEM_LIMIT),
        cost_estimate=cost(2 * rows * length * columns, 2 * length * columns + 4 * rows * length),
        name=f"row_transform_{chunk}",
    )(images, table_t)


def swap_halves(values):
    width = values.shape[1]
    if width % 128 == 0:
        return pltpu.roll(values, width // 2, axis=1)
    return jnp.concatenate([values[:, width // 2 :], values[:, : width // 2]], axis=1)


def stack_kernel(rates, loc_epochs, z_ref, table_ref, coef_ref, lane_ref, *out_refs):
    width = z_ref.shape[1] // loc_epochs
    cols = width // 2
    block = table_ref.shape[0]
    groups = block // width
    pairs = rates * loc_epochs
    step = pl.program_id(0)
    products = jnp.dot(table_ref[...], z_ref[...], preferred_element_type=jnp.float32)
    products = products.reshape(groups, 2, cols, loc_epochs * width)
    even = products[:, 0].reshape(groups * cols, loc_epochs * width)
    odd = products[:, 1].reshape(groups * cols, loc_epochs * width)
    first = lax.broadcasted_iota(jnp.int32, (groups * cols, width), 0) == 0
    for rate in range(rates):
        straight, crossed, lead = [0.0, 0.0], [0.0, 0.0], [0.0, 0.0]
        for epoch in range(loc_epochs):
            pair = rate * loc_epochs + epoch
            even_part = even[:, epoch * width : (epoch + 1) * width]
            odd_part = odd[:, epoch * width : (epoch + 1) * width]
            cos_row = coef_ref[:, pair : pair + 1]
            sin_row = coef_ref[:, pairs + pair : pairs + pair + 1]
            turned = (
                cos_row * even_part + sin_row * odd_part,
                cos_row * odd_part - sin_row * even_part,
            )
            factors = [lane_ref[kind * pairs + pair : kind * pairs + pair + 1, :] for kind in range(4)]
            for which in range(2):
                straight[which] += turned[which] * factors[0]
                crossed[which] += turned[which] * factors[1]
                lead[which] += even_part[:8] * factors[2 + which]
        even_sum = straight[0] + swap_halves(crossed[0])
        odd_sum = straight[1] + swap_halves(crossed[1])
        lead_sum = lead[0] + swap_halves(lead[1])
        even_sum = jnp.where(first & (step == 0), lead_sum[0:1], even_sum)
        both = jnp.stack(
            [part.reshape(groups, cols, width) for part in (even_sum, odd_sum)], axis=1
        )
        out_refs[rate][...] = both.reshape(block, width).astype(jnp.bfloat16)


def stack_rates(spectra, table, coefs, lane_factors, rates, loc_epochs, chunk):
    length, lanes = spectra.shape
    width = lanes // loc_epochs
    return pl.pallas_call(
        functools.partial(stack_kernel, rates, loc_epochs),
        grid=(length // BLOCK,),
        in_specs=[
            pl.BlockSpec(spectra.shape, lambda i: (0, 0)),
            pl.BlockSpec((BLOCK, length), lambda i: (i, 0)),
            pl.BlockSpec((BLOCK // 2, coefs.shape[1]), lambda i: (i, 0)),
            pl.BlockSpec(lane_factors.shape, lambda i: (0, 0)),
        ],
        out_specs=[pl.BlockSpec((BLOCK, width), lambda i: (i, 0))] * rates,
        out_shape=[jax.ShapeDtypeStruct((length, width), jnp.bfloat16)] * rates,
        compiler_params=pltpu.CompilerParams(vmem_limit_bytes=VMEM_LIMIT),
        cost_estimate=cost(2 * length * length * lanes, 2 * length * length + 4 * length * lanes),
        name=f"stack_rates_{chunk}",
    )(spectra, table, coefs, lane_factors)


CONTRACT_FIRST = (((0,), (0,)), ((), ()))


def inverse_kernel(own_ref, other_ref, table_ref, out_ref, sums):
    dests, _, loc_rows = out_ref.shape

    @pl.when(pl.program_id(0) == 0)
    def _():
        total = own_ref[...].astype(jnp.float32) + other_ref[...].astype(jnp.float32)
        sums[...] = total.T.astype(jnp.bfloat16)

    back = jnp.dot(sums[...], table_ref[...], preferred_element_type=jnp.float32)
    back = back.astype(jnp.bfloat16)
    for dest in range(dests):
        out_ref[dest] = back[:, dest * loc_rows : (dest + 1) * loc_rows]


def inverse_columns(own, other, table, row_count, chunk):
    length, width = own.shape
    loc_rows = length // row_count
    dests = BLOCK // loc_rows
    return pl.pallas_call(
        inverse_kernel,
        grid=(length // BLOCK,),
        in_specs=[
            pl.BlockSpec(own.shape, lambda i: (0, 0)),
            pl.BlockSpec(own.shape, lambda i: (0, 0)),
            pl.BlockSpec((length, BLOCK), lambda i: (0, i)),
        ],
        out_specs=pl.BlockSpec((dests, width, loc_rows), lambda i: (i, 0, 0)),
        out_shape=jax.ShapeDtypeStruct((row_count, width, loc_rows), jnp.bfloat16),
        scratch_shapes=[pltpu.VMEM((width, length), jnp.bfloat16)],
        compiler_params=pltpu.CompilerParams(vmem_limit_bytes=VMEM_LIMIT),
        cost_estimate=cost(2 * length * length * width, 2 * length * length + 6 * length * width),
        name=f"inverse_columns_{chunk}",
    )(own, other, table)


def image_kernel(has_partial, back_ref, table_ref, *refs):
    out_ref, left = refs[-2:]

    @pl.when(pl.program_id(0) == 0)
    def _():
        left[...] = back_ref[...].T

    pixels = jnp.dot(left[...], table_ref[...], preferred_element_type=jnp.float32)
    if has_partial:
        pixels = pixels + refs[0][0]
    out_ref[0] = pixels


def image_rows(back, table, partial, chunk):
    depth, rows = back.shape
    length = table.shape[0]
    image_spec = pl.BlockSpec((1, rows, BLOCK), lambda i: (0, 0, i))
    partials = [] if partial is None else [partial]
    return pl.pallas_call(
        functools.partial(image_kernel, partial is not None),
        grid=(length // BLOCK,),
        in_specs=[
            pl.BlockSpec(back.shape, lambda i: (0, 0)),
            pl.BlockSpec((depth, BLOCK), lambda i: (chunk, i)),
        ]
        + [image_spec] * len(partials),
        out_specs=image_spec,
        out_shape=jax.ShapeDtypeStruct((1, rows, length), jnp.float32),
        scratch_shapes=[pltpu.VMEM((rows, depth), jnp.bfloat16)],
        compiler_params=pltpu.CompilerParams(vmem_limit_bytes=VMEM_LIMIT),
        cost_estimate=cost(2 * rows * depth * length, 2 * depth * length + 8 * rows * length),
        name=f"image_rows_{chunk}",
    )(back, table, *partials)


def turn_angle(turns, whole):
    return (turns % whole).astype(jnp.float32) * (2.0 * math.pi / whole)


def row_factors(shift_y, length):
    half = length // 2
    freqs = jnp.arange(half, dtype=jnp.int32)[:, None]
    angles = turn_angle((freqs - half) * shift_y[None, :], SUBPIX * length)
    return jnp.concatenate(
        [
            jnp.where(freqs == 0, 1.0, 2.0 * jnp.cos(angles)),
            jnp.where(freqs == 0, 0.0, 2.0 * jnp.sin(angles)),
        ],
        axis=1,
    )


def column_factors(shift_y, shift_x, scale, first_freq, cols, length):
    half = length // 2
    shift_y, shift_x = shift_y[:, None], shift_x[:, None]
    lane = jnp.arange(2 * cols, dtype=jnp.int32)[None, :]
    freqs = first_freq + lane % cols
    is_sine = lane >= cols
    paired = freqs == 0
    zero_col = paired & ~is_sine
    angles = turn_angle(shift_x * (freqs - half), SUBPIX * length)
    ramp_cos = jnp.where(paired, scale, 2.0 * scale * jnp.cos(angles))
    ramp_sin = jnp.where(paired, 0.0, 2.0 * scale * jnp.sin(angles))
    ramp_sin = jnp.where(is_sine, ramp_sin, -ramp_sin)
    cos_x = jnp.cos(turn_angle(shift_x, 2 * SUBPIX))
    cos_y = jnp.cos(turn_angle(shift_y, 2 * SUBPIX))
    cos_xy = jnp.cos(turn_angle(shift_x + shift_y, 2 * SUBPIX))
    main = jnp.where(zero_col, cos_y, cos_xy)
    lead = jnp.where(zero_col, 1.0, cos_x)
    return jnp.concatenate([main * ramp_cos, main * ramp_sin, lead * ramp_cos, lead * ramp_sin])


def local(images, rate_vectors, epoch_times):
    loc_epochs, loc_rows, length = images.shape
    row_count = lax.axis_size("row")
    row_pos, core = lax.axis_index("row"), lax.axis_index("epoch")
    rates, epochs = rate_vectors.shape[0], epoch_times.shape[0]
    chunks = max(1, min(CHUNKS, length // 2 // row_count // MIN_COLS))
    cols = length // 2 // row_count // chunks
    table = packed_table(length, cols)
    table_t = jnp.asarray(np.ascontiguousarray(table.T))
    table = jnp.asarray(table)
    period = SUBPIX * length
    own_times = lax.dynamic_slice_in_dim(epoch_times, core * loc_epochs, loc_epochs)
    own_first = jnp.where(core == 0, rate_vectors, rate_vectors[::-1])
    shift_y = (own_first[:, 0:1] * own_times[None, :] % period).reshape(-1)
    shift_x = (own_first[:, 1:2] * own_times[None, :] % period).reshape(-1)
    coefs = row_factors(shift_y, length)
    scale = 1.0 / math.sqrt(epochs)

    def exchange(values):
        if row_count > PAIRWISE_LIMIT:
            return lax.all_to_all(values, "row", 0, 0, tiled=True)
        received = values
        for offset in PAIR_ORDER:
            sent = lax.dynamic_index_in_dim(values, row_pos ^ offset, 0, keepdims=True)
            pairs = [(index, index ^ offset) for index in range(row_count)]
            arrived = lax.ppermute(sent, "row", pairs)
            received = lax.dynamic_update_slice_in_dim(received, arrived, row_pos ^ offset, 0)
        return received

    spectra = [
        exchange(row_transform(images, table_t, chunk, chunks, row_count))
        for chunk in range(chunks)
    ]
    backs = []
    for chunk in range(chunks):
        first_freq = (chunk * row_count + row_pos) * cols
        factors = column_factors(shift_y, shift_x, scale, first_freq, cols, length)
        own, other = stack_rates(
            spectra[chunk].reshape(length, -1), table, coefs, factors, rates, loc_epochs, chunk
        )
        other = lax.ppermute(other, "epoch", [(0, 1), (1, 0)])
        backs.append(exchange(inverse_columns(own, other, table, row_count, chunk)))
    result = None
    for chunk in range(chunks):
        result = image_rows(backs[chunk].reshape(-1, loc_rows), table, result, chunk)
    return result


def solution(mesh):
    in_specs = (P(("group", "epoch"), "row", None), P(), P())
    out_specs = P(("group", "epoch"), "row", None)
    return jax.shard_map(local, mesh=mesh, in_specs=in_specs, out_specs=out_specs, check_vma=False)
```

```python
import functools
import math

import jax
import jax.numpy as jnp
import ml_dtypes
import numpy as np
from jax import lax
from jax.experimental import pallas as pl
from jax.experimental.pallas import tpu as pltpu
from jax.sharding import PartitionSpec as P

SUBPIX = 16
BLOCK = 512
IMAGE_BLOCK = 256
VMEM_LIMIT = 40 * 1024 * 1024
HBM = pl.BlockSpec(memory_space=pltpu.HBM)
ANYWHERE = pl.BlockSpec(memory_space=pl.ANY)


def packed_freqs(length, cols):
    index = np.arange(length // 2, dtype=np.int32)
    quarter = length // 4
    return 2 * (index % quarter) + index // quarter


def packed_table(length, cols):
    half = length // 2
    freqs = packed_freqs(length, cols)
    positions = np.arange(half, dtype=np.int32)
    turns = freqs[:, None] * positions[None, :] % length
    angles = turns.astype(np.float32) * np.float32(2.0 * math.pi / length)
    factor = np.float32(1.0 / math.sqrt(length))
    cosine = np.cos(angles) * factor
    sine = np.sin(angles) * factor
    sine[0] = np.where(positions % 2 == 0, factor, -factor)
    blocks = np.stack([cosine.reshape(-1, cols, half), sine.reshape(-1, cols, half)], axis=1)
    return blocks.reshape(length, half).astype(ml_dtypes.bfloat16)


def cost(flops, bytes_accessed):
    return pl.CostEstimate(flops=flops, bytes_accessed=bytes_accessed, transcendentals=0)


def start_copies(pairs, sems):
    copies = [
        pltpu.make_async_copy(source, target, sems.at[index])
        for index, (source, target) in enumerate(pairs)
    ]
    for copy in copies:
        copy.start()
    return copies


def wait_copies(copies):
    for copy in copies:
        copy.wait()


def fold(first, second):
    first, second = first.astype(jnp.float32), second.astype(jnp.float32)
    return (first + second).astype(jnp.bfloat16), (first - second).astype(jnp.bfloat16)


def row_kernel(
    images_hbm, table_hbm, out_hbm, images, table, folded, staged, image_sems, table_sems, out_sems
):
    loc_epochs, loc_rows, length = images.shape
    half = length // 2
    devices, _, _, width = staged.shape
    steps = length // BLOCK
    dests = devices // steps
    half_rows = loc_rows // 2
    image_parts = [
        (loc, slice(part * half_rows, (part + 1) * half_rows))
        for loc in range(loc_epochs)
        for part in range(2)
    ]
    image_copies = start_copies(
        [(images_hbm.at[loc, rows], images.at[loc, rows]) for loc, rows in image_parts], image_sems
    )
    table_copies = start_copies(
        [
            (table_hbm.at[:, step * BLOCK : (step + 1) * BLOCK], table.at[step])
            for step in range(steps)
        ],
        table_sems,
    )
    for copy, (loc, rows) in zip(image_copies, image_parts):
        copy.wait()
        at = slice(loc * loc_rows + rows.start, loc * loc_rows + rows.stop)
        folded[0, at], folded[1, at] = fold(images[loc, rows, :half], images[loc, rows, half:])
    out_copies = []
    for step in range(steps):
        table_copies[step].wait()
        pixels = folded[2 * step // steps]
        terms = jnp.dot(pixels, table[step], preferred_element_type=jnp.float32)
        terms = terms.astype(jnp.bfloat16)
        for dest in range(dests):
            for loc in range(loc_epochs):
                staged[step * dests + dest, loc] = terms[
                    loc * loc_rows : (loc + 1) * loc_rows, dest * width : (dest + 1) * width
                ]
        at = pl.ds(step * dests, dests)
        out_copies.append(pltpu.make_async_copy(staged.at[at], out_hbm.at[at], out_sems.at[step]))
        out_copies[-1].start()
    wait_copies(out_copies)


def row_transform(images, table_t, devices):
    loc_epochs, loc_rows, length = images.shape
    half = length // 2
    rows = loc_epochs * loc_rows
    steps = length // BLOCK
    out = (devices, loc_epochs, loc_rows, length // devices)
    return pl.pallas_call(
        row_kernel,
        in_specs=[HBM, HBM],
        out_specs=HBM,
        out_shape=jax.ShapeDtypeStruct(out, jnp.bfloat16),
        scratch_shapes=[
            pltpu.VMEM(images.shape, jnp.bfloat16),
            pltpu.VMEM((steps, half, BLOCK), jnp.bfloat16),
            pltpu.VMEM((2, rows, half), jnp.bfloat16),
            pltpu.VMEM(out, jnp.bfloat16),
            pltpu.SemaphoreType.DMA((2 * loc_epochs,)),
            pltpu.SemaphoreType.DMA((steps,)),
            pltpu.SemaphoreType.DMA((steps,)),
        ],
        compiler_params=pltpu.CompilerParams(vmem_limit_bytes=VMEM_LIMIT),
        cost_estimate=cost(2 * rows * half * length, 2 * half * length + 4 * rows * length),
        name="row_transform",
    )(images, table_t)


def swap_halves(values):
    width = values.shape[1]
    if width % 128 == 0:
        return pltpu.roll(values, width // 2, axis=1)
    return jnp.concatenate([values[:, width // 2 :], values[:, : width // 2]], axis=1)


def ramp_sums(products, coefs, factors, rates, epochs, leads):
    block = products.shape[0]
    width = products.shape[1] // epochs
    cols = width // 2
    groups = block // width
    pairs = rates * epochs
    products = products.reshape(groups, 2, cols, epochs * width)
    even = products[:, 0].reshape(groups * cols, epochs * width)
    odd = products[:, 1].reshape(groups * cols, epochs * width)
    results = []
    for rate in range(rates):
        straight, crossed, lead = [0.0, 0.0], [0.0, 0.0], [0.0, 0.0]
        for epoch in range(epochs):
            pair = rate * epochs + epoch
            even_part = even[:, epoch * width : (epoch + 1) * width]
            odd_part = odd[:, epoch * width : (epoch + 1) * width]
            cos_row = coefs[:, pair : pair + 1]
            sin_row = coefs[:, pairs + pair : pairs + pair + 1]
            turned = (
                cos_row * even_part + sin_row * odd_part,
                cos_row * odd_part - sin_row * even_part,
            )
            lanes = [factors[kind * pairs + pair : kind * pairs + pair + 1, :] for kind in range(4)]
            for which in range(2):
                straight[which] += turned[which] * lanes[0]
                crossed[which] += turned[which] * lanes[1]
                if leads:
                    lead[which] += even_part[:8] * lanes[2 + which]
        even_sum = straight[0] + swap_halves(crossed[0])
        odd_sum = straight[1] + swap_halves(crossed[1])
        if leads:
            lead_sum = lead[0] + swap_halves(lead[1])
            first = lax.broadcasted_iota(jnp.int32, even_sum.shape, 0) == 0
            even_sum = jnp.where(first, lead_sum[0:1], even_sum)
        both = jnp.stack(
            [part.reshape(groups, cols, width) for part in (even_sum, odd_sum)], axis=1
        )
        results.append(both.reshape(block, width))
    return results


def column_kernel(
    epoch_count,
    rates,
    z_any,
    table_hbm,
    coef_any,
    factor_any,
    out_hbm,
    received,
    table,
    coefs,
    factors,
    folded,
    sums,
    staged,
    z_sems,
    table_sems,
    small_sems,
    out_sems,
):
    devices, loc_epochs, loc_rows, width = received.shape
    row_count = devices // epoch_count
    epochs = epoch_count * loc_epochs
    length, half = table.shape
    steps = length // BLOCK
    z_parts = z_sems.shape[0]
    per_part = devices // z_parts
    z_copies = start_copies(
        [
            (z_any.at[pl.ds(part * per_part, per_part)], received.at[pl.ds(part * per_part, per_part)])
            for part in range(z_parts)
        ],
        z_sems,
    )
    small_copies = start_copies([(coef_any, coefs), (factor_any, factors)], small_sems)
    table_copies = start_copies(
        [
            (table_hbm.at[pl.ds(step * BLOCK, BLOCK)], table.at[pl.ds(step * BLOCK, BLOCK)])
            for step in range(steps)
        ],
        table_sems,
    )
    wait_copies(z_copies)
    for row in range(row_count // 2):
        sides = []
        for source in (row, row + row_count // 2):
            parts = [
                received[source * epoch_count + core, loc]
                for core in range(epoch_count)
                for loc in range(loc_epochs)
            ]
            sides.append(jnp.concatenate(parts, axis=1))
        at = slice(row * loc_rows, (row + 1) * loc_rows)
        folded[0, at], folded[1, at] = fold(sides[0], sides[1])
    wait_copies(small_copies)
    for step in range(steps):
        at = slice(step * BLOCK, (step + 1) * BLOCK)
        table_copies[step].wait()
        products = jnp.dot(
            table[at], folded[2 * step // steps], preferred_element_type=jnp.float32
        )
        block_coefs = coefs[step * BLOCK // 2 : (step + 1) * BLOCK // 2]
        results = ramp_sums(products, block_coefs, factors, rates, epochs, step == 0)
        for rate in range(rates):
            sums[rate * width : (rate + 1) * width, at] = results[rate].T.astype(jnp.bfloat16)
    loc_rates = rates // epoch_count
    blocks = max(1, half // BLOCK)
    out_copies = []
    for block in range(blocks):
        at = slice(block * BLOCK, (block + 1) * BLOCK)
        even, odd = [
            jnp.dot(
                sums[:, part * half : (part + 1) * half],
                table[part * half : (part + 1) * half, at],
                preferred_element_type=jnp.float32,
            )
            for part in range(2)
        ]
        rows_here = BLOCK // loc_rows
        for side, back in enumerate((even + odd, even - odd)):
            back = back.astype(jnp.bfloat16)
            first = side * row_count // 2 + block * rows_here
            for row in range(rows_here):
                for rate in range(rates):
                    dest = (first + row) * epoch_count + rate // loc_rates
                    staged[dest, rate % loc_rates] = back[
                        rate * width : (rate + 1) * width, row * loc_rows : (row + 1) * loc_rows
                    ]
            span = pl.ds(first * epoch_count, rows_here * epoch_count)
            out_copies.append(
                pltpu.make_async_copy(
                    staged.at[span], out_hbm.at[span], out_sems.at[2 * block + side]
                )
            )
            out_copies[-1].start()
    wait_copies(out_copies)


def column_stage(spectra, table, coefs, factors, epoch_count, rates):
    devices, loc_epochs, loc_rows, width = spectra.shape
    length, half = table.shape
    epochs = epoch_count * loc_epochs
    steps = length // BLOCK
    out = (devices, rates // epoch_count, width, loc_rows)
    return pl.pallas_call(
        functools.partial(column_kernel, epoch_count, rates),
        in_specs=[ANYWHERE, HBM, ANYWHERE, ANYWHERE],
        out_specs=HBM,
        out_shape=jax.ShapeDtypeStruct(out, jnp.bfloat16),
        scratch_shapes=[
            pltpu.VMEM(spectra.shape, jnp.bfloat16),
            pltpu.VMEM(table.shape, jnp.bfloat16),
            pltpu.VMEM(coefs.shape, jnp.float32),
            pltpu.VMEM(factors.shape, jnp.float32),
            pltpu.VMEM((2, half, epochs * width), jnp.bfloat16),
            pltpu.VMEM((rates * width, length), jnp.bfloat16),
            pltpu.VMEM(out, jnp.bfloat16),
            pltpu.SemaphoreType.DMA((4,)),
            pltpu.SemaphoreType.DMA((steps,)),
            pltpu.SemaphoreType.DMA((2,)),
            pltpu.SemaphoreType.DMA((2 * max(1, half // BLOCK),)),
        ],
        compiler_params=pltpu.CompilerParams(vmem_limit_bytes=VMEM_LIMIT),
        cost_estimate=cost(
            2 * length * half * (epochs + rates) * width, 2 * length * half + 4 * spectra.size
        ),
        name="column_stage",
    )(spectra, table, coefs, factors)


def image_kernel(
    back_any, table_hbm, out_hbm, back, table, left, staged, back_sem, table_sems, out_sems
):
    length, half = table_hbm.shape
    blocks = half // IMAGE_BLOCK
    back_copy = pltpu.make_async_copy(back_any, back, back_sem)
    back_copy.start()
    table_copies = start_copies(
        [
            (table_hbm.at[:, block * IMAGE_BLOCK : (block + 1) * IMAGE_BLOCK], table.at[block])
            for block in range(blocks)
        ],
        table_sems,
    )
    back_copy.wait()
    left[...] = back[...].T
    out_copies = []
    for block in range(blocks):
        table_copies[block].wait()
        even, odd = [
            jnp.dot(
                left[:, part * half : (part + 1) * half],
                table[block, part * half : (part + 1) * half],
                preferred_element_type=jnp.float32,
            )
            for part in range(2)
        ]
        for side, pixels in enumerate((even + odd, even - odd)):
            at = slice(side * half + block * IMAGE_BLOCK, side * half + (block + 1) * IMAGE_BLOCK)
            staged[:, at] = pixels
            out_copies.append(
                pltpu.make_async_copy(
                    staged.at[:, at], out_hbm.at[0, :, at], out_sems.at[2 * block + side]
                )
            )
            out_copies[-1].start()
    wait_copies(out_copies)


def image_rows(back, table):
    rows = back.shape[1]
    length, half = table.shape
    blocks = half // IMAGE_BLOCK
    return pl.pallas_call(
        image_kernel,
        in_specs=[ANYWHERE, HBM],
        out_specs=HBM,
        out_shape=jax.ShapeDtypeStruct((1, rows, length), jnp.float32),
        scratch_shapes=[
            pltpu.VMEM(back.shape, jnp.bfloat16),
            pltpu.VMEM((blocks, length, IMAGE_BLOCK), jnp.bfloat16),
            pltpu.VMEM((rows, length), jnp.bfloat16),
            pltpu.VMEM((rows, length), jnp.float32),
            pltpu.SemaphoreType.DMA,
            pltpu.SemaphoreType.DMA((blocks,)),
            pltpu.SemaphoreType.DMA((2 * blocks,)),
        ],
        compiler_params=pltpu.CompilerParams(vmem_limit_bytes=VMEM_LIMIT),
        cost_estimate=cost(2 * rows * half * length, 2 * half * length + 6 * rows * length),
        name="image_rows",
    )(back, table)


def turn_angle(turns, whole):
    return (turns % whole).astype(jnp.float32) * (2.0 * math.pi / whole)


def row_factors(shift_y, cols, length):
    freqs = jnp.asarray(packed_freqs(length, cols))[:, None]
    angles = turn_angle((freqs - length // 2) * shift_y[None, :], SUBPIX * length)
    return jnp.concatenate(
        [
            jnp.where(freqs == 0, 1.0, 2.0 * jnp.cos(angles)),
            jnp.where(freqs == 0, 0.0, 2.0 * jnp.sin(angles)),
        ],
        axis=1,
    )


def column_factors(shift_y, shift_x, scale, device, devices, cols, length):
    half = length // 2
    shift_y, shift_x = shift_y[:, None], shift_x[:, None]
    lane = jnp.arange(2 * cols, dtype=jnp.int32)[None, :]
    index = device * cols + lane % cols
    freqs = 2 * (index % (half // 2)) + index // (half // 2)
    is_sine = lane >= cols
    paired = freqs == 0
    zero_col = paired & ~is_sine
    angles = turn_angle(shift_x * (freqs - half), SUBPIX * length)
    ramp_cos = jnp.where(paired, scale, 2.0 * scale * jnp.cos(angles))
    ramp_sin = jnp.where(paired, 0.0, 2.0 * scale * jnp.sin(angles))
    ramp_sin = jnp.where(is_sine, ramp_sin, -ramp_sin)
    cos_x = jnp.cos(turn_angle(shift_x, 2 * SUBPIX))
    cos_y = jnp.cos(turn_angle(shift_y, 2 * SUBPIX))
    cos_xy = jnp.cos(turn_angle(shift_x + shift_y, 2 * SUBPIX))
    main = jnp.where(zero_col, cos_y, cos_xy)
    lead = jnp.where(zero_col, 1.0, cos_x)
    return jnp.concatenate([main * ramp_cos, main * ramp_sin, lead * ramp_cos, lead * ramp_sin])


def local(images, rate_vectors, epoch_times):
    _, loc_rows, length = images.shape
    epoch_count = lax.axis_size("epoch")
    devices = lax.axis_size("row") * epoch_count
    device = lax.axis_index("row") * epoch_count + lax.axis_index("epoch")
    rates, epochs = rate_vectors.shape[0], epoch_times.shape[0]
    cols = length // 2 // devices
    table = packed_table(length, cols)
    table_t = jnp.asarray(np.ascontiguousarray(table.T))
    table = jnp.asarray(table)
    period = SUBPIX * length
    shift_y = (rate_vectors[:, 0:1] * epoch_times[None, :] % period).reshape(-1)
    shift_x = (rate_vectors[:, 1:2] * epoch_times[None, :] % period).reshape(-1)
    coefs = row_factors(shift_y, cols, length)
    scale = 1.0 / math.sqrt(epochs)
    factors = column_factors(shift_y, shift_x, scale, device, devices, cols, length)

    def exchange(values):
        return lax.all_to_all(values, ("row", "epoch"), 0, 0, tiled=True)

    spectra = exchange(row_transform(images, table_t, devices))
    back = exchange(column_stage(spectra, table, coefs, factors, epoch_count, rates))
    return image_rows(back.reshape(length, loc_rows), table)


def solution(mesh):
    in_specs = (P(("group", "epoch"), "row", None), P(), P())
    out_specs = P(("group", "epoch"), "row", None)
    return jax.shard_map(local, mesh=mesh, in_specs=in_specs, out_specs=out_specs, check_vma=False)
```

```python
import functools
import math

import jax
import jax.numpy as jnp
import ml_dtypes
import numpy as np
from jax import lax
from jax.experimental import pallas as pl
from jax.experimental.pallas import tpu as pltpu
from jax.sharding import PartitionSpec as P

SUBPIX = 16
BLOCK = 512
IMAGE_BLOCK = 256
VMEM_LIMIT = 58 * 1024 * 1024
HBM = pl.BlockSpec(memory_space=pltpu.HBM)
ANYWHERE = pl.BlockSpec(memory_space=pl.ANY)


def packed_freqs(length, cols):
    index = np.arange(length // 2, dtype=np.int32)
    quarter = length // 4
    return 2 * (index % quarter) + index // quarter


def packed_table(length, cols):
    half = length // 2
    freqs = packed_freqs(length, cols)
    positions = np.arange(half, dtype=np.int32)
    turns = freqs[:, None] * positions[None, :] % length
    angles = turns.astype(np.float32) * np.float32(2.0 * math.pi / length)
    factor = np.float32(1.0 / math.sqrt(length))
    cosine = np.cos(angles) * factor
    sine = np.sin(angles) * factor
    sine[0] = np.where(positions % 2 == 0, factor, -factor)
    blocks = np.stack([cosine.reshape(-1, cols, half), sine.reshape(-1, cols, half)], axis=1)
    return blocks.reshape(length, half).astype(ml_dtypes.bfloat16)


def cost(flops, bytes_accessed):
    return pl.CostEstimate(flops=flops, bytes_accessed=bytes_accessed, transcendentals=0)


def start_copies(pairs, sems):
    copies = [
        pltpu.make_async_copy(source, target, sems.at[index])
        for index, (source, target) in enumerate(pairs)
    ]
    for copy in copies:
        copy.start()
    return copies


def wait_copies(copies):
    for copy in copies:
        copy.wait()


def fold(first, second):
    first, second = first.astype(jnp.float32), second.astype(jnp.float32)
    return (first + second).astype(jnp.bfloat16), (first - second).astype(jnp.bfloat16)


def row_kernel(
    images_hbm, table_hbm, out_hbm, images, table, folded, staged, image_sems, table_sems, out_sems
):
    loc_epochs, loc_rows, length = images.shape
    half = length // 2
    devices, _, _, width = staged.shape
    steps = length // BLOCK
    dests = devices // steps
    half_rows = loc_rows // 2
    image_parts = [
        (loc, slice(part * half_rows, (part + 1) * half_rows))
        for loc in range(loc_epochs)
        for part in range(2)
    ]
    image_copies = start_copies(
        [(images_hbm.at[loc, rows], images.at[loc, rows]) for loc, rows in image_parts], image_sems
    )
    table_copies = start_copies(
        [
            (table_hbm.at[:, step * BLOCK : (step + 1) * BLOCK], table.at[step])
            for step in range(steps)
        ],
        table_sems,
    )
    for copy, (loc, rows) in zip(image_copies, image_parts):
        copy.wait()
        at = slice(loc * loc_rows + rows.start, loc * loc_rows + rows.stop)
        folded[0, at], folded[1, at] = fold(images[loc, rows, :half], images[loc, rows, half:])
    out_copies = []
    for step in range(steps):
        table_copies[step].wait()
        pixels = folded[2 * step // steps]
        terms = jnp.dot(pixels, table[step], preferred_element_type=jnp.float32)
        terms = terms.astype(jnp.bfloat16)
        for dest in range(dests):
            for loc in range(loc_epochs):
                staged[step * dests + dest, loc] = terms[
                    loc * loc_rows : (loc + 1) * loc_rows, dest * width : (dest + 1) * width
                ]
        at = pl.ds(step * dests, dests)
        out_copies.append(pltpu.make_async_copy(staged.at[at], out_hbm.at[at], out_sems.at[step]))
        out_copies[-1].start()
    wait_copies(out_copies)


def row_transform(images, table_t, devices):
    loc_epochs, loc_rows, length = images.shape
    half = length // 2
    rows = loc_epochs * loc_rows
    steps = length // BLOCK
    out = (devices, loc_epochs, loc_rows, length // devices)
    return pl.pallas_call(
        row_kernel,
        in_specs=[HBM, HBM],
        out_specs=HBM,
        out_shape=jax.ShapeDtypeStruct(out, jnp.bfloat16),
        scratch_shapes=[
            pltpu.VMEM(images.shape, jnp.bfloat16),
            pltpu.VMEM((steps, half, BLOCK), jnp.bfloat16),
            pltpu.VMEM((2, rows, half), jnp.bfloat16),
            pltpu.VMEM(out, jnp.bfloat16),
            pltpu.SemaphoreType.DMA((2 * loc_epochs,)),
            pltpu.SemaphoreType.DMA((steps,)),
            pltpu.SemaphoreType.DMA((steps,)),
        ],
        compiler_params=pltpu.CompilerParams(vmem_limit_bytes=VMEM_LIMIT),
        cost_estimate=cost(2 * rows * half * length, 2 * half * length + 4 * rows * length),
        name="row_transform",
    )(images, table_t)


def swap_halves(values):
    width = values.shape[1]
    if width % 128 == 0:
        return pltpu.roll(values, width // 2, axis=1)
    return jnp.concatenate([values[:, width // 2 :], values[:, : width // 2]], axis=1)


def ramp_sums(products, coefs, factors, rates, epochs, leads):
    block = products.shape[0]
    width = products.shape[1] // epochs
    cols = width // 2
    groups = block // width
    pairs = rates * epochs
    products = products.reshape(groups, 2, cols, epochs * width)
    even = products[:, 0].reshape(groups * cols, epochs * width)
    odd = products[:, 1].reshape(groups * cols, epochs * width)
    results = []
    for rate in range(rates):
        straight, crossed, lead = [0.0, 0.0], [0.0, 0.0], [0.0, 0.0]
        for epoch in range(epochs):
            pair = rate * epochs + epoch
            even_part = even[:, epoch * width : (epoch + 1) * width]
            odd_part = odd[:, epoch * width : (epoch + 1) * width]
            cos_row = coefs[:, pair : pair + 1]
            sin_row = coefs[:, pairs + pair : pairs + pair + 1]
            turned = (
                cos_row * even_part + sin_row * odd_part,
                cos_row * odd_part - sin_row * even_part,
            )
            lanes = [factors[kind * pairs + pair : kind * pairs + pair + 1, :] for kind in range(4)]
            for which in range(2):
                straight[which] += turned[which] * lanes[0]
                crossed[which] += turned[which] * lanes[1]
                if leads:
                    lead[which] += even_part[:8] * lanes[2 + which]
        even_sum = straight[0] + swap_halves(crossed[0])
        odd_sum = straight[1] + swap_halves(crossed[1])
        if leads:
            lead_sum = lead[0] + swap_halves(lead[1])
            first = lax.broadcasted_iota(jnp.int32, even_sum.shape, 0) == 0
            even_sum = jnp.where(first, lead_sum[0:1], even_sum)
        both = jnp.stack(
            [part.reshape(groups, cols, width) for part in (even_sum, odd_sum)], axis=1
        )
        results.append(both.reshape(block, width))
    return results


def column_kernel(
    epoch_count,
    rates,
    z_any,
    table_hbm,
    coef_any,
    factor_any,
    out_hbm,
    received,
    table,
    coefs,
    factors,
    folded,
    sums,
    staged,
    z_sems,
    table_sems,
    small_sems,
    out_sems,
):
    devices, loc_epochs, loc_rows, width = received.shape
    row_count = devices // epoch_count
    epochs = epoch_count * loc_epochs
    length, half = table.shape
    steps = length // BLOCK
    z_parts = z_sems.shape[0]
    per_part = devices // z_parts
    z_copies = start_copies(
        [
            (z_any.at[pl.ds(part * per_part, per_part)], received.at[pl.ds(part * per_part, per_part)])
            for part in range(z_parts)
        ],
        z_sems,
    )
    small_copies = start_copies([(coef_any, coefs), (factor_any, factors)], small_sems)
    table_copies = start_copies(
        [
            (table_hbm.at[pl.ds(step * BLOCK, BLOCK)], table.at[pl.ds(step * BLOCK, BLOCK)])
            for step in range(steps)
        ],
        table_sems,
    )
    wait_copies(z_copies)
    for row in range(row_count // 2):
        sides = []
        for source in (row, row + row_count // 2):
            parts = [
                received[source * epoch_count + core, loc]
                for core in range(epoch_count)
                for loc in range(loc_epochs)
            ]
            sides.append(jnp.concatenate(parts, axis=1))
        at = slice(row * loc_rows, (row + 1) * loc_rows)
        folded[0, at], folded[1, at] = fold(sides[0], sides[1])
    wait_copies(small_copies)
    for step in range(steps):
        at = slice(step * BLOCK, (step + 1) * BLOCK)
        table_copies[step].wait()
        products = jnp.dot(
            table[at], folded[2 * step // steps], preferred_element_type=jnp.float32
        )
        block_coefs = coefs[step * BLOCK // 2 : (step + 1) * BLOCK // 2]
        results = ramp_sums(products, block_coefs, factors, rates, epochs, step == 0)
        for rate in range(rates):
            sums[rate * width : (rate + 1) * width, at] = results[rate].T.astype(jnp.bfloat16)
    loc_rates = rates // epoch_count
    blocks = max(1, half // BLOCK)
    out_copies = []
    for block in range(blocks):
        at = slice(block * BLOCK, (block + 1) * BLOCK)
        even, odd = [
            jnp.dot(
                sums[:, part * half : (part + 1) * half],
                table[part * half : (part + 1) * half, at],
                preferred_element_type=jnp.float32,
            )
            for part in range(2)
        ]
        rows_here = BLOCK // loc_rows
        for side, back in enumerate((even + odd, even - odd)):
            back = back.astype(jnp.bfloat16)
            first = side * row_count // 2 + block * rows_here
            for row in range(rows_here):
                for rate in range(rates):
                    dest = (first + row) * epoch_count + rate // loc_rates
                    staged[dest, rate % loc_rates] = back[
                        rate * width : (rate + 1) * width, row * loc_rows : (row + 1) * loc_rows
                    ]
            span = pl.ds(first * epoch_count, rows_here * epoch_count)
            out_copies.append(
                pltpu.make_async_copy(
                    staged.at[span], out_hbm.at[span], out_sems.at[2 * block + side]
                )
            )
            out_copies[-1].start()
    wait_copies(out_copies)


def column_stage(spectra, table, coefs, factors, epoch_count, rates):
    devices, loc_epochs, loc_rows, width = spectra.shape
    length, half = table.shape
    epochs = epoch_count * loc_epochs
    steps = length // BLOCK
    out = (devices, rates // epoch_count, width, loc_rows)
    return pl.pallas_call(
        functools.partial(column_kernel, epoch_count, rates),
        in_specs=[ANYWHERE, HBM, ANYWHERE, ANYWHERE],
        out_specs=HBM,
        out_shape=jax.ShapeDtypeStruct(out, jnp.bfloat16),
        scratch_shapes=[
            pltpu.VMEM(spectra.shape, jnp.bfloat16),
            pltpu.VMEM(table.shape, jnp.bfloat16),
            pltpu.VMEM(coefs.shape, jnp.float32),
            pltpu.VMEM(factors.shape, jnp.float32),
            pltpu.VMEM((2, half, epochs * width), jnp.bfloat16),
            pltpu.VMEM((rates * width, length), jnp.bfloat16),
            pltpu.VMEM(out, jnp.bfloat16),
            pltpu.SemaphoreType.DMA((4,)),
            pltpu.SemaphoreType.DMA((steps,)),
            pltpu.SemaphoreType.DMA((2,)),
            pltpu.SemaphoreType.DMA((2 * max(1, half // BLOCK),)),
        ],
        compiler_params=pltpu.CompilerParams(vmem_limit_bytes=VMEM_LIMIT),
        cost_estimate=cost(
            2 * length * half * (epochs + rates) * width, 2 * length * half + 4 * spectra.size
        ),
        name="column_stage",
    )(spectra, table, coefs, factors)


def image_kernel(
    back_any, table_hbm, out_hbm, back, table, left, staged, back_sem, table_sems, out_sems
):
    length, half = table_hbm.shape
    blocks = half // IMAGE_BLOCK
    back_copy = pltpu.make_async_copy(back_any, back, back_sem)
    back_copy.start()
    table_copies = start_copies(
        [
            (table_hbm.at[:, block * IMAGE_BLOCK : (block + 1) * IMAGE_BLOCK], table.at[block])
            for block in range(blocks)
        ],
        table_sems,
    )
    back_copy.wait()
    left[...] = back[...].T
    out_copies = []
    for block in range(blocks):
        table_copies[block].wait()
        even, odd = [
            jnp.dot(
                left[:, part * half : (part + 1) * half],
                table[block, part * half : (part + 1) * half],
                preferred_element_type=jnp.float32,
            )
            for part in range(2)
        ]
        for side, pixels in enumerate((even + odd, even - odd)):
            at = slice(side * half + block * IMAGE_BLOCK, side * half + (block + 1) * IMAGE_BLOCK)
            staged[:, at] = pixels
            out_copies.append(
                pltpu.make_async_copy(
                    staged.at[:, at], out_hbm.at[0, :, at], out_sems.at[2 * block + side]
                )
            )
            out_copies[-1].start()
    wait_copies(out_copies)


def image_rows(back, table):
    rows = back.shape[1]
    length, half = table.shape
    blocks = half // IMAGE_BLOCK
    return pl.pallas_call(
        image_kernel,
        in_specs=[ANYWHERE, HBM],
        out_specs=HBM,
        out_shape=jax.ShapeDtypeStruct((1, rows, length), jnp.float32),
        scratch_shapes=[
            pltpu.VMEM(back.shape, jnp.bfloat16),
            pltpu.VMEM((blocks, length, IMAGE_BLOCK), jnp.bfloat16),
            pltpu.VMEM((rows, length), jnp.bfloat16),
            pltpu.VMEM((rows, length), jnp.float32),
            pltpu.SemaphoreType.DMA,
            pltpu.SemaphoreType.DMA((blocks,)),
            pltpu.SemaphoreType.DMA((2 * blocks,)),
        ],
        compiler_params=pltpu.CompilerParams(vmem_limit_bytes=VMEM_LIMIT),
        cost_estimate=cost(2 * rows * half * length, 2 * half * length + 6 * rows * length),
        name="image_rows",
    )(back, table)


def turn_angle(turns, whole):
    return (turns % whole).astype(jnp.float32) * (2.0 * math.pi / whole)


def row_factors(shift_y, cols, length):
    freqs = jnp.asarray(packed_freqs(length, cols))[:, None]
    angles = turn_angle((freqs - length // 2) * shift_y[None, :], SUBPIX * length)
    return jnp.concatenate(
        [
            jnp.where(freqs == 0, 1.0, 2.0 * jnp.cos(angles)),
            jnp.where(freqs == 0, 0.0, 2.0 * jnp.sin(angles)),
        ],
        axis=1,
    )


def column_factors(shift_y, shift_x, scale, device, devices, cols, length):
    half = length // 2
    shift_y, shift_x = shift_y[:, None], shift_x[:, None]
    lane = jnp.arange(2 * cols, dtype=jnp.int32)[None, :]
    index = device * cols + lane % cols
    freqs = 2 * (index % (half // 2)) + index // (half // 2)
    is_sine = lane >= cols
    paired = freqs == 0
    zero_col = paired & ~is_sine
    angles = turn_angle(shift_x * (freqs - half), SUBPIX * length)
    ramp_cos = jnp.where(paired, scale, 2.0 * scale * jnp.cos(angles))
    ramp_sin = jnp.where(paired, 0.0, 2.0 * scale * jnp.sin(angles))
    ramp_sin = jnp.where(is_sine, ramp_sin, -ramp_sin)
    cos_x = jnp.cos(turn_angle(shift_x, 2 * SUBPIX))
    cos_y = jnp.cos(turn_angle(shift_y, 2 * SUBPIX))
    cos_xy = jnp.cos(turn_angle(shift_x + shift_y, 2 * SUBPIX))
    main = jnp.where(zero_col, cos_y, cos_xy)
    lead = jnp.where(zero_col, 1.0, cos_x)
    return jnp.concatenate([main * ramp_cos, main * ramp_sin, lead * ramp_cos, lead * ramp_sin])


def local(images, rate_vectors, epoch_times):
    _, loc_rows, length = images.shape
    epoch_count = lax.axis_size("epoch")
    devices = lax.axis_size("row") * epoch_count
    device = lax.axis_index("row") * epoch_count + lax.axis_index("epoch")
    rates, epochs = rate_vectors.shape[0], epoch_times.shape[0]
    cols = length // 2 // devices
    table = packed_table(length, cols)
    table_t = jnp.asarray(np.ascontiguousarray(table.T))
    table = jnp.asarray(table)
    period = SUBPIX * length
    shift_y = (rate_vectors[:, 0:1] * epoch_times[None, :] % period).reshape(-1)
    shift_x = (rate_vectors[:, 1:2] * epoch_times[None, :] % period).reshape(-1)
    coefs = row_factors(shift_y, cols, length)
    scale = 1.0 / math.sqrt(epochs)
    factors = column_factors(shift_y, shift_x, scale, device, devices, cols, length)

    def exchange(values):
        return lax.all_to_all(values, ("row", "epoch"), 0, 0, tiled=True)

    spectra = exchange(row_transform(images, table_t, devices))
    back = exchange(column_stage(spectra, table, coefs, factors, epoch_count, rates))
    return image_rows(back.reshape(length, loc_rows), table)


def solution(mesh):
    in_specs = (P(("group", "epoch"), "row", None), P(), P())
    out_specs = P(("group", "epoch"), "row", None)
    return jax.shard_map(local, mesh=mesh, in_specs=in_specs, out_specs=out_specs, check_vma=False)
```

```python
import functools
import math

import jax
import jax.numpy as jnp
import ml_dtypes
import numpy as np
from jax import lax
from jax.experimental import pallas as pl
from jax.experimental.pallas import tpu as pltpu
from jax.sharding import PartitionSpec as P

SUBPIX = 16
GROUP = 128
BLOCK = 512
IMAGE_BLOCK = 256
ROW_CHUNK = 16
MIB = 1024 * 1024
CONTRACT_LAST = (((1,), (1,)), ((), ()))
HBM = pl.BlockSpec(memory_space=pltpu.HBM)
ANYWHERE = pl.BlockSpec(memory_space=pl.ANY)


def packed_table(length):
    half = length // 2
    index = np.arange(half, dtype=np.int32)
    freqs = 2 * (index % (half // 2)) + index // (half // 2)
    positions = np.arange(half, dtype=np.int32)
    turns = freqs[:, None] * positions[None, :] % length
    angles = turns.astype(np.float32) * np.float32(2.0 * math.pi / length)
    factor = np.float32(1.0 / math.sqrt(length))
    cosine = np.cos(angles) * factor
    sine = np.sin(angles) * factor
    sine[0] = np.where(positions % 2 == 0, factor, -factor)
    groups = np.stack([cosine.reshape(-1, GROUP, half), sine.reshape(-1, GROUP, half)], axis=1)
    return groups.reshape(length, half).astype(ml_dtypes.bfloat16)


def cost(flops, bytes_accessed):
    return pl.CostEstimate(flops=flops, bytes_accessed=bytes_accessed, transcendentals=0)


def start_copies(pairs, sems):
    copies = [
        pltpu.make_async_copy(source, target, sems.at[index])
        for index, (source, target) in enumerate(pairs)
    ]
    for copy in copies:
        copy.start()
    return copies


def wait_copies(copies):
    for copy in copies:
        copy.wait()


def fold(first, second):
    first, second = first.astype(jnp.float32), second.astype(jnp.float32)
    return (first + second).astype(jnp.bfloat16), (first - second).astype(jnp.bfloat16)


def row_kernel(
    images_hbm, table_hbm, out_hbm, images, table, folded, staged, image_sems, table_sems, out_sems
):
    loc_epochs, loc_rows, length = images.shape
    half = length // 2
    devices, _, width, _ = staged.shape
    cols = width // 2
    steps = length // BLOCK
    per_step = devices // steps
    per_group = GROUP // cols
    half_rows = loc_rows // 2
    image_parts = [
        (loc, slice(part * half_rows, (part + 1) * half_rows))
        for loc in range(loc_epochs)
        for part in range(2)
    ]
    image_copies = start_copies(
        [(images_hbm.at[loc, rows], images.at[loc, rows]) for loc, rows in image_parts], image_sems
    )
    table_copies = start_copies(
        [
            (table_hbm.at[pl.ds(step * BLOCK, BLOCK)], table.at[pl.ds(step * BLOCK, BLOCK)])
            for step in range(steps)
        ],
        table_sems,
    )
    for copy, (loc, rows) in zip(image_copies, image_parts):
        copy.wait()
        at = slice(loc * loc_rows + rows.start, loc * loc_rows + rows.stop)
        folded[0, at], folded[1, at] = fold(images[loc, rows, :half], images[loc, rows, half:])
    out_copies = []
    for step in range(steps):
        table_copies[step].wait()
        terms = lax.dot_general(
            table[step * BLOCK : (step + 1) * BLOCK],
            folded[2 * step // steps],
            CONTRACT_LAST,
            preferred_element_type=jnp.float32,
        )
        for dest in range(per_step):
            start = dest // per_group * 2 * GROUP + dest % per_group * cols
            parts = [terms[first : first + cols] for first in (start, start + GROUP)]
            block = jnp.concatenate(parts, axis=0).astype(jnp.bfloat16)
            for loc in range(loc_epochs):
                staged[step * per_step + dest, loc] = block[:, loc * loc_rows : (loc + 1) * loc_rows]
        at = pl.ds(step * per_step, per_step)
        out_copies.append(pltpu.make_async_copy(staged.at[at], out_hbm.at[at], out_sems.at[step]))
        out_copies[-1].start()
    wait_copies(out_copies)


def row_transform(images, table, devices):
    loc_epochs, loc_rows, length = images.shape
    half = length // 2
    rows = loc_epochs * loc_rows
    steps = length // BLOCK
    out = (devices, loc_epochs, length // devices, loc_rows)
    return pl.pallas_call(
        row_kernel,
        in_specs=[HBM, HBM],
        out_specs=HBM,
        out_shape=jax.ShapeDtypeStruct(out, jnp.bfloat16),
        scratch_shapes=[
            pltpu.VMEM(images.shape, jnp.bfloat16),
            pltpu.VMEM(table.shape, jnp.bfloat16),
            pltpu.VMEM((2, rows, half), jnp.bfloat16),
            pltpu.VMEM(out, jnp.bfloat16),
            pltpu.SemaphoreType.DMA((2 * loc_epochs,)),
            pltpu.SemaphoreType.DMA((steps,)),
            pltpu.SemaphoreType.DMA((steps,)),
        ],
        compiler_params=pltpu.CompilerParams(vmem_limit_bytes=58 * MIB),
        cost_estimate=cost(2 * rows * half * length, 2 * half * length + 4 * rows * length),
        name="row_transform",
    )(images, table)


def turn_angle(turns, whole):
    return (turns & (whole - 1)).astype(jnp.float32) * (2.0 * math.pi / whole)


def spread_pairs(scalars, lanes):
    pair = lax.broadcasted_iota(jnp.int32, (len(scalars), lanes), 0)
    values = jnp.zeros((len(scalars), lanes), jnp.int32)
    for index, scalar in enumerate(scalars):
        values = jnp.where(pair == index, scalar, values)
    return values


def packed_freqs(index, half):
    return 2 * (index & (half // 2 - 1)) + (index >= half // 2).astype(jnp.int32)


def row_factors(shift_y, half):
    shifts = spread_pairs(shift_y, half)
    freqs = packed_freqs(lax.broadcasted_iota(jnp.int32, shifts.shape, 1), half)
    angles = turn_angle((freqs - half) * shifts, SUBPIX * 2 * half)
    cos_rows = jnp.where(freqs == 0, 1.0, 2.0 * jnp.cos(angles))
    return cos_rows, jnp.where(freqs == 0, 0.0, 2.0 * jnp.sin(angles))


def column_factors(shift_y, shift_x, scale, device, cols, half):
    shifts_y, shifts_x = spread_pairs(shift_y, GROUP), spread_pairs(shift_x, GROUP)
    lane = lax.broadcasted_iota(jnp.int32, shifts_x.shape, 1)
    freqs = packed_freqs(device * cols + (lane & (cols - 1)), half)
    is_sine = (lane & cols) > 0
    paired = freqs == 0
    zero_col = paired & jnp.logical_not(is_sine)
    angles = turn_angle(shifts_x * (freqs - half), SUBPIX * 2 * half)
    ramp_cos = jnp.where(paired, scale, 2.0 * scale * jnp.cos(angles))
    ramp_sin = jnp.where(paired, 0.0, 2.0 * scale * jnp.sin(angles))
    ramp_sin = jnp.where(is_sine, ramp_sin, -ramp_sin)
    cos_x = jnp.cos(turn_angle(shifts_x, 2 * SUBPIX))
    cos_y = jnp.cos(turn_angle(shifts_y, 2 * SUBPIX))
    cos_xy = jnp.cos(turn_angle(shifts_x + shifts_y, 2 * SUBPIX))
    main = jnp.where(zero_col, cos_y, cos_xy)
    lead = jnp.where(zero_col, 1.0, cos_x)
    return jnp.concatenate(
        [main * ramp_cos, main * ramp_sin, lead * ramp_cos, lead * ramp_sin], axis=0
    )


def column_kernel(
    epoch_count,
    rate_smem,
    time_smem,
    z_any,
    table_any,
    out_hbm,
    received,
    table,
    rows_cos,
    rows_sin,
    spread,
    folded,
    products,
    sums,
    staged,
    z_sems,
    table_sems,
    out_sems,
):
    devices, loc_epochs, width, loc_rows = received.shape
    row_count = devices // epoch_count
    epochs = epoch_count * loc_epochs
    rates = rate_smem.shape[0]
    pairs = rates * epochs
    cols = width // 2
    length, half = table.shape
    steps = length // BLOCK
    z_parts = z_sems.shape[0]
    per_part = devices // z_parts
    z_copies = start_copies(
        [
            (z_any.at[pl.ds(part * per_part, per_part)], received.at[pl.ds(part * per_part, per_part)])
            for part in range(z_parts)
        ],
        z_sems,
    )
    table_copies = start_copies(
        [
            (table_any.at[pl.ds(step * BLOCK, BLOCK)], table.at[pl.ds(step * BLOCK, BLOCK)])
            for step in range(steps)
        ],
        table_sems,
    )
    device = lax.axis_index("row") * epoch_count + lax.axis_index("epoch")
    period = SUBPIX * length
    shift_y, shift_x = [
        [
            rate_smem[rate, axis] * time_smem[epoch] & (period - 1)
            for rate in range(rates)
            for epoch in range(epochs)
        ]
        for axis in range(2)
    ]
    rows_cos[...], rows_sin[...] = row_factors(shift_y, half)
    factors = column_factors(shift_y, shift_x, 1.0 / math.sqrt(epochs), device, cols, half).T
    for kind in range(4):
        for pair in range(pairs):
            at = kind * pairs + pair
            spread[kind, pair] = jnp.broadcast_to(factors[:width, at : at + 1], (width, GROUP))

    wait_copies(z_copies)
    per_tile = max(1, GROUP // loc_rows)
    for tile in range(row_count // 2 // per_tile):
        for core in range(epoch_count):
            for loc in range(loc_epochs):
                sides = []
                for side in range(2):
                    first = side * row_count // 2 + tile * per_tile
                    parts = [
                        received[(first + part) * epoch_count + core, loc] for part in range(per_tile)
                    ]
                    sides.append(parts[0] if per_tile == 1 else jnp.concatenate(parts, axis=1))
                at_row = (core * loc_epochs + loc) * width
                at_lane = tile * per_tile * loc_rows
                at = (slice(at_row, at_row + width), slice(at_lane, at_lane + per_tile * loc_rows))
                plus, minus = fold(sides[0], sides[1])
                folded[(0,) + at] = plus
                folded[(1,) + at] = minus

    chunk = min(ROW_CHUNK, cols)

    def add_ramped(step, group):
        tile = (step * BLOCK // 2 // GROUP + group) * GROUP
        at_even = group * 2 * GROUP
        at_odd = at_even + GROUP
        for rate in range(rates):
            for start in range(0, cols, chunk):
                real = slice(start, start + chunk)
                imag = slice(cols + start, cols + start + chunk)
                totals = [[0.0, 0.0], [0.0, 0.0]]
                leads = [0.0, 0.0]
                for epoch in range(epochs):
                    pair = rate * epochs + epoch
                    cos_row = rows_cos[pair : pair + 1, tile : tile + GROUP]
                    sin_row = rows_sin[pair : pair + 1, tile : tile + GROUP]
                    turned, evens = [], []
                    for part in (real, imag):
                        at = slice(epoch * width + part.start, epoch * width + part.stop)
                        even = products[step % 2, at, at_even : at_even + GROUP]
                        odd = products[step % 2, at, at_odd : at_odd + GROUP]
                        turned.append(
                            (cos_row * even + sin_row * odd, cos_row * odd - sin_row * even)
                        )
                        evens.append(even)
                    straight = [spread[0, pair, part] for part in (real, imag)]
                    crossed = [spread[1, pair, part] for part in (real, imag)]
                    for part in range(2):
                        for which in range(2):
                            totals[part][which] += (
                                straight[part] * turned[part][which]
                                + crossed[1 - part] * turned[1 - part][which]
                            )
                        if step == 0 and group == 0:
                            own, other = (real, imag) if part == 0 else (imag, real)
                            leads[part] += (
                                spread[2, pair, own] * evens[part]
                                + spread[3, pair, other] * evens[1 - part]
                            )
                for part, rows in enumerate((real, imag)):
                    even_sum, odd_sum = totals[part]
                    if step == 0 and group == 0:
                        first = lax.broadcasted_iota(jnp.int32, even_sum.shape, 1) == 0
                        even_sum = jnp.where(first, leads[part], even_sum)
                    at = slice(rate * width + rows.start, rate * width + rows.stop)
                    sums[at, step * BLOCK + at_even : step * BLOCK + at_even + GROUP] = even_sum.astype(
                        jnp.bfloat16
                    )
                    sums[at, step * BLOCK + at_odd : step * BLOCK + at_odd + GROUP] = odd_sum.astype(
                        jnp.bfloat16
                    )

    for step in range(steps):
        table_copies[step].wait()
        products[step % 2] = lax.dot_general(
            folded[2 * step // steps],
            table[step * BLOCK : (step + 1) * BLOCK],
            CONTRACT_LAST,
            preferred_element_type=jnp.float32,
        )
        for group in range(BLOCK // 2 // GROUP):
            add_ramped(step, group)

    loc_rates = rates // epoch_count
    blocks = max(1, half // BLOCK)
    out_copies = []
    for block in range(blocks):
        at = slice(block * BLOCK, (block + 1) * BLOCK)
        even, odd = [
            jnp.dot(
                sums[:, part * half : (part + 1) * half],
                table[part * half : (part + 1) * half, at],
                preferred_element_type=jnp.float32,
            )
            for part in range(2)
        ]
        rows_here = BLOCK // loc_rows
        for side, back in enumerate((even + odd, even - odd)):
            back = back.astype(jnp.bfloat16)
            first = side * row_count // 2 + block * rows_here
            for row in range(rows_here):
                for rate in range(rates):
                    dest = (first + row) * epoch_count + rate // loc_rates
                    staged[dest, rate % loc_rates] = back[
                        rate * width : (rate + 1) * width, row * loc_rows : (row + 1) * loc_rows
                    ]
            span = pl.ds(first * epoch_count, rows_here * epoch_count)
            out_copies.append(
                pltpu.make_async_copy(
                    staged.at[span], out_hbm.at[span], out_sems.at[2 * block + side]
                )
            )
            out_copies[-1].start()
    wait_copies(out_copies)


def column_stage(rate_vectors, epoch_times, spectra, table, epoch_count):
    devices, loc_epochs, width, loc_rows = spectra.shape
    length, half = table.shape
    epochs, rates = epoch_times.shape[0], rate_vectors.shape[0]
    steps = length // BLOCK
    out = (devices, rates // epoch_count, width, loc_rows)
    scalars = pl.BlockSpec(memory_space=pltpu.SMEM)
    return pl.pallas_call(
        functools.partial(column_kernel, epoch_count),
        in_specs=[scalars, scalars, ANYWHERE, ANYWHERE],
        out_specs=HBM,
        out_shape=jax.ShapeDtypeStruct(out, jnp.bfloat16),
        scratch_shapes=[
            pltpu.VMEM(spectra.shape, jnp.bfloat16),
            pltpu.VMEM(table.shape, jnp.bfloat16),
            pltpu.VMEM((rates * epochs, half), jnp.float32),
            pltpu.VMEM((rates * epochs, half), jnp.float32),
            pltpu.VMEM((4, rates * epochs, width, GROUP), jnp.float32),
            pltpu.VMEM((2, epochs * width, half), jnp.bfloat16),
            pltpu.VMEM((2, epochs * width, BLOCK), jnp.float32),
            pltpu.VMEM((rates * width, length), jnp.bfloat16),
            pltpu.VMEM(out, jnp.bfloat16),
            pltpu.SemaphoreType.DMA((4,)),
            pltpu.SemaphoreType.DMA((steps,)),
            pltpu.SemaphoreType.DMA((2 * max(1, half // BLOCK),)),
        ],
        compiler_params=pltpu.CompilerParams(vmem_limit_bytes=40 * MIB),
        cost_estimate=cost(
            2 * length * half * (epochs + rates) * width, 2 * length * half + 4 * spectra.size
        ),
        name="column_stage",
    )(rate_vectors, epoch_times, spectra, table)


def image_kernel(
    back_any, table_hbm, out_hbm, back, table, left, staged, back_sem, table_sems, out_sems
):
    length, half = table_hbm.shape
    blocks = half // IMAGE_BLOCK
    back_copy = pltpu.make_async_copy(back_any, back, back_sem)
    back_copy.start()
    table_copies = start_copies(
        [
            (table_hbm.at[:, block * IMAGE_BLOCK : (block + 1) * IMAGE_BLOCK], table.at[block])
            for block in range(blocks)
        ],
        table_sems,
    )
    back_copy.wait()
    width = back.shape[1]
    cols = width // 2
    per_group = GROUP // cols
    for group in range(back.shape[0] // per_group):
        members = [back[group * per_group + place].astype(jnp.float32) for place in range(per_group)]
        parts = [member[:cols] for member in members] + [member[cols:] for member in members]
        whole = jnp.concatenate(parts, axis=0)
        left[:, group * 2 * GROUP : (group + 1) * 2 * GROUP] = whole.T.astype(jnp.bfloat16)
    out_copies = []
    for block in range(blocks):
        table_copies[block].wait()
        even, odd = [
            jnp.dot(
                left[:, part * half : (part + 1) * half],
                table[block, part * half : (part + 1) * half],
                preferred_element_type=jnp.float32,
            )
            for part in range(2)
        ]
        for side, pixels in enumerate((even + odd, even - odd)):
            at = slice(side * half + block * IMAGE_BLOCK, side * half + (block + 1) * IMAGE_BLOCK)
            staged[:, at] = pixels
            out_copies.append(
                pltpu.make_async_copy(
                    staged.at[:, at], out_hbm.at[0, :, at], out_sems.at[2 * block + side]
                )
            )
            out_copies[-1].start()
    wait_copies(out_copies)


def image_rows(back, table):
    rows = back.shape[2]
    length, half = table.shape
    blocks = half // IMAGE_BLOCK
    return pl.pallas_call(
        image_kernel,
        in_specs=[ANYWHERE, ANYWHERE],
        out_specs=HBM,
        out_shape=jax.ShapeDtypeStruct((1, rows, length), jnp.float32),
        scratch_shapes=[
            pltpu.VMEM(back.shape, jnp.bfloat16),
            pltpu.VMEM((blocks, length, IMAGE_BLOCK), jnp.bfloat16),
            pltpu.VMEM((rows, length), jnp.bfloat16),
            pltpu.VMEM((rows, length), jnp.float32),
            pltpu.SemaphoreType.DMA,
            pltpu.SemaphoreType.DMA((blocks,)),
            pltpu.SemaphoreType.DMA((2 * blocks,)),
        ],
        compiler_params=pltpu.CompilerParams(vmem_limit_bytes=40 * MIB),
        cost_estimate=cost(2 * rows * half * length, 2 * half * length + 6 * rows * length),
        name="image_rows",
    )(back, table)


def local(images, rate_vectors, epoch_times):
    _, loc_rows, length = images.shape
    epoch_count = lax.axis_size("epoch")
    devices = lax.axis_size("row") * epoch_count
    table = jnp.asarray(packed_table(length))

    def exchange(values):
        return lax.all_to_all(values, ("row", "epoch"), 0, 0, tiled=True)

    spectra = exchange(row_transform(images, table, devices))
    back = exchange(column_stage(rate_vectors, epoch_times, spectra, table, epoch_count))
    return image_rows(back.reshape(devices, length // devices, loc_rows), table)


def solution(mesh):
    in_specs = (P(("group", "epoch"), "row", None), P(), P())
    out_specs = P(("group", "epoch"), "row", None)
    return jax.shard_map(local, mesh=mesh, in_specs=in_specs, out_specs=out_specs, check_vma=False)
```

```python
import functools
import math

import jax
import jax.numpy as jnp
import ml_dtypes
import numpy as np
from jax import lax
from jax.experimental import pallas as pl
from jax.experimental.pallas import tpu as pltpu
from jax.sharding import PartitionSpec as P

SUBPIX = 16
GROUP = 128
BLOCK = 512
IMAGE_BLOCK = 256
ROW_CHUNK = 16
MIB = 1024 * 1024
CONTRACT_LAST = (((1,), (1,)), ((), ()))
HBM = pl.BlockSpec(memory_space=pltpu.HBM)
IN_VMEM = pl.BlockSpec(memory_space=pltpu.VMEM)


def packed_table(length):
    half = length // 2
    index = np.arange(half, dtype=np.int32)
    freqs = 2 * (index % (half // 2)) + index // (half // 2)
    positions = np.arange(half, dtype=np.int32)
    turns = freqs[:, None] * positions[None, :] % length
    angles = turns.astype(np.float32) * np.float32(2.0 * math.pi / length)
    factor = np.float32(1.0 / math.sqrt(length))
    cosine = np.cos(angles) * factor
    sine = np.sin(angles) * factor
    sine[0] = np.where(positions % 2 == 0, factor, -factor)
    groups = np.stack([cosine.reshape(-1, GROUP, half), sine.reshape(-1, GROUP, half)], axis=1)
    return groups.reshape(length, half).astype(ml_dtypes.bfloat16)


def cost(flops, bytes_accessed):
    return pl.CostEstimate(flops=flops, bytes_accessed=bytes_accessed, transcendentals=0)


def wait_copies(copies):
    for copy in copies:
        copy.wait()


def fold(first, second):
    first, second = first.astype(jnp.float32), second.astype(jnp.float32)
    return (first + second).astype(jnp.bfloat16), (first - second).astype(jnp.bfloat16)


def row_kernel(
    images_hbm, table_hbm, out_hbm, images, table, folded, staged, image_sems, table_sems, out_sems
):
    loc_epochs, loc_rows, length = images.shape
    half = length // 2
    devices, _, width, _ = staged.shape
    cols = width // 2
    steps = length // BLOCK
    per_step = devices // steps
    per_group = GROUP // cols
    image_copies = [
        pltpu.make_async_copy(images_hbm.at[loc], images.at[loc], image_sems.at[loc])
        for loc in range(loc_epochs)
    ]
    table_copies = [
        pltpu.make_async_copy(
            table_hbm.at[pl.ds(step * BLOCK, BLOCK)],
            table.at[pl.ds(step * BLOCK, BLOCK)],
            table_sems.at[step],
        )
        for step in range(steps)
    ]
    for copy in image_copies + table_copies[:1]:
        copy.start()
    for loc in range(loc_epochs):
        image_copies[loc].wait()
        at = slice(loc * loc_rows, (loc + 1) * loc_rows)
        folded[0, at], folded[1, at] = fold(images[loc, :, :half], images[loc, :, half:])
    for copy in table_copies[1:]:
        copy.start()
    out_copies = []
    for step in range(steps):
        table_copies[step].wait()
        terms = lax.dot_general(
            table[step * BLOCK : (step + 1) * BLOCK],
            folded[2 * step // steps],
            CONTRACT_LAST,
            preferred_element_type=jnp.float32,
        )
        for dest in range(per_step):
            start = dest // per_group * 2 * GROUP + dest % per_group * cols
            parts = [terms[first : first + cols] for first in (start, start + GROUP)]
            block = jnp.concatenate(parts, axis=0).astype(jnp.bfloat16)
            for loc in range(loc_epochs):
                staged[step * per_step + dest, loc] = block[:, loc * loc_rows : (loc + 1) * loc_rows]
        at = pl.ds(step * per_step, per_step)
        out_copies.append(pltpu.make_async_copy(staged.at[at], out_hbm.at[at], out_sems.at[step]))
        out_copies[-1].start()
    wait_copies(out_copies)


def row_transform(images, table, devices):
    loc_epochs, loc_rows, length = images.shape
    half = length // 2
    rows = loc_epochs * loc_rows
    steps = length // BLOCK
    out = (devices, loc_epochs, length // devices, loc_rows)
    return pl.pallas_call(
        row_kernel,
        in_specs=[HBM, HBM],
        out_specs=HBM,
        out_shape=jax.ShapeDtypeStruct(out, jnp.bfloat16),
        scratch_shapes=[
            pltpu.VMEM(images.shape, jnp.bfloat16),
            pltpu.VMEM(table.shape, jnp.bfloat16),
            pltpu.VMEM((2, rows, half), jnp.bfloat16),
            pltpu.VMEM(out, jnp.bfloat16),
            pltpu.SemaphoreType.DMA((loc_epochs,)),
            pltpu.SemaphoreType.DMA((steps,)),
            pltpu.SemaphoreType.DMA((steps,)),
        ],
        compiler_params=pltpu.CompilerParams(vmem_limit_bytes=58 * MIB),
        cost_estimate=cost(2 * rows * half * length, 2 * half * length + 4 * rows * length),
        name="row_transform",
    )(images, table)


def turn_angle(turns, whole):
    return (turns & (whole - 1)).astype(jnp.float32) * (2.0 * math.pi / whole)


def spread_pairs(scalars, lanes):
    pair = lax.broadcasted_iota(jnp.int32, (len(scalars), lanes), 0)
    values = jnp.zeros((len(scalars), lanes), jnp.int32)
    for index, scalar in enumerate(scalars):
        values = jnp.where(pair == index, scalar, values)
    return values


def packed_freqs(index, half):
    return 2 * (index & (half // 2 - 1)) + (index >= half // 2).astype(jnp.int32)


def row_factors(shift_y, half):
    shifts = spread_pairs(shift_y, half)
    freqs = packed_freqs(lax.broadcasted_iota(jnp.int32, shifts.shape, 1), half)
    angles = turn_angle((freqs - half) * shifts, SUBPIX * 2 * half)
    cos_rows = jnp.where(freqs == 0, 1.0, 2.0 * jnp.cos(angles))
    return cos_rows, jnp.where(freqs == 0, 0.0, 2.0 * jnp.sin(angles))


def column_factors(shift_y, shift_x, scale, device, cols, half):
    shifts_y, shifts_x = spread_pairs(shift_y, GROUP), spread_pairs(shift_x, GROUP)
    lane = lax.broadcasted_iota(jnp.int32, shifts_x.shape, 1)
    freqs = packed_freqs(device * cols + (lane & (cols - 1)), half)
    is_sine = (lane & cols) > 0
    paired = freqs == 0
    zero_col = paired & jnp.logical_not(is_sine)
    angles = turn_angle(shifts_x * (freqs - half), SUBPIX * 2 * half)
    ramp_cos = jnp.where(paired, scale, 2.0 * scale * jnp.cos(angles))
    ramp_sin = jnp.where(paired, 0.0, 2.0 * scale * jnp.sin(angles))
    ramp_sin = jnp.where(is_sine, ramp_sin, -ramp_sin)
    cos_x = jnp.cos(turn_angle(shifts_x, 2 * SUBPIX))
    cos_y = jnp.cos(turn_angle(shifts_y, 2 * SUBPIX))
    cos_xy = jnp.cos(turn_angle(shifts_x + shifts_y, 2 * SUBPIX))
    main = jnp.where(zero_col, cos_y, cos_xy)
    lead = jnp.where(zero_col, 1.0, cos_x)
    return jnp.concatenate(
        [main * ramp_cos, main * ramp_sin, lead * ramp_cos, lead * ramp_sin], axis=0
    )


def column_kernel(
    epoch_count,
    rate_smem,
    time_smem,
    received,
    table,
    out_hbm,
    rows_cos,
    rows_sin,
    spread,
    folded,
    products,
    sums,
    staged,
    out_sems,
):
    devices, loc_epochs, width, loc_rows = received.shape
    row_count = devices // epoch_count
    epochs = epoch_count * loc_epochs
    rates = rate_smem.shape[0]
    pairs = rates * epochs
    cols = width // 2
    length, half = table.shape
    steps = length // BLOCK
    device = lax.axis_index("row") * epoch_count + lax.axis_index("epoch")
    period = SUBPIX * length
    shift_y, shift_x = [
        [
            rate_smem[rate, axis] * time_smem[epoch] & (period - 1)
            for rate in range(rates)
            for epoch in range(epochs)
        ]
        for axis in range(2)
    ]
    rows_cos[...], rows_sin[...] = row_factors(shift_y, half)
    factors = column_factors(shift_y, shift_x, 1.0 / math.sqrt(epochs), device, cols, half).T
    for kind in range(4):
        for pair in range(pairs):
            at = kind * pairs + pair
            spread[kind, pair] = jnp.broadcast_to(factors[:width, at : at + 1], (width, GROUP))

    per_tile = max(1, GROUP // loc_rows)
    for tile in range(row_count // 2 // per_tile):
        for core in range(epoch_count):
            for loc in range(loc_epochs):
                sides = []
                for side in range(2):
                    first = side * row_count // 2 + tile * per_tile
                    parts = [
                        received[(first + part) * epoch_count + core, loc] for part in range(per_tile)
                    ]
                    sides.append(parts[0] if per_tile == 1 else jnp.concatenate(parts, axis=1))
                at_row = (core * loc_epochs + loc) * width
                at_lane = tile * per_tile * loc_rows
                at = (slice(at_row, at_row + width), slice(at_lane, at_lane + per_tile * loc_rows))
                plus, minus = fold(sides[0], sides[1])
                folded[(0,) + at] = plus
                folded[(1,) + at] = minus

    chunk = min(ROW_CHUNK, cols)

    def add_ramped(step, group):
        tile = (step * BLOCK // 2 // GROUP + group) * GROUP
        at_even = group * 2 * GROUP
        at_odd = at_even + GROUP
        for rate in range(rates):
            for start in range(0, cols, chunk):
                real = slice(start, start + chunk)
                imag = slice(cols + start, cols + start + chunk)
                totals = [[0.0, 0.0], [0.0, 0.0]]
                leads = [0.0, 0.0]
                for epoch in range(epochs):
                    pair = rate * epochs + epoch
                    cos_row = rows_cos[pair : pair + 1, tile : tile + GROUP]
                    sin_row = rows_sin[pair : pair + 1, tile : tile + GROUP]
                    turned, evens = [], []
                    for part in (real, imag):
                        at = slice(epoch * width + part.start, epoch * width + part.stop)
                        even = products[step % 2, at, at_even : at_even + GROUP]
                        odd = products[step % 2, at, at_odd : at_odd + GROUP]
                        turned.append(
                            (cos_row * even + sin_row * odd, cos_row * odd - sin_row * even)
                        )
                        evens.append(even)
                    straight = [spread[0, pair, part] for part in (real, imag)]
                    crossed = [spread[1, pair, part] for part in (real, imag)]
                    for part in range(2):
                        for which in range(2):
                            totals[part][which] += (
                                straight[part] * turned[part][which]
                                + crossed[1 - part] * turned[1 - part][which]
                            )
                        if step == 0 and group == 0:
                            own, other = (real, imag) if part == 0 else (imag, real)
                            leads[part] += (
                                spread[2, pair, own] * evens[part]
                                + spread[3, pair, other] * evens[1 - part]
                            )
                for part, rows in enumerate((real, imag)):
                    even_sum, odd_sum = totals[part]
                    if step == 0 and group == 0:
                        first = lax.broadcasted_iota(jnp.int32, even_sum.shape, 1) == 0
                        even_sum = jnp.where(first, leads[part], even_sum)
                    at = slice(rate * width + rows.start, rate * width + rows.stop)
                    sums[at, step * BLOCK + at_even : step * BLOCK + at_even + GROUP] = even_sum.astype(
                        jnp.bfloat16
                    )
                    sums[at, step * BLOCK + at_odd : step * BLOCK + at_odd + GROUP] = odd_sum.astype(
                        jnp.bfloat16
                    )

    for step in range(steps):
        products[step % 2] = lax.dot_general(
            folded[2 * step // steps],
            table[step * BLOCK : (step + 1) * BLOCK],
            CONTRACT_LAST,
            preferred_element_type=jnp.float32,
        )
        for group in range(BLOCK // 2 // GROUP):
            add_ramped(step, group)

    loc_rates = rates // epoch_count
    blocks = max(1, half // BLOCK)
    out_copies = []
    for block in range(blocks):
        at = slice(block * BLOCK, (block + 1) * BLOCK)
        even, odd = [
            jnp.dot(
                sums[:, part * half : (part + 1) * half],
                table[part * half : (part + 1) * half, at],
                preferred_element_type=jnp.float32,
            )
            for part in range(2)
        ]
        rows_here = BLOCK // loc_rows
        for side, back in enumerate((even + odd, even - odd)):
            back = back.astype(jnp.bfloat16)
            first = side * row_count // 2 + block * rows_here
            for row in range(rows_here):
                for rate in range(rates):
                    dest = (first + row) * epoch_count + rate // loc_rates
                    staged[dest, rate % loc_rates] = back[
                        rate * width : (rate + 1) * width, row * loc_rows : (row + 1) * loc_rows
                    ]
            span = pl.ds(first * epoch_count, rows_here * epoch_count)
            out_copies.append(
                pltpu.make_async_copy(
                    staged.at[span], out_hbm.at[span], out_sems.at[2 * block + side]
                )
            )
            out_copies[-1].start()
    wait_copies(out_copies)


def column_stage(rate_vectors, epoch_times, spectra, table, epoch_count):
    devices, loc_epochs, width, loc_rows = spectra.shape
    length, half = table.shape
    epochs, rates = epoch_times.shape[0], rate_vectors.shape[0]
    out = (devices, rates // epoch_count, width, loc_rows)
    scalars = pl.BlockSpec(memory_space=pltpu.SMEM)
    return pl.pallas_call(
        functools.partial(column_kernel, epoch_count),
        in_specs=[scalars, scalars, IN_VMEM, IN_VMEM],
        out_specs=HBM,
        out_shape=jax.ShapeDtypeStruct(out, jnp.bfloat16),
        scratch_shapes=[
            pltpu.VMEM((rates * epochs, half), jnp.float32),
            pltpu.VMEM((rates * epochs, half), jnp.float32),
            pltpu.VMEM((4, rates * epochs, width, GROUP), jnp.float32),
            pltpu.VMEM((2, epochs * width, half), jnp.bfloat16),
            pltpu.VMEM((2, epochs * width, BLOCK), jnp.float32),
            pltpu.VMEM((rates * width, length), jnp.bfloat16),
            pltpu.VMEM(out, jnp.bfloat16),
            pltpu.SemaphoreType.DMA((2 * max(1, half // BLOCK),)),
        ],
        compiler_params=pltpu.CompilerParams(vmem_limit_bytes=40 * MIB),
        cost_estimate=cost(
            2 * length * half * (epochs + rates) * width, 2 * length * half + 4 * spectra.size
        ),
        name="column_stage",
    )(rate_vectors, epoch_times, spectra, table)


def image_kernel(back, table, out_hbm, left, staged, out_sems):
    length, half = table.shape
    blocks = half // IMAGE_BLOCK
    width = back.shape[1]
    cols = width // 2
    per_group = GROUP // cols
    for group in range(back.shape[0] // per_group):
        members = [back[group * per_group + place].astype(jnp.float32) for place in range(per_group)]
        parts = [member[:cols] for member in members] + [member[cols:] for member in members]
        whole = jnp.concatenate(parts, axis=0)
        left[:, group * 2 * GROUP : (group + 1) * 2 * GROUP] = whole.T.astype(jnp.bfloat16)
    out_copies = []
    for block in range(blocks):
        at_block = slice(block * IMAGE_BLOCK, (block + 1) * IMAGE_BLOCK)
        even, odd = [
            jnp.dot(
                left[:, part * half : (part + 1) * half],
                table[part * half : (part + 1) * half, at_block],
                preferred_element_type=jnp.float32,
            )
            for part in range(2)
        ]
        for side, pixels in enumerate((even + odd, even - odd)):
            at = slice(side * half + block * IMAGE_BLOCK, side * half + (block + 1) * IMAGE_BLOCK)
            staged[:, at] = pixels
            out_copies.append(
                pltpu.make_async_copy(
                    staged.at[:, at], out_hbm.at[0, :, at], out_sems.at[2 * block + side]
                )
            )
            out_copies[-1].start()
    wait_copies(out_copies)


def image_rows(back, table):
    rows = back.shape[2]
    length, half = table.shape
    blocks = half // IMAGE_BLOCK
    return pl.pallas_call(
        image_kernel,
        in_specs=[IN_VMEM, IN_VMEM],
        out_specs=HBM,
        out_shape=jax.ShapeDtypeStruct((1, rows, length), jnp.float32),
        scratch_shapes=[
            pltpu.VMEM((rows, length), jnp.bfloat16),
            pltpu.VMEM((rows, length), jnp.float32),
            pltpu.SemaphoreType.DMA((2 * blocks,)),
        ],
        compiler_params=pltpu.CompilerParams(vmem_limit_bytes=40 * MIB),
        cost_estimate=cost(2 * rows * half * length, 2 * half * length + 6 * rows * length),
        name="image_rows",
    )(back, table)


def local(images, rate_vectors, epoch_times):
    _, loc_rows, length = images.shape
    epoch_count = lax.axis_size("epoch")
    devices = lax.axis_size("row") * epoch_count
    table = jnp.asarray(packed_table(length))

    def exchange(values):
        return lax.all_to_all(values, ("row", "epoch"), 0, 0, tiled=True)

    spectra = exchange(row_transform(images, table, devices))
    back = exchange(column_stage(rate_vectors, epoch_times, spectra, table, epoch_count))
    return image_rows(back.reshape(devices, length // devices, loc_rows), table)


def solution(mesh):
    in_specs = (P(("group", "epoch"), "row", None), P(), P())
    out_specs = P(("group", "epoch"), "row", None)
    return jax.shard_map(local, mesh=mesh, in_specs=in_specs, out_specs=out_specs, check_vma=False)
```

```python
import functools
import math

import jax
import jax.numpy as jnp
import ml_dtypes
import numpy as np
from jax import lax
from jax.experimental import pallas as pl
from jax.experimental.pallas import tpu as pltpu
from jax.sharding import PartitionSpec as P

SUBPIX = 16
GROUP = 128
BLOCK = 512
IMAGE_BLOCK = 256
ROW_CHUNK = 16
MIB = 1024 * 1024
CONTRACT_LAST = (((1,), (1,)), ((), ()))
HBM = pl.BlockSpec(memory_space=pltpu.HBM)
IN_VMEM = pl.BlockSpec(memory_space=pltpu.VMEM)


def packed_freqs(index, half, where=jnp.where):
    even = 4 * index - where(index < half // 4, 0, half - 2)
    return where(index < half // 2, even, 2 * index - half + 1)


def packed_tables(length):
    half, quarter = length // 2, length // 4
    freqs = packed_freqs(np.arange(half, dtype=np.int32), half, np.where)
    positions = np.arange(half, dtype=np.int32)
    turns = freqs[:, None] * positions[None, :] % length
    angles = turns.astype(np.float32) * np.float32(2.0 * math.pi / length)
    factor = np.float32(1.0 / math.sqrt(length))
    cosine = np.cos(angles) * factor
    sine = np.sin(angles) * factor
    sine[0] = np.where(positions % 2 == 0, factor, -factor)
    groups = np.stack([cosine.reshape(-1, GROUP, half), sine.reshape(-1, GROUP, half)], axis=1)
    table = groups.reshape(length, half).astype(ml_dtypes.bfloat16)
    return np.ascontiguousarray(table[:half, :quarter]), table[half:]


def cost(flops, bytes_accessed):
    return pl.CostEstimate(flops=flops, bytes_accessed=bytes_accessed, transcendentals=0)


def wait_copies(copies):
    for copy in copies:
        copy.wait()


def fold(quarters):
    first, second, third, fourth = [part.astype(jnp.float32) for part in quarters]
    near, far = first + third, second + fourth
    folds = near + far, near - far, first - third, second - fourth
    return [part.astype(jnp.bfloat16) for part in folds]


def row_kernel(
    images_hbm,
    even_hbm,
    odd_hbm,
    out_hbm,
    images,
    even_table,
    odd_table,
    even_fold,
    odd_fold,
    staged,
    image_sems,
    table_sems,
    out_sems,
):
    loc_epochs, loc_rows, length = images.shape
    half, quarter = length // 2, length // 4
    devices, _, width, _ = staged.shape
    cols = width // 2
    steps = length // BLOCK
    per_step = devices // steps
    per_group = GROUP // cols
    image_copies = [
        pltpu.make_async_copy(images_hbm.at[loc], images.at[loc], image_sems.at[loc])
        for loc in range(loc_epochs)
    ]
    table_copies = [
        pltpu.make_async_copy(
            source.at[pl.ds(block * BLOCK, BLOCK)],
            target.at[pl.ds(block * BLOCK, BLOCK)],
            table_sems.at[first + block],
        )
        for first, source, target in ((0, even_hbm, even_table), (steps // 2, odd_hbm, odd_table))
        for block in range(steps // 2)
    ]
    for copy in image_copies[:1] + table_copies[: steps // 2]:
        copy.start()
    out_copies = []
    for loc in range(loc_epochs):
        image_copies[loc].wait()
        if loc == 0:
            for copy in table_copies[steps // 2 :] + image_copies[1:]:
                copy.start()
        folds = fold([images[loc, :, at * quarter : (at + 1) * quarter] for at in range(4)])
        even_fold[0], even_fold[1] = folds[:2]
        odd_fold[:, :quarter], odd_fold[:, quarter:] = folds[2:]
        for step in range(steps):
            if loc == 0:
                table_copies[step].wait()
            at = slice(step % (steps // 2) * BLOCK, (step % (steps // 2) + 1) * BLOCK)
            if step < steps // 2:
                left, right = even_table[at], even_fold[4 * step // steps]
            else:
                left, right = odd_table[at], odd_fold[...]
            terms = lax.dot_general(left, right, CONTRACT_LAST, preferred_element_type=jnp.float32)
            for dest in range(per_step):
                start = dest // per_group * 2 * GROUP + dest % per_group * cols
                parts = [terms[first : first + cols] for first in (start, start + GROUP)]
                block = jnp.concatenate(parts, axis=0).astype(jnp.bfloat16)
                staged[step * per_step + dest, loc] = block
            at = pl.ds(step * per_step, per_step)
            out_copies.append(
                pltpu.make_async_copy(
                    staged.at[at, loc], out_hbm.at[at, loc], out_sems.at[loc * steps + step]
                )
            )
            out_copies[-1].start()
    wait_copies(out_copies)


def row_transform(images, even_table, odd_table, devices):
    loc_epochs, loc_rows, length = images.shape
    half, quarter = length // 2, length // 4
    rows = loc_epochs * loc_rows
    steps = length // BLOCK
    out = (devices, loc_epochs, length // devices, loc_rows)
    return pl.pallas_call(
        row_kernel,
        in_specs=[HBM, HBM, HBM],
        out_specs=HBM,
        out_shape=jax.ShapeDtypeStruct(out, jnp.bfloat16),
        scratch_shapes=[
            pltpu.VMEM(images.shape, jnp.bfloat16),
            pltpu.VMEM(even_table.shape, jnp.bfloat16),
            pltpu.VMEM(odd_table.shape, jnp.bfloat16),
            pltpu.VMEM((2, loc_rows, quarter), jnp.bfloat16),
            pltpu.VMEM((loc_rows, half), jnp.bfloat16),
            pltpu.VMEM(out, jnp.bfloat16),
            pltpu.SemaphoreType.DMA((loc_epochs,)),
            pltpu.SemaphoreType.DMA((steps,)),
            pltpu.SemaphoreType.DMA((loc_epochs * steps,)),
        ],
        compiler_params=pltpu.CompilerParams(vmem_limit_bytes=58 * MIB),
        cost_estimate=cost(
            2 * rows * (even_table.size + odd_table.size), 3 * half * half + 4 * rows * length
        ),
        name="row_transform",
    )(images, even_table, odd_table)


def turn_angle(turns, whole):
    return (turns & (whole - 1)).astype(jnp.float32) * (2.0 * math.pi / whole)


def spread_pairs(scalars, lanes):
    pair = lax.broadcasted_iota(jnp.int32, (len(scalars), lanes), 0)
    values = jnp.zeros((len(scalars), lanes), jnp.int32)
    for index, scalar in enumerate(scalars):
        values = jnp.where(pair == index, scalar, values)
    return values


def row_factors(shift_y, half):
    shifts = spread_pairs(shift_y, half)
    freqs = packed_freqs(lax.broadcasted_iota(jnp.int32, shifts.shape, 1), half)
    angles = turn_angle((freqs - half) * shifts, SUBPIX * 2 * half)
    cos_rows = jnp.where(freqs == 0, 1.0, 2.0 * jnp.cos(angles))
    return cos_rows, jnp.where(freqs == 0, 0.0, 2.0 * jnp.sin(angles))


def column_factors(shift_y, shift_x, scale, device, cols, half):
    shifts_y, shifts_x = spread_pairs(shift_y, GROUP), spread_pairs(shift_x, GROUP)
    lane = lax.broadcasted_iota(jnp.int32, shifts_x.shape, 1)
    freqs = packed_freqs(device * cols + (lane & (cols - 1)), half)
    is_sine = (lane & cols) > 0
    paired = freqs == 0
    zero_col = paired & jnp.logical_not(is_sine)
    angles = turn_angle(shifts_x * (freqs - half), SUBPIX * 2 * half)
    ramp_cos = jnp.where(paired, scale, 2.0 * scale * jnp.cos(angles))
    ramp_sin = jnp.where(paired, 0.0, 2.0 * scale * jnp.sin(angles))
    ramp_sin = jnp.where(is_sine, ramp_sin, -ramp_sin)
    cos_x = jnp.cos(turn_angle(shifts_x, 2 * SUBPIX))
    cos_y = jnp.cos(turn_angle(shifts_y, 2 * SUBPIX))
    cos_xy = jnp.cos(turn_angle(shifts_x + shifts_y, 2 * SUBPIX))
    main = jnp.where(zero_col, cos_y, cos_xy)
    lead = jnp.where(zero_col, 1.0, cos_x)
    return jnp.concatenate(
        [main * ramp_cos, main * ramp_sin, lead * ramp_cos, lead * ramp_sin], axis=0
    )


def column_kernel(
    epoch_count,
    rate_smem,
    time_smem,
    received,
    even_table,
    odd_table,
    out_hbm,
    rows_cos,
    rows_sin,
    spread,
    even_fold,
    odd_fold,
    products,
    sums,
    staged,
    out_sems,
):
    devices, loc_epochs, width, loc_rows = received.shape
    row_count = devices // epoch_count
    epochs = epoch_count * loc_epochs
    rates = rate_smem.shape[0]
    pairs = rates * epochs
    cols = width // 2
    half, quarter = even_table.shape
    length = 2 * half
    steps = length // BLOCK
    device = lax.axis_index("row") * epoch_count + lax.axis_index("epoch")
    period = SUBPIX * length
    shift_y, shift_x = [
        [
            rate_smem[rate, axis] * time_smem[epoch] & (period - 1)
            for rate in range(rates)
            for epoch in range(epochs)
        ]
        for axis in range(2)
    ]
    per_tile = max(1, GROUP // loc_rows)
    tile_rows = per_tile * loc_rows
    for tile in range(row_count // 4 // per_tile):
        at_lane = slice(tile * tile_rows, (tile + 1) * tile_rows)
        far_lane = slice(quarter + at_lane.start, quarter + at_lane.stop)
        for core in range(epoch_count):
            for loc in range(loc_epochs):
                quarters = []
                for side in range(4):
                    first = side * row_count // 4 + tile * per_tile
                    parts = [
                        received[(first + part) * epoch_count + core, loc] for part in range(per_tile)
                    ]
                    quarters.append(parts[0] if per_tile == 1 else jnp.concatenate(parts, axis=1))
                at_row = (core * loc_epochs + loc) * width
                at = slice(at_row, at_row + width)
                folds = fold(quarters)
                even_fold[0, at, at_lane], even_fold[1, at, at_lane] = folds[:2]
                odd_fold[at, at_lane], odd_fold[at, far_lane] = folds[2:]

    def multiply(step):
        at = slice(step % (steps // 2) * BLOCK, (step % (steps // 2) + 1) * BLOCK)
        if step < steps // 2:
            left, right = even_fold[4 * step // steps], even_table[at]
        else:
            left, right = odd_fold[...], odd_table[at]
        products[step % 2] = lax.dot_general(
            left, right, CONTRACT_LAST, preferred_element_type=jnp.float32
        )

    multiply(0)
    rows_cos[...], rows_sin[...] = row_factors(shift_y, half)
    factors = column_factors(shift_y, shift_x, 1.0 / math.sqrt(epochs), device, cols, half).T
    for kind in range(4):
        for pair in range(pairs):
            at = kind * pairs + pair
            spread[kind, pair] = jnp.broadcast_to(factors[:width, at : at + 1], (width, GROUP))

    chunk = min(ROW_CHUNK, cols)

    def add_ramped(step, group):
        tile = (step * BLOCK // 2 // GROUP + group) * GROUP
        at_even = group * 2 * GROUP
        at_odd = at_even + GROUP
        for rate in range(rates):
            for start in range(0, cols, chunk):
                real = slice(start, start + chunk)
                imag = slice(cols + start, cols + start + chunk)
                totals = [[0.0, 0.0], [0.0, 0.0]]
                leads = [0.0, 0.0]
                for epoch in range(epochs):
                    pair = rate * epochs + epoch
                    cos_row = rows_cos[pair : pair + 1, tile : tile + GROUP]
                    sin_row = rows_sin[pair : pair + 1, tile : tile + GROUP]
                    turned, evens = [], []
                    for part in (real, imag):
                        at = slice(epoch * width + part.start, epoch * width + part.stop)
                        even = products[step % 2, at, at_even : at_even + GROUP]
                        odd = products[step % 2, at, at_odd : at_odd + GROUP]
                        turned.append(
                            (cos_row * even + sin_row * odd, cos_row * odd - sin_row * even)
                        )
                        evens.append(even)
                    straight = [spread[0, pair, part] for part in (real, imag)]
                    crossed = [spread[1, pair, part] for part in (real, imag)]
                    for part in range(2):
                        for which in range(2):
                            totals[part][which] += (
                                straight[part] * turned[part][which]
                                + crossed[1 - part] * turned[1 - part][which]
                            )
                        if step == 0 and group == 0:
                            own, other = (real, imag) if part == 0 else (imag, real)
                            leads[part] += (
                                spread[2, pair, own] * evens[part]
                                + spread[3, pair, other] * evens[1 - part]
                            )
                for part, rows in enumerate((real, imag)):
                    even_sum, odd_sum = totals[part]
                    if step == 0 and group == 0:
                        first = lax.broadcasted_iota(jnp.int32, even_sum.shape, 1) == 0
                        even_sum = jnp.where(first, leads[part], even_sum)
                    at = slice(rate * width + rows.start, rate * width + rows.stop)
                    sums[at, step * BLOCK + at_even : step * BLOCK + at_even + GROUP] = even_sum.astype(
                        jnp.bfloat16
                    )
                    sums[at, step * BLOCK + at_odd : step * BLOCK + at_odd + GROUP] = odd_sum.astype(
                        jnp.bfloat16
                    )

    for step in range(steps):
        if step + 1 < steps:
            multiply(step + 1)
        for group in range(BLOCK // 2 // GROUP):
            add_ramped(step, group)

    loc_rates = rates // epoch_count
    out_copies = []

    def send(side, back):
        back = back.astype(jnp.bfloat16)
        rows_here = quarter // loc_rows
        for row in range(rows_here):
            for rate in range(rates):
                dest = (side * rows_here + row) * epoch_count + rate // loc_rates
                staged[dest, rate % loc_rates] = back[
                    rate * width : (rate + 1) * width, row * loc_rows : (row + 1) * loc_rows
                ]
        span = pl.ds(side * rows_here * epoch_count, rows_here * epoch_count)
        out_copies.append(
            pltpu.make_async_copy(staged.at[span], out_hbm.at[span], out_sems.at[side])
        )
        out_copies[-1].start()

    inverse_parts(sums, even_table, odd_table, slice(0, quarter), quarter, send)
    wait_copies(out_copies)


def inverse_parts(left, even_table, odd_table, at, quarter, send):
    half = 2 * quarter
    far = slice(quarter + at.start, quarter + at.stop)

    def product(first, depth, right):
        return jnp.dot(left[:, first : first + depth], right, preferred_element_type=jnp.float32)

    zero = product(0, quarter, even_table[:quarter, at])
    two = product(quarter, quarter, even_table[quarter:, at])
    for position, even, span in ((0, zero + two, at), (1, zero - two, far)):
        odd = product(half, half, odd_table[:, span])
        send(position, even + odd)
        send(position + 2, even - odd)


def column_stage(rate_vectors, epoch_times, spectra, even_table, odd_table, epoch_count):
    devices, loc_epochs, width, loc_rows = spectra.shape
    half, quarter = even_table.shape
    length = 2 * half
    epochs, rates = epoch_times.shape[0], rate_vectors.shape[0]
    out = (devices, rates // epoch_count, width, loc_rows)
    scalars = pl.BlockSpec(memory_space=pltpu.SMEM)
    return pl.pallas_call(
        functools.partial(column_kernel, epoch_count),
        in_specs=[scalars, scalars, IN_VMEM, IN_VMEM, IN_VMEM],
        out_specs=HBM,
        out_shape=jax.ShapeDtypeStruct(out, jnp.bfloat16),
        scratch_shapes=[
            pltpu.VMEM((rates * epochs, half), jnp.float32),
            pltpu.VMEM((rates * epochs, half), jnp.float32),
            pltpu.VMEM((4, rates * epochs, width, GROUP), jnp.float32),
            pltpu.VMEM((2, epochs * width, quarter), jnp.bfloat16),
            pltpu.VMEM((epochs * width, half), jnp.bfloat16),
            pltpu.VMEM((2, epochs * width, BLOCK), jnp.float32),
            pltpu.VMEM((rates * width, length), jnp.bfloat16),
            pltpu.VMEM(out, jnp.bfloat16),
            pltpu.SemaphoreType.DMA((4,)),
        ],
        compiler_params=pltpu.CompilerParams(vmem_limit_bytes=40 * MIB),
        cost_estimate=cost(
            2 * (even_table.size + odd_table.size) * (epochs + rates) * width,
            3 * half * half + 4 * spectra.size,
        ),
        name="column_stage",
    )(rate_vectors, epoch_times, spectra, even_table, odd_table)


def image_kernel(back, even_table, odd_table, out_hbm, left, staged, out_sems):
    quarter = even_table.shape[1]
    width = back.shape[1]
    cols = width // 2
    per_group = GROUP // cols
    for group in range(back.shape[0] // per_group):
        members = [back[group * per_group + place].astype(jnp.float32) for place in range(per_group)]
        parts = [member[:cols] for member in members] + [member[cols:] for member in members]
        whole = jnp.concatenate(parts, axis=0)
        left[:, group * 2 * GROUP : (group + 1) * 2 * GROUP] = whole.T.astype(jnp.bfloat16)
    out_copies = []
    for block in range(quarter // IMAGE_BLOCK):

        def send(side, pixels):
            start = side * quarter + block * IMAGE_BLOCK
            at = slice(start, start + IMAGE_BLOCK)
            staged[:, at] = pixels
            out_copies.append(
                pltpu.make_async_copy(
                    staged.at[:, at], out_hbm.at[0, :, at], out_sems.at[4 * block + side]
                )
            )
            out_copies[-1].start()

        at = slice(block * IMAGE_BLOCK, (block + 1) * IMAGE_BLOCK)
        inverse_parts(left, even_table, odd_table, at, quarter, send)
    wait_copies(out_copies)


def image_rows(back, even_table, odd_table):
    rows = back.shape[2]
    half, quarter = even_table.shape
    length = 2 * half
    return pl.pallas_call(
        image_kernel,
        in_specs=[IN_VMEM, IN_VMEM, IN_VMEM],
        out_specs=HBM,
        out_shape=jax.ShapeDtypeStruct((1, rows, length), jnp.float32),
        scratch_shapes=[
            pltpu.VMEM((rows, length), jnp.bfloat16),
            pltpu.VMEM((rows, length), jnp.float32),
            pltpu.SemaphoreType.DMA((length // IMAGE_BLOCK,)),
        ],
        compiler_params=pltpu.CompilerParams(vmem_limit_bytes=40 * MIB),
        cost_estimate=cost(
            2 * rows * (even_table.size + odd_table.size), 3 * half * half + 6 * rows * length
        ),
        name="image_rows",
    )(back, even_table, odd_table)


def local(images, rate_vectors, epoch_times):
    _, loc_rows, length = images.shape
    epoch_count = lax.axis_size("epoch")
    devices = lax.axis_size("row") * epoch_count
    even_table, odd_table = [jnp.asarray(part) for part in packed_tables(length)]

    def exchange(values):
        return lax.all_to_all(values, ("row", "epoch"), 0, 0, tiled=True)

    spectra = exchange(row_transform(images, even_table, odd_table, devices))
    back = exchange(
        column_stage(rate_vectors, epoch_times, spectra, even_table, odd_table, epoch_count)
    )
    return image_rows(
        back.reshape(devices, length // devices, loc_rows), even_table, odd_table
    )


def solution(mesh):
    in_specs = (P(("group", "epoch"), "row", None), P(), P())
    out_specs = P(("group", "epoch"), "row", None)
    return jax.shard_map(local, mesh=mesh, in_specs=in_specs, out_specs=out_specs, check_vma=False)
```

```python
import functools
import math

import jax
import jax.numpy as jnp
import ml_dtypes
import numpy as np
from jax import lax
from jax.experimental import pallas as pl
from jax.experimental.pallas import tpu as pltpu
from jax.sharding import PartitionSpec as P

SUBPIX = 16
GROUP = 128
BLOCK = 512
IMAGE_BLOCK = 256
ROW_CHUNK = 16
MIB = 1024 * 1024
CONTRACT_LAST = (((1,), (1,)), ((), ()))
HBM = pl.BlockSpec(memory_space=pltpu.HBM)
IN_VMEM = pl.BlockSpec(memory_space=pltpu.VMEM)


def packed_freqs(index, half, where=jnp.where):
    even = 4 * index - where(index < half // 4, 0, half - 2)
    return where(index < half // 2, even, 2 * index - half + 1)


def packed_tables(length):
    half, quarter = length // 2, length // 4
    freqs = packed_freqs(np.arange(half, dtype=np.int32), half, np.where)
    positions = np.arange(half, dtype=np.int32)
    turns = freqs[:, None] * positions[None, :] % length
    angles = turns.astype(np.float32) * np.float32(2.0 * math.pi / length)
    factor = np.float32(1.0 / math.sqrt(length))
    cosine = np.cos(angles) * factor
    sine = np.sin(angles) * factor
    sine[0] = np.where(positions % 2 == 0, factor, -factor)
    groups = np.stack([cosine.reshape(-1, GROUP, half), sine.reshape(-1, GROUP, half)], axis=1)
    table = groups.reshape(length, half).astype(ml_dtypes.bfloat16)
    return np.ascontiguousarray(table[:half, :quarter]), table[half:]


def cost(flops, bytes_accessed):
    return pl.CostEstimate(flops=flops, bytes_accessed=bytes_accessed, transcendentals=0)


def in_space(array, space):
    return pltpu.with_memory_space_constraint(array, space)


def wait_copies(copies):
    for copy in copies:
        copy.wait()


def fold(quarters):
    first, second, third, fourth = [part.astype(jnp.float32) for part in quarters]
    near, far = first + third, second + fourth
    folds = near + far, near - far, first - third, second - fourth
    return [part.astype(jnp.bfloat16) for part in folds]


def row_kernel(
    images_hbm,
    even_hbm,
    odd_hbm,
    out_ref,
    images,
    even_table,
    odd_table,
    even_fold,
    odd_fold,
    image_sems,
    table_sems,
):
    loc_epochs, loc_rows, length = images.shape
    half, quarter = length // 2, length // 4
    devices, _, width, _ = out_ref.shape
    cols = width // 2
    steps = length // BLOCK
    per_step = devices // steps
    per_group = GROUP // cols
    image_copies = [
        pltpu.make_async_copy(images_hbm.at[loc], images.at[loc], image_sems.at[loc])
        for loc in range(loc_epochs)
    ]
    table_copies = [
        pltpu.make_async_copy(
            source.at[pl.ds(block * BLOCK, BLOCK)],
            target.at[pl.ds(block * BLOCK, BLOCK)],
            table_sems.at[first + block],
        )
        for first, source, target in ((0, even_hbm, even_table), (steps // 2, odd_hbm, odd_table))
        for block in range(steps // 2)
    ]
    for copy in image_copies[:1] + table_copies + image_copies[1:]:
        copy.start()
    for loc in range(loc_epochs):
        image_copies[loc].wait()
        folds = fold([images[loc, :, at * quarter : (at + 1) * quarter] for at in range(4)])
        even_fold[0], even_fold[1] = folds[:2]
        odd_fold[:, :quarter], odd_fold[:, quarter:] = folds[2:]
        for step in range(steps):
            if loc == 0:
                table_copies[step].wait()
            at = slice(step % (steps // 2) * BLOCK, (step % (steps // 2) + 1) * BLOCK)
            if step < steps // 2:
                left, right = even_table[at], even_fold[4 * step // steps]
            else:
                left, right = odd_table[at], odd_fold[...]
            terms = lax.dot_general(left, right, CONTRACT_LAST, preferred_element_type=jnp.float32)
            for dest in range(per_step):
                start = dest // per_group * 2 * GROUP + dest % per_group * cols
                parts = [terms[first : first + cols] for first in (start, start + GROUP)]
                block = jnp.concatenate(parts, axis=0).astype(jnp.bfloat16)
                out_ref[step * per_step + dest, loc] = block


def row_transform(images, even_table, odd_table, devices):
    loc_epochs, loc_rows, length = images.shape
    half, quarter = length // 2, length // 4
    rows = loc_epochs * loc_rows
    steps = length // BLOCK
    out = (devices, loc_epochs, length // devices, loc_rows)
    return pl.pallas_call(
        row_kernel,
        in_specs=[HBM, HBM, HBM],
        out_specs=IN_VMEM,
        out_shape=pltpu.VMEM(out, jnp.bfloat16),
        scratch_shapes=[
            pltpu.VMEM(images.shape, jnp.bfloat16),
            pltpu.VMEM(even_table.shape, jnp.bfloat16),
            pltpu.VMEM(odd_table.shape, jnp.bfloat16),
            pltpu.VMEM((2, loc_rows, quarter), jnp.bfloat16),
            pltpu.VMEM((loc_rows, half), jnp.bfloat16),
            pltpu.SemaphoreType.DMA((loc_epochs,)),
            pltpu.SemaphoreType.DMA((steps,)),
        ],
        compiler_params=pltpu.CompilerParams(vmem_limit_bytes=40 * MIB),
        cost_estimate=cost(
            2 * rows * (even_table.size + odd_table.size), 3 * half * half + 4 * rows * length
        ),
        name="row_transform",
    )(*(in_space(part, pltpu.HBM) for part in (images, even_table, odd_table)))


def turn_angle(turns, whole):
    return (turns & (whole - 1)).astype(jnp.float32) * (2.0 * math.pi / whole)


def spread_pairs(scalars, lanes):
    pair = lax.broadcasted_iota(jnp.int32, (len(scalars), lanes), 0)
    values = jnp.zeros((len(scalars), lanes), jnp.int32)
    for index, scalar in enumerate(scalars):
        values = jnp.where(pair == index, scalar, values)
    return values


def row_factors(shift_y, half):
    shifts = spread_pairs(shift_y, half)
    freqs = packed_freqs(lax.broadcasted_iota(jnp.int32, shifts.shape, 1), half)
    angles = turn_angle((freqs - half) * shifts, SUBPIX * 2 * half)
    cos_rows = jnp.where(freqs == 0, 1.0, 2.0 * jnp.cos(angles))
    return cos_rows, jnp.where(freqs == 0, 0.0, 2.0 * jnp.sin(angles))


def column_factors(shift_y, shift_x, scale, device, cols, half):
    shifts_y, shifts_x = spread_pairs(shift_y, GROUP), spread_pairs(shift_x, GROUP)
    lane = lax.broadcasted_iota(jnp.int32, shifts_x.shape, 1)
    freqs = packed_freqs(device * cols + (lane & (cols - 1)), half)
    is_sine = (lane & cols) > 0
    paired = freqs == 0
    zero_col = paired & jnp.logical_not(is_sine)
    angles = turn_angle(shifts_x * (freqs - half), SUBPIX * 2 * half)
    ramp_cos = jnp.where(paired, scale, 2.0 * scale * jnp.cos(angles))
    ramp_sin = jnp.where(paired, 0.0, 2.0 * scale * jnp.sin(angles))
    ramp_sin = jnp.where(is_sine, ramp_sin, -ramp_sin)
    cos_x = jnp.cos(turn_angle(shifts_x, 2 * SUBPIX))
    cos_y = jnp.cos(turn_angle(shifts_y, 2 * SUBPIX))
    cos_xy = jnp.cos(turn_angle(shifts_x + shifts_y, 2 * SUBPIX))
    main = jnp.where(zero_col, cos_y, cos_xy)
    lead = jnp.where(zero_col, 1.0, cos_x)
    return jnp.concatenate(
        [main * ramp_cos, main * ramp_sin, lead * ramp_cos, lead * ramp_sin], axis=0
    )


def column_kernel(
    epoch_count,
    rate_smem,
    time_smem,
    received,
    even_table,
    odd_table,
    out_ref,
    rows_cos,
    rows_sin,
    spread,
    even_fold,
    odd_fold,
    products,
    sums,
):
    devices, loc_epochs, width, loc_rows = received.shape
    row_count = devices // epoch_count
    epochs = epoch_count * loc_epochs
    rates = rate_smem.shape[0]
    pairs = rates * epochs
    cols = width // 2
    half, quarter = even_table.shape
    length = 2 * half
    steps = length // BLOCK
    device = lax.axis_index("row") * epoch_count + lax.axis_index("epoch")
    period = SUBPIX * length
    shift_y, shift_x = [
        [
            rate_smem[rate, axis] * time_smem[epoch] & (period - 1)
            for rate in range(rates)
            for epoch in range(epochs)
        ]
        for axis in range(2)
    ]
    per_tile = max(1, GROUP // loc_rows)
    tile_rows = per_tile * loc_rows
    for tile in range(row_count // 4 // per_tile):
        at_lane = slice(tile * tile_rows, (tile + 1) * tile_rows)
        far_lane = slice(quarter + at_lane.start, quarter + at_lane.stop)
        for core in range(epoch_count):
            for loc in range(loc_epochs):
                quarters = []
                for side in range(4):
                    first = side * row_count // 4 + tile * per_tile
                    parts = [
                        received[(first + part) * epoch_count + core, loc] for part in range(per_tile)
                    ]
                    quarters.append(parts[0] if per_tile == 1 else jnp.concatenate(parts, axis=1))
                at_row = (core * loc_epochs + loc) * width
                at = slice(at_row, at_row + width)
                folds = fold(quarters)
                even_fold[0, at, at_lane], even_fold[1, at, at_lane] = folds[:2]
                odd_fold[at, at_lane], odd_fold[at, far_lane] = folds[2:]

    def multiply(step):
        at = slice(step % (steps // 2) * BLOCK, (step % (steps // 2) + 1) * BLOCK)
        if step < steps // 2:
            left, right = even_fold[4 * step // steps], even_table[at]
        else:
            left, right = odd_fold[...], odd_table[at]
        products[step % 2] = lax.dot_general(
            left, right, CONTRACT_LAST, preferred_element_type=jnp.float32
        )

    multiply(0)
    rows_cos[...], rows_sin[...] = row_factors(shift_y, half)
    factors = column_factors(shift_y, shift_x, 1.0 / math.sqrt(epochs), device, cols, half).T
    for kind in range(4):
        for pair in range(pairs):
            at = kind * pairs + pair
            spread[kind, pair] = jnp.broadcast_to(factors[:width, at : at + 1], (width, GROUP))

    chunk = min(ROW_CHUNK, cols)

    def add_ramped(step, group):
        tile = (step * BLOCK // 2 // GROUP + group) * GROUP
        at_even = group * 2 * GROUP
        at_odd = at_even + GROUP
        for rate in range(rates):
            for start in range(0, cols, chunk):
                real = slice(start, start + chunk)
                imag = slice(cols + start, cols + start + chunk)
                totals = [[0.0, 0.0], [0.0, 0.0]]
                leads = [0.0, 0.0]
                for epoch in range(epochs):
                    pair = rate * epochs + epoch
                    cos_row = rows_cos[pair : pair + 1, tile : tile + GROUP]
                    sin_row = rows_sin[pair : pair + 1, tile : tile + GROUP]
                    turned, evens = [], []
                    for part in (real, imag):
                        at = slice(epoch * width + part.start, epoch * width + part.stop)
                        even = products[step % 2, at, at_even : at_even + GROUP]
                        odd = products[step % 2, at, at_odd : at_odd + GROUP]
                        turned.append(
                            (cos_row * even + sin_row * odd, cos_row * odd - sin_row * even)
                        )
                        evens.append(even)
                    straight = [spread[0, pair, part] for part in (real, imag)]
                    crossed = [spread[1, pair, part] for part in (real, imag)]
                    for part in range(2):
                        for which in range(2):
                            totals[part][which] += (
                                straight[part] * turned[part][which]
                                + crossed[1 - part] * turned[1 - part][which]
                            )
                        if step == 0 and group == 0:
                            own, other = (real, imag) if part == 0 else (imag, real)
                            leads[part] += (
                                spread[2, pair, own] * evens[part]
                                + spread[3, pair, other] * evens[1 - part]
                            )
                for part, rows in enumerate((real, imag)):
                    even_sum, odd_sum = totals[part]
                    if step == 0 and group == 0:
                        first = lax.broadcasted_iota(jnp.int32, even_sum.shape, 1) == 0
                        even_sum = jnp.where(first, leads[part], even_sum)
                    at = slice(rate * width + rows.start, rate * width + rows.stop)
                    sums[at, step * BLOCK + at_even : step * BLOCK + at_even + GROUP] = even_sum.astype(
                        jnp.bfloat16
                    )
                    sums[at, step * BLOCK + at_odd : step * BLOCK + at_odd + GROUP] = odd_sum.astype(
                        jnp.bfloat16
                    )

    for step in range(steps):
        if step + 1 < steps:
            multiply(step + 1)
        for group in range(BLOCK // 2 // GROUP):
            add_ramped(step, group)

    loc_rates = rates // epoch_count

    def send(side, back):
        back = back.astype(jnp.bfloat16)
        rows_here = quarter // loc_rows
        for row in range(rows_here):
            for rate in range(rates):
                dest = (side * rows_here + row) * epoch_count + rate // loc_rates
                out_ref[dest, rate % loc_rates] = back[
                    rate * width : (rate + 1) * width, row * loc_rows : (row + 1) * loc_rows
                ]

    inverse_parts(sums, even_table, odd_table, slice(0, quarter), quarter, send)


def inverse_parts(left, even_table, odd_table, at, quarter, send):
    half = 2 * quarter
    far = slice(quarter + at.start, quarter + at.stop)

    def product(first, depth, right):
        return jnp.dot(left[:, first : first + depth], right, preferred_element_type=jnp.float32)

    zero = product(0, quarter, even_table[:quarter, at])
    two = product(quarter, quarter, even_table[quarter:, at])
    for position, even, span in ((0, zero + two, at), (1, zero - two, far)):
        odd = product(half, half, odd_table[:, span])
        send(position, even + odd)
        send(position + 2, even - odd)


def column_stage(rate_vectors, epoch_times, spectra, even_table, odd_table, epoch_count):
    devices, loc_epochs, width, loc_rows = spectra.shape
    half, quarter = even_table.shape
    length = 2 * half
    epochs, rates = epoch_times.shape[0], rate_vectors.shape[0]
    out = (devices, rates // epoch_count, width, loc_rows)
    scalars = pl.BlockSpec(memory_space=pltpu.SMEM)
    return pl.pallas_call(
        functools.partial(column_kernel, epoch_count),
        in_specs=[scalars, scalars, IN_VMEM, IN_VMEM, IN_VMEM],
        out_specs=IN_VMEM,
        out_shape=pltpu.VMEM(out, jnp.bfloat16),
        scratch_shapes=[
            pltpu.VMEM((rates * epochs, half), jnp.float32),
            pltpu.VMEM((rates * epochs, half), jnp.float32),
            pltpu.VMEM((4, rates * epochs, width, GROUP), jnp.float32),
            pltpu.VMEM((2, epochs * width, quarter), jnp.bfloat16),
            pltpu.VMEM((epochs * width, half), jnp.bfloat16),
            pltpu.VMEM((2, epochs * width, BLOCK), jnp.float32),
            pltpu.VMEM((rates * width, length), jnp.bfloat16),
        ],
        compiler_params=pltpu.CompilerParams(vmem_limit_bytes=40 * MIB),
        cost_estimate=cost(
            2 * (even_table.size + odd_table.size) * (epochs + rates) * width,
            3 * half * half + 4 * spectra.size,
        ),
        name="column_stage",
    )(
        rate_vectors,
        epoch_times,
        *(in_space(part, pltpu.VMEM) for part in (spectra, even_table, odd_table)),
    )


def image_kernel(back, even_table, odd_table, out_hbm, left, staged, out_sems):
    quarter = even_table.shape[1]
    width = back.shape[1]
    cols = width // 2
    per_group = GROUP // cols
    for group in range(back.shape[0] // per_group):
        members = [back[group * per_group + place].astype(jnp.float32) for place in range(per_group)]
        parts = [member[:cols] for member in members] + [member[cols:] for member in members]
        whole = jnp.concatenate(parts, axis=0)
        left[:, group * 2 * GROUP : (group + 1) * 2 * GROUP] = whole.T.astype(jnp.bfloat16)
    out_copies = []
    for block in range(quarter // IMAGE_BLOCK):

        def send(side, pixels):
            start = side * quarter + block * IMAGE_BLOCK
            at = slice(start, start + IMAGE_BLOCK)
            staged[:, at] = pixels
            out_copies.append(
                pltpu.make_async_copy(
                    staged.at[:, at], out_hbm.at[0, :, at], out_sems.at[4 * block + side]
                )
            )
            out_copies[-1].start()

        at = slice(block * IMAGE_BLOCK, (block + 1) * IMAGE_BLOCK)
        inverse_parts(left, even_table, odd_table, at, quarter, send)
    wait_copies(out_copies)


def image_rows(back, even_table, odd_table):
    rows = back.shape[2]
    half, quarter = even_table.shape
    length = 2 * half
    return pl.pallas_call(
        image_kernel,
        in_specs=[IN_VMEM, IN_VMEM, IN_VMEM],
        out_specs=HBM,
        out_shape=jax.ShapeDtypeStruct((1, rows, length), jnp.float32),
        scratch_shapes=[
            pltpu.VMEM((rows, length), jnp.bfloat16),
            pltpu.VMEM((rows, length), jnp.float32),
            pltpu.SemaphoreType.DMA((length // IMAGE_BLOCK,)),
        ],
        compiler_params=pltpu.CompilerParams(vmem_limit_bytes=40 * MIB),
        cost_estimate=cost(
            2 * rows * (even_table.size + odd_table.size), 3 * half * half + 6 * rows * length
        ),
        name="image_rows",
    )(*(in_space(part, pltpu.VMEM) for part in (back, even_table, odd_table)))


def local(images, rate_vectors, epoch_times):
    _, loc_rows, length = images.shape
    epoch_count = lax.axis_size("epoch")
    devices = lax.axis_size("row") * epoch_count
    even_table, odd_table = [jnp.asarray(part) for part in packed_tables(length)]

    def exchange(values):
        return lax.all_to_all(values, ("row", "epoch"), 0, 0, tiled=True)

    spectra = exchange(row_transform(images, even_table, odd_table, devices))
    back = exchange(
        column_stage(rate_vectors, epoch_times, spectra, even_table, odd_table, epoch_count)
    )
    return image_rows(
        back.reshape(devices, length // devices, loc_rows), even_table, odd_table
    )


def solution(mesh):
    in_specs = (P(("group", "epoch"), "row", None), P(), P())
    out_specs = P(("group", "epoch"), "row", None)
    return jax.shard_map(local, mesh=mesh, in_specs=in_specs, out_specs=out_specs, check_vma=False)
```

```python
import functools
import math

import jax
import jax.numpy as jnp
import ml_dtypes
import numpy as np
from jax import lax
from jax.experimental import pallas as pl
from jax.experimental.pallas import tpu as pltpu
from jax.sharding import PartitionSpec as P

SUBPIX = 16
GROUP = 128
BLOCK = 512
IMAGE_BLOCK = 256
ROW_CHUNK = 16
MIB = 1024 * 1024
CONTRACT_LAST = (((1,), (1,)), ((), ()))
HBM = pl.BlockSpec(memory_space=pltpu.HBM)
IN_VMEM = pl.BlockSpec(memory_space=pltpu.VMEM)


def packed_freqs(index, half, where=jnp.where):
    even = 4 * index - where(index < half // 4, 0, half - 2)
    return where(index < half // 2, even, 2 * index - half + 1)


def packed_tables(length):
    half, quarter = length // 2, length // 4
    freqs = packed_freqs(np.arange(half, dtype=np.int32), half, np.where)
    positions = np.arange(half, dtype=np.int32)
    turns = freqs[:, None] * positions[None, :] % length
    angles = turns.astype(np.float32) * np.float32(2.0 * math.pi / length)
    factor = np.float32(1.0 / math.sqrt(length))
    cosine = np.cos(angles) * factor
    sine = np.sin(angles) * factor
    sine[0] = np.where(positions % 2 == 0, factor, -factor)
    groups = np.stack([cosine.reshape(-1, GROUP, half), sine.reshape(-1, GROUP, half)], axis=1)
    table = groups.reshape(length, half).astype(ml_dtypes.bfloat16)
    return np.ascontiguousarray(table[:half, :quarter]), table[half:]


def cost(flops, bytes_accessed):
    return pl.CostEstimate(flops=flops, bytes_accessed=bytes_accessed, transcendentals=0)


def in_space(array, space):
    return pltpu.with_memory_space_constraint(array, space)


def wait_copies(copies):
    for copy in copies:
        copy.wait()


def fold(quarters):
    first, second, third, fourth = [part.astype(jnp.float32) for part in quarters]
    near, far = first + third, second + fourth
    folds = near + far, near - far, first - third, second - fourth
    return [part.astype(jnp.bfloat16) for part in folds]


def row_kernel(
    images_hbm,
    even_hbm,
    odd_hbm,
    out_ref,
    images,
    even_table,
    odd_table,
    even_fold,
    odd_fold,
    image_sems,
    table_sems,
):
    loc_epochs, loc_rows, length = images.shape
    half, quarter = length // 2, length // 4
    devices, _, width, _ = out_ref.shape
    cols = width // 2
    steps = length // BLOCK
    per_step = devices // steps
    per_group = GROUP // cols
    image_copies = [
        pltpu.make_async_copy(images_hbm.at[loc], images.at[loc], image_sems.at[loc])
        for loc in range(loc_epochs)
    ]
    table_copies = [
        pltpu.make_async_copy(
            source.at[pl.ds(block * BLOCK, BLOCK)],
            target.at[pl.ds(block * BLOCK, BLOCK)],
            table_sems.at[first + block],
        )
        for first, source, target in ((0, even_hbm, even_table), (steps // 2, odd_hbm, odd_table))
        for block in range(steps // 2)
    ]
    for copy in image_copies[:1] + table_copies + image_copies[1:]:
        copy.start()
    for loc in range(loc_epochs):
        image_copies[loc].wait()
        folds = fold([images[loc, :, at * quarter : (at + 1) * quarter] for at in range(4)])
        even_fold[0], even_fold[1] = folds[:2]
        odd_fold[:, :quarter], odd_fold[:, quarter:] = folds[2:]
        for step in range(steps):
            if loc == 0:
                table_copies[step].wait()
            at = slice(step % (steps // 2) * BLOCK, (step % (steps // 2) + 1) * BLOCK)
            if step < steps // 2:
                left, right = even_table[at], even_fold[4 * step // steps]
            else:
                left, right = odd_table[at], odd_fold[...]
            terms = lax.dot_general(left, right, CONTRACT_LAST, preferred_element_type=jnp.float32)
            for dest in range(per_step):
                start = dest // per_group * 2 * GROUP + dest % per_group * cols
                parts = [terms[first : first + cols] for first in (start, start + GROUP)]
                block = jnp.concatenate(parts, axis=0).astype(jnp.bfloat16)
                out_ref[step * per_step + dest, loc] = block


def row_transform(images, even_table, odd_table, devices):
    loc_epochs, loc_rows, length = images.shape
    half, quarter = length // 2, length // 4
    rows = loc_epochs * loc_rows
    steps = length // BLOCK
    out = (devices, loc_epochs, length // devices, loc_rows)
    return pl.pallas_call(
        row_kernel,
        in_specs=[HBM, HBM, HBM],
        out_specs=IN_VMEM,
        out_shape=pltpu.VMEM(out, jnp.bfloat16),
        scratch_shapes=[
            pltpu.VMEM(images.shape, jnp.bfloat16),
            pltpu.VMEM(even_table.shape, jnp.bfloat16),
            pltpu.VMEM(odd_table.shape, jnp.bfloat16),
            pltpu.VMEM((2, loc_rows, quarter), jnp.bfloat16),
            pltpu.VMEM((loc_rows, half), jnp.bfloat16),
            pltpu.SemaphoreType.DMA((loc_epochs,)),
            pltpu.SemaphoreType.DMA((steps,)),
        ],
        compiler_params=pltpu.CompilerParams(vmem_limit_bytes=40 * MIB),
        cost_estimate=cost(
            2 * rows * (even_table.size + odd_table.size), 3 * half * half + 4 * rows * length
        ),
        name="row_transform",
    )(*(in_space(part, pltpu.HBM) for part in (images, even_table, odd_table)))


def turn_angle(turns, whole):
    return (turns & (whole - 1)).astype(jnp.float32) * (2.0 * math.pi / whole)


def spread_pairs(scalars, lanes):
    pair = lax.broadcasted_iota(jnp.int32, (len(scalars), lanes), 0)
    values = jnp.zeros((len(scalars), lanes), jnp.int32)
    for index, scalar in enumerate(scalars):
        values = jnp.where(pair == index, scalar, values)
    return values


def row_factors(shift_y, half):
    shifts = spread_pairs(shift_y, half)
    freqs = packed_freqs(lax.broadcasted_iota(jnp.int32, shifts.shape, 1), half)
    angles = turn_angle((freqs - half) * shifts, SUBPIX * 2 * half)
    cos_rows = jnp.where(freqs == 0, 1.0, 2.0 * jnp.cos(angles))
    return cos_rows, jnp.where(freqs == 0, 0.0, 2.0 * jnp.sin(angles))


def column_factors(shift_y, shift_x, scale, device, cols, half):
    shifts_y, shifts_x = spread_pairs(shift_y, GROUP), spread_pairs(shift_x, GROUP)
    lane = lax.broadcasted_iota(jnp.int32, shifts_x.shape, 1)
    freqs = packed_freqs(device * cols + (lane & (cols - 1)), half)
    is_sine = (lane & cols) > 0
    paired = freqs == 0
    zero_col = paired & jnp.logical_not(is_sine)
    angles = turn_angle(shifts_x * (freqs - half), SUBPIX * 2 * half)
    ramp_cos = jnp.where(paired, scale, 2.0 * scale * jnp.cos(angles))
    ramp_sin = jnp.where(paired, 0.0, 2.0 * scale * jnp.sin(angles))
    ramp_sin = jnp.where(is_sine, ramp_sin, -ramp_sin)
    cos_x = jnp.cos(turn_angle(shifts_x, 2 * SUBPIX))
    cos_y = jnp.cos(turn_angle(shifts_y, 2 * SUBPIX))
    cos_xy = jnp.cos(turn_angle(shifts_x + shifts_y, 2 * SUBPIX))
    main = jnp.where(zero_col, cos_y, cos_xy)
    lead = jnp.where(zero_col, 1.0, cos_x)
    return jnp.concatenate(
        [main * ramp_cos, main * ramp_sin, lead * ramp_cos, lead * ramp_sin], axis=0
    )


def column_kernel(
    epoch_count,
    rate_smem,
    time_smem,
    received,
    even_table,
    odd_table,
    out_ref,
    rows_cos,
    rows_sin,
    spread,
    even_fold,
    odd_fold,
    products,
    sums,
):
    devices, loc_epochs, width, loc_rows = received.shape
    row_count = devices // epoch_count
    epochs = epoch_count * loc_epochs
    rates = rate_smem.shape[0]
    pairs = rates * epochs
    cols = width // 2
    half, quarter = even_table.shape
    length = 2 * half
    steps = length // BLOCK
    device = lax.axis_index("epoch") * row_count + lax.axis_index("row")
    period = SUBPIX * length
    shift_y, shift_x = [
        [
            rate_smem[rate, axis] * time_smem[epoch] & (period - 1)
            for rate in range(rates)
            for epoch in range(epochs)
        ]
        for axis in range(2)
    ]
    per_tile = max(1, GROUP // loc_rows)
    tile_rows = per_tile * loc_rows
    for tile in range(row_count // 4 // per_tile):
        at_lane = slice(tile * tile_rows, (tile + 1) * tile_rows)
        far_lane = slice(quarter + at_lane.start, quarter + at_lane.stop)
        for core in range(epoch_count):
            for loc in range(loc_epochs):
                quarters = []
                for side in range(4):
                    first = side * row_count // 4 + tile * per_tile
                    parts = [
                        received[core * row_count + first + part, loc] for part in range(per_tile)
                    ]
                    quarters.append(parts[0] if per_tile == 1 else jnp.concatenate(parts, axis=1))
                at_row = (core * loc_epochs + loc) * width
                at = slice(at_row, at_row + width)
                folds = fold(quarters)
                even_fold[0, at, at_lane], even_fold[1, at, at_lane] = folds[:2]
                odd_fold[at, at_lane], odd_fold[at, far_lane] = folds[2:]

    def multiply(step):
        at = slice(step % (steps // 2) * BLOCK, (step % (steps // 2) + 1) * BLOCK)
        if step < steps // 2:
            left, right = even_fold[4 * step // steps], even_table[at]
        else:
            left, right = odd_fold[...], odd_table[at]
        products[step % 2] = lax.dot_general(
            left, right, CONTRACT_LAST, preferred_element_type=jnp.float32
        )

    multiply(0)
    rows_cos[...], rows_sin[...] = row_factors(shift_y, half)
    factors = column_factors(shift_y, shift_x, 1.0 / math.sqrt(epochs), device, cols, half).T
    for kind in range(4):
        for pair in range(pairs):
            at = kind * pairs + pair
            spread[kind, pair] = jnp.broadcast_to(factors[:width, at : at + 1], (width, GROUP))

    chunk = min(ROW_CHUNK, cols)

    def add_ramped(step, group):
        tile = (step * BLOCK // 2 // GROUP + group) * GROUP
        at_even = group * 2 * GROUP
        at_odd = at_even + GROUP
        for rate in range(rates):
            for start in range(0, cols, chunk):
                real = slice(start, start + chunk)
                imag = slice(cols + start, cols + start + chunk)
                totals = [[0.0, 0.0], [0.0, 0.0]]
                leads = [0.0, 0.0]
                for epoch in range(epochs):
                    pair = rate * epochs + epoch
                    cos_row = rows_cos[pair : pair + 1, tile : tile + GROUP]
                    sin_row = rows_sin[pair : pair + 1, tile : tile + GROUP]
                    turned, evens = [], []
                    for part in (real, imag):
                        at = slice(epoch * width + part.start, epoch * width + part.stop)
                        even = products[step % 2, at, at_even : at_even + GROUP]
                        odd = products[step % 2, at, at_odd : at_odd + GROUP]
                        turned.append(
                            (cos_row * even + sin_row * odd, cos_row * odd - sin_row * even)
                        )
                        evens.append(even)
                    straight = [spread[0, pair, part] for part in (real, imag)]
                    crossed = [spread[1, pair, part] for part in (real, imag)]
                    for part in range(2):
                        for which in range(2):
                            totals[part][which] += (
                                straight[part] * turned[part][which]
                                + crossed[1 - part] * turned[1 - part][which]
                            )
                        if step == 0 and group == 0:
                            own, other = (real, imag) if part == 0 else (imag, real)
                            leads[part] += (
                                spread[2, pair, own] * evens[part]
                                + spread[3, pair, other] * evens[1 - part]
                            )
                for part, rows in enumerate((real, imag)):
                    even_sum, odd_sum = totals[part]
                    if step == 0 and group == 0:
                        first = lax.broadcasted_iota(jnp.int32, even_sum.shape, 1) == 0
                        even_sum = jnp.where(first, leads[part], even_sum)
                    at = slice(rate * width + rows.start, rate * width + rows.stop)
                    sums[at, step * BLOCK + at_even : step * BLOCK + at_even + GROUP] = even_sum.astype(
                        jnp.bfloat16
                    )
                    sums[at, step * BLOCK + at_odd : step * BLOCK + at_odd + GROUP] = odd_sum.astype(
                        jnp.bfloat16
                    )

    for step in range(steps):
        if step + 1 < steps:
            multiply(step + 1)
        for group in range(BLOCK // 2 // GROUP):
            add_ramped(step, group)

    loc_rates = rates // epoch_count

    def send(side, back):
        back = back.astype(jnp.bfloat16)
        rows_here = quarter // loc_rows
        for row in range(rows_here):
            for rate in range(rates):
                dest = rate // loc_rates * row_count + side * rows_here + row
                out_ref[dest, rate % loc_rates] = back[
                    rate * width : (rate + 1) * width, row * loc_rows : (row + 1) * loc_rows
                ]

    inverse_parts(sums, even_table, odd_table, slice(0, quarter), quarter, send)


def inverse_parts(left, even_table, odd_table, at, quarter, send):
    half = 2 * quarter
    far = slice(quarter + at.start, quarter + at.stop)

    def product(first, depth, right):
        return jnp.dot(left[:, first : first + depth], right, preferred_element_type=jnp.float32)

    zero = product(0, quarter, even_table[:quarter, at])
    two = product(quarter, quarter, even_table[quarter:, at])
    for position, even, span in ((0, zero + two, at), (1, zero - two, far)):
        odd = product(half, half, odd_table[:, span])
        send(position, even + odd)
        send(position + 2, even - odd)


def column_stage(rate_vectors, epoch_times, spectra, even_table, odd_table, epoch_count):
    devices, loc_epochs, width, loc_rows = spectra.shape
    half, quarter = even_table.shape
    length = 2 * half
    epochs, rates = epoch_times.shape[0], rate_vectors.shape[0]
    out = (devices, rates // epoch_count, width, loc_rows)
    scalars = pl.BlockSpec(memory_space=pltpu.SMEM)
    return pl.pallas_call(
        functools.partial(column_kernel, epoch_count),
        in_specs=[scalars, scalars, IN_VMEM, IN_VMEM, IN_VMEM],
        out_specs=IN_VMEM,
        out_shape=pltpu.VMEM(out, jnp.bfloat16),
        scratch_shapes=[
            pltpu.VMEM((rates * epochs, half), jnp.float32),
            pltpu.VMEM((rates * epochs, half), jnp.float32),
            pltpu.VMEM((4, rates * epochs, width, GROUP), jnp.float32),
            pltpu.VMEM((2, epochs * width, quarter), jnp.bfloat16),
            pltpu.VMEM((epochs * width, half), jnp.bfloat16),
            pltpu.VMEM((2, epochs * width, BLOCK), jnp.float32),
            pltpu.VMEM((rates * width, length), jnp.bfloat16),
        ],
        compiler_params=pltpu.CompilerParams(vmem_limit_bytes=40 * MIB),
        cost_estimate=cost(
            2 * (even_table.size + odd_table.size) * (epochs + rates) * width,
            3 * half * half + 4 * spectra.size,
        ),
        name="column_stage",
    )(
        rate_vectors,
        epoch_times,
        *(in_space(part, pltpu.VMEM) for part in (spectra, even_table, odd_table)),
    )


def image_kernel(back, even_table, odd_table, out_hbm, left, staged, out_sems):
    quarter = even_table.shape[1]
    width = back.shape[1]
    cols = width // 2
    per_group = GROUP // cols
    for group in range(back.shape[0] // per_group):
        members = [back[group * per_group + place].astype(jnp.float32) for place in range(per_group)]
        parts = [member[:cols] for member in members] + [member[cols:] for member in members]
        whole = jnp.concatenate(parts, axis=0)
        left[:, group * 2 * GROUP : (group + 1) * 2 * GROUP] = whole.T.astype(jnp.bfloat16)
    out_copies = []
    for block in range(quarter // IMAGE_BLOCK):

        def send(side, pixels):
            start = side * quarter + block * IMAGE_BLOCK
            at = slice(start, start + IMAGE_BLOCK)
            staged[:, at] = pixels
            out_copies.append(
                pltpu.make_async_copy(
                    staged.at[:, at], out_hbm.at[0, :, at], out_sems.at[4 * block + side]
                )
            )
            out_copies[-1].start()

        at = slice(block * IMAGE_BLOCK, (block + 1) * IMAGE_BLOCK)
        inverse_parts(left, even_table, odd_table, at, quarter, send)
    wait_copies(out_copies)


def image_rows(back, even_table, odd_table):
    rows = back.shape[2]
    half, quarter = even_table.shape
    length = 2 * half
    return pl.pallas_call(
        image_kernel,
        in_specs=[IN_VMEM, IN_VMEM, IN_VMEM],
        out_specs=HBM,
        out_shape=jax.ShapeDtypeStruct((1, rows, length), jnp.float32),
        scratch_shapes=[
            pltpu.VMEM((rows, length), jnp.bfloat16),
            pltpu.VMEM((rows, length), jnp.float32),
            pltpu.SemaphoreType.DMA((length // IMAGE_BLOCK,)),
        ],
        compiler_params=pltpu.CompilerParams(vmem_limit_bytes=40 * MIB),
        cost_estimate=cost(
            2 * rows * (even_table.size + odd_table.size), 3 * half * half + 6 * rows * length
        ),
        name="image_rows",
    )(*(in_space(part, pltpu.VMEM) for part in (back, even_table, odd_table)))


def local(images, rate_vectors, epoch_times):
    _, loc_rows, length = images.shape
    epoch_count = lax.axis_size("epoch")
    devices = lax.axis_size("row") * epoch_count
    even_table, odd_table = [jnp.asarray(part) for part in packed_tables(length)]

    def exchange(values):
        return lax.all_to_all(values, ("epoch", "row"), 0, 0, tiled=True)

    spectra = exchange(row_transform(images, even_table, odd_table, devices))
    back = exchange(
        column_stage(rate_vectors, epoch_times, spectra, even_table, odd_table, epoch_count)
    )
    return image_rows(
        back.reshape(devices, length // devices, loc_rows), even_table, odd_table
    )


def solution(mesh):
    in_specs = (P(("group", "epoch"), "row", None), P(), P())
    out_specs = P(("group", "epoch"), "row", None)
    return jax.shard_map(local, mesh=mesh, in_specs=in_specs, out_specs=out_specs, check_vma=False)
```

```python
import functools
import math

import jax
import jax.numpy as jnp
import ml_dtypes
import numpy as np
from jax import lax
from jax.experimental import pallas as pl
from jax.experimental.pallas import tpu as pltpu
from jax.sharding import PartitionSpec as P

SUBPIX = 16
GROUP = 128
BLOCK = 512
IMAGE_BLOCK = 256
ROW_CHUNK = 16
MIB = 1024 * 1024
CONTRACT_LAST = (((1,), (1,)), ((), ()))
HBM = pl.BlockSpec(memory_space=pltpu.HBM)
IN_VMEM = pl.BlockSpec(memory_space=pltpu.VMEM)


def packed_freqs(index, half, where=jnp.where):
    even = 4 * index - where(index < half // 4, 0, half - 2)
    return where(index < half // 2, even, 2 * index - half + 1)


def packed_tables(length):
    half, quarter = length // 2, length // 4
    freqs = packed_freqs(np.arange(half, dtype=np.int32), half, np.where)
    positions = np.arange(half, dtype=np.int32)
    turns = freqs[:, None] * positions[None, :] % length
    angles = turns.astype(np.float32) * np.float32(2.0 * math.pi / length)
    factor = np.float32(1.0 / math.sqrt(length))
    cosine = np.cos(angles) * factor
    sine = np.sin(angles) * factor
    sine[0] = np.where(positions % 2 == 0, factor, -factor)
    groups = np.stack([cosine.reshape(-1, GROUP, half), sine.reshape(-1, GROUP, half)], axis=1)
    table = groups.reshape(length, half).astype(ml_dtypes.bfloat16)
    return np.ascontiguousarray(table[:half, :quarter]), table[half:]


def cost(flops, bytes_accessed):
    return pl.CostEstimate(flops=flops, bytes_accessed=bytes_accessed, transcendentals=0)


def in_space(array, space):
    return pltpu.with_memory_space_constraint(array, space)


def wait_copies(copies):
    for copy in copies:
        copy.wait()


def fold(quarters):
    first, second, third, fourth = [part.astype(jnp.float32) for part in quarters]
    near, far = first + third, second + fourth
    folds = near + far, near - far, first - third, second - fourth
    return [part.astype(jnp.bfloat16) for part in folds]


def row_kernel(
    images_hbm,
    even_hbm,
    odd_hbm,
    out_ref,
    images,
    even_table,
    odd_table,
    even_fold,
    odd_fold,
    image_sems,
    table_sems,
):
    loc_epochs, loc_rows, length = images.shape
    half, quarter = length // 2, length // 4
    devices, _, width, _ = out_ref.shape
    cols = width // 2
    steps = length // BLOCK
    per_group = GROUP // cols
    image_copies = [
        pltpu.make_async_copy(images_hbm.at[loc], images.at[loc], image_sems.at[loc])
        for loc in range(loc_epochs)
    ]
    table_copies = [
        pltpu.make_async_copy(
            source.at[pl.ds(block * BLOCK, BLOCK)],
            target.at[pl.ds(block * BLOCK, BLOCK)],
            table_sems.at[first + block],
        )
        for first, source, target in ((0, even_hbm, even_table), (steps // 2, odd_hbm, odd_table))
        for block in range(steps // 2)
    ]
    for copy in image_copies[:1] + table_copies + image_copies[1:]:
        copy.start()
    for loc in range(loc_epochs):
        image_copies[loc].wait()
        folds = fold([images[loc, :, at * quarter : (at + 1) * quarter] for at in range(4)])
        even_fold[0], even_fold[1] = folds[:2]
        odd_fold[:, :quarter], odd_fold[:, quarter:] = folds[2:]
        for step, rows in enumerate((BLOCK, BLOCK, half)):
            if loc == 0:
                wait_copies(table_copies[step : step + rows // BLOCK])
            if step < steps // 2:
                left, right = even_table[step * BLOCK : (step + 1) * BLOCK], even_fold[step]
            else:
                left, right = odd_table[...], odd_fold[...]
            terms = lax.dot_general(left, right, CONTRACT_LAST, preferred_element_type=jnp.float32)
            for dest in range(rows // width):
                start = dest // per_group * 2 * GROUP + dest % per_group * cols
                parts = [terms[first : first + cols] for first in (start, start + GROUP)]
                block = jnp.concatenate(parts, axis=0).astype(jnp.bfloat16)
                out_ref[step * BLOCK // width + dest, loc] = block


def row_transform(images, even_table, odd_table, devices):
    loc_epochs, loc_rows, length = images.shape
    half, quarter = length // 2, length // 4
    rows = loc_epochs * loc_rows
    steps = length // BLOCK
    out = (devices, loc_epochs, length // devices, loc_rows)
    return pl.pallas_call(
        row_kernel,
        in_specs=[HBM, HBM, HBM],
        out_specs=IN_VMEM,
        out_shape=pltpu.VMEM(out, jnp.bfloat16),
        scratch_shapes=[
            pltpu.VMEM(images.shape, jnp.bfloat16),
            pltpu.VMEM(even_table.shape, jnp.bfloat16),
            pltpu.VMEM(odd_table.shape, jnp.bfloat16),
            pltpu.VMEM((2, loc_rows, quarter), jnp.bfloat16),
            pltpu.VMEM((loc_rows, half), jnp.bfloat16),
            pltpu.SemaphoreType.DMA((loc_epochs,)),
            pltpu.SemaphoreType.DMA((steps,)),
        ],
        compiler_params=pltpu.CompilerParams(vmem_limit_bytes=40 * MIB),
        cost_estimate=cost(
            2 * rows * (even_table.size + odd_table.size), 3 * half * half + 4 * rows * length
        ),
        name="row_transform",
    )(*(in_space(part, pltpu.HBM) for part in (images, even_table, odd_table)))


def turn_angle(turns, whole):
    return (turns & (whole - 1)).astype(jnp.float32) * (2.0 * math.pi / whole)


def spread_pairs(scalars, lanes):
    pair = lax.broadcasted_iota(jnp.int32, (len(scalars), lanes), 0)
    values = jnp.zeros((len(scalars), lanes), jnp.int32)
    for index, scalar in enumerate(scalars):
        values = jnp.where(pair == index, scalar, values)
    return values


def row_factors(shift_y, half):
    shifts = spread_pairs(shift_y, half)
    freqs = packed_freqs(lax.broadcasted_iota(jnp.int32, shifts.shape, 1), half)
    angles = turn_angle((freqs - half) * shifts, SUBPIX * 2 * half)
    cos_rows = jnp.where(freqs == 0, 1.0, 2.0 * jnp.cos(angles))
    return cos_rows, jnp.where(freqs == 0, 0.0, 2.0 * jnp.sin(angles))


def column_factors(shift_y, shift_x, scale, device, cols, half):
    shifts_y, shifts_x = spread_pairs(shift_y, GROUP), spread_pairs(shift_x, GROUP)
    lane = lax.broadcasted_iota(jnp.int32, shifts_x.shape, 1)
    freqs = packed_freqs(device * cols + (lane & (cols - 1)), half)
    is_sine = (lane & cols) > 0
    paired = freqs == 0
    zero_col = paired & jnp.logical_not(is_sine)
    angles = turn_angle(shifts_x * (freqs - half), SUBPIX * 2 * half)
    ramp_cos = jnp.where(paired, scale, 2.0 * scale * jnp.cos(angles))
    ramp_sin = jnp.where(paired, 0.0, 2.0 * scale * jnp.sin(angles))
    ramp_sin = jnp.where(is_sine, ramp_sin, -ramp_sin)
    cos_x = jnp.cos(turn_angle(shifts_x, 2 * SUBPIX))
    cos_y = jnp.cos(turn_angle(shifts_y, 2 * SUBPIX))
    cos_xy = jnp.cos(turn_angle(shifts_x + shifts_y, 2 * SUBPIX))
    main = jnp.where(zero_col, cos_y, cos_xy)
    lead = jnp.where(zero_col, 1.0, cos_x)
    return jnp.concatenate(
        [main * ramp_cos, main * ramp_sin, lead * ramp_cos, lead * ramp_sin], axis=0
    )


def column_kernel(
    epoch_count,
    rate_smem,
    time_smem,
    received,
    even_turned,
    odd_turned,
    even_table,
    odd_table,
    out_ref,
    rows_cos,
    rows_sin,
    spread,
    even_fold,
    odd_fold,
    products,
    sums,
):
    devices, loc_epochs, width, loc_rows = received.shape
    row_count = devices // epoch_count
    epochs = epoch_count * loc_epochs
    rates = rate_smem.shape[0]
    pairs = rates * epochs
    cols = width // 2
    half, quarter = even_table.shape
    length = 2 * half
    steps = length // BLOCK
    device = lax.axis_index("row") * epoch_count + lax.axis_index("epoch")
    period = SUBPIX * length
    shift_y, shift_x = [
        [
            rate_smem[rate, axis] * time_smem[epoch] & (period - 1)
            for rate in range(rates)
            for epoch in range(epochs)
        ]
        for axis in range(2)
    ]
    per_tile = max(1, GROUP // loc_rows)
    tile_rows = per_tile * loc_rows
    for tile in range(row_count // 4 // per_tile):
        at_lane = slice(tile * tile_rows, (tile + 1) * tile_rows)
        far_lane = slice(quarter + at_lane.start, quarter + at_lane.stop)
        for core in range(epoch_count):
            for loc in range(loc_epochs):
                quarters = []
                for side in range(4):
                    first = side * row_count // 4 + tile * per_tile
                    parts = [
                        received[(first + part) * epoch_count + core, loc] for part in range(per_tile)
                    ]
                    quarters.append(parts[0] if per_tile == 1 else jnp.concatenate(parts, axis=1))
                at_row = (core * loc_epochs + loc) * width
                at = slice(at_row, at_row + width)
                folds = fold(quarters)
                even_fold[0, at, at_lane], even_fold[1, at, at_lane] = folds[:2]
                odd_fold[at, at_lane], odd_fold[at, far_lane] = folds[2:]

    def multiply(step):
        at = slice(step % (steps // 2) * BLOCK, (step % (steps // 2) + 1) * BLOCK)
        if step < steps // 2:
            left, right = even_fold[4 * step // steps], even_turned[:, at]
        else:
            left, right = odd_fold[...], odd_turned[:, at]
        products[step % 2] = jnp.dot(left, right, preferred_element_type=jnp.float32)

    multiply(0)
    rows_cos[...], rows_sin[...] = row_factors(shift_y, half)
    factors = column_factors(shift_y, shift_x, 1.0 / math.sqrt(epochs), device, cols, half).T
    for kind in range(4):
        for pair in range(pairs):
            at = kind * pairs + pair
            spread[kind, pair] = jnp.broadcast_to(factors[:width, at : at + 1], (width, GROUP))

    chunk = min(ROW_CHUNK, cols)

    def add_ramped(step, group):
        tile = (step * BLOCK // 2 // GROUP + group) * GROUP
        at_even = group * 2 * GROUP
        at_odd = at_even + GROUP
        for rate in range(rates):
            for start in range(0, cols, chunk):
                real = slice(start, start + chunk)
                imag = slice(cols + start, cols + start + chunk)
                totals = [[0.0, 0.0], [0.0, 0.0]]
                leads = [0.0, 0.0]
                for epoch in range(epochs):
                    pair = rate * epochs + epoch
                    cos_row = rows_cos[pair : pair + 1, tile : tile + GROUP]
                    sin_row = rows_sin[pair : pair + 1, tile : tile + GROUP]
                    turned, evens = [], []
                    for part in (real, imag):
                        at = slice(epoch * width + part.start, epoch * width + part.stop)
                        even = products[step % 2, at, at_even : at_even + GROUP]
                        odd = products[step % 2, at, at_odd : at_odd + GROUP]
                        turned.append(
                            (cos_row * even + sin_row * odd, cos_row * odd - sin_row * even)
                        )
                        evens.append(even)
                    straight = [spread[0, pair, part] for part in (real, imag)]
                    crossed = [spread[1, pair, part] for part in (real, imag)]
                    for part in range(2):
                        for which in range(2):
                            totals[part][which] += (
                                straight[part] * turned[part][which]
                                + crossed[1 - part] * turned[1 - part][which]
                            )
                        if step == 0 and group == 0:
                            own, other = (real, imag) if part == 0 else (imag, real)
                            leads[part] += (
                                spread[2, pair, own] * evens[part]
                                + spread[3, pair, other] * evens[1 - part]
                            )
                for part, rows in enumerate((real, imag)):
                    even_sum, odd_sum = totals[part]
                    if step == 0 and group == 0:
                        first = lax.broadcasted_iota(jnp.int32, even_sum.shape, 1) == 0
                        even_sum = jnp.where(first, leads[part], even_sum)
                    at = slice(rate * width + rows.start, rate * width + rows.stop)
                    sums[at, step * BLOCK + at_even : step * BLOCK + at_even + GROUP] = even_sum.astype(
                        jnp.bfloat16
                    )
                    sums[at, step * BLOCK + at_odd : step * BLOCK + at_odd + GROUP] = odd_sum.astype(
                        jnp.bfloat16
                    )

    for step in range(steps):
        if step + 1 < steps:
            multiply(step + 1)
        for group in range(BLOCK // 2 // GROUP):
            add_ramped(step, group)

    loc_rates = rates // epoch_count

    def send(side, back):
        back = back.astype(jnp.bfloat16)
        rows_here = quarter // loc_rows
        for row in range(rows_here):
            for rate in range(rates):
                dest = (side * rows_here + row) * epoch_count + rate // loc_rates
                out_ref[dest, rate % loc_rates] = back[
                    rate * width : (rate + 1) * width, row * loc_rows : (row + 1) * loc_rows
                ]

    inverse_parts(sums, even_table, odd_table, slice(0, quarter), quarter, send)


def inverse_parts(left, even_table, odd_table, at, quarter, send):
    half = 2 * quarter
    far = slice(quarter + at.start, quarter + at.stop)

    def product(first, depth, right):
        return jnp.dot(left[:, first : first + depth], right, preferred_element_type=jnp.float32)

    zero = product(0, quarter, even_table[:quarter, at])
    two = product(quarter, quarter, even_table[quarter:, at])
    for position, even, span in ((0, zero + two, at), (1, zero - two, far)):
        odd = product(half, half, odd_table[:, span])
        send(position, even + odd)
        send(position + 2, even - odd)


def column_stage(rate_vectors, epoch_times, spectra, turned_tables, tables, epoch_count):
    devices, loc_epochs, width, loc_rows = spectra.shape
    half, quarter = tables[0].shape
    length = 2 * half
    epochs, rates = epoch_times.shape[0], rate_vectors.shape[0]
    out = (devices, rates // epoch_count, width, loc_rows)
    scalars = pl.BlockSpec(memory_space=pltpu.SMEM)
    return pl.pallas_call(
        functools.partial(column_kernel, epoch_count),
        in_specs=[scalars, scalars] + [IN_VMEM] * 5,
        out_specs=IN_VMEM,
        out_shape=pltpu.VMEM(out, jnp.bfloat16),
        scratch_shapes=[
            pltpu.VMEM((rates * epochs, half), jnp.float32),
            pltpu.VMEM((rates * epochs, half), jnp.float32),
            pltpu.VMEM((4, rates * epochs, width, GROUP), jnp.float32),
            pltpu.VMEM((2, epochs * width, quarter), jnp.bfloat16),
            pltpu.VMEM((epochs * width, half), jnp.bfloat16),
            pltpu.VMEM((2, epochs * width, BLOCK), jnp.float32),
            pltpu.VMEM((rates * width, length), jnp.bfloat16),
        ],
        compiler_params=pltpu.CompilerParams(vmem_limit_bytes=40 * MIB),
        cost_estimate=cost(
            3 * half * half * (epochs + rates) * width, 6 * half * half + 4 * spectra.size
        ),
        name="column_stage",
    )(
        rate_vectors,
        epoch_times,
        *(in_space(part, pltpu.VMEM) for part in (spectra, *turned_tables, *tables)),
    )


def image_kernel(back, even_table, odd_table, out_hbm, left, staged, out_sems):
    quarter = even_table.shape[1]
    _, width, rows = back.shape
    cols = width // 2
    per_group = GROUP // cols
    for group in range(back.shape[0] // per_group):
        members = [back[group * per_group + place] for place in range(per_group)]
        if cols % 16 != 0 or rows % 128 != 0:
            members = [member.astype(jnp.float32) for member in members]
        parts = [member[:cols] for member in members] + [member[cols:] for member in members]
        whole = jnp.concatenate(parts, axis=0)
        left[:, group * 2 * GROUP : (group + 1) * 2 * GROUP] = whole.T.astype(jnp.bfloat16)
    out_copies = []
    for block in range(quarter // IMAGE_BLOCK):

        def send(side, pixels):
            start = side * quarter + block * IMAGE_BLOCK
            at = slice(start, start + IMAGE_BLOCK)
            staged[:, at] = pixels
            out_copies.append(
                pltpu.make_async_copy(
                    staged.at[:, at], out_hbm.at[0, :, at], out_sems.at[4 * block + side]
                )
            )
            out_copies[-1].start()

        at = slice(block * IMAGE_BLOCK, (block + 1) * IMAGE_BLOCK)
        inverse_parts(left, even_table, odd_table, at, quarter, send)
    wait_copies(out_copies)


def image_rows(back, even_table, odd_table):
    rows = back.shape[2]
    half, quarter = even_table.shape
    length = 2 * half
    return pl.pallas_call(
        image_kernel,
        in_specs=[IN_VMEM, IN_VMEM, IN_VMEM],
        out_specs=HBM,
        out_shape=jax.ShapeDtypeStruct((1, rows, length), jnp.float32),
        scratch_shapes=[
            pltpu.VMEM((rows, length), jnp.bfloat16),
            pltpu.VMEM((rows, length), jnp.float32),
            pltpu.SemaphoreType.DMA((length // IMAGE_BLOCK,)),
        ],
        compiler_params=pltpu.CompilerParams(vmem_limit_bytes=40 * MIB),
        cost_estimate=cost(
            2 * rows * (even_table.size + odd_table.size), 3 * half * half + 6 * rows * length
        ),
        name="image_rows",
    )(*(in_space(part, pltpu.VMEM) for part in (back, even_table, odd_table)))


def local(images, rate_vectors, epoch_times):
    _, loc_rows, length = images.shape
    epoch_count = lax.axis_size("epoch")
    devices = lax.axis_size("row") * epoch_count
    tables = packed_tables(length)
    turned_tables = [jnp.asarray(np.ascontiguousarray(part.T)) for part in tables]
    tables = [jnp.asarray(part) for part in tables]

    def exchange(values):
        return lax.all_to_all(values, ("row", "epoch"), 0, 0, tiled=True)

    spectra = exchange(row_transform(images, *tables, devices))
    back = exchange(
        column_stage(rate_vectors, epoch_times, spectra, turned_tables, tables, epoch_count)
    )
    return image_rows(back.reshape(devices, length // devices, loc_rows), *tables)


def solution(mesh):
    in_specs = (P(("group", "epoch"), "row", None), P(), P())
    out_specs = P(("group", "epoch"), "row", None)
    return jax.shard_map(local, mesh=mesh, in_specs=in_specs, out_specs=out_specs, check_vma=False)
```

```python
import functools
import math

import jax
import jax.numpy as jnp
import ml_dtypes
import numpy as np
from jax import lax
from jax.experimental import pallas as pl
from jax.experimental.pallas import tpu as pltpu
from jax.sharding import PartitionSpec as P

SUBPIX = 16
GROUP = 128
BLOCK = 512
IMAGE_BLOCK = 256
ROW_CHUNK = 16
MIB = 1024 * 1024
CONTRACT_LAST = (((1,), (1,)), ((), ()))
HBM = pl.BlockSpec(memory_space=pltpu.HBM)
IN_VMEM = pl.BlockSpec(memory_space=pltpu.VMEM)


def packed_freqs(index, half, where=jnp.where):
    even = 4 * index - where(index < half // 4, 0, half - 2)
    return where(index < half // 2, even, 2 * index - half + 1)


def packed_tables(length):
    half, quarter = length // 2, length // 4
    freqs = packed_freqs(np.arange(half, dtype=np.int32), half, np.where)
    positions = np.arange(half, dtype=np.int32)
    turns = freqs[:, None] * positions[None, :] % length
    angles = turns.astype(np.float32) * np.float32(2.0 * math.pi / length)
    factor = np.float32(1.0 / math.sqrt(length))
    cosine = np.cos(angles) * factor
    sine = np.sin(angles) * factor
    sine[0] = np.where(positions % 2 == 0, factor, -factor)
    groups = np.stack([cosine.reshape(-1, GROUP, half), sine.reshape(-1, GROUP, half)], axis=1)
    table = groups.reshape(length, half).astype(ml_dtypes.bfloat16)
    return np.ascontiguousarray(table[:half, :quarter]), table[half:]


def cost(flops, bytes_accessed):
    return pl.CostEstimate(flops=flops, bytes_accessed=bytes_accessed, transcendentals=0)


def in_space(array, space):
    return pltpu.with_memory_space_constraint(array, space)


def wait_copies(copies):
    for copy in copies:
        copy.wait()


def fold(quarters):
    first, second, third, fourth = quarters
    near, far = first + third, second + fourth
    return near + far, near - far, first - third, second - fourth


def row_kernel(
    images_hbm,
    even_hbm,
    odd_hbm,
    out_ref,
    images,
    even_table,
    odd_table,
    even_fold,
    odd_fold,
    image_sems,
    table_sems,
):
    loc_epochs, loc_rows, length = images.shape
    half, quarter = length // 2, length // 4
    devices, _, width, _ = out_ref.shape
    cols = width // 2
    steps = length // BLOCK
    per_step = devices // steps
    per_group = GROUP // cols
    image_copies = [
        pltpu.make_async_copy(images_hbm.at[loc], images.at[loc], image_sems.at[loc])
        for loc in range(loc_epochs)
    ]
    table_copies = [
        pltpu.make_async_copy(
            source.at[pl.ds(block * BLOCK, BLOCK)],
            target.at[pl.ds(block * BLOCK, BLOCK)],
            table_sems.at[first + block],
        )
        for first, source, target in ((0, even_hbm, even_table), (steps // 2, odd_hbm, odd_table))
        for block in range(steps // 2)
    ]
    for copy in image_copies[:1] + table_copies + image_copies[1:]:
        copy.start()
    for loc in range(loc_epochs):
        image_copies[loc].wait()
        folds = fold([images[loc, :, at * quarter : (at + 1) * quarter] for at in range(4)])
        even_fold[0], even_fold[1] = folds[:2]
        odd_fold[:, :quarter], odd_fold[:, quarter:] = folds[2:]
        for step in range(steps):
            if loc == 0:
                table_copies[step].wait()
            at = slice(step % (steps // 2) * BLOCK, (step % (steps // 2) + 1) * BLOCK)
            if step < steps // 2:
                left, right = even_table[at], even_fold[4 * step // steps]
            else:
                left, right = odd_table[at], odd_fold[...]
            terms = lax.dot_general(left, right, CONTRACT_LAST, preferred_element_type=jnp.float32)
            for dest in range(per_step):
                start = dest // per_group * 2 * GROUP + dest % per_group * cols
                parts = [terms[first : first + cols] for first in (start, start + GROUP)]
                block = jnp.concatenate(parts, axis=0).astype(jnp.bfloat16)
                out_ref[step * per_step + dest, loc] = block


def row_transform(images, even_table, odd_table, devices):
    loc_epochs, loc_rows, length = images.shape
    half, quarter = length // 2, length // 4
    rows = loc_epochs * loc_rows
    steps = length // BLOCK
    out = (devices, loc_epochs, length // devices, loc_rows)
    return pl.pallas_call(
        row_kernel,
        in_specs=[HBM, HBM, HBM],
        out_specs=IN_VMEM,
        out_shape=pltpu.VMEM(out, jnp.bfloat16),
        scratch_shapes=[
            pltpu.VMEM(images.shape, jnp.bfloat16),
            pltpu.VMEM(even_table.shape, jnp.bfloat16),
            pltpu.VMEM(odd_table.shape, jnp.bfloat16),
            pltpu.VMEM((2, loc_rows, quarter), jnp.bfloat16),
            pltpu.VMEM((loc_rows, half), jnp.bfloat16),
            pltpu.SemaphoreType.DMA((loc_epochs,)),
            pltpu.SemaphoreType.DMA((steps,)),
        ],
        compiler_params=pltpu.CompilerParams(vmem_limit_bytes=40 * MIB),
        cost_estimate=cost(
            2 * rows * (even_table.size + odd_table.size), 3 * half * half + 4 * rows * length
        ),
        name="row_transform",
    )(*(in_space(part, pltpu.HBM) for part in (images, even_table, odd_table)))


def turn_angle(turns, whole):
    return (turns & (whole - 1)).astype(jnp.float32) * (2.0 * math.pi / whole)


def spread_pairs(scalars, lanes):
    pair = lax.broadcasted_iota(jnp.int32, (len(scalars), lanes), 0)
    values = jnp.zeros((len(scalars), lanes), jnp.int32)
    for index, scalar in enumerate(scalars):
        values = jnp.where(pair == index, scalar, values)
    return values


def row_factors(shift_y, half):
    shifts = spread_pairs(shift_y, half)
    freqs = packed_freqs(lax.broadcasted_iota(jnp.int32, shifts.shape, 1), half)
    angles = turn_angle((freqs - half) * shifts, SUBPIX * 2 * half)
    cos_rows = jnp.where(freqs == 0, 1.0, 2.0 * jnp.cos(angles))
    return cos_rows, jnp.where(freqs == 0, 0.0, 2.0 * jnp.sin(angles))


def column_factors(shift_y, shift_x, scale, device, cols, half):
    shifts_y, shifts_x = spread_pairs(shift_y, GROUP), spread_pairs(shift_x, GROUP)
    lane = lax.broadcasted_iota(jnp.int32, shifts_x.shape, 1)
    freqs = packed_freqs(device * cols + (lane & (cols - 1)), half)
    is_sine = (lane & cols) > 0
    paired = freqs == 0
    zero_col = paired & jnp.logical_not(is_sine)
    angles = turn_angle(shifts_x * (freqs - half), SUBPIX * 2 * half)
    ramp_cos = jnp.where(paired, scale, 2.0 * scale * jnp.cos(angles))
    ramp_sin = jnp.where(paired, 0.0, 2.0 * scale * jnp.sin(angles))
    ramp_sin = jnp.where(is_sine, ramp_sin, -ramp_sin)
    cos_x = jnp.cos(turn_angle(shifts_x, 2 * SUBPIX))
    cos_y = jnp.cos(turn_angle(shifts_y, 2 * SUBPIX))
    cos_xy = jnp.cos(turn_angle(shifts_x + shifts_y, 2 * SUBPIX))
    main = jnp.where(zero_col, cos_y, cos_xy)
    lead = jnp.where(zero_col, 1.0, cos_x)
    return jnp.concatenate(
        [main * ramp_cos, main * ramp_sin, lead * ramp_cos, lead * ramp_sin], axis=0
    )


def column_kernel(
    epoch_count,
    rate_smem,
    time_smem,
    received,
    even_table,
    odd_table,
    out_ref,
    rows_cos,
    rows_sin,
    spread,
    even_fold,
    odd_fold,
    products,
    sums,
):
    devices, loc_epochs, width, loc_rows = received.shape
    row_count = devices // epoch_count
    epochs = epoch_count * loc_epochs
    rates = rate_smem.shape[0]
    pairs = rates * epochs
    cols = width // 2
    half, quarter = even_table.shape
    length = 2 * half
    steps = length // BLOCK
    device = lax.axis_index("row") * epoch_count + lax.axis_index("epoch")
    period = SUBPIX * length
    shift_y, shift_x = [
        [
            rate_smem[rate, axis] * time_smem[epoch] & (period - 1)
            for rate in range(rates)
            for epoch in range(epochs)
        ]
        for axis in range(2)
    ]
    per_tile = max(1, GROUP // loc_rows)
    tile_rows = per_tile * loc_rows
    for tile in range(row_count // 4 // per_tile):
        at_lane = slice(tile * tile_rows, (tile + 1) * tile_rows)
        far_lane = slice(quarter + at_lane.start, quarter + at_lane.stop)
        for core in range(epoch_count):
            for loc in range(loc_epochs):
                quarters = []
                for side in range(4):
                    first = side * row_count // 4 + tile * per_tile
                    parts = [
                        received[(first + part) * epoch_count + core, loc] for part in range(per_tile)
                    ]
                    quarters.append(parts[0] if per_tile == 1 else jnp.concatenate(parts, axis=1))
                at_row = (core * loc_epochs + loc) * width
                at = slice(at_row, at_row + width)
                folds = fold(quarters)
                even_fold[0, at, at_lane], even_fold[1, at, at_lane] = folds[:2]
                odd_fold[at, at_lane], odd_fold[at, far_lane] = folds[2:]

    def multiply(step):
        at = slice(step % (steps // 2) * BLOCK, (step % (steps // 2) + 1) * BLOCK)
        if step < steps // 2:
            left, right = even_fold[4 * step // steps], even_table[at]
        else:
            left, right = odd_fold[...], odd_table[at]
        products[step % 2] = lax.dot_general(
            left, right, CONTRACT_LAST, preferred_element_type=jnp.float32
        )

    multiply(0)
    rows_cos[...], rows_sin[...] = row_factors(shift_y, half)
    factors = column_factors(shift_y, shift_x, 1.0 / math.sqrt(epochs), device, cols, half).T
    for kind in range(4):
        for pair in range(pairs):
            at = kind * pairs + pair
            spread[kind, pair] = jnp.broadcast_to(factors[:width, at : at + 1], (width, GROUP))

    chunk = min(ROW_CHUNK, cols)

    def add_ramped(step, group):
        tile = (step * BLOCK // 2 // GROUP + group) * GROUP
        at_even = group * 2 * GROUP
        at_odd = at_even + GROUP
        for rate in range(rates):
            for start in range(0, cols, chunk):
                real = slice(start, start + chunk)
                imag = slice(cols + start, cols + start + chunk)
                totals = [[0.0, 0.0], [0.0, 0.0]]
                leads = [0.0, 0.0]
                for epoch in range(epochs):
                    pair = rate * epochs + epoch
                    cos_row = rows_cos[pair : pair + 1, tile : tile + GROUP]
                    sin_row = rows_sin[pair : pair + 1, tile : tile + GROUP]
                    turned, evens = [], []
                    for part in (real, imag):
                        at = slice(epoch * width + part.start, epoch * width + part.stop)
                        even = products[step % 2, at, at_even : at_even + GROUP]
                        odd = products[step % 2, at, at_odd : at_odd + GROUP]
                        turned.append(
                            (cos_row * even + sin_row * odd, cos_row * odd - sin_row * even)
                        )
                        evens.append(even)
                    straight = [spread[0, pair, part] for part in (real, imag)]
                    crossed = [spread[1, pair, part] for part in (real, imag)]
                    for part in range(2):
                        for which in range(2):
                            totals[part][which] += (
                                straight[part] * turned[part][which]
                                + crossed[1 - part] * turned[1 - part][which]
                            )
                        if step == 0 and group == 0:
                            own, other = (real, imag) if part == 0 else (imag, real)
                            leads[part] += (
                                spread[2, pair, own] * evens[part]
                                + spread[3, pair, other] * evens[1 - part]
                            )
                for part, rows in enumerate((real, imag)):
                    even_sum, odd_sum = totals[part]
                    if step == 0 and group == 0:
                        first = lax.broadcasted_iota(jnp.int32, even_sum.shape, 1) == 0
                        even_sum = jnp.where(first, leads[part], even_sum)
                    at = slice(rate * width + rows.start, rate * width + rows.stop)
                    sums[at, step * BLOCK + at_even : step * BLOCK + at_even + GROUP] = even_sum.astype(
                        jnp.bfloat16
                    )
                    sums[at, step * BLOCK + at_odd : step * BLOCK + at_odd + GROUP] = odd_sum.astype(
                        jnp.bfloat16
                    )

    for step in range(steps):
        if step + 1 < steps:
            multiply(step + 1)
        for group in range(BLOCK // 2 // GROUP):
            add_ramped(step, group)

    loc_rates = rates // epoch_count

    def send(side, back):
        back = back.astype(jnp.bfloat16)
        rows_here = quarter // loc_rows
        for row in range(rows_here):
            for rate in range(rates):
                dest = (side * rows_here + row) * epoch_count + rate // loc_rates
                out_ref[dest, rate % loc_rates] = back[
                    rate * width : (rate + 1) * width, row * loc_rows : (row + 1) * loc_rows
                ]

    inverse_parts(sums, even_table, odd_table, slice(0, quarter), quarter, send)


def inverse_parts(left, even_table, odd_table, at, quarter, send):
    half = 2 * quarter
    far = slice(quarter + at.start, quarter + at.stop)

    def product(first, depth, right):
        return jnp.dot(left[:, first : first + depth], right, preferred_element_type=jnp.float32)

    zero = product(0, quarter, even_table[:quarter, at])
    two = product(quarter, quarter, even_table[quarter:, at])
    for position, even, span in ((0, zero + two, at), (1, zero - two, far)):
        odd = product(half, half, odd_table[:, span])
        send(position, even + odd)
        send(position + 2, even - odd)


def column_stage(rate_vectors, epoch_times, spectra, even_table, odd_table, epoch_count):
    devices, loc_epochs, width, loc_rows = spectra.shape
    half, quarter = even_table.shape
    length = 2 * half
    epochs, rates = epoch_times.shape[0], rate_vectors.shape[0]
    out = (devices, rates // epoch_count, width, loc_rows)
    scalars = pl.BlockSpec(memory_space=pltpu.SMEM)
    return pl.pallas_call(
        functools.partial(column_kernel, epoch_count),
        in_specs=[scalars, scalars, IN_VMEM, IN_VMEM, IN_VMEM],
        out_specs=IN_VMEM,
        out_shape=pltpu.VMEM(out, jnp.bfloat16),
        scratch_shapes=[
            pltpu.VMEM((rates * epochs, half), jnp.float32),
            pltpu.VMEM((rates * epochs, half), jnp.float32),
            pltpu.VMEM((4, rates * epochs, width, GROUP), jnp.float32),
            pltpu.VMEM((2, epochs * width, quarter), jnp.bfloat16),
            pltpu.VMEM((epochs * width, half), jnp.bfloat16),
            pltpu.VMEM((2, epochs * width, BLOCK), jnp.float32),
            pltpu.VMEM((rates * width, length), jnp.bfloat16),
        ],
        compiler_params=pltpu.CompilerParams(vmem_limit_bytes=40 * MIB),
        cost_estimate=cost(
            2 * (even_table.size + odd_table.size) * (epochs + rates) * width,
            3 * half * half + 4 * spectra.size,
        ),
        name="column_stage",
    )(
        rate_vectors,
        epoch_times,
        *(in_space(part, pltpu.VMEM) for part in (spectra, even_table, odd_table)),
    )


def image_kernel(back, even_table, odd_table, out_hbm, left, staged, out_sems):
    quarter = even_table.shape[1]
    _, width, rows = back.shape
    cols = width // 2
    per_group = GROUP // cols
    for group in range(back.shape[0] // per_group):
        members = [back[group * per_group + place] for place in range(per_group)]
        if cols % 16 != 0 or rows % 128 != 0:
            members = [member.astype(jnp.float32) for member in members]
        parts = [member[:cols] for member in members] + [member[cols:] for member in members]
        whole = jnp.concatenate(parts, axis=0)
        left[:, group * 2 * GROUP : (group + 1) * 2 * GROUP] = whole.T.astype(jnp.bfloat16)
    out_copies = []
    for block in range(quarter // IMAGE_BLOCK):

        def send(side, pixels):
            start = side * quarter + block * IMAGE_BLOCK
            at = slice(start, start + IMAGE_BLOCK)
            staged[:, at] = pixels
            out_copies.append(
                pltpu.make_async_copy(
                    staged.at[:, at], out_hbm.at[0, :, at], out_sems.at[4 * block + side]
                )
            )
            out_copies[-1].start()

        at = slice(block * IMAGE_BLOCK, (block + 1) * IMAGE_BLOCK)
        inverse_parts(left, even_table, odd_table, at, quarter, send)
    wait_copies(out_copies)


def image_rows(back, even_table, odd_table):
    rows = back.shape[2]
    half, quarter = even_table.shape
    length = 2 * half
    return pl.pallas_call(
        image_kernel,
        in_specs=[IN_VMEM, IN_VMEM, IN_VMEM],
        out_specs=HBM,
        out_shape=jax.ShapeDtypeStruct((1, rows, length), jnp.float32),
        scratch_shapes=[
            pltpu.VMEM((rows, length), jnp.bfloat16),
            pltpu.VMEM((rows, length), jnp.float32),
            pltpu.SemaphoreType.DMA((length // IMAGE_BLOCK,)),
        ],
        compiler_params=pltpu.CompilerParams(vmem_limit_bytes=40 * MIB),
        cost_estimate=cost(
            2 * rows * (even_table.size + odd_table.size), 3 * half * half + 6 * rows * length
        ),
        name="image_rows",
    )(*(in_space(part, pltpu.VMEM) for part in (back, even_table, odd_table)))


def local(images, rate_vectors, epoch_times):
    _, loc_rows, length = images.shape
    epoch_count = lax.axis_size("epoch")
    devices = lax.axis_size("row") * epoch_count
    even_table, odd_table = [jnp.asarray(part) for part in packed_tables(length)]

    def exchange(values):
        return lax.all_to_all(values, ("row", "epoch"), 0, 0, tiled=True)

    spectra = exchange(row_transform(images, even_table, odd_table, devices))
    back = exchange(
        column_stage(rate_vectors, epoch_times, spectra, even_table, odd_table, epoch_count)
    )
    return image_rows(
        back.reshape(devices, length // devices, loc_rows), even_table, odd_table
    )


def solution(mesh):
    in_specs = (P(("group", "epoch"), "row", None), P(), P())
    out_specs = P(("group", "epoch"), "row", None)
    return jax.shard_map(local, mesh=mesh, in_specs=in_specs, out_specs=out_specs, check_vma=False)
```

```python
import functools
import math

import jax
import jax.numpy as jnp
import ml_dtypes
import numpy as np
from jax import lax
from jax.experimental import pallas as pl
from jax.experimental.pallas import tpu as pltpu
from jax.sharding import PartitionSpec as P

SUBPIX = 16
GROUP = 128
BLOCK = 512
IMAGE_BLOCK = 256
ROW_CHUNK = 16
MIB = 1024 * 1024
CONTRACT_LAST = (((1,), (1,)), ((), ()))
HBM = pl.BlockSpec(memory_space=pltpu.HBM)
IN_VMEM = pl.BlockSpec(memory_space=pltpu.VMEM)


def packed_freqs(index, half, where=jnp.where):
    even = 4 * index - where(index < half // 4, 0, half - 2)
    return where(index < half // 2, even, 2 * index - half + 1)


def packed_tables(length):
    half, quarter = length // 2, length // 4
    freqs = packed_freqs(np.arange(half, dtype=np.int32), half, np.where)
    positions = np.arange(half, dtype=np.int32)
    turns = freqs[:, None] * positions[None, :] % length
    angles = turns.astype(np.float32) * np.float32(2.0 * math.pi / length)
    factor = np.float32(1.0 / math.sqrt(length))
    cosine = np.cos(angles) * factor
    sine = np.sin(angles) * factor
    sine[0] = np.where(positions % 2 == 0, factor, -factor)
    groups = np.stack([cosine.reshape(-1, GROUP, half), sine.reshape(-1, GROUP, half)], axis=1)
    table = groups.reshape(length, half).astype(ml_dtypes.bfloat16)
    return np.ascontiguousarray(table[:half, :quarter]), table[half:]


def cost(flops, bytes_accessed):
    return pl.CostEstimate(flops=flops, bytes_accessed=bytes_accessed, transcendentals=0)


def in_space(array, space):
    return pltpu.with_memory_space_constraint(array, space)


def wait_copies(copies):
    for copy in copies:
        copy.wait()


def fold(quarters):
    first, second, third, fourth = quarters
    near, far = first + third, second + fourth
    return near + far, near - far, first - third, second - fourth


def row_kernel(
    images_hbm,
    even_hbm,
    odd_hbm,
    out_ref,
    images,
    even_table,
    odd_table,
    even_fold,
    odd_fold,
    image_sems,
    table_sems,
):
    loc_epochs, loc_rows, length = images.shape
    half, quarter = length // 2, length // 4
    devices, _, width, _ = out_ref.shape
    cols = width // 2
    steps = length // BLOCK
    per_step = devices // steps
    per_group = GROUP // cols
    image_copies = [
        pltpu.make_async_copy(images_hbm.at[loc], images.at[loc], image_sems.at[loc])
        for loc in range(loc_epochs)
    ]
    table_copies = [
        pltpu.make_async_copy(
            source.at[pl.ds(block * BLOCK, BLOCK)],
            target.at[pl.ds(block * BLOCK, BLOCK)],
            table_sems.at[first + block],
        )
        for first, source, target in ((0, even_hbm, even_table), (steps // 2, odd_hbm, odd_table))
        for block in range(steps // 2)
    ]
    for copy in image_copies[:1] + table_copies + image_copies[1:]:
        copy.start()
    for loc in range(loc_epochs):
        image_copies[loc].wait()
        folds = fold([images[loc, :, at * quarter : (at + 1) * quarter] for at in range(4)])
        even_fold[0], even_fold[1] = folds[:2]
        odd_fold[:, :quarter], odd_fold[:, quarter:] = folds[2:]
        for step in range(steps):
            if loc == 0:
                table_copies[step].wait()
            at = slice(step % (steps // 2) * BLOCK, (step % (steps // 2) + 1) * BLOCK)
            if step < steps // 2:
                left, right = even_table[at], even_fold[4 * step // steps]
            else:
                left, right = odd_table[at], odd_fold[...]
            terms = lax.dot_general(left, right, CONTRACT_LAST, preferred_element_type=jnp.float32)
            for dest in range(per_step):
                start = dest // per_group * 2 * GROUP + dest % per_group * cols
                parts = [terms[first : first + cols] for first in (start, start + GROUP)]
                block = jnp.concatenate(parts, axis=0).astype(jnp.bfloat16)
                out_ref[step * per_step + dest, loc] = block


def row_transform(images, even_table, odd_table, devices):
    loc_epochs, loc_rows, length = images.shape
    half, quarter = length // 2, length // 4
    rows = loc_epochs * loc_rows
    steps = length // BLOCK
    out = (devices, loc_epochs, length // devices, loc_rows)
    return pl.pallas_call(
        row_kernel,
        in_specs=[HBM, HBM, HBM],
        out_specs=IN_VMEM,
        out_shape=pltpu.VMEM(out, jnp.bfloat16),
        scratch_shapes=[
            pltpu.VMEM(images.shape, jnp.bfloat16),
            pltpu.VMEM(even_table.shape, jnp.bfloat16),
            pltpu.VMEM(odd_table.shape, jnp.bfloat16),
            pltpu.VMEM((2, loc_rows, quarter), jnp.bfloat16),
            pltpu.VMEM((loc_rows, half), jnp.bfloat16),
            pltpu.SemaphoreType.DMA((loc_epochs,)),
            pltpu.SemaphoreType.DMA((steps,)),
        ],
        compiler_params=pltpu.CompilerParams(vmem_limit_bytes=40 * MIB),
        cost_estimate=cost(
            2 * rows * (even_table.size + odd_table.size), 3 * half * half + 4 * rows * length
        ),
        name="row_transform",
    )(*(in_space(part, pltpu.HBM) for part in (images, even_table, odd_table)))


def turn_angle(turns, whole):
    return (turns & (whole - 1)).astype(jnp.float32) * (2.0 * math.pi / whole)


def spread_pairs(scalars, lanes):
    pair = lax.broadcasted_iota(jnp.int32, (len(scalars), lanes), 0)
    values = jnp.zeros((len(scalars), lanes), jnp.int32)
    for index, scalar in enumerate(scalars):
        values = jnp.where(pair == index, scalar, values)
    return values


def row_factors(shift_y, half):
    shifts = spread_pairs(shift_y, half)
    freqs = packed_freqs(lax.broadcasted_iota(jnp.int32, shifts.shape, 1), half)
    angles = turn_angle((freqs - half) * shifts, SUBPIX * 2 * half)
    cos_rows = jnp.where(freqs == 0, 1.0, 2.0 * jnp.cos(angles))
    return cos_rows, jnp.where(freqs == 0, 0.0, 2.0 * jnp.sin(angles))


def column_factors(shift_y, shift_x, scale, device, cols, half):
    shifts_y, shifts_x = spread_pairs(shift_y, GROUP), spread_pairs(shift_x, GROUP)
    lane = lax.broadcasted_iota(jnp.int32, shifts_x.shape, 1)
    freqs = packed_freqs(device * cols + (lane & (cols - 1)), half)
    is_sine = (lane & cols) > 0
    paired = freqs == 0
    zero_col = paired & jnp.logical_not(is_sine)
    angles = turn_angle(shifts_x * (freqs - half), SUBPIX * 2 * half)
    ramp_cos = jnp.where(paired, scale, 2.0 * scale * jnp.cos(angles))
    ramp_sin = jnp.where(paired, 0.0, 2.0 * scale * jnp.sin(angles))
    ramp_sin = jnp.where(is_sine, ramp_sin, -ramp_sin)
    cos_x = jnp.cos(turn_angle(shifts_x, 2 * SUBPIX))
    cos_y = jnp.cos(turn_angle(shifts_y, 2 * SUBPIX))
    cos_xy = jnp.cos(turn_angle(shifts_x + shifts_y, 2 * SUBPIX))
    main = jnp.where(zero_col, cos_y, cos_xy)
    lead = jnp.where(zero_col, 1.0, cos_x)
    return jnp.concatenate(
        [main * ramp_cos, main * ramp_sin, lead * ramp_cos, lead * ramp_sin], axis=0
    )


def aligned(value, multiple):
    return value if isinstance(value, int) else pl.multiple_of(value, multiple)


def loop_over(count, body):
    pl.loop(0, count)(body)


def unroll_over(count, body):
    for index in range(count):
        body(index)


def column_kernel(
    epoch_count,
    rate_smem,
    time_smem,
    received,
    even_table,
    odd_table,
    out_ref,
    rows_cos,
    rows_sin,
    spread,
    even_fold,
    odd_fold,
    products,
    sums,
):
    devices, loc_epochs, width, loc_rows = received.shape
    row_count = devices // epoch_count
    epochs = epoch_count * loc_epochs
    rates = rate_smem.shape[0]
    pairs = rates * epochs
    cols = width // 2
    half, quarter = even_table.shape
    length = 2 * half
    steps = length // BLOCK
    device = lax.axis_index("row") * epoch_count + lax.axis_index("epoch")
    period = SUBPIX * length
    shift_y, shift_x = [
        [
            rate_smem[rate, axis] * time_smem[epoch] & (period - 1)
            for rate in range(rates)
            for epoch in range(epochs)
        ]
        for axis in range(2)
    ]
    per_tile = max(1, GROUP // loc_rows)
    tile_rows = per_tile * loc_rows
    for tile in range(row_count // 4 // per_tile):
        at_lane = slice(tile * tile_rows, (tile + 1) * tile_rows)
        far_lane = slice(quarter + at_lane.start, quarter + at_lane.stop)
        for core in range(epoch_count):
            for loc in range(loc_epochs):
                quarters = []
                for side in range(4):
                    first = side * row_count // 4 + tile * per_tile
                    parts = [
                        received[(first + part) * epoch_count + core, loc] for part in range(per_tile)
                    ]
                    quarters.append(parts[0] if per_tile == 1 else jnp.concatenate(parts, axis=1))
                at_row = (core * loc_epochs + loc) * width
                at = slice(at_row, at_row + width)
                folds = fold(quarters)
                even_fold[0, at, at_lane], even_fold[1, at, at_lane] = folds[:2]
                odd_fold[at, at_lane], odd_fold[at, far_lane] = folds[2:]

    def multiply(step):
        at = slice(step % (steps // 2) * BLOCK, (step % (steps // 2) + 1) * BLOCK)
        if step < steps // 2:
            left, right = even_fold[4 * step // steps], even_table[at]
        else:
            left, right = odd_fold[...], odd_table[at]
        products[step % 2] = lax.dot_general(
            left, right, CONTRACT_LAST, preferred_element_type=jnp.float32
        )

    multiply(0)
    for target, values in zip((rows_cos, rows_sin), row_factors(shift_y, half)):
        for pair in range(pairs):
            target[pair] = values[pair : pair + 1]
    factors = column_factors(shift_y, shift_x, 1.0 / math.sqrt(epochs), device, cols, half).T
    for kind in range(4):
        for pair in range(pairs):
            at = kind * pairs + pair
            spread[kind, pair] = jnp.broadcast_to(factors[:width, at : at + 1], (width, GROUP))

    chunk = min(ROW_CHUNK, cols)

    chunks = cols // chunk
    repeat = loop_over if chunk == ROW_CHUNK else unroll_over
    groups = BLOCK // 2 // GROUP

    def place(index):
        rate, part = index // chunks, index % chunks
        return rate, aligned(part * chunk, chunk), aligned(cols + part * chunk, chunk)

    def add_ramped(step, index):
        group, index = index // (rates * chunks), index % (rates * chunks)
        rate, real, imag = place(index)
        tile = aligned((step * groups + group) * GROUP, GROUP)
        at_even = aligned(group * 2 * GROUP, GROUP)
        at_odd = aligned(at_even + GROUP, GROUP)
        totals = [[0.0, 0.0], [0.0, 0.0]]
        for epoch in range(epochs):
            pair = rate * epochs + epoch
            cos_row = rows_cos[pair, :, pl.ds(tile, GROUP)]
            sin_row = rows_sin[pair, :, pl.ds(tile, GROUP)]
            turned = []
            for start in (real, imag):
                at = pl.ds(aligned(epoch * width + start, chunk), chunk)
                even = products[step % 2, at, pl.ds(at_even, GROUP)]
                odd = products[step % 2, at, pl.ds(at_odd, GROUP)]
                turned.append((cos_row * even + sin_row * odd, cos_row * odd - sin_row * even))
            straight = [spread[0, pair, pl.ds(start, chunk)] for start in (real, imag)]
            crossed = [spread[1, pair, pl.ds(start, chunk)] for start in (real, imag)]
            for part in range(2):
                for which in range(2):
                    totals[part][which] += (
                        straight[part] * turned[part][which]
                        + crossed[1 - part] * turned[1 - part][which]
                    )
        for part, start in enumerate((real, imag)):
            at = pl.ds(aligned(rate * width + start, chunk), chunk)
            for which, lane in enumerate((at_even, at_odd)):
                lane = aligned(step * BLOCK + lane, GROUP)
                sums[at, pl.ds(lane, GROUP)] = totals[part][which].astype(jnp.bfloat16)

    def replace_lead(index):
        rate, real, imag = place(index)
        leads = [0.0, 0.0]
        for epoch in range(epochs):
            pair = rate * epochs + epoch
            evens = [
                products[0, pl.ds(aligned(epoch * width + start, chunk), chunk), :GROUP]
                for start in (real, imag)
            ]
            for part, (own, other) in enumerate(((real, imag), (imag, real))):
                leads[part] += (
                    spread[2, pair, pl.ds(own, chunk)] * evens[part]
                    + spread[3, pair, pl.ds(other, chunk)] * evens[1 - part]
                )
        for part, start in enumerate((real, imag)):
            at = pl.ds(aligned(rate * width + start, chunk), chunk)
            first = lax.broadcasted_iota(jnp.int32, leads[part].shape, 1) == 0
            kept = sums[at, :GROUP].astype(jnp.float32)
            sums[at, :GROUP] = jnp.where(first, leads[part], kept).astype(jnp.bfloat16)

    for step in range(steps):
        repeat(groups * rates * chunks, functools.partial(add_ramped, step))
        if step == 0:
            repeat(rates * chunks, replace_lead)
        if step + 1 < steps:
            multiply(step + 1)

    loc_rates = rates // epoch_count

    def send(side, back):
        back = back.astype(jnp.bfloat16)
        rows_here = quarter // loc_rows
        for row in range(rows_here):
            for rate in range(rates):
                dest = (side * rows_here + row) * epoch_count + rate // loc_rates
                out_ref[dest, rate % loc_rates] = back[
                    rate * width : (rate + 1) * width, row * loc_rows : (row + 1) * loc_rows
                ]

    inverse_parts(sums, even_table, odd_table, slice(0, quarter), quarter, send)


def inverse_parts(left, even_table, odd_table, at, quarter, send):
    half = 2 * quarter
    far = slice(quarter + at.start, quarter + at.stop)

    def product(first, depth, right):
        return jnp.dot(left[:, first : first + depth], right, preferred_element_type=jnp.float32)

    zero = product(0, quarter, even_table[:quarter, at])
    two = product(quarter, quarter, even_table[quarter:, at])
    for position, even, span in ((0, zero + two, at), (1, zero - two, far)):
        odd = product(half, half, odd_table[:, span])
        send(position, even + odd)
        send(position + 2, even - odd)


def column_stage(rate_vectors, epoch_times, spectra, even_table, odd_table, epoch_count):
    devices, loc_epochs, width, loc_rows = spectra.shape
    half, quarter = even_table.shape
    length = 2 * half
    epochs, rates = epoch_times.shape[0], rate_vectors.shape[0]
    out = (devices, rates // epoch_count, width, loc_rows)
    scalars = pl.BlockSpec(memory_space=pltpu.SMEM)
    return pl.pallas_call(
        functools.partial(column_kernel, epoch_count),
        in_specs=[scalars, scalars, IN_VMEM, IN_VMEM, IN_VMEM],
        out_specs=IN_VMEM,
        out_shape=pltpu.VMEM(out, jnp.bfloat16),
        scratch_shapes=[
            pltpu.VMEM((rates * epochs, 1, half), jnp.float32),
            pltpu.VMEM((rates * epochs, 1, half), jnp.float32),
            pltpu.VMEM((4, rates * epochs, width, GROUP), jnp.float32),
            pltpu.VMEM((2, epochs * width, quarter), jnp.bfloat16),
            pltpu.VMEM((epochs * width, half), jnp.bfloat16),
            pltpu.VMEM((2, epochs * width, BLOCK), jnp.float32),
            pltpu.VMEM((rates * width, length), jnp.bfloat16),
        ],
        compiler_params=pltpu.CompilerParams(vmem_limit_bytes=40 * MIB),
        cost_estimate=cost(
            2 * (even_table.size + odd_table.size) * (epochs + rates) * width,
            3 * half * half + 4 * spectra.size,
        ),
        name="column_stage",
    )(
        rate_vectors,
        epoch_times,
        *(in_space(part, pltpu.VMEM) for part in (spectra, even_table, odd_table)),
    )


def image_kernel(back, even_table, odd_table, out_hbm, left, staged, out_sems):
    quarter = even_table.shape[1]
    _, width, rows = back.shape
    cols = width // 2
    per_group = GROUP // cols
    for group in range(back.shape[0] // per_group):
        members = [back[group * per_group + place] for place in range(per_group)]
        if cols % 16 != 0 or rows % 128 != 0:
            members = [member.astype(jnp.float32) for member in members]
        parts = [member[:cols] for member in members] + [member[cols:] for member in members]
        whole = jnp.concatenate(parts, axis=0)
        left[:, group * 2 * GROUP : (group + 1) * 2 * GROUP] = whole.T.astype(jnp.bfloat16)
    out_copies = []
    for block in range(quarter // IMAGE_BLOCK):

        def send(side, pixels):
            start = side * quarter + block * IMAGE_BLOCK
            at = slice(start, start + IMAGE_BLOCK)
            staged[:, at] = pixels
            out_copies.append(
                pltpu.make_async_copy(
                    staged.at[:, at], out_hbm.at[0, :, at], out_sems.at[4 * block + side]
                )
            )
            out_copies[-1].start()

        at = slice(block * IMAGE_BLOCK, (block + 1) * IMAGE_BLOCK)
        inverse_parts(left, even_table, odd_table, at, quarter, send)
    wait_copies(out_copies)


def image_rows(back, even_table, odd_table):
    rows = back.shape[2]
    half, quarter = even_table.shape
    length = 2 * half
    return pl.pallas_call(
        image_kernel,
        in_specs=[IN_VMEM, IN_VMEM, IN_VMEM],
        out_specs=HBM,
        out_shape=jax.ShapeDtypeStruct((1, rows, length), jnp.float32),
        scratch_shapes=[
            pltpu.VMEM((rows, length), jnp.bfloat16),
            pltpu.VMEM((rows, length), jnp.float32),
            pltpu.SemaphoreType.DMA((length // IMAGE_BLOCK,)),
        ],
        compiler_params=pltpu.CompilerParams(vmem_limit_bytes=40 * MIB),
        cost_estimate=cost(
            2 * rows * (even_table.size + odd_table.size), 3 * half * half + 6 * rows * length
        ),
        name="image_rows",
    )(*(in_space(part, pltpu.VMEM) for part in (back, even_table, odd_table)))


def local(images, rate_vectors, epoch_times):
    _, loc_rows, length = images.shape
    epoch_count = lax.axis_size("epoch")
    devices = lax.axis_size("row") * epoch_count
    even_table, odd_table = [jnp.asarray(part) for part in packed_tables(length)]

    def exchange(values):
        return lax.all_to_all(values, ("row", "epoch"), 0, 0, tiled=True)

    spectra = exchange(row_transform(images, even_table, odd_table, devices))
    back = exchange(
        column_stage(rate_vectors, epoch_times, spectra, even_table, odd_table, epoch_count)
    )
    return image_rows(
        back.reshape(devices, length // devices, loc_rows), even_table, odd_table
    )


def solution(mesh):
    in_specs = (P(("group", "epoch"), "row", None), P(), P())
    out_specs = P(("group", "epoch"), "row", None)
    return jax.shard_map(local, mesh=mesh, in_specs=in_specs, out_specs=out_specs, check_vma=False)
```

```python
import functools
import math

import jax
import jax.numpy as jnp
import ml_dtypes
import numpy as np
from jax import lax
from jax.experimental import pallas as pl
from jax.experimental.pallas import tpu as pltpu
from jax.sharding import PartitionSpec as P

SUBPIX = 16
GROUP = 128
BLOCK = 512
IMAGE_BLOCK = 256
ROW_CHUNK = 16
PIECES = 4
MIB = 1024 * 1024
CONTRACT_LAST = (((1,), (1,)), ((), ()))
HBM = pl.BlockSpec(memory_space=pltpu.HBM)
IN_VMEM = pl.BlockSpec(memory_space=pltpu.VMEM)


def packed_freqs(index, half, where=jnp.where):
    even = 4 * index - where(index < half // 4, 0, half - 2)
    return where(index < half // 2, even, 2 * index - half + 1)


def packed_tables(length):
    half, quarter = length // 2, length // 4
    freqs = packed_freqs(np.arange(half, dtype=np.int32), half, np.where)
    positions = np.arange(half, dtype=np.int32)
    turns = freqs[:, None] * positions[None, :] % length
    angles = turns.astype(np.float32) * np.float32(2.0 * math.pi / length)
    factor = np.float32(1.0 / math.sqrt(length))
    cosine = np.cos(angles) * factor
    sine = np.sin(angles) * factor
    sine[0] = np.where(positions % 2 == 0, factor, -factor)
    groups = np.stack([cosine.reshape(-1, GROUP, half), sine.reshape(-1, GROUP, half)], axis=1)
    table = groups.reshape(length, half).astype(ml_dtypes.bfloat16)
    return np.ascontiguousarray(table[:half, :quarter]), table[half:]


def cost(flops, bytes_accessed):
    return pl.CostEstimate(flops=flops, bytes_accessed=bytes_accessed, transcendentals=0)


def in_space(array, space):
    return pltpu.with_memory_space_constraint(array, space)


def wait_copies(copies):
    for copy in copies:
        copy.wait()


def fold(quarters):
    first, second, third, fourth = quarters
    near, far = first + third, second + fourth
    return near + far, near - far, first - third, second - fourth


def row_kernel(
    images_hbm,
    even_hbm,
    odd_hbm,
    out_ref,
    images,
    even_table,
    odd_table,
    even_fold,
    odd_fold,
    image_sems,
    table_sems,
):
    loc_epochs, loc_rows, length = images.shape
    half, quarter = length // 2, length // 4
    devices, _, width, _ = out_ref.shape
    cols = width // 2
    steps = length // BLOCK
    per_step = devices // steps
    per_group = GROUP // cols
    def copies(source, target, sems, pieces):
        rows = source.shape[0] // pieces
        spans = [pl.ds(piece * rows, rows) for piece in range(pieces)]
        return [
            pltpu.make_async_copy(source.at[span], target.at[span], sems.at[piece])
            for piece, span in enumerate(spans)
        ]

    pieces = max(1, min(PIECES, loc_rows // 16))
    image_copies = [
        copies(images_hbm.at[loc], images.at[loc], image_sems.at[loc], 1 if loc else pieces)
        for loc in range(loc_epochs)
    ]
    even_copies = copies(even_hbm, even_table, table_sems.at[0], PIECES)
    odd_copies = copies(odd_hbm, odd_table, table_sems.at[1], 2)
    halfway = PIECES // 2
    table_copies = [even_copies[:halfway], even_copies[halfway:], odd_copies[:1], odd_copies[1:]]
    for copy in image_copies[0] + even_copies + odd_copies + sum(image_copies[1:], []):
        copy.start()
    for loc in range(loc_epochs):
        wait_copies(image_copies[loc])
        folds = fold([images[loc, :, at * quarter : (at + 1) * quarter] for at in range(4)])
        even_fold[0], even_fold[1] = folds[:2]
        odd_fold[:, :quarter], odd_fold[:, quarter:] = folds[2:]
        for step in range(steps):
            if loc == 0:
                wait_copies(table_copies[step])
            at = slice(step % (steps // 2) * BLOCK, (step % (steps // 2) + 1) * BLOCK)
            if step < steps // 2:
                left, right = even_table[at], even_fold[4 * step // steps]
            else:
                left, right = odd_table[at], odd_fold[...]
            terms = lax.dot_general(left, right, CONTRACT_LAST, preferred_element_type=jnp.float32)
            for dest in range(per_step):
                start = dest // per_group * 2 * GROUP + dest % per_group * cols
                parts = [terms[first : first + cols] for first in (start, start + GROUP)]
                block = jnp.concatenate(parts, axis=0).astype(jnp.bfloat16)
                out_ref[step * per_step + dest, loc] = block


def row_transform(images, even_table, odd_table, devices):
    loc_epochs, loc_rows, length = images.shape
    half, quarter = length // 2, length // 4
    rows = loc_epochs * loc_rows
    steps = length // BLOCK
    out = (devices, loc_epochs, length // devices, loc_rows)
    return pl.pallas_call(
        row_kernel,
        in_specs=[HBM, HBM, HBM],
        out_specs=IN_VMEM,
        out_shape=pltpu.VMEM(out, jnp.bfloat16),
        scratch_shapes=[
            pltpu.VMEM(images.shape, jnp.bfloat16),
            pltpu.VMEM(even_table.shape, jnp.bfloat16),
            pltpu.VMEM(odd_table.shape, jnp.bfloat16),
            pltpu.VMEM((2, loc_rows, quarter), jnp.bfloat16),
            pltpu.VMEM((loc_rows, half), jnp.bfloat16),
            pltpu.SemaphoreType.DMA((loc_epochs, PIECES)),
            pltpu.SemaphoreType.DMA((2, PIECES)),
        ],
        compiler_params=pltpu.CompilerParams(vmem_limit_bytes=40 * MIB),
        cost_estimate=cost(
            2 * rows * (even_table.size + odd_table.size), 3 * half * half + 4 * rows * length
        ),
        name="row_transform",
    )(*(in_space(part, pltpu.HBM) for part in (images, even_table, odd_table)))


def cos_sin(turns, whole):
    quarter, eighth = whole // 4, whole // 8
    shifted = (turns + eighth) & (whole - 1)
    quadrant = shifted >> (quarter.bit_length() - 1)
    angle = ((shifted & (quarter - 1)) - eighth).astype(jnp.float32) * (2.0 * math.pi / whole)
    square = angle * angle
    sine, cosine = 1.0 / 362880.0, 1.0 / 40320.0
    for divisor in (-5040.0, 120.0, -6.0, 1.0):
        sine = sine * square + 1.0 / divisor
    for divisor in (-720.0, 24.0, -2.0, 1.0):
        cosine = cosine * square + 1.0 / divisor
    sine = sine * angle
    odd = (quadrant & 1) == 1
    first, second = jnp.where(odd, sine, cosine), jnp.where(odd, cosine, sine)
    return (
        jnp.where(((quadrant + 1) & 2) == 2, -first, first),
        jnp.where(quadrant >= 2, -second, second),
    )


def spread_pairs(scalars, lanes):
    pair = lax.broadcasted_iota(jnp.int32, (len(scalars), lanes), 0)
    values = jnp.zeros((len(scalars), lanes), jnp.int32)
    for index, scalar in enumerate(scalars):
        values = jnp.where(pair == index, scalar, values)
    return values


def row_factors(shift_y, half):
    shifts = spread_pairs(shift_y, half)
    freqs = packed_freqs(lax.broadcasted_iota(jnp.int32, shifts.shape, 1), half)
    cosine, sine = cos_sin((freqs - half) * shifts, SUBPIX * 2 * half)
    return jnp.where(freqs == 0, 1.0, 2.0 * cosine), jnp.where(freqs == 0, 0.0, 2.0 * sine)


def column_factors(shift_y, shift_x, scale, device, cols, half):
    shifts_y, shifts_x = spread_pairs(shift_y, GROUP), spread_pairs(shift_x, GROUP)
    lane = lax.broadcasted_iota(jnp.int32, shifts_x.shape, 1)
    freqs = packed_freqs(device * cols + (lane & (cols - 1)), half)
    is_sine = (lane & cols) > 0
    paired = freqs == 0
    zero_col = paired & jnp.logical_not(is_sine)
    cosine, sine = cos_sin(shifts_x * (freqs - half), SUBPIX * 2 * half)
    ramp_cos = jnp.where(paired, scale, 2.0 * scale * cosine)
    ramp_sin = jnp.where(paired, 0.0, 2.0 * scale * sine)
    ramp_sin = jnp.where(is_sine, ramp_sin, -ramp_sin)
    cos_x, cos_y, cos_xy = [
        cos_sin(shifts, 2 * SUBPIX)[0] for shifts in (shifts_x, shifts_y, shifts_x + shifts_y)
    ]
    main = jnp.where(zero_col, cos_y, cos_xy)
    lead = jnp.where(zero_col, 1.0, cos_x)
    return jnp.concatenate(
        [main * ramp_cos, main * ramp_sin, lead * ramp_cos, lead * ramp_sin], axis=0
    )


def column_kernel(
    epoch_count,
    rate_smem,
    time_smem,
    received,
    even_table,
    odd_table,
    out_ref,
    rows_cos,
    rows_sin,
    spread,
    even_fold,
    odd_fold,
    products,
    sums,
):
    devices, loc_epochs, width, loc_rows = received.shape
    row_count = devices // epoch_count
    epochs = epoch_count * loc_epochs
    rates = rate_smem.shape[0]
    pairs = rates * epochs
    cols = width // 2
    half, quarter = even_table.shape
    length = 2 * half
    steps = length // BLOCK
    device = lax.axis_index("row") * epoch_count + lax.axis_index("epoch")
    period = SUBPIX * length
    shift_y, shift_x = [
        [
            rate_smem[rate, axis] * time_smem[epoch] & (period - 1)
            for rate in range(rates)
            for epoch in range(epochs)
        ]
        for axis in range(2)
    ]
    per_tile = max(1, GROUP // loc_rows)
    tile_rows = per_tile * loc_rows
    for tile in range(row_count // 4 // per_tile):
        at_lane = slice(tile * tile_rows, (tile + 1) * tile_rows)
        far_lane = slice(quarter + at_lane.start, quarter + at_lane.stop)
        for core in range(epoch_count):
            for loc in range(loc_epochs):
                quarters = []
                for side in range(4):
                    first = side * row_count // 4 + tile * per_tile
                    parts = [
                        received[(first + part) * epoch_count + core, loc] for part in range(per_tile)
                    ]
                    quarters.append(parts[0] if per_tile == 1 else jnp.concatenate(parts, axis=1))
                at_row = (core * loc_epochs + loc) * width
                at = slice(at_row, at_row + width)
                folds = fold(quarters)
                even_fold[0, at, at_lane], even_fold[1, at, at_lane] = folds[:2]
                odd_fold[at, at_lane], odd_fold[at, far_lane] = folds[2:]

    def multiply(step):
        at = slice(step % (steps // 2) * BLOCK, (step % (steps // 2) + 1) * BLOCK)
        if step < steps // 2:
            left, right = even_fold[4 * step // steps], even_table[at]
        else:
            left, right = odd_fold[...], odd_table[at]
        products[step % 2] = lax.dot_general(
            left, right, CONTRACT_LAST, preferred_element_type=jnp.float32
        )

    multiply(0)
    rows_cos[...], rows_sin[...] = row_factors(shift_y, half)
    factors = column_factors(shift_y, shift_x, 1.0 / math.sqrt(epochs), device, cols, half).T
    for kind in range(4):
        for pair in range(pairs):
            at = kind * pairs + pair
            spread[kind, pair] = jnp.broadcast_to(factors[:width, at : at + 1], (width, GROUP))

    chunk = min(ROW_CHUNK, cols)

    def add_ramped(step, group):
        tile = (step * BLOCK // 2 // GROUP + group) * GROUP
        at_even = group * 2 * GROUP
        at_odd = at_even + GROUP
        for rate in range(rates):
            for start in range(0, cols, chunk):
                real = slice(start, start + chunk)
                imag = slice(cols + start, cols + start + chunk)
                totals = [[0.0, 0.0], [0.0, 0.0]]
                leads = [0.0, 0.0]
                for epoch in range(epochs):
                    pair = rate * epochs + epoch
                    cos_row = rows_cos[pair : pair + 1, tile : tile + GROUP]
                    sin_row = rows_sin[pair : pair + 1, tile : tile + GROUP]
                    turned, evens = [], []
                    for part in (real, imag):
                        at = slice(epoch * width + part.start, epoch * width + part.stop)
                        even = products[step % 2, at, at_even : at_even + GROUP]
                        odd = products[step % 2, at, at_odd : at_odd + GROUP]
                        turned.append(
                            (cos_row * even + sin_row * odd, cos_row * odd - sin_row * even)
                        )
                        evens.append(even)
                    straight = [spread[0, pair, part] for part in (real, imag)]
                    crossed = [spread[1, pair, part] for part in (real, imag)]
                    for part in range(2):
                        for which in range(2):
                            totals[part][which] += (
                                straight[part] * turned[part][which]
                                + crossed[1 - part] * turned[1 - part][which]
                            )
                        if step == 0 and group == 0:
                            own, other = (real, imag) if part == 0 else (imag, real)
                            leads[part] += (
                                spread[2, pair, own] * evens[part]
                                + spread[3, pair, other] * evens[1 - part]
                            )
                for part, rows in enumerate((real, imag)):
                    even_sum, odd_sum = totals[part]
                    if step == 0 and group == 0:
                        first = lax.broadcasted_iota(jnp.int32, even_sum.shape, 1) == 0
                        even_sum = jnp.where(first, leads[part], even_sum)
                    at = slice(rate * width + rows.start, rate * width + rows.stop)
                    sums[at, step * BLOCK + at_even : step * BLOCK + at_even + GROUP] = even_sum.astype(
                        jnp.bfloat16
                    )
                    sums[at, step * BLOCK + at_odd : step * BLOCK + at_odd + GROUP] = odd_sum.astype(
                        jnp.bfloat16
                    )

    for step in range(steps):
        if step + 1 < steps:
            multiply(step + 1)
        for group in range(BLOCK // 2 // GROUP):
            add_ramped(step, group)

    loc_rates = rates // epoch_count

    def send(side, back):
        back = back.astype(jnp.bfloat16)
        rows_here = quarter // loc_rows
        for row in range(rows_here):
            for rate in range(rates):
                dest = (side * rows_here + row) * epoch_count + rate // loc_rates
                out_ref[dest, rate % loc_rates] = back[
                    rate * width : (rate + 1) * width, row * loc_rows : (row + 1) * loc_rows
                ]

    inverse_parts(sums, even_table, odd_table, slice(0, quarter), quarter, send)


def inverse_parts(left, even_table, odd_table, at, quarter, send):
    half = 2 * quarter
    far = slice(quarter + at.start, quarter + at.stop)

    def product(first, depth, right):
        return jnp.dot(left[:, first : first + depth], right, preferred_element_type=jnp.float32)

    zero = product(0, quarter, even_table[:quarter, at])
    two = product(quarter, quarter, even_table[quarter:, at])
    for position, even, span in ((0, zero + two, at), (1, zero - two, far)):
        odd = product(half, half, odd_table[:, span])
        send(position, even + odd)
        send(position + 2, even - odd)


def column_stage(rate_vectors, epoch_times, spectra, even_table, odd_table, epoch_count):
    devices, loc_epochs, width, loc_rows = spectra.shape
    half, quarter = even_table.shape
    length = 2 * half
    epochs, rates = epoch_times.shape[0], rate_vectors.shape[0]
    out = (devices, rates // epoch_count, width, loc_rows)
    scalars = pl.BlockSpec(memory_space=pltpu.SMEM)
    return pl.pallas_call(
        functools.partial(column_kernel, epoch_count),
        in_specs=[scalars, scalars, IN_VMEM, IN_VMEM, IN_VMEM],
        out_specs=IN_VMEM,
        out_shape=pltpu.VMEM(out, jnp.bfloat16),
        scratch_shapes=[
            pltpu.VMEM((rates * epochs, half), jnp.float32),
            pltpu.VMEM((rates * epochs, half), jnp.float32),
            pltpu.VMEM((4, rates * epochs, width, GROUP), jnp.float32),
            pltpu.VMEM((2, epochs * width, quarter), jnp.bfloat16),
            pltpu.VMEM((epochs * width, half), jnp.bfloat16),
            pltpu.VMEM((2, epochs * width, BLOCK), jnp.float32),
            pltpu.VMEM((rates * width, length), jnp.bfloat16),
        ],
        compiler_params=pltpu.CompilerParams(vmem_limit_bytes=40 * MIB),
        cost_estimate=cost(
            2 * (even_table.size + odd_table.size) * (epochs + rates) * width,
            3 * half * half + 4 * spectra.size,
        ),
        name="column_stage",
    )(
        rate_vectors,
        epoch_times,
        *(in_space(part, pltpu.VMEM) for part in (spectra, even_table, odd_table)),
    )


def image_kernel(back, even_table, odd_table, out_hbm, left, staged, out_sems):
    quarter = even_table.shape[1]
    _, width, rows = back.shape
    cols = width // 2
    per_group = GROUP // cols
    for group in range(back.shape[0] // per_group):
        members = [back[group * per_group + place] for place in range(per_group)]
        if cols % 16 != 0 or rows % 128 != 0:
            members = [member.astype(jnp.float32) for member in members]
        parts = [member[:cols] for member in members] + [member[cols:] for member in members]
        whole = jnp.concatenate(parts, axis=0)
        left[:, group * 2 * GROUP : (group + 1) * 2 * GROUP] = whole.T.astype(jnp.bfloat16)
    out_copies = []
    for block in range(quarter // IMAGE_BLOCK):

        def send(side, pixels):
            start = side * quarter + block * IMAGE_BLOCK
            at = slice(start, start + IMAGE_BLOCK)
            staged[:, at] = pixels
            out_copies.append(
                pltpu.make_async_copy(
                    staged.at[:, at], out_hbm.at[0, :, at], out_sems.at[4 * block + side]
                )
            )
            out_copies[-1].start()

        at = slice(block * IMAGE_BLOCK, (block + 1) * IMAGE_BLOCK)
        inverse_parts(left, even_table, odd_table, at, quarter, send)
    wait_copies(out_copies)


def image_rows(back, even_table, odd_table):
    rows = back.shape[2]
    half, quarter = even_table.shape
    length = 2 * half
    return pl.pallas_call(
        image_kernel,
        in_specs=[IN_VMEM, IN_VMEM, IN_VMEM],
        out_specs=HBM,
        out_shape=jax.ShapeDtypeStruct((1, rows, length), jnp.float32),
        scratch_shapes=[
            pltpu.VMEM((rows, length), jnp.bfloat16),
            pltpu.VMEM((rows, length), jnp.float32),
            pltpu.SemaphoreType.DMA((length // IMAGE_BLOCK,)),
        ],
        compiler_params=pltpu.CompilerParams(vmem_limit_bytes=40 * MIB),
        cost_estimate=cost(
            2 * rows * (even_table.size + odd_table.size), 3 * half * half + 6 * rows * length
        ),
        name="image_rows",
    )(*(in_space(part, pltpu.VMEM) for part in (back, even_table, odd_table)))


def local(images, rate_vectors, epoch_times):
    _, loc_rows, length = images.shape
    epoch_count = lax.axis_size("epoch")
    devices = lax.axis_size("row") * epoch_count
    even_table, odd_table = [jnp.asarray(part) for part in packed_tables(length)]

    def exchange(values):
        return lax.all_to_all(values, ("row", "epoch"), 0, 0, tiled=True)

    spectra = exchange(row_transform(images, even_table, odd_table, devices))
    back = exchange(
        column_stage(rate_vectors, epoch_times, spectra, even_table, odd_table, epoch_count)
    )
    return image_rows(
        back.reshape(devices, length // devices, loc_rows), even_table, odd_table
    )


def solution(mesh):
    in_specs = (P(("group", "epoch"), "row", None), P(), P())
    out_specs = P(("group", "epoch"), "row", None)
    return jax.shard_map(local, mesh=mesh, in_specs=in_specs, out_specs=out_specs, check_vma=False)
```

```python
import functools
import math

import jax
import jax.numpy as jnp
import ml_dtypes
import numpy as np
from jax import lax
from jax.experimental import pallas as pl
from jax.experimental.pallas import tpu as pltpu
from jax.sharding import PartitionSpec as P

SUBPIX = 16
GROUP = 128
BLOCK = 512
IMAGE_BLOCK = 512
ROW_CHUNK = 16
PIECES = 4
MIB = 1024 * 1024
CONTRACT_LAST = (((1,), (1,)), ((), ()))
HBM = pl.BlockSpec(memory_space=pltpu.HBM)
IN_VMEM = pl.BlockSpec(memory_space=pltpu.VMEM)


def packed_freqs(index, half, where=jnp.where):
    even = 4 * index - where(index < half // 4, 0, half - 2)
    return where(index < half // 2, even, 2 * index - half + 1)


def packed_tables(length):
    half, quarter = length // 2, length // 4
    freqs = packed_freqs(np.arange(half, dtype=np.int32), half, np.where)
    positions = np.arange(half, dtype=np.int32)
    turns = freqs[:, None] * positions[None, :] % length
    angles = turns.astype(np.float32) * np.float32(2.0 * math.pi / length)
    factor = np.float32(1.0 / math.sqrt(length))
    cosine = np.cos(angles) * factor
    sine = np.sin(angles) * factor
    sine[0] = np.where(positions % 2 == 0, factor, -factor)
    groups = np.stack([cosine.reshape(-1, GROUP, half), sine.reshape(-1, GROUP, half)], axis=1)
    table = groups.reshape(length, half).astype(ml_dtypes.bfloat16)
    return np.ascontiguousarray(table[:half, :quarter]), table[half:]


def cost(flops, bytes_accessed):
    return pl.CostEstimate(flops=flops, bytes_accessed=bytes_accessed, transcendentals=0)


def in_space(array, space):
    return pltpu.with_memory_space_constraint(array, space)


def wait_copies(copies):
    for copy in copies:
        copy.wait()


def fold(quarters):
    first, second, third, fourth = quarters
    near, far = first + third, second + fourth
    return near + far, near - far, first - third, second - fourth


def row_kernel(
    images_hbm,
    even_hbm,
    odd_hbm,
    out_ref,
    images,
    even_table,
    odd_table,
    even_fold,
    odd_fold,
    image_sems,
    table_sems,
):
    loc_epochs, loc_rows, length = images.shape
    half, quarter = length // 2, length // 4
    devices, _, width, _ = out_ref.shape
    cols = width // 2
    steps = length // BLOCK
    per_step = devices // steps
    per_group = GROUP // cols
    def copies(source, target, sems, pieces):
        rows = source.shape[0] // pieces
        spans = [pl.ds(piece * rows, rows) for piece in range(pieces)]
        return [
            pltpu.make_async_copy(source.at[span], target.at[span], sems.at[piece])
            for piece, span in enumerate(spans)
        ]

    pieces = max(1, min(PIECES, loc_rows // 16))
    image_copies = [
        copies(images_hbm.at[loc], images.at[loc], image_sems.at[loc], pieces)
        for loc in range(loc_epochs)
    ]
    even_copies = copies(even_hbm, even_table, table_sems.at[0], PIECES)
    odd_copies = copies(odd_hbm, odd_table, table_sems.at[1], 2)
    halfway = PIECES // 2
    table_copies = [even_copies[:halfway], even_copies[halfway:], odd_copies[:1], odd_copies[1:]]
    for copy in sum(image_copies, []) + even_copies + odd_copies:
        copy.start()
    for loc in range(loc_epochs):
        wait_copies(image_copies[loc])
        at = slice(loc * loc_rows, (loc + 1) * loc_rows)
        folds = fold([images[loc, :, part * quarter : (part + 1) * quarter] for part in range(4)])
        even_fold[0, at], even_fold[1, at] = folds[:2]
        odd_fold[at, :quarter], odd_fold[at, quarter:] = folds[2:]
    for step in range(steps):
        wait_copies(table_copies[step])
        at = slice(step % (steps // 2) * BLOCK, (step % (steps // 2) + 1) * BLOCK)
        if step < steps // 2:
            left, right = even_table[at], even_fold[4 * step // steps]
        else:
            left, right = odd_table[at], odd_fold[...]
        terms = lax.dot_general(left, right, CONTRACT_LAST, preferred_element_type=jnp.float32)
        for dest in range(per_step):
            start = dest // per_group * 2 * GROUP + dest % per_group * cols
            parts = [terms[first : first + cols] for first in (start, start + GROUP)]
            block = jnp.concatenate(parts, axis=0).astype(jnp.bfloat16)
            for loc in range(loc_epochs):
                out_ref[step * per_step + dest, loc] = block[:, loc * loc_rows : (loc + 1) * loc_rows]


def row_transform(images, even_table, odd_table, devices):
    loc_epochs, loc_rows, length = images.shape
    half, quarter = length // 2, length // 4
    rows = loc_epochs * loc_rows
    steps = length // BLOCK
    out = (devices, loc_epochs, length // devices, loc_rows)
    return pl.pallas_call(
        row_kernel,
        in_specs=[HBM, HBM, HBM],
        out_specs=IN_VMEM,
        out_shape=pltpu.VMEM(out, jnp.bfloat16),
        scratch_shapes=[
            pltpu.VMEM(images.shape, jnp.bfloat16),
            pltpu.VMEM(even_table.shape, jnp.bfloat16),
            pltpu.VMEM(odd_table.shape, jnp.bfloat16),
            pltpu.VMEM((2, rows, quarter), jnp.bfloat16),
            pltpu.VMEM((rows, half), jnp.bfloat16),
            pltpu.SemaphoreType.DMA((loc_epochs, PIECES)),
            pltpu.SemaphoreType.DMA((2, PIECES)),
        ],
        compiler_params=pltpu.CompilerParams(vmem_limit_bytes=40 * MIB),
        cost_estimate=cost(
            2 * rows * (even_table.size + odd_table.size), 3 * half * half + 4 * rows * length
        ),
        name="row_transform",
    )(*(in_space(part, pltpu.HBM) for part in (images, even_table, odd_table)))


def cos_sin(turns, whole):
    quarter, eighth = whole // 4, whole // 8
    shifted = (turns + eighth) & (whole - 1)
    quadrant = shifted >> (quarter.bit_length() - 1)
    angle = ((shifted & (quarter - 1)) - eighth).astype(jnp.float32) * (2.0 * math.pi / whole)
    square = angle * angle
    sine, cosine = 1.0 / 362880.0, 1.0 / 40320.0
    for divisor in (-5040.0, 120.0, -6.0, 1.0):
        sine = sine * square + 1.0 / divisor
    for divisor in (-720.0, 24.0, -2.0, 1.0):
        cosine = cosine * square + 1.0 / divisor
    sine = sine * angle
    odd = (quadrant & 1) == 1
    first, second = jnp.where(odd, sine, cosine), jnp.where(odd, cosine, sine)
    return (
        jnp.where(((quadrant + 1) & 2) == 2, -first, first),
        jnp.where(quadrant >= 2, -second, second),
    )


def spread_pairs(scalars, lanes):
    pair = lax.broadcasted_iota(jnp.int32, (len(scalars), lanes), 0)
    values = jnp.zeros((len(scalars), lanes), jnp.int32)
    for index, scalar in enumerate(scalars):
        values = jnp.where(pair == index, scalar, values)
    return values


def row_factors(shift_y, half):
    shifts = spread_pairs(shift_y, half)
    freqs = packed_freqs(lax.broadcasted_iota(jnp.int32, shifts.shape, 1), half)
    cosine, sine = cos_sin((freqs - half) * shifts, SUBPIX * 2 * half)
    return jnp.where(freqs == 0, 1.0, 2.0 * cosine), jnp.where(freqs == 0, 0.0, 2.0 * sine)


def column_factors(shift_y, shift_x, scale, device, cols, half):
    shifts_y, shifts_x = spread_pairs(shift_y, GROUP), spread_pairs(shift_x, GROUP)
    lane = lax.broadcasted_iota(jnp.int32, shifts_x.shape, 1)
    freqs = packed_freqs(device * cols + (lane & (cols - 1)), half)
    is_sine = (lane & cols) > 0
    paired = freqs == 0
    zero_col = paired & jnp.logical_not(is_sine)
    cosine, sine = cos_sin(shifts_x * (freqs - half), SUBPIX * 2 * half)
    ramp_cos = jnp.where(paired, scale, 2.0 * scale * cosine)
    ramp_sin = jnp.where(paired, 0.0, 2.0 * scale * sine)
    ramp_sin = jnp.where(is_sine, ramp_sin, -ramp_sin)
    cos_x, cos_y, cos_xy = [
        cos_sin(shifts, 2 * SUBPIX)[0] for shifts in (shifts_x, shifts_y, shifts_x + shifts_y)
    ]
    main = jnp.where(zero_col, cos_y, cos_xy)
    lead = jnp.where(zero_col, 1.0, cos_x)
    return jnp.concatenate(
        [main * ramp_cos, main * ramp_sin, lead * ramp_cos, lead * ramp_sin], axis=0
    )


def column_kernel(
    epoch_count,
    rate_smem,
    time_smem,
    received,
    even_table,
    odd_table,
    out_ref,
    rows_cos,
    rows_sin,
    spread,
    even_fold,
    odd_fold,
    products,
    sums,
):
    devices, loc_epochs, width, loc_rows = received.shape
    row_count = devices // epoch_count
    epochs = epoch_count * loc_epochs
    rates = rate_smem.shape[0]
    pairs = rates * epochs
    cols = width // 2
    half, quarter = even_table.shape
    length = 2 * half
    steps = length // BLOCK
    device = lax.axis_index("row") * epoch_count + lax.axis_index("epoch")
    period = SUBPIX * length
    shift_y, shift_x = [
        [
            rate_smem[rate, axis] * time_smem[epoch] & (period - 1)
            for rate in range(rates)
            for epoch in range(epochs)
        ]
        for axis in range(2)
    ]
    per_tile = max(1, GROUP // loc_rows)
    tile_rows = per_tile * loc_rows
    for tile in range(row_count // 4 // per_tile):
        at_lane = slice(tile * tile_rows, (tile + 1) * tile_rows)
        far_lane = slice(quarter + at_lane.start, quarter + at_lane.stop)
        for core in range(epoch_count):
            for loc in range(loc_epochs):
                quarters = []
                for side in range(4):
                    first = side * row_count // 4 + tile * per_tile
                    parts = [
                        received[(first + part) * epoch_count + core, loc] for part in range(per_tile)
                    ]
                    quarters.append(parts[0] if per_tile == 1 else jnp.concatenate(parts, axis=1))
                at_row = (core * loc_epochs + loc) * width
                at = slice(at_row, at_row + width)
                folds = fold(quarters)
                even_fold[0, at, at_lane], even_fold[1, at, at_lane] = folds[:2]
                odd_fold[at, at_lane], odd_fold[at, far_lane] = folds[2:]

    def multiply(step):
        at = slice(step % (steps // 2) * BLOCK, (step % (steps // 2) + 1) * BLOCK)
        if step < steps // 2:
            left, right = even_fold[4 * step // steps], even_table[at]
        else:
            left, right = odd_fold[...], odd_table[at]
        products[step % 2] = lax.dot_general(
            left, right, CONTRACT_LAST, preferred_element_type=jnp.float32
        )

    multiply(0)
    rows_cos[...], rows_sin[...] = row_factors(shift_y, half)
    factors = column_factors(shift_y, shift_x, 1.0 / math.sqrt(epochs), device, cols, half).T
    for kind in range(4):
        for pair in range(pairs):
            at = kind * pairs + pair
            spread[kind, pair] = jnp.broadcast_to(factors[:width, at : at + 1], (width, GROUP))

    chunk = min(ROW_CHUNK, cols)

    def add_ramped(step, group):
        tile = (step * BLOCK // 2 // GROUP + group) * GROUP
        at_even = group * 2 * GROUP
        at_odd = at_even + GROUP
        for rate in range(rates):
            for start in range(0, cols, chunk):
                real = slice(start, start + chunk)
                imag = slice(cols + start, cols + start + chunk)
                totals = [[0.0, 0.0], [0.0, 0.0]]
                leads = [0.0, 0.0]
                for epoch in range(epochs):
                    pair = rate * epochs + epoch
                    cos_row = rows_cos[pair : pair + 1, tile : tile + GROUP]
                    sin_row = rows_sin[pair : pair + 1, tile : tile + GROUP]
                    turned, evens = [], []
                    for part in (real, imag):
                        at = slice(epoch * width + part.start, epoch * width + part.stop)
                        even = products[step % 2, at, at_even : at_even + GROUP]
                        odd = products[step % 2, at, at_odd : at_odd + GROUP]
                        turned.append(
                            (cos_row * even + sin_row * odd, cos_row * odd - sin_row * even)
                        )
                        evens.append(even)
                    straight = [spread[0, pair, part] for part in (real, imag)]
                    crossed = [spread[1, pair, part] for part in (real, imag)]
                    for part in range(2):
                        for which in range(2):
                            totals[part][which] += (
                                straight[part] * turned[part][which]
                                + crossed[1 - part] * turned[1 - part][which]
                            )
                        if step == 0 and group == 0:
                            own, other = (real, imag) if part == 0 else (imag, real)
                            leads[part] += (
                                spread[2, pair, own] * evens[part]
                                + spread[3, pair, other] * evens[1 - part]
                            )
                for part, rows in enumerate((real, imag)):
                    even_sum, odd_sum = totals[part]
                    if step == 0 and group == 0:
                        first = lax.broadcasted_iota(jnp.int32, even_sum.shape, 1) == 0
                        even_sum = jnp.where(first, leads[part], even_sum)
                    at = slice(rate * width + rows.start, rate * width + rows.stop)
                    sums[at, step * BLOCK + at_even : step * BLOCK + at_even + GROUP] = even_sum.astype(
                        jnp.bfloat16
                    )
                    sums[at, step * BLOCK + at_odd : step * BLOCK + at_odd + GROUP] = odd_sum.astype(
                        jnp.bfloat16
                    )

    for step in range(steps):
        if step + 1 < steps:
            multiply(step + 1)
        for group in range(BLOCK // 2 // GROUP):
            add_ramped(step, group)

    loc_rates = rates // epoch_count

    def send(side, back):
        back = back.astype(jnp.bfloat16)
        rows_here = quarter // loc_rows
        for row in range(rows_here):
            for rate in range(rates):
                dest = (side * rows_here + row) * epoch_count + rate // loc_rates
                out_ref[dest, rate % loc_rates] = back[
                    rate * width : (rate + 1) * width, row * loc_rows : (row + 1) * loc_rows
                ]

    inverse_parts(sums, even_table, odd_table, slice(0, quarter), quarter, send)


def inverse_parts(left, even_table, odd_table, at, quarter, send):
    half = 2 * quarter
    far = slice(quarter + at.start, quarter + at.stop)

    def product(first, depth, right):
        return jnp.dot(left[:, first : first + depth], right, preferred_element_type=jnp.float32)

    zero = product(0, quarter, even_table[:quarter, at])
    two = product(quarter, quarter, even_table[quarter:, at])
    for position, even, span in ((0, zero + two, at), (1, zero - two, far)):
        odd = product(half, half, odd_table[:, span])
        send(position, even + odd)
        send(position + 2, even - odd)


def column_stage(rate_vectors, epoch_times, spectra, even_table, odd_table, epoch_count):
    devices, loc_epochs, width, loc_rows = spectra.shape
    half, quarter = even_table.shape
    length = 2 * half
    epochs, rates = epoch_times.shape[0], rate_vectors.shape[0]
    out = (devices, rates // epoch_count, width, loc_rows)
    scalars = pl.BlockSpec(memory_space=pltpu.SMEM)
    return pl.pallas_call(
        functools.partial(column_kernel, epoch_count),
        in_specs=[scalars, scalars, IN_VMEM, IN_VMEM, IN_VMEM],
        out_specs=IN_VMEM,
        out_shape=pltpu.VMEM(out, jnp.bfloat16),
        scratch_shapes=[
            pltpu.VMEM((rates * epochs, half), jnp.float32),
            pltpu.VMEM((rates * epochs, half), jnp.float32),
            pltpu.VMEM((4, rates * epochs, width, GROUP), jnp.float32),
            pltpu.VMEM((2, epochs * width, quarter), jnp.bfloat16),
            pltpu.VMEM((epochs * width, half), jnp.bfloat16),
            pltpu.VMEM((2, epochs * width, BLOCK), jnp.float32),
            pltpu.VMEM((rates * width, length), jnp.bfloat16),
        ],
        compiler_params=pltpu.CompilerParams(vmem_limit_bytes=40 * MIB),
        cost_estimate=cost(
            2 * (even_table.size + odd_table.size) * (epochs + rates) * width,
            3 * half * half + 4 * spectra.size,
        ),
        name="column_stage",
    )(
        rate_vectors,
        epoch_times,
        *(in_space(part, pltpu.VMEM) for part in (spectra, even_table, odd_table)),
    )


def image_kernel(back, even_table, odd_table, out_hbm, left, staged, out_sems):
    quarter = even_table.shape[1]
    _, width, rows = back.shape
    cols = width // 2
    per_group = GROUP // cols
    for group in range(back.shape[0] // per_group):
        members = [back[group * per_group + place] for place in range(per_group)]
        if cols % 16 != 0 or rows % 128 != 0:
            members = [member.astype(jnp.float32) for member in members]
        parts = [member[:cols] for member in members] + [member[cols:] for member in members]
        whole = jnp.concatenate(parts, axis=0)
        left[:, group * 2 * GROUP : (group + 1) * 2 * GROUP] = whole.T.astype(jnp.bfloat16)
    out_copies = []
    for block in range(quarter // IMAGE_BLOCK):

        def send(side, pixels):
            start = side * quarter + block * IMAGE_BLOCK
            at = slice(start, start + IMAGE_BLOCK)
            staged[:, at] = pixels
            out_copies.append(
                pltpu.make_async_copy(
                    staged.at[:, at], out_hbm.at[0, :, at], out_sems.at[4 * block + side]
                )
            )
            out_copies[-1].start()

        at = slice(block * IMAGE_BLOCK, (block + 1) * IMAGE_BLOCK)
        inverse_parts(left, even_table, odd_table, at, quarter, send)
    wait_copies(out_copies)


def image_rows(back, even_table, odd_table):
    rows = back.shape[2]
    half, quarter = even_table.shape
    length = 2 * half
    return pl.pallas_call(
        image_kernel,
        in_specs=[IN_VMEM, IN_VMEM, IN_VMEM],
        out_specs=HBM,
        out_shape=jax.ShapeDtypeStruct((1, rows, length), jnp.float32),
        scratch_shapes=[
            pltpu.VMEM((rows, length), jnp.bfloat16),
            pltpu.VMEM((rows, length), jnp.float32),
            pltpu.SemaphoreType.DMA((length // IMAGE_BLOCK,)),
        ],
        compiler_params=pltpu.CompilerParams(vmem_limit_bytes=40 * MIB),
        cost_estimate=cost(
            2 * rows * (even_table.size + odd_table.size), 3 * half * half + 6 * rows * length
        ),
        name="image_rows",
    )(*(in_space(part, pltpu.VMEM) for part in (back, even_table, odd_table)))


def local(images, rate_vectors, epoch_times):
    _, loc_rows, length = images.shape
    epoch_count = lax.axis_size("epoch")
    devices = lax.axis_size("row") * epoch_count
    even_table, odd_table = [jnp.asarray(part) for part in packed_tables(length)]

    def exchange(values):
        return lax.all_to_all(values, ("row", "epoch"), 0, 0, tiled=True)

    spectra = exchange(row_transform(images, even_table, odd_table, devices))
    back = exchange(
        column_stage(rate_vectors, epoch_times, spectra, even_table, odd_table, epoch_count)
    )
    return image_rows(
        back.reshape(devices, length // devices, loc_rows), even_table, odd_table
    )


def solution(mesh):
    in_specs = (P(("group", "epoch"), "row", None), P(), P())
    out_specs = P(("group", "epoch"), "row", None)
    return jax.shard_map(local, mesh=mesh, in_specs=in_specs, out_specs=out_specs, check_vma=False)
```

```python
import functools
import math

import jax
import jax.numpy as jnp
import ml_dtypes
import numpy as np
from jax import lax
from jax.experimental import pallas as pl
from jax.experimental.pallas import tpu as pltpu
from jax.sharding import PartitionSpec as P

SUBPIX = 16
GROUP = 128
BLOCK = 512
IMAGE_BLOCK = 512
ROW_CHUNK = 16
PIECES = 4
MIB = 1024 * 1024
CONTRACT_LAST = (((1,), (1,)), ((), ()))
HBM = pl.BlockSpec(memory_space=pltpu.HBM)
IN_VMEM = pl.BlockSpec(memory_space=pltpu.VMEM)


def packed_freqs(index, half):
    count = half // 4
    kind = index >> (count.bit_length() - 1)
    return 4 * (index & (count - 1)) + 2 * (kind & 1) + (kind >> 1)


def packed_tables(length):
    half, quarter = length // 2, length // 4
    freqs = packed_freqs(np.arange(half, dtype=np.int32), half)
    positions = np.arange(half, dtype=np.int32)
    turns = freqs[:, None] * positions[None, :] % length
    angles = turns.astype(np.float32) * np.float32(2.0 * math.pi / length)
    factor = np.float32(1.0 / math.sqrt(length))
    cosine = np.cos(angles) * factor
    sine = np.sin(angles) * factor
    sine[0] = np.where(positions % 2 == 0, factor, -factor)
    groups = np.stack([cosine.reshape(-1, GROUP, half), sine.reshape(-1, GROUP, half)], axis=1)
    table = groups.reshape(length, half).astype(ml_dtypes.bfloat16)
    return np.ascontiguousarray(table[:half, :quarter]), table[half:]


def cost(flops, bytes_accessed):
    return pl.CostEstimate(flops=flops, bytes_accessed=bytes_accessed, transcendentals=0)


def in_space(array, space):
    return pltpu.with_memory_space_constraint(array, space)


def wait_copies(copies):
    for copy in copies:
        copy.wait()


def fold(quarters):
    first, second, third, fourth = quarters
    near, far = first + third, second + fourth
    return near + far, near - far, first - third, second - fourth


def row_kernel(
    images_hbm,
    even_hbm,
    odd_hbm,
    out_ref,
    images,
    even_table,
    odd_table,
    folded,
    image_sems,
    table_sems,
):
    loc_epochs, loc_rows, length = images.shape
    half, quarter = length // 2, length // 4
    devices, _, width, _ = out_ref.shape
    cols = width // 2
    steps = length // BLOCK
    per_step = devices // steps
    per_group = GROUP // cols
    def copies(source, target, sems, pieces):
        rows = source.shape[0] // pieces
        spans = [pl.ds(piece * rows, rows) for piece in range(pieces)]
        return [
            pltpu.make_async_copy(source.at[span], target.at[span], sems.at[piece])
            for piece, span in enumerate(spans)
        ]

    pieces = max(1, min(PIECES, loc_rows // 16))
    image_copies = [
        copies(images_hbm.at[loc], images.at[loc], image_sems.at[loc], pieces)
        for loc in range(loc_epochs)
    ]
    even_copies = copies(even_hbm, even_table, table_sems.at[0], PIECES)
    odd_copies = copies(odd_hbm.at[:, :quarter], odd_table, table_sems.at[1], 2)
    halfway = PIECES // 2
    table_copies = [even_copies[:halfway], even_copies[halfway:], odd_copies[:1], odd_copies[1:]]
    for copy in sum(image_copies, []) + even_copies + odd_copies:
        copy.start()
    for loc in range(loc_epochs):
        wait_copies(image_copies[loc])
        at = slice(loc * loc_rows, (loc + 1) * loc_rows)
        folds = fold([images[loc, :, part * quarter : (part + 1) * quarter] for part in range(4)])
        for part in range(4):
            folded[part, at] = folds[part]
    for step in range(steps):
        wait_copies(table_copies[step])
        at = slice(step % (steps // 2) * BLOCK, (step % (steps // 2) + 1) * BLOCK)
        left = (even_table if step < steps // 2 else odd_table)[at]
        sources = [step] if step < steps // 2 else [2, 3]
        terms = [
            lax.dot_general(
                left, folded[source], CONTRACT_LAST, preferred_element_type=jnp.float32
            )
            for source in sources
        ]
        for dest in range(per_step):
            start = dest // per_group * 2 * GROUP + dest % per_group * cols
            cosine, sine = [slice(first, first + cols) for first in (start, start + GROUP)]
            parts = [terms[0][cosine], terms[0][sine]]
            if step == 2:
                parts = [parts[0] - terms[1][sine], parts[1] + terms[1][cosine]]
            if step == 3:
                parts = [parts[0] + terms[1][sine], parts[1] - terms[1][cosine]]
            block = jnp.concatenate(parts, axis=0).astype(jnp.bfloat16)
            for loc in range(loc_epochs):
                out_ref[step * per_step + dest, loc] = block[:, loc * loc_rows : (loc + 1) * loc_rows]


def row_transform(images, even_table, odd_table, devices):
    loc_epochs, loc_rows, length = images.shape
    half, quarter = length // 2, length // 4
    rows = loc_epochs * loc_rows
    steps = length // BLOCK
    out = (devices, loc_epochs, length // devices, loc_rows)
    return pl.pallas_call(
        row_kernel,
        in_specs=[HBM, HBM, HBM],
        out_specs=IN_VMEM,
        out_shape=pltpu.VMEM(out, jnp.bfloat16),
        scratch_shapes=[
            pltpu.VMEM(images.shape, jnp.bfloat16),
            pltpu.VMEM(even_table.shape, jnp.bfloat16),
            pltpu.VMEM(even_table.shape, jnp.bfloat16),
            pltpu.VMEM((4, rows, quarter), jnp.bfloat16),
            pltpu.SemaphoreType.DMA((loc_epochs, PIECES)),
            pltpu.SemaphoreType.DMA((2, PIECES)),
        ],
        compiler_params=pltpu.CompilerParams(vmem_limit_bytes=40 * MIB),
        cost_estimate=cost(
            2 * rows * (even_table.size + odd_table.size), 3 * half * half + 4 * rows * length
        ),
        name="row_transform",
    )(*(in_space(part, pltpu.HBM) for part in (images, even_table, odd_table)))


def cos_sin(turns, whole):
    quarter, eighth = whole // 4, whole // 8
    shifted = (turns + eighth) & (whole - 1)
    quadrant = shifted >> (quarter.bit_length() - 1)
    angle = ((shifted & (quarter - 1)) - eighth).astype(jnp.float32) * (2.0 * math.pi / whole)
    square = angle * angle
    sine, cosine = 1.0 / 362880.0, 1.0 / 40320.0
    for divisor in (-5040.0, 120.0, -6.0, 1.0):
        sine = sine * square + 1.0 / divisor
    for divisor in (-720.0, 24.0, -2.0, 1.0):
        cosine = cosine * square + 1.0 / divisor
    sine = sine * angle
    odd = (quadrant & 1) == 1
    first, second = jnp.where(odd, sine, cosine), jnp.where(odd, cosine, sine)
    return (
        jnp.where(((quadrant + 1) & 2) == 2, -first, first),
        jnp.where(quadrant >= 2, -second, second),
    )


def spread_pairs(scalars, lanes):
    pair = lax.broadcasted_iota(jnp.int32, (len(scalars), lanes), 0)
    values = jnp.zeros((len(scalars), lanes), jnp.int32)
    for index, scalar in enumerate(scalars):
        values = jnp.where(pair == index, scalar, values)
    return values


def row_factors(shift_y, half):
    shifts = spread_pairs(shift_y, half)
    freqs = packed_freqs(lax.broadcasted_iota(jnp.int32, shifts.shape, 1), half)
    cosine, sine = cos_sin((freqs - half) * shifts, SUBPIX * 2 * half)
    return jnp.where(freqs == 0, 1.0, 2.0 * cosine), jnp.where(freqs == 0, 0.0, 2.0 * sine)


def column_factors(shift_y, shift_x, scale, device, cols, half):
    shifts_y, shifts_x = spread_pairs(shift_y, GROUP), spread_pairs(shift_x, GROUP)
    lane = lax.broadcasted_iota(jnp.int32, shifts_x.shape, 1)
    freqs = packed_freqs(device * cols + (lane & (cols - 1)), half)
    is_sine = (lane & cols) > 0
    paired = freqs == 0
    zero_col = paired & jnp.logical_not(is_sine)
    cosine, sine = cos_sin(shifts_x * (freqs - half), SUBPIX * 2 * half)
    ramp_cos = jnp.where(paired, scale, 2.0 * scale * cosine)
    ramp_sin = jnp.where(paired, 0.0, 2.0 * scale * sine)
    ramp_sin = jnp.where(is_sine, ramp_sin, -ramp_sin)
    cos_x, cos_y, cos_xy = [
        cos_sin(shifts, 2 * SUBPIX)[0] for shifts in (shifts_x, shifts_y, shifts_x + shifts_y)
    ]
    main = jnp.where(zero_col, cos_y, cos_xy)
    lead = jnp.where(zero_col, 1.0, cos_x)
    return jnp.concatenate(
        [main * ramp_cos, main * ramp_sin, lead * ramp_cos, lead * ramp_sin], axis=0
    )


def column_kernel(
    epoch_count,
    rate_smem,
    time_smem,
    received,
    even_table,
    odd_table,
    out_ref,
    rows_cos,
    rows_sin,
    spread,
    even_fold,
    odd_fold,
    products,
    sums,
):
    devices, loc_epochs, width, loc_rows = received.shape
    row_count = devices // epoch_count
    epochs = epoch_count * loc_epochs
    rates = rate_smem.shape[0]
    pairs = rates * epochs
    cols = width // 2
    half, quarter = even_table.shape
    length = 2 * half
    steps = length // BLOCK
    device = lax.axis_index("row") * epoch_count + lax.axis_index("epoch")
    period = SUBPIX * length
    shift_y, shift_x = [
        [
            rate_smem[rate, axis] * time_smem[epoch] & (period - 1)
            for rate in range(rates)
            for epoch in range(epochs)
        ]
        for axis in range(2)
    ]
    per_tile = max(1, GROUP // loc_rows)
    tile_rows = per_tile * loc_rows
    for tile in range(row_count // 4 // per_tile):
        at_lane = slice(tile * tile_rows, (tile + 1) * tile_rows)
        far_lane = slice(quarter + at_lane.start, quarter + at_lane.stop)
        for core in range(epoch_count):
            for loc in range(loc_epochs):
                quarters = []
                for side in range(4):
                    first = side * row_count // 4 + tile * per_tile
                    parts = [
                        received[(first + part) * epoch_count + core, loc] for part in range(per_tile)
                    ]
                    quarters.append(parts[0] if per_tile == 1 else jnp.concatenate(parts, axis=1))
                at_row = (core * loc_epochs + loc) * width
                at = slice(at_row, at_row + width)
                folds = fold(quarters)
                even_fold[0, at, at_lane], even_fold[1, at, at_lane] = folds[:2]
                odd_fold[at, at_lane], odd_fold[at, far_lane] = folds[2:]

    def multiply(step):
        at = slice(step % (steps // 2) * BLOCK, (step % (steps // 2) + 1) * BLOCK)
        if step < steps // 2:
            left, right = even_fold[4 * step // steps], even_table[at]
        else:
            left, right = odd_fold[...], odd_table[at]
        products[step % 2] = lax.dot_general(
            left, right, CONTRACT_LAST, preferred_element_type=jnp.float32
        )

    multiply(0)
    rows_cos[...], rows_sin[...] = row_factors(shift_y, half)
    factors = column_factors(shift_y, shift_x, 1.0 / math.sqrt(epochs), device, cols, half).T
    for kind in range(4):
        for pair in range(pairs):
            at = kind * pairs + pair
            spread[kind, pair] = jnp.broadcast_to(factors[:width, at : at + 1], (width, GROUP))

    chunk = min(ROW_CHUNK, cols)

    def add_ramped(step, group):
        tile = (step * BLOCK // 2 // GROUP + group) * GROUP
        at_even = group * 2 * GROUP
        at_odd = at_even + GROUP
        for rate in range(rates):
            for start in range(0, cols, chunk):
                real = slice(start, start + chunk)
                imag = slice(cols + start, cols + start + chunk)
                totals = [[0.0, 0.0], [0.0, 0.0]]
                leads = [0.0, 0.0]
                for epoch in range(epochs):
                    pair = rate * epochs + epoch
                    cos_row = rows_cos[pair : pair + 1, tile : tile + GROUP]
                    sin_row = rows_sin[pair : pair + 1, tile : tile + GROUP]
                    turned, evens = [], []
                    for part in (real, imag):
                        at = slice(epoch * width + part.start, epoch * width + part.stop)
                        even = products[step % 2, at, at_even : at_even + GROUP]
                        odd = products[step % 2, at, at_odd : at_odd + GROUP]
                        turned.append(
                            (cos_row * even + sin_row * odd, cos_row * odd - sin_row * even)
                        )
                        evens.append(even)
                    straight = [spread[0, pair, part] for part in (real, imag)]
                    crossed = [spread[1, pair, part] for part in (real, imag)]
                    for part in range(2):
                        for which in range(2):
                            totals[part][which] += (
                                straight[part] * turned[part][which]
                                + crossed[1 - part] * turned[1 - part][which]
                            )
                        if step == 0 and group == 0:
                            own, other = (real, imag) if part == 0 else (imag, real)
                            leads[part] += (
                                spread[2, pair, own] * evens[part]
                                + spread[3, pair, other] * evens[1 - part]
                            )
                for part, rows in enumerate((real, imag)):
                    even_sum, odd_sum = totals[part]
                    if step == 0 and group == 0:
                        first = lax.broadcasted_iota(jnp.int32, even_sum.shape, 1) == 0
                        even_sum = jnp.where(first, leads[part], even_sum)
                    at = slice(rate * width + rows.start, rate * width + rows.stop)
                    sums[at, step * BLOCK + at_even : step * BLOCK + at_even + GROUP] = even_sum.astype(
                        jnp.bfloat16
                    )
                    sums[at, step * BLOCK + at_odd : step * BLOCK + at_odd + GROUP] = odd_sum.astype(
                        jnp.bfloat16
                    )

    for step in range(steps):
        if step + 1 < steps:
            multiply(step + 1)
        for group in range(BLOCK // 2 // GROUP):
            add_ramped(step, group)

    loc_rates = rates // epoch_count

    def send(side, back):
        back = back.astype(jnp.bfloat16)
        rows_here = quarter // loc_rows
        for row in range(rows_here):
            for rate in range(rates):
                dest = (side * rows_here + row) * epoch_count + rate // loc_rates
                out_ref[dest, rate % loc_rates] = back[
                    rate * width : (rate + 1) * width, row * loc_rows : (row + 1) * loc_rows
                ]

    inverse_parts(sums, even_table, odd_table, slice(0, quarter), quarter, send)


def inverse_parts(left, even_table, odd_table, at, quarter, send):
    half = 2 * quarter
    far = slice(quarter + at.start, quarter + at.stop)

    def product(first, depth, right):
        return jnp.dot(left[:, first : first + depth], right, preferred_element_type=jnp.float32)

    zero = product(0, quarter, even_table[:quarter, at])
    two = product(quarter, quarter, even_table[quarter:, at])
    for position, even, span in ((0, zero + two, at), (1, zero - two, far)):
        odd = product(half, half, odd_table[:, span])
        send(position, even + odd)
        send(position + 2, even - odd)


def column_stage(rate_vectors, epoch_times, spectra, even_table, odd_table, epoch_count):
    devices, loc_epochs, width, loc_rows = spectra.shape
    half, quarter = even_table.shape
    length = 2 * half
    epochs, rates = epoch_times.shape[0], rate_vectors.shape[0]
    out = (devices, rates // epoch_count, width, loc_rows)
    scalars = pl.BlockSpec(memory_space=pltpu.SMEM)
    return pl.pallas_call(
        functools.partial(column_kernel, epoch_count),
        in_specs=[scalars, scalars, IN_VMEM, IN_VMEM, IN_VMEM],
        out_specs=IN_VMEM,
        out_shape=pltpu.VMEM(out, jnp.bfloat16),
        scratch_shapes=[
            pltpu.VMEM((rates * epochs, half), jnp.float32),
            pltpu.VMEM((rates * epochs, half), jnp.float32),
            pltpu.VMEM((4, rates * epochs, width, GROUP), jnp.float32),
            pltpu.VMEM((2, epochs * width, quarter), jnp.bfloat16),
            pltpu.VMEM((epochs * width, half), jnp.bfloat16),
            pltpu.VMEM((2, epochs * width, BLOCK), jnp.float32),
            pltpu.VMEM((rates * width, length), jnp.bfloat16),
        ],
        compiler_params=pltpu.CompilerParams(vmem_limit_bytes=40 * MIB),
        cost_estimate=cost(
            2 * (even_table.size + odd_table.size) * (epochs + rates) * width,
            3 * half * half + 4 * spectra.size,
        ),
        name="column_stage",
    )(
        rate_vectors,
        epoch_times,
        *(in_space(part, pltpu.VMEM) for part in (spectra, even_table, odd_table)),
    )


def image_kernel(back, even_table, odd_table, out_hbm, left, staged, out_sems):
    quarter = even_table.shape[1]
    _, width, rows = back.shape
    cols = width // 2
    per_group = GROUP // cols
    for group in range(back.shape[0] // per_group):
        members = [back[group * per_group + place] for place in range(per_group)]
        if cols % 16 != 0 or rows % 128 != 0:
            members = [member.astype(jnp.float32) for member in members]
        parts = [member[:cols] for member in members] + [member[cols:] for member in members]
        whole = jnp.concatenate(parts, axis=0)
        left[:, group * 2 * GROUP : (group + 1) * 2 * GROUP] = whole.T.astype(jnp.bfloat16)
    out_copies = []
    for block in range(quarter // IMAGE_BLOCK):

        def send(side, pixels):
            start = side * quarter + block * IMAGE_BLOCK
            at = slice(start, start + IMAGE_BLOCK)
            staged[:, at] = pixels
            out_copies.append(
                pltpu.make_async_copy(
                    staged.at[:, at], out_hbm.at[0, :, at], out_sems.at[4 * block + side]
                )
            )
            out_copies[-1].start()

        at = slice(block * IMAGE_BLOCK, (block + 1) * IMAGE_BLOCK)
        inverse_parts(left, even_table, odd_table, at, quarter, send)
    wait_copies(out_copies)


def image_rows(back, even_table, odd_table):
    rows = back.shape[2]
    half, quarter = even_table.shape
    length = 2 * half
    return pl.pallas_call(
        image_kernel,
        in_specs=[IN_VMEM, IN_VMEM, IN_VMEM],
        out_specs=HBM,
        out_shape=jax.ShapeDtypeStruct((1, rows, length), jnp.float32),
        scratch_shapes=[
            pltpu.VMEM((rows, length), jnp.bfloat16),
            pltpu.VMEM((rows, length), jnp.float32),
            pltpu.SemaphoreType.DMA((length // IMAGE_BLOCK,)),
        ],
        compiler_params=pltpu.CompilerParams(vmem_limit_bytes=40 * MIB),
        cost_estimate=cost(
            2 * rows * (even_table.size + odd_table.size), 3 * half * half + 6 * rows * length
        ),
        name="image_rows",
    )(*(in_space(part, pltpu.VMEM) for part in (back, even_table, odd_table)))


def local(images, rate_vectors, epoch_times):
    _, loc_rows, length = images.shape
    epoch_count = lax.axis_size("epoch")
    devices = lax.axis_size("row") * epoch_count
    even_table, odd_table = [jnp.asarray(part) for part in packed_tables(length)]

    def exchange(values):
        return lax.all_to_all(values, ("row", "epoch"), 0, 0, tiled=True)

    spectra = exchange(row_transform(images, even_table, odd_table, devices))
    back = exchange(
        column_stage(rate_vectors, epoch_times, spectra, even_table, odd_table, epoch_count)
    )
    return image_rows(
        back.reshape(devices, length // devices, loc_rows), even_table, odd_table
    )


def solution(mesh):
    in_specs = (P(("group", "epoch"), "row", None), P(), P())
    out_specs = P(("group", "epoch"), "row", None)
    return jax.shard_map(local, mesh=mesh, in_specs=in_specs, out_specs=out_specs, check_vma=False)
```

```python
import functools
import math

import jax
import jax.numpy as jnp
import ml_dtypes
import numpy as np
from jax import lax
from jax.experimental import pallas as pl
from jax.experimental.pallas import tpu as pltpu
from jax.sharding import PartitionSpec as P

SUBPIX = 16
GROUP = 128
BLOCK = 512
IMAGE_BLOCK = 512
ROW_CHUNK = 16
PIECES = 4
MIB = 1024 * 1024
CONTRACT_LAST = (((1,), (1,)), ((), ()))
HBM = pl.BlockSpec(memory_space=pltpu.HBM)
IN_VMEM = pl.BlockSpec(memory_space=pltpu.VMEM)


def packed_freqs(index, half):
    count = half // 4
    kind = index >> (count.bit_length() - 1)
    return 4 * (index & (count - 1)) + 2 * (kind & 1) + (kind >> 1)


def packed_tables(length):
    half, quarter = length // 2, length // 4
    freqs = packed_freqs(np.arange(half, dtype=np.int32), half)
    positions = np.arange(half, dtype=np.int32)
    turns = freqs[:, None] * positions[None, :] % length
    angles = turns.astype(np.float32) * np.float32(2.0 * math.pi / length)
    factor = np.float32(1.0 / math.sqrt(length))
    cosine = np.cos(angles) * factor
    sine = np.sin(angles) * factor
    sine[0] = np.where(positions % 2 == 0, factor, -factor)
    groups = np.stack([cosine.reshape(-1, GROUP, half), sine.reshape(-1, GROUP, half)], axis=1)
    table = groups.reshape(length, half).astype(ml_dtypes.bfloat16)
    return np.ascontiguousarray(table[:half, :quarter]), table[half:]


def cost(flops, bytes_accessed):
    return pl.CostEstimate(flops=flops, bytes_accessed=bytes_accessed, transcendentals=0)


def in_space(array, space):
    return pltpu.with_memory_space_constraint(array, space)


def wait_copies(copies):
    for copy in copies:
        copy.wait()


def fold(quarters):
    first, second, third, fourth = quarters
    near, far = first + third, second + fourth
    return near + far, near - far, first - third, second - fourth


def row_kernel(
    images_hbm,
    even_hbm,
    odd_hbm,
    out_ref,
    images,
    even_table,
    odd_table,
    folded,
    image_sems,
    table_sems,
):
    loc_epochs, loc_rows, length = images.shape
    half, quarter = length // 2, length // 4
    devices, _, width, _ = out_ref.shape
    cols = width // 2
    steps = length // BLOCK
    per_step = devices // steps
    per_group = GROUP // cols
    def copies(source, target, sems, pieces):
        rows = source.shape[0] // pieces
        spans = [pl.ds(piece * rows, rows) for piece in range(pieces)]
        return [
            pltpu.make_async_copy(source.at[span], target.at[span], sems.at[piece])
            for piece, span in enumerate(spans)
        ]

    pieces = max(1, min(PIECES, loc_rows // 16))
    image_copies = [
        copies(images_hbm.at[loc], images.at[loc], image_sems.at[loc], pieces)
        for loc in range(loc_epochs)
    ]
    even_copies = copies(even_hbm, even_table, table_sems.at[0], PIECES)
    odd_copies = copies(odd_hbm.at[:, :quarter], odd_table, table_sems.at[1], 2)
    halfway = PIECES // 2
    table_copies = [even_copies[:halfway], even_copies[halfway:], odd_copies[:1], odd_copies[1:]]
    for copy in sum(image_copies, []) + even_copies + odd_copies:
        copy.start()
    for loc in range(loc_epochs):
        wait_copies(image_copies[loc])
        at = slice(loc * loc_rows, (loc + 1) * loc_rows)
        folds = fold([images[loc, :, part * quarter : (part + 1) * quarter] for part in range(4)])
        for part in range(4):
            folded[part, at] = folds[part]
    for step in range(steps):
        wait_copies(table_copies[step])
        at = slice(step % (steps // 2) * BLOCK, (step % (steps // 2) + 1) * BLOCK)
        left = (even_table if step < steps // 2 else odd_table)[at]
        sources = [step] if step < steps // 2 else [2, 3]
        terms = [
            lax.dot_general(
                left, folded[source], CONTRACT_LAST, preferred_element_type=jnp.float32
            )
            for source in sources
        ]
        for dest in range(per_step):
            start = dest // per_group * 2 * GROUP + dest % per_group * cols
            cosine, sine = [slice(first, first + cols) for first in (start, start + GROUP)]
            parts = [terms[0][cosine], terms[0][sine]]
            if step == 2:
                parts = [parts[0] - terms[1][sine], parts[1] + terms[1][cosine]]
            if step == 3:
                parts = [parts[0] + terms[1][sine], parts[1] - terms[1][cosine]]
            block = jnp.concatenate(parts, axis=0).astype(jnp.bfloat16)
            for loc in range(loc_epochs):
                out_ref[step * per_step + dest, loc] = block[:, loc * loc_rows : (loc + 1) * loc_rows]


def row_transform(images, even_table, odd_table, devices):
    loc_epochs, loc_rows, length = images.shape
    half, quarter = length // 2, length // 4
    rows = loc_epochs * loc_rows
    steps = length // BLOCK
    out = (devices, loc_epochs, length // devices, loc_rows)
    return pl.pallas_call(
        row_kernel,
        in_specs=[HBM, HBM, HBM],
        out_specs=IN_VMEM,
        out_shape=pltpu.VMEM(out, jnp.bfloat16),
        scratch_shapes=[
            pltpu.VMEM(images.shape, jnp.bfloat16),
            pltpu.VMEM(even_table.shape, jnp.bfloat16),
            pltpu.VMEM(even_table.shape, jnp.bfloat16),
            pltpu.VMEM((4, rows, quarter), jnp.bfloat16),
            pltpu.SemaphoreType.DMA((loc_epochs, PIECES)),
            pltpu.SemaphoreType.DMA((2, PIECES)),
        ],
        compiler_params=pltpu.CompilerParams(vmem_limit_bytes=40 * MIB),
        cost_estimate=cost(
            2 * rows * (even_table.size + odd_table.size), 3 * half * half + 4 * rows * length
        ),
        name="row_transform",
    )(*(in_space(part, pltpu.HBM) for part in (images, even_table, odd_table)))


def cos_sin(turns, whole):
    quarter, eighth = whole // 4, whole // 8
    shifted = (turns + eighth) & (whole - 1)
    quadrant = shifted >> (quarter.bit_length() - 1)
    angle = ((shifted & (quarter - 1)) - eighth).astype(jnp.float32) * (2.0 * math.pi / whole)
    square = angle * angle
    sine, cosine = 1.0 / 362880.0, 1.0 / 40320.0
    for divisor in (-5040.0, 120.0, -6.0, 1.0):
        sine = sine * square + 1.0 / divisor
    for divisor in (-720.0, 24.0, -2.0, 1.0):
        cosine = cosine * square + 1.0 / divisor
    sine = sine * angle
    odd = (quadrant & 1) == 1
    first, second = jnp.where(odd, sine, cosine), jnp.where(odd, cosine, sine)
    return (
        jnp.where(((quadrant + 1) & 2) == 2, -first, first),
        jnp.where(quadrant >= 2, -second, second),
    )


def spread_pairs(scalars, lanes):
    pair = lax.broadcasted_iota(jnp.int32, (len(scalars), lanes), 0)
    values = jnp.zeros((len(scalars), lanes), jnp.int32)
    for index, scalar in enumerate(scalars):
        values = jnp.where(pair == index, scalar, values)
    return values


def row_factors(shift_y, half):
    shifts = spread_pairs(shift_y, half)
    freqs = packed_freqs(lax.broadcasted_iota(jnp.int32, shifts.shape, 1), half)
    cosine, sine = cos_sin((freqs - half) * shifts, SUBPIX * 2 * half)
    return jnp.where(freqs == 0, 1.0, 2.0 * cosine), jnp.where(freqs == 0, 0.0, 2.0 * sine)


def column_factors(shift_y, shift_x, scale, device, cols, half):
    shifts_y, shifts_x = spread_pairs(shift_y, GROUP), spread_pairs(shift_x, GROUP)
    lane = lax.broadcasted_iota(jnp.int32, shifts_x.shape, 1)
    freqs = packed_freqs(device * cols + (lane & (cols - 1)), half)
    is_sine = (lane & cols) > 0
    paired = freqs == 0
    zero_col = paired & jnp.logical_not(is_sine)
    cosine, sine = cos_sin(shifts_x * (freqs - half), SUBPIX * 2 * half)
    ramp_cos = jnp.where(paired, scale, 2.0 * scale * cosine)
    ramp_sin = jnp.where(paired, 0.0, 2.0 * scale * sine)
    ramp_sin = jnp.where(is_sine, ramp_sin, -ramp_sin)
    cos_x, cos_y, cos_xy = [
        cos_sin(shifts, 2 * SUBPIX)[0] for shifts in (shifts_x, shifts_y, shifts_x + shifts_y)
    ]
    main = jnp.where(zero_col, cos_y, cos_xy)
    lead = jnp.where(zero_col, 1.0, cos_x)
    return jnp.concatenate(
        [main * ramp_cos, main * ramp_sin, lead * ramp_cos, lead * ramp_sin], axis=0
    )


def column_kernel(
    epoch_count,
    rate_smem,
    time_smem,
    received,
    even_table,
    odd_table,
    out_ref,
    rows_cos,
    rows_sin,
    spread,
    even_fold,
    odd_fold,
    products,
    sums,
    parts,
):
    devices, loc_epochs, width, loc_rows = received.shape
    row_count = devices // epoch_count
    epochs = epoch_count * loc_epochs
    rates = rate_smem.shape[0]
    pairs = rates * epochs
    cols = width // 2
    half, quarter = even_table.shape
    length = 2 * half
    steps = length // BLOCK
    device = lax.axis_index("row") * epoch_count + lax.axis_index("epoch")
    period = SUBPIX * length
    shift_y, shift_x = [
        [
            rate_smem[rate, axis] * time_smem[epoch] & (period - 1)
            for rate in range(rates)
            for epoch in range(epochs)
        ]
        for axis in range(2)
    ]
    per_tile = max(1, GROUP // loc_rows)
    tile_rows = per_tile * loc_rows
    for tile in range(row_count // 4 // per_tile):
        at_lane = slice(tile * tile_rows, (tile + 1) * tile_rows)
        far_lane = slice(quarter + at_lane.start, quarter + at_lane.stop)
        for core in range(epoch_count):
            for loc in range(loc_epochs):
                quarters = []
                for side in range(4):
                    first = side * row_count // 4 + tile * per_tile
                    blocks = [
                        received[(first + part) * epoch_count + core, loc] for part in range(per_tile)
                    ]
                    quarters.append(blocks[0] if per_tile == 1 else jnp.concatenate(blocks, axis=1))
                at_row = (core * loc_epochs + loc) * width
                at = slice(at_row, at_row + width)
                folds = fold(quarters)
                even_fold[0, at, at_lane], even_fold[1, at, at_lane] = folds[:2]
                odd_fold[at, at_lane], odd_fold[at, far_lane] = folds[2:]

    def multiply(step):
        at = slice(step % (steps // 2) * BLOCK, (step % (steps // 2) + 1) * BLOCK)
        if step < steps // 2:
            left, right = even_fold[4 * step // steps], even_table[at]
        else:
            left, right = odd_fold[...], odd_table[at]
        products[step % 2] = lax.dot_general(
            left, right, CONTRACT_LAST, preferred_element_type=jnp.float32
        )

    multiply(0)
    rows_cos[...], rows_sin[...] = row_factors(shift_y, half)
    factors = column_factors(shift_y, shift_x, 1.0 / math.sqrt(epochs), device, cols, half).T
    for kind in range(4):
        for pair in range(pairs):
            at = kind * pairs + pair
            spread[kind, pair] = jnp.broadcast_to(factors[:width, at : at + 1], (width, GROUP))

    chunk = min(ROW_CHUNK, cols)

    def add_ramped(step, group):
        tile = (step * BLOCK // 2 // GROUP + group) * GROUP
        at_even = group * 2 * GROUP
        at_odd = at_even + GROUP
        for rate in range(rates):
            for start in range(0, cols, chunk):
                real = slice(start, start + chunk)
                imag = slice(cols + start, cols + start + chunk)
                totals = [[0.0, 0.0], [0.0, 0.0]]
                leads = [0.0, 0.0]
                for epoch in range(epochs):
                    pair = rate * epochs + epoch
                    cos_row = rows_cos[pair : pair + 1, tile : tile + GROUP]
                    sin_row = rows_sin[pair : pair + 1, tile : tile + GROUP]
                    turned, evens = [], []
                    for part in (real, imag):
                        at = slice(epoch * width + part.start, epoch * width + part.stop)
                        even = products[step % 2, at, at_even : at_even + GROUP]
                        odd = products[step % 2, at, at_odd : at_odd + GROUP]
                        turned.append(
                            (cos_row * even + sin_row * odd, cos_row * odd - sin_row * even)
                        )
                        evens.append(even)
                    straight = [spread[0, pair, part] for part in (real, imag)]
                    crossed = [spread[1, pair, part] for part in (real, imag)]
                    for part in range(2):
                        for which in range(2):
                            totals[part][which] += (
                                straight[part] * turned[part][which]
                                + crossed[1 - part] * turned[1 - part][which]
                            )
                        if step == 0 and group == 0:
                            own, other = (real, imag) if part == 0 else (imag, real)
                            leads[part] += (
                                spread[2, pair, own] * evens[part]
                                + spread[3, pair, other] * evens[1 - part]
                            )
                for part, rows in enumerate((real, imag)):
                    even_sum, odd_sum = totals[part]
                    if step == 0 and group == 0:
                        first = lax.broadcasted_iota(jnp.int32, even_sum.shape, 1) == 0
                        even_sum = jnp.where(first, leads[part], even_sum)
                    at = slice(rate * width + rows.start, rate * width + rows.stop)
                    sums[at, step * BLOCK + at_even : step * BLOCK + at_even + GROUP] = even_sum.astype(
                        jnp.bfloat16
                    )
                    sums[at, step * BLOCK + at_odd : step * BLOCK + at_odd + GROUP] = odd_sum.astype(
                        jnp.bfloat16
                    )

    def invert(step):
        at = slice(step % (steps // 2) * BLOCK, (step % (steps // 2) + 1) * BLOCK)
        table = even_table if step < steps // 2 else odd_table
        for side in range(table.shape[1] // quarter):
            yield jnp.dot(
                sums[:, step * BLOCK : (step + 1) * BLOCK],
                table[at, side * quarter : (side + 1) * quarter],
                preferred_element_type=jnp.float32,
            )

    for step in range(steps):
        if step + 1 < steps:
            multiply(step + 1)
        if step > 0:
            for side, part in enumerate(invert(step - 1)):
                parts[step - 1 + side] = part
        for group in range(BLOCK // 2 // GROUP):
            add_ramped(step, group)

    loc_rates = rates // epoch_count

    def send(side, back):
        back = back.astype(jnp.bfloat16)
        rows_here = quarter // loc_rows
        for row in range(rows_here):
            for rate in range(rates):
                dest = (side * rows_here + row) * epoch_count + rate // loc_rates
                out_ref[dest, rate % loc_rates] = back[
                    rate * width : (rate + 1) * width, row * loc_rows : (row + 1) * loc_rows
                ]

    for side, part in enumerate(invert(steps - 1)):
        even = parts[0] + parts[1] if side == 0 else parts[0] - parts[1]
        odd = parts[2 + side] + part
        send(side, even + odd)
        send(side + 2, even - odd)


def inverse_parts(left, even_table, odd_table, at, quarter, send):
    half = 2 * quarter
    far = slice(quarter + at.start, quarter + at.stop)

    def product(first, depth, right):
        return jnp.dot(left[:, first : first + depth], right, preferred_element_type=jnp.float32)

    zero = product(0, quarter, even_table[:quarter, at])
    two = product(quarter, quarter, even_table[quarter:, at])
    for position, even, span in ((0, zero + two, at), (1, zero - two, far)):
        odd = product(half, half, odd_table[:, span])
        send(position, even + odd)
        send(position + 2, even - odd)


def column_stage(rate_vectors, epoch_times, spectra, even_table, odd_table, epoch_count):
    devices, loc_epochs, width, loc_rows = spectra.shape
    half, quarter = even_table.shape
    length = 2 * half
    epochs, rates = epoch_times.shape[0], rate_vectors.shape[0]
    out = (devices, rates // epoch_count, width, loc_rows)
    scalars = pl.BlockSpec(memory_space=pltpu.SMEM)
    return pl.pallas_call(
        functools.partial(column_kernel, epoch_count),
        in_specs=[scalars, scalars, IN_VMEM, IN_VMEM, IN_VMEM],
        out_specs=IN_VMEM,
        out_shape=pltpu.VMEM(out, jnp.bfloat16),
        scratch_shapes=[
            pltpu.VMEM((rates * epochs, half), jnp.float32),
            pltpu.VMEM((rates * epochs, half), jnp.float32),
            pltpu.VMEM((4, rates * epochs, width, GROUP), jnp.float32),
            pltpu.VMEM((2, epochs * width, quarter), jnp.bfloat16),
            pltpu.VMEM((epochs * width, half), jnp.bfloat16),
            pltpu.VMEM((2, epochs * width, BLOCK), jnp.float32),
            pltpu.VMEM((rates * width, length), jnp.bfloat16),
            pltpu.VMEM((4, rates * width, quarter), jnp.float32),
        ],
        compiler_params=pltpu.CompilerParams(vmem_limit_bytes=40 * MIB),
        cost_estimate=cost(
            2 * (even_table.size + odd_table.size) * (epochs + rates) * width,
            3 * half * half + 4 * spectra.size,
        ),
        name="column_stage",
    )(
        rate_vectors,
        epoch_times,
        *(in_space(part, pltpu.VMEM) for part in (spectra, even_table, odd_table)),
    )


def image_kernel(back, even_table, odd_table, out_hbm, left, staged, out_sems):
    quarter = even_table.shape[1]
    _, width, rows = back.shape
    cols = width // 2
    per_group = GROUP // cols
    for group in range(back.shape[0] // per_group):
        members = [back[group * per_group + place] for place in range(per_group)]
        if cols % 16 != 0 or rows % 128 != 0:
            members = [member.astype(jnp.float32) for member in members]
        parts = [member[:cols] for member in members] + [member[cols:] for member in members]
        whole = jnp.concatenate(parts, axis=0)
        left[:, group * 2 * GROUP : (group + 1) * 2 * GROUP] = whole.T.astype(jnp.bfloat16)
    out_copies = []
    for block in range(quarter // IMAGE_BLOCK):

        def send(side, pixels):
            start = side * quarter + block * IMAGE_BLOCK
            at = slice(start, start + IMAGE_BLOCK)
            staged[:, at] = pixels
            out_copies.append(
                pltpu.make_async_copy(
                    staged.at[:, at], out_hbm.at[0, :, at], out_sems.at[4 * block + side]
                )
            )
            out_copies[-1].start()

        at = slice(block * IMAGE_BLOCK, (block + 1) * IMAGE_BLOCK)
        inverse_parts(left, even_table, odd_table, at, quarter, send)
    wait_copies(out_copies)


def image_rows(back, even_table, odd_table):
    rows = back.shape[2]
    half, quarter = even_table.shape
    length = 2 * half
    return pl.pallas_call(
        image_kernel,
        in_specs=[IN_VMEM, IN_VMEM, IN_VMEM],
        out_specs=HBM,
        out_shape=jax.ShapeDtypeStruct((1, rows, length), jnp.float32),
        scratch_shapes=[
            pltpu.VMEM((rows, length), jnp.bfloat16),
            pltpu.VMEM((rows, length), jnp.float32),
            pltpu.SemaphoreType.DMA((length // IMAGE_BLOCK,)),
        ],
        compiler_params=pltpu.CompilerParams(vmem_limit_bytes=40 * MIB),
        cost_estimate=cost(
            2 * rows * (even_table.size + odd_table.size), 3 * half * half + 6 * rows * length
        ),
        name="image_rows",
    )(*(in_space(part, pltpu.VMEM) for part in (back, even_table, odd_table)))


def local(images, rate_vectors, epoch_times):
    _, loc_rows, length = images.shape
    epoch_count = lax.axis_size("epoch")
    devices = lax.axis_size("row") * epoch_count
    even_table, odd_table = [jnp.asarray(part) for part in packed_tables(length)]

    def exchange(values):
        return lax.all_to_all(values, ("row", "epoch"), 0, 0, tiled=True)

    spectra = exchange(row_transform(images, even_table, odd_table, devices))
    back = exchange(
        column_stage(rate_vectors, epoch_times, spectra, even_table, odd_table, epoch_count)
    )
    return image_rows(
        back.reshape(devices, length // devices, loc_rows), even_table, odd_table
    )


def solution(mesh):
    in_specs = (P(("group", "epoch"), "row", None), P(), P())
    out_specs = P(("group", "epoch"), "row", None)
    return jax.shard_map(local, mesh=mesh, in_specs=in_specs, out_specs=out_specs, check_vma=False)
```

```python
import functools
import math

import jax
import jax.numpy as jnp
import ml_dtypes
import numpy as np
from jax import lax
from jax.experimental import pallas as pl
from jax.experimental.pallas import tpu as pltpu
from jax.sharding import PartitionSpec as P

SUBPIX = 16
GROUP = 128
BLOCK = 512
IMAGE_BLOCK = 512
ROW_CHUNK = 16
PIECES = 4
MIB = 1024 * 1024
CONTRACT_LAST = (((1,), (1,)), ((), ()))
HBM = pl.BlockSpec(memory_space=pltpu.HBM)
IN_VMEM = pl.BlockSpec(memory_space=pltpu.VMEM)


def packed_freqs(index, half):
    count = half // 4
    kind = index >> (count.bit_length() - 1)
    return 4 * (index & (count - 1)) + 2 * (kind & 1) + (kind >> 1)


def packed_tables(length):
    half, quarter = length // 2, length // 4
    freqs = packed_freqs(np.arange(half, dtype=np.int32), half)
    positions = np.arange(half, dtype=np.int32)
    turns = freqs[:, None] * positions[None, :] % length
    angles = turns.astype(np.float32) * np.float32(2.0 * math.pi / length)
    factor = np.float32(1.0 / math.sqrt(length))
    cosine = np.cos(angles) * factor
    sine = np.sin(angles) * factor
    sine[0] = np.where(positions % 2 == 0, factor, -factor)
    groups = np.stack([cosine.reshape(-1, GROUP, half), sine.reshape(-1, GROUP, half)], axis=1)
    table = groups.reshape(length, half).astype(ml_dtypes.bfloat16)
    return np.ascontiguousarray(table[:half, :quarter]), table[half:]


def cost(flops, bytes_accessed):
    return pl.CostEstimate(flops=flops, bytes_accessed=bytes_accessed, transcendentals=0)


def in_space(array, space):
    return pltpu.with_memory_space_constraint(array, space)


def wait_copies(copies):
    for copy in copies:
        copy.wait()


def fold(quarters):
    first, second, third, fourth = quarters
    near, far = first + third, second + fourth
    return near + far, near - far, first - third, second - fourth


def row_kernel(
    images_hbm,
    even_hbm,
    odd_hbm,
    out_ref,
    images,
    even_table,
    odd_table,
    folded,
    image_sems,
    table_sems,
):
    loc_epochs, loc_rows, length = images.shape
    half, quarter = length // 2, length // 4
    devices, _, width, _ = out_ref.shape
    cols = width // 2
    steps = length // BLOCK
    per_step = devices // steps
    per_group = GROUP // cols
    def copies(source, target, sems, pieces):
        rows = source.shape[0] // pieces
        spans = [pl.ds(piece * rows, rows) for piece in range(pieces)]
        return [
            pltpu.make_async_copy(source.at[span], target.at[span], sems.at[piece])
            for piece, span in enumerate(spans)
        ]

    pieces = max(1, min(PIECES, loc_rows // 16))
    image_copies = [
        copies(images_hbm.at[loc], images.at[loc], image_sems.at[loc], pieces)
        for loc in range(loc_epochs)
    ]
    even_copies = copies(even_hbm, even_table, table_sems.at[0], PIECES)
    odd_copies = copies(odd_hbm.at[:, :quarter], odd_table, table_sems.at[1], 2)
    halfway = PIECES // 2
    table_copies = [even_copies[:halfway], even_copies[halfway:], odd_copies[:1], odd_copies[1:]]
    for copy in sum(image_copies, []) + even_copies + odd_copies:
        copy.start()
    for loc in range(loc_epochs):
        wait_copies(image_copies[loc])
        at = slice(loc * loc_rows, (loc + 1) * loc_rows)
        folds = fold([images[loc, :, part * quarter : (part + 1) * quarter] for part in range(4)])
        for part in range(4):
            folded[part, at] = folds[part]
    for step in range(steps):
        wait_copies(table_copies[step])
        at = slice(step % (steps // 2) * BLOCK, (step % (steps // 2) + 1) * BLOCK)
        left = (even_table if step < steps // 2 else odd_table)[at]
        sources = [step] if step < steps // 2 else [2, 3]
        terms = [
            lax.dot_general(
                left, folded[source], CONTRACT_LAST, preferred_element_type=jnp.float32
            )
            for source in sources
        ]
        for dest in range(per_step):
            start = dest // per_group * 2 * GROUP + dest % per_group * cols
            cosine, sine = [slice(first, first + cols) for first in (start, start + GROUP)]
            parts = [terms[0][cosine], terms[0][sine]]
            if step == 2:
                parts = [parts[0] - terms[1][sine], parts[1] + terms[1][cosine]]
            if step == 3:
                parts = [parts[0] + terms[1][sine], parts[1] - terms[1][cosine]]
            block = jnp.concatenate(parts, axis=0).astype(jnp.bfloat16)
            for loc in range(loc_epochs):
                out_ref[step * per_step + dest, loc] = block[:, loc * loc_rows : (loc + 1) * loc_rows]


def row_transform(images, even_table, odd_table, devices):
    loc_epochs, loc_rows, length = images.shape
    half, quarter = length // 2, length // 4
    rows = loc_epochs * loc_rows
    steps = length // BLOCK
    out = (devices, loc_epochs, length // devices, loc_rows)
    return pl.pallas_call(
        row_kernel,
        in_specs=[HBM, HBM, HBM],
        out_specs=IN_VMEM,
        out_shape=pltpu.VMEM(out, jnp.bfloat16),
        scratch_shapes=[
            pltpu.VMEM(images.shape, jnp.bfloat16),
            pltpu.VMEM(even_table.shape, jnp.bfloat16),
            pltpu.VMEM(even_table.shape, jnp.bfloat16),
            pltpu.VMEM((4, rows, quarter), jnp.bfloat16),
            pltpu.SemaphoreType.DMA((loc_epochs, PIECES)),
            pltpu.SemaphoreType.DMA((2, PIECES)),
        ],
        compiler_params=pltpu.CompilerParams(vmem_limit_bytes=32 * MIB),
        cost_estimate=cost(
            2 * rows * (even_table.size + odd_table.size), 3 * half * half + 4 * rows * length
        ),
        name="row_transform",
    )(*(in_space(part, pltpu.HBM) for part in (images, even_table, odd_table)))


def cos_sin(turns, whole):
    quarter, eighth = whole // 4, whole // 8
    shifted = (turns + eighth) & (whole - 1)
    quadrant = shifted >> (quarter.bit_length() - 1)
    angle = ((shifted & (quarter - 1)) - eighth).astype(jnp.float32) * (2.0 * math.pi / whole)
    square = angle * angle
    sine, cosine = 1.0 / 362880.0, 1.0 / 40320.0
    for divisor in (-5040.0, 120.0, -6.0, 1.0):
        sine = sine * square + 1.0 / divisor
    for divisor in (-720.0, 24.0, -2.0, 1.0):
        cosine = cosine * square + 1.0 / divisor
    sine = sine * angle
    odd = (quadrant & 1) == 1
    first, second = jnp.where(odd, sine, cosine), jnp.where(odd, cosine, sine)
    return (
        jnp.where(((quadrant + 1) & 2) == 2, -first, first),
        jnp.where(quadrant >= 2, -second, second),
    )


def spread_pairs(scalars, lanes):
    pair = lax.broadcasted_iota(jnp.int32, (len(scalars), lanes), 0)
    values = jnp.zeros((len(scalars), lanes), jnp.int32)
    for index, scalar in enumerate(scalars):
        values = jnp.where(pair == index, scalar, values)
    return values


def row_factors(shift_y, half):
    shifts = spread_pairs(shift_y, half)
    freqs = packed_freqs(lax.broadcasted_iota(jnp.int32, shifts.shape, 1), half)
    cosine, sine = cos_sin((freqs - half) * shifts, SUBPIX * 2 * half)
    return jnp.where(freqs == 0, 1.0, 2.0 * cosine), jnp.where(freqs == 0, 0.0, 2.0 * sine)


def column_factors(shift_y, shift_x, scale, device, cols, half):
    shifts_y, shifts_x = spread_pairs(shift_y, GROUP), spread_pairs(shift_x, GROUP)
    lane = lax.broadcasted_iota(jnp.int32, shifts_x.shape, 1)
    freqs = packed_freqs(device * cols + (lane & (cols - 1)), half)
    is_sine = (lane & cols) > 0
    paired = freqs == 0
    zero_col = paired & jnp.logical_not(is_sine)
    cosine, sine = cos_sin(shifts_x * (freqs - half), SUBPIX * 2 * half)
    ramp_cos = jnp.where(paired, scale, 2.0 * scale * cosine)
    ramp_sin = jnp.where(paired, 0.0, 2.0 * scale * sine)
    ramp_sin = jnp.where(is_sine, ramp_sin, -ramp_sin)
    cos_x, cos_y, cos_xy = [
        cos_sin(shifts, 2 * SUBPIX)[0] for shifts in (shifts_x, shifts_y, shifts_x + shifts_y)
    ]
    main = jnp.where(zero_col, cos_y, cos_xy)
    lead = jnp.where(zero_col, 1.0, cos_x)
    return jnp.concatenate(
        [main * ramp_cos, main * ramp_sin, lead * ramp_cos, lead * ramp_sin], axis=0
    )


def prepare_kernel(
    epoch_count,
    rate_smem,
    time_smem,
    even_hbm,
    odd_hbm,
    after,
    even_table,
    odd_table,
    rows_cos,
    rows_sin,
    spread,
    sems,
):
    del after
    even_copy = pltpu.make_async_copy(even_hbm, even_table, sems.at[0])
    odd_copy = pltpu.make_async_copy(odd_hbm, odd_table, sems.at[1])
    even_copy.start()
    odd_copy.start()
    rates, epochs = rate_smem.shape[0], time_smem.shape[0]
    pairs = rates * epochs
    width = spread.shape[2]
    cols = width // 2
    half = even_table.shape[0]
    length = 2 * half
    device = lax.axis_index("row") * epoch_count + lax.axis_index("epoch")
    period = SUBPIX * length
    shift_y, shift_x = [
        [
            rate_smem[rate, axis] * time_smem[epoch] & (period - 1)
            for rate in range(rates)
            for epoch in range(epochs)
        ]
        for axis in range(2)
    ]
    rows_cos[...], rows_sin[...] = row_factors(shift_y, half)
    factors = column_factors(shift_y, shift_x, 1.0 / math.sqrt(epochs), device, cols, half).T
    for kind in range(4):
        for pair in range(pairs):
            at = kind * pairs + pair
            spread[kind, pair] = jnp.broadcast_to(factors[:width, at : at + 1], (width, GROUP))
    even_copy.wait()
    odd_copy.wait()


def prepare(rate_vectors, epoch_times, even_table, odd_table, after, epoch_count, width):
    pairs = rate_vectors.shape[0] * epoch_times.shape[0]
    scalars = pl.BlockSpec(memory_space=pltpu.SMEM)
    half = even_table.shape[0]
    return pl.pallas_call(
        functools.partial(prepare_kernel, epoch_count),
        in_specs=[scalars, scalars, HBM, HBM, pl.BlockSpec(memory_space=pl.ANY)],
        out_specs=[IN_VMEM] * 5,
        out_shape=[
            pltpu.VMEM(even_table.shape, jnp.bfloat16),
            pltpu.VMEM(odd_table.shape, jnp.bfloat16),
            pltpu.VMEM((pairs, half), jnp.float32),
            pltpu.VMEM((pairs, half), jnp.float32),
            pltpu.VMEM((4, pairs, width, GROUP), jnp.float32),
        ],
        scratch_shapes=[pltpu.SemaphoreType.DMA((2,))],
        compiler_params=pltpu.CompilerParams(vmem_limit_bytes=24 * MIB),
        cost_estimate=cost(10 * MIB, 4 * MIB),
        name="prepare",
    )(
        rate_vectors,
        epoch_times,
        in_space(even_table, pltpu.HBM),
        in_space(odd_table, pltpu.HBM),
        after,
    )


def column_kernel(
    epoch_count,
    rates,
    received,
    even_table,
    odd_table,
    rows_cos,
    rows_sin,
    spread,
    out_ref,
    even_fold,
    odd_fold,
    products,
    sums,
):
    devices, loc_epochs, width, loc_rows = received.shape
    row_count = devices // epoch_count
    epochs = epoch_count * loc_epochs
    cols = width // 2
    half, quarter = even_table.shape
    length = 2 * half
    steps = length // BLOCK
    per_tile = max(1, GROUP // loc_rows)
    tile_rows = per_tile * loc_rows
    for tile in range(row_count // 4 // per_tile):
        at_lane = slice(tile * tile_rows, (tile + 1) * tile_rows)
        far_lane = slice(quarter + at_lane.start, quarter + at_lane.stop)
        for core in range(epoch_count):
            for loc in range(loc_epochs):
                quarters = []
                for side in range(4):
                    first = side * row_count // 4 + tile * per_tile
                    parts = [
                        received[(first + part) * epoch_count + core, loc] for part in range(per_tile)
                    ]
                    quarters.append(parts[0] if per_tile == 1 else jnp.concatenate(parts, axis=1))
                at_row = (core * loc_epochs + loc) * width
                at = slice(at_row, at_row + width)
                folds = fold(quarters)
                even_fold[0, at, at_lane], even_fold[1, at, at_lane] = folds[:2]
                odd_fold[at, at_lane], odd_fold[at, far_lane] = folds[2:]

    def multiply(step):
        at = slice(step % (steps // 2) * BLOCK, (step % (steps // 2) + 1) * BLOCK)
        if step < steps // 2:
            left, right = even_fold[4 * step // steps], even_table[at]
        else:
            left, right = odd_fold[...], odd_table[at]
        products[step % 2] = lax.dot_general(
            left, right, CONTRACT_LAST, preferred_element_type=jnp.float32
        )

    multiply(0)
    chunk = min(ROW_CHUNK, cols)

    def add_ramped(step, group):
        tile = (step * BLOCK // 2 // GROUP + group) * GROUP
        at_even = group * 2 * GROUP
        at_odd = at_even + GROUP
        for rate in range(rates):
            for start in range(0, cols, chunk):
                real = slice(start, start + chunk)
                imag = slice(cols + start, cols + start + chunk)
                totals = [[0.0, 0.0], [0.0, 0.0]]
                leads = [0.0, 0.0]
                for epoch in range(epochs):
                    pair = rate * epochs + epoch
                    cos_row = rows_cos[pair : pair + 1, tile : tile + GROUP]
                    sin_row = rows_sin[pair : pair + 1, tile : tile + GROUP]
                    turned, evens = [], []
                    for part in (real, imag):
                        at = slice(epoch * width + part.start, epoch * width + part.stop)
                        even = products[step % 2, at, at_even : at_even + GROUP]
                        odd = products[step % 2, at, at_odd : at_odd + GROUP]
                        turned.append(
                            (cos_row * even + sin_row * odd, cos_row * odd - sin_row * even)
                        )
                        evens.append(even)
                    straight = [spread[0, pair, part] for part in (real, imag)]
                    crossed = [spread[1, pair, part] for part in (real, imag)]
                    for part in range(2):
                        for which in range(2):
                            totals[part][which] += (
                                straight[part] * turned[part][which]
                                + crossed[1 - part] * turned[1 - part][which]
                            )
                        if step == 0 and group == 0:
                            own, other = (real, imag) if part == 0 else (imag, real)
                            leads[part] += (
                                spread[2, pair, own] * evens[part]
                                + spread[3, pair, other] * evens[1 - part]
                            )
                for part, rows in enumerate((real, imag)):
                    even_sum, odd_sum = totals[part]
                    if step == 0 and group == 0:
                        first = lax.broadcasted_iota(jnp.int32, even_sum.shape, 1) == 0
                        even_sum = jnp.where(first, leads[part], even_sum)
                    at = slice(rate * width + rows.start, rate * width + rows.stop)
                    sums[at, step * BLOCK + at_even : step * BLOCK + at_even + GROUP] = even_sum.astype(
                        jnp.bfloat16
                    )
                    sums[at, step * BLOCK + at_odd : step * BLOCK + at_odd + GROUP] = odd_sum.astype(
                        jnp.bfloat16
                    )

    for step in range(steps):
        if step + 1 < steps:
            multiply(step + 1)
        for group in range(BLOCK // 2 // GROUP):
            add_ramped(step, group)

    loc_rates = rates // epoch_count

    def send(side, back):
        back = back.astype(jnp.bfloat16)
        rows_here = quarter // loc_rows
        for row in range(rows_here):
            for rate in range(rates):
                dest = (side * rows_here + row) * epoch_count + rate // loc_rates
                out_ref[dest, rate % loc_rates] = back[
                    rate * width : (rate + 1) * width, row * loc_rows : (row + 1) * loc_rows
                ]

    inverse_parts(sums, even_table, odd_table, slice(0, quarter), quarter, send)


def inverse_parts(left, even_table, odd_table, at, quarter, send):
    half = 2 * quarter
    far = slice(quarter + at.start, quarter + at.stop)

    def product(first, depth, right):
        return jnp.dot(left[:, first : first + depth], right, preferred_element_type=jnp.float32)

    zero = product(0, quarter, even_table[:quarter, at])
    two = product(quarter, quarter, even_table[quarter:, at])
    for position, even, span in ((0, zero + two, at), (1, zero - two, far)):
        odd = product(half, half, odd_table[:, span])
        send(position, even + odd)
        send(position + 2, even - odd)


def column_stage(spectra, prepared, epoch_count, rates):
    devices, loc_epochs, width, loc_rows = spectra.shape
    half, quarter = prepared[0].shape
    length = 2 * half
    epochs = epoch_count * loc_epochs
    out = (devices, rates // epoch_count, width, loc_rows)
    return pl.pallas_call(
        functools.partial(column_kernel, epoch_count, rates),
        in_specs=[IN_VMEM] * 6,
        out_specs=IN_VMEM,
        out_shape=pltpu.VMEM(out, jnp.bfloat16),
        scratch_shapes=[
            pltpu.VMEM((2, epochs * width, quarter), jnp.bfloat16),
            pltpu.VMEM((epochs * width, half), jnp.bfloat16),
            pltpu.VMEM((2, epochs * width, BLOCK), jnp.float32),
            pltpu.VMEM((rates * width, length), jnp.bfloat16),
        ],
        compiler_params=pltpu.CompilerParams(vmem_limit_bytes=32 * MIB),
        cost_estimate=cost(
            3 * half * half * (epochs + rates) * width,
            3 * half * half + 4 * spectra.size,
        ),
        name="column_stage",
    )(*(in_space(part, pltpu.VMEM) for part in (spectra, *prepared)))


def image_kernel(back, even_table, odd_table, out_hbm, left, staged, out_sems):
    quarter = even_table.shape[1]
    _, width, rows = back.shape
    cols = width // 2
    per_group = GROUP // cols
    for group in range(back.shape[0] // per_group):
        members = [back[group * per_group + place] for place in range(per_group)]
        if cols % 16 != 0 or rows % 128 != 0:
            members = [member.astype(jnp.float32) for member in members]
        parts = [member[:cols] for member in members] + [member[cols:] for member in members]
        whole = jnp.concatenate(parts, axis=0)
        left[:, group * 2 * GROUP : (group + 1) * 2 * GROUP] = whole.T.astype(jnp.bfloat16)
    out_copies = []
    for block in range(quarter // IMAGE_BLOCK):

        def send(side, pixels):
            start = side * quarter + block * IMAGE_BLOCK
            at = slice(start, start + IMAGE_BLOCK)
            staged[:, at] = pixels
            out_copies.append(
                pltpu.make_async_copy(
                    staged.at[:, at], out_hbm.at[0, :, at], out_sems.at[4 * block + side]
                )
            )
            out_copies[-1].start()

        at = slice(block * IMAGE_BLOCK, (block + 1) * IMAGE_BLOCK)
        inverse_parts(left, even_table, odd_table, at, quarter, send)
    wait_copies(out_copies)


def image_rows(back, even_table, odd_table):
    rows = back.shape[2]
    half, quarter = even_table.shape
    length = 2 * half
    return pl.pallas_call(
        image_kernel,
        in_specs=[IN_VMEM, IN_VMEM, IN_VMEM],
        out_specs=HBM,
        out_shape=jax.ShapeDtypeStruct((1, rows, length), jnp.float32),
        scratch_shapes=[
            pltpu.VMEM((rows, length), jnp.bfloat16),
            pltpu.VMEM((rows, length), jnp.float32),
            pltpu.SemaphoreType.DMA((length // IMAGE_BLOCK,)),
        ],
        compiler_params=pltpu.CompilerParams(vmem_limit_bytes=32 * MIB),
        cost_estimate=cost(
            2 * rows * (even_table.size + odd_table.size), 3 * half * half + 6 * rows * length
        ),
        name="image_rows",
    )(*(in_space(part, pltpu.VMEM) for part in (back, even_table, odd_table)))


def local(images, rate_vectors, epoch_times):
    _, loc_rows, length = images.shape
    epoch_count = lax.axis_size("epoch")
    devices = lax.axis_size("row") * epoch_count
    even_table, odd_table = [jnp.asarray(part) for part in packed_tables(length)]

    def exchange(values):
        return lax.all_to_all(values, ("row", "epoch"), 0, 0, tiled=True)

    row_spectra = row_transform(images, even_table, odd_table, devices)
    prepared = prepare(
        rate_vectors,
        epoch_times,
        even_table,
        odd_table,
        row_spectra,
        epoch_count,
        length // devices,
    )
    spectra = exchange(row_spectra)
    back = exchange(column_stage(spectra, prepared, epoch_count, rate_vectors.shape[0]))
    return image_rows(back.reshape(devices, length // devices, loc_rows), *prepared[:2])


def solution(mesh):
    in_specs = (P(("group", "epoch"), "row", None), P(), P())
    out_specs = P(("group", "epoch"), "row", None)
    return jax.shard_map(local, mesh=mesh, in_specs=in_specs, out_specs=out_specs, check_vma=False)
```

```python
import functools
import math

import jax
import jax.numpy as jnp
import ml_dtypes
import numpy as np
from jax import lax
from jax.experimental import pallas as pl
from jax.experimental.pallas import tpu as pltpu
from jax.sharding import PartitionSpec as P

SUBPIX = 16
GROUP = 128
BLOCK = 512
IMAGE_BLOCK = 512
ROW_CHUNK = 16
PIECES = 4
MIB = 1024 * 1024
CONTRACT_LAST = (((1,), (1,)), ((), ()))
HBM = pl.BlockSpec(memory_space=pltpu.HBM)
IN_VMEM = pl.BlockSpec(memory_space=pltpu.VMEM)


def packed_freqs(index, half):
    count = half // 4
    kind = index >> (count.bit_length() - 1)
    return 4 * (index & (count - 1)) + 2 * (kind & 1) + (kind >> 1)


def packed_tables(length):
    half, quarter = length // 2, length // 4
    freqs = packed_freqs(np.arange(half, dtype=np.int32), half)
    positions = np.arange(half, dtype=np.int32)
    turns = freqs[:, None] * positions[None, :] % length
    angles = turns.astype(np.float32) * np.float32(2.0 * math.pi / length)
    factor = np.float32(1.0 / math.sqrt(length))
    cosine = np.cos(angles) * factor
    sine = np.sin(angles) * factor
    sine[0] = np.where(positions % 2 == 0, factor, -factor)
    groups = np.stack([cosine.reshape(-1, GROUP, half), sine.reshape(-1, GROUP, half)], axis=1)
    table = groups.reshape(length, half).astype(ml_dtypes.bfloat16)
    return np.ascontiguousarray(table[:half, :quarter]), table[half:]


def cost(flops, bytes_accessed):
    return pl.CostEstimate(flops=flops, bytes_accessed=bytes_accessed, transcendentals=0)


def in_space(array, space):
    return pltpu.with_memory_space_constraint(array, space)


def wait_copies(copies):
    for copy in copies:
        copy.wait()


def fold(quarters):
    first, second, third, fourth = quarters
    near, far = first + third, second + fourth
    return near + far, near - far, first - third, second - fourth


def row_kernel(
    images_hbm,
    even_hbm,
    odd_hbm,
    out_ref,
    images,
    even_table,
    odd_table,
    folded,
    image_sems,
    table_sems,
):
    loc_epochs, loc_rows, length = images.shape
    half, quarter = length // 2, length // 4
    devices, _, width, _ = out_ref.shape
    cols = width // 2
    steps = length // BLOCK
    per_step = devices // steps
    per_group = GROUP // cols
    def copies(source, target, sems, pieces):
        rows = source.shape[0] // pieces
        spans = [pl.ds(piece * rows, rows) for piece in range(pieces)]
        return [
            pltpu.make_async_copy(source.at[span], target.at[span], sems.at[piece])
            for piece, span in enumerate(spans)
        ]

    pieces = max(1, min(PIECES, loc_rows // 16))
    image_copies = [
        copies(images_hbm.at[loc], images.at[loc], image_sems.at[loc], pieces)
        for loc in range(loc_epochs)
    ]
    even_copies = copies(even_hbm, even_table, table_sems.at[0], PIECES)
    odd_copies = copies(odd_hbm.at[:, :quarter], odd_table, table_sems.at[1], 2)
    halfway = PIECES // 2
    table_copies = [even_copies[:halfway], even_copies[halfway:], odd_copies[:1], odd_copies[1:]]
    for copy in sum(image_copies, []) + even_copies:
        copy.start()
    for loc in range(loc_epochs):
        wait_copies(image_copies[loc])
        if loc == loc_epochs - 1:
            for copy in odd_copies:
                copy.start()
        at = slice(loc * loc_rows, (loc + 1) * loc_rows)
        folds = fold([images[loc, :, part * quarter : (part + 1) * quarter] for part in range(4)])
        for part in range(4):
            folded[part, at] = folds[part]
    for step in range(steps):
        wait_copies(table_copies[step])
        at = slice(step % (steps // 2) * BLOCK, (step % (steps // 2) + 1) * BLOCK)
        left = (even_table if step < steps // 2 else odd_table)[at]
        sources = [step] if step < steps // 2 else [2, 3]
        terms = [
            lax.dot_general(
                left, folded[source], CONTRACT_LAST, preferred_element_type=jnp.float32
            )
            for source in sources
        ]
        for dest in range(per_step):
            start = dest // per_group * 2 * GROUP + dest % per_group * cols
            cosine, sine = [slice(first, first + cols) for first in (start, start + GROUP)]
            parts = [terms[0][cosine], terms[0][sine]]
            if step == 2:
                parts = [parts[0] - terms[1][sine], parts[1] + terms[1][cosine]]
            if step == 3:
                parts = [parts[0] + terms[1][sine], parts[1] - terms[1][cosine]]
            block = jnp.concatenate(parts, axis=0).astype(jnp.bfloat16)
            for loc in range(loc_epochs):
                out_ref[step * per_step + dest, loc] = block[:, loc * loc_rows : (loc + 1) * loc_rows]


def row_transform(images, even_table, odd_table, devices):
    loc_epochs, loc_rows, length = images.shape
    half, quarter = length // 2, length // 4
    rows = loc_epochs * loc_rows
    steps = length // BLOCK
    out = (devices, loc_epochs, length // devices, loc_rows)
    return pl.pallas_call(
        row_kernel,
        in_specs=[HBM, HBM, HBM],
        out_specs=IN_VMEM,
        out_shape=pltpu.VMEM(out, jnp.bfloat16),
        scratch_shapes=[
            pltpu.VMEM(images.shape, jnp.bfloat16),
            pltpu.VMEM(even_table.shape, jnp.bfloat16),
            pltpu.VMEM(even_table.shape, jnp.bfloat16),
            pltpu.VMEM((4, rows, quarter), jnp.bfloat16),
            pltpu.SemaphoreType.DMA((loc_epochs, PIECES)),
            pltpu.SemaphoreType.DMA((2, PIECES)),
        ],
        compiler_params=pltpu.CompilerParams(vmem_limit_bytes=40 * MIB),
        cost_estimate=cost(
            2 * rows * (even_table.size + odd_table.size), 3 * half * half + 4 * rows * length
        ),
        name="row_transform",
    )(*(in_space(part, pltpu.HBM) for part in (images, even_table, odd_table)))


def cos_sin(turns, whole):
    quarter, eighth = whole // 4, whole // 8
    shifted = (turns + eighth) & (whole - 1)
    quadrant = shifted >> (quarter.bit_length() - 1)
    angle = ((shifted & (quarter - 1)) - eighth).astype(jnp.float32) * (2.0 * math.pi / whole)
    square = angle * angle
    sine, cosine = 1.0 / 362880.0, 1.0 / 40320.0
    for divisor in (-5040.0, 120.0, -6.0, 1.0):
        sine = sine * square + 1.0 / divisor
    for divisor in (-720.0, 24.0, -2.0, 1.0):
        cosine = cosine * square + 1.0 / divisor
    sine = sine * angle
    odd = (quadrant & 1) == 1
    first, second = jnp.where(odd, sine, cosine), jnp.where(odd, cosine, sine)
    return (
        jnp.where(((quadrant + 1) & 2) == 2, -first, first),
        jnp.where(quadrant >= 2, -second, second),
    )


def spread_pairs(scalars, lanes):
    pair = lax.broadcasted_iota(jnp.int32, (len(scalars), lanes), 0)
    values = jnp.zeros((len(scalars), lanes), jnp.int32)
    for index, scalar in enumerate(scalars):
        values = jnp.where(pair == index, scalar, values)
    return values


def row_factors(shift_y, half):
    shifts = spread_pairs(shift_y, half)
    freqs = packed_freqs(lax.broadcasted_iota(jnp.int32, shifts.shape, 1), half)
    cosine, sine = cos_sin((freqs - half) * shifts, SUBPIX * 2 * half)
    return jnp.where(freqs == 0, 1.0, 2.0 * cosine), jnp.where(freqs == 0, 0.0, 2.0 * sine)


def column_factors(shift_y, shift_x, scale, device, cols, half):
    shifts_y, shifts_x = spread_pairs(shift_y, GROUP), spread_pairs(shift_x, GROUP)
    lane = lax.broadcasted_iota(jnp.int32, shifts_x.shape, 1)
    freqs = packed_freqs(device * cols + (lane & (cols - 1)), half)
    is_sine = (lane & cols) > 0
    paired = freqs == 0
    zero_col = paired & jnp.logical_not(is_sine)
    cosine, sine = cos_sin(shifts_x * (freqs - half), SUBPIX * 2 * half)
    ramp_cos = jnp.where(paired, scale, 2.0 * scale * cosine)
    ramp_sin = jnp.where(paired, 0.0, 2.0 * scale * sine)
    ramp_sin = jnp.where(is_sine, ramp_sin, -ramp_sin)
    cos_x, cos_y, cos_xy = [
        cos_sin(shifts, 2 * SUBPIX)[0] for shifts in (shifts_x, shifts_y, shifts_x + shifts_y)
    ]
    main = jnp.where(zero_col, cos_y, cos_xy)
    lead = jnp.where(zero_col, 1.0, cos_x)
    return jnp.concatenate(
        [main * ramp_cos, main * ramp_sin, lead * ramp_cos, lead * ramp_sin], axis=0
    )


def column_kernel(
    epoch_count,
    rate_smem,
    time_smem,
    received,
    even_table,
    odd_table,
    out_ref,
    rows_cos,
    rows_sin,
    spread,
    even_fold,
    odd_fold,
    products,
    sums,
):
    devices, loc_epochs, width, loc_rows = received.shape
    row_count = devices // epoch_count
    epochs = epoch_count * loc_epochs
    rates = rate_smem.shape[0]
    pairs = rates * epochs
    cols = width // 2
    half, quarter = even_table.shape
    length = 2 * half
    steps = length // BLOCK
    device = lax.axis_index("row") * epoch_count + lax.axis_index("epoch")
    period = SUBPIX * length
    shift_y, shift_x = [
        [
            rate_smem[rate, axis] * time_smem[epoch] & (period - 1)
            for rate in range(rates)
            for epoch in range(epochs)
        ]
        for axis in range(2)
    ]
    per_tile = max(1, GROUP // loc_rows)
    tile_rows = per_tile * loc_rows
    for tile in range(row_count // 4 // per_tile):
        at_lane = slice(tile * tile_rows, (tile + 1) * tile_rows)
        far_lane = slice(quarter + at_lane.start, quarter + at_lane.stop)
        for core in range(epoch_count):
            for loc in range(loc_epochs):
                quarters = []
                for side in range(4):
                    first = side * row_count // 4 + tile * per_tile
                    parts = [
                        received[(first + part) * epoch_count + core, loc] for part in range(per_tile)
                    ]
                    quarters.append(parts[0] if per_tile == 1 else jnp.concatenate(parts, axis=1))
                at_row = (core * loc_epochs + loc) * width
                at = slice(at_row, at_row + width)
                folds = fold(quarters)
                even_fold[0, at, at_lane], even_fold[1, at, at_lane] = folds[:2]
                odd_fold[at, at_lane], odd_fold[at, far_lane] = folds[2:]

    def multiply(step):
        at = slice(step % (steps // 2) * BLOCK, (step % (steps // 2) + 1) * BLOCK)
        if step < steps // 2:
            left, right = even_fold[4 * step // steps], even_table[at]
        else:
            left, right = odd_fold[...], odd_table[at]
        products[step % 2] = lax.dot_general(
            left, right, CONTRACT_LAST, preferred_element_type=jnp.float32
        )

    multiply(0)
    rows_cos[...], rows_sin[...] = row_factors(shift_y, half)
    factors = column_factors(shift_y, shift_x, 1.0 / math.sqrt(epochs), device, cols, half).T
    for kind in range(4):
        for pair in range(pairs):
            at = kind * pairs + pair
            spread[kind, pair] = jnp.broadcast_to(factors[:width, at : at + 1], (width, GROUP))

    chunk = min(ROW_CHUNK, cols)

    def add_ramped(step, group):
        tile = (step * BLOCK // 2 // GROUP + group) * GROUP
        at_even = group * 2 * GROUP
        at_odd = at_even + GROUP
        for start in range(0, cols, chunk):
            real = slice(start, start + chunk)
            imag = slice(cols + start, cols + start + chunk)
            totals = [[[0.0, 0.0], [0.0, 0.0]] for _ in range(rates)]
            leads = [[0.0, 0.0] for _ in range(rates)]
            for epoch in range(epochs):
                loaded = []
                for part in (real, imag):
                    at = slice(epoch * width + part.start, epoch * width + part.stop)
                    loaded.append(
                        [
                            products[step % 2, at, first : first + GROUP]
                            for first in (at_even, at_odd)
                        ]
                    )
                for rate in range(rates):
                    pair = rate * epochs + epoch
                    cos_row = rows_cos[pair : pair + 1, tile : tile + GROUP]
                    sin_row = rows_sin[pair : pair + 1, tile : tile + GROUP]
                    turned = [
                        (cos_row * even + sin_row * odd, cos_row * odd - sin_row * even)
                        for even, odd in loaded
                    ]
                    straight = [spread[0, pair, part] for part in (real, imag)]
                    crossed = [spread[1, pair, part] for part in (real, imag)]
                    for part in range(2):
                        for which in range(2):
                            totals[rate][part][which] += (
                                straight[part] * turned[part][which]
                                + crossed[1 - part] * turned[1 - part][which]
                            )
                        if step == 0 and group == 0:
                            own, other = (real, imag) if part == 0 else (imag, real)
                            leads[rate][part] += (
                                spread[2, pair, own] * loaded[part][0]
                                + spread[3, pair, other] * loaded[1 - part][0]
                            )
            for rate in range(rates):
                for part, rows in enumerate((real, imag)):
                    even_sum, odd_sum = totals[rate][part]
                    if step == 0 and group == 0:
                        first = lax.broadcasted_iota(jnp.int32, even_sum.shape, 1) == 0
                        even_sum = jnp.where(first, leads[rate][part], even_sum)
                    at = slice(rate * width + rows.start, rate * width + rows.stop)
                    for values, lane in ((even_sum, at_even), (odd_sum, at_odd)):
                        lane = step * BLOCK + lane
                        sums[at, lane : lane + GROUP] = values.astype(jnp.bfloat16)

    for step in range(steps):
        if step + 1 < steps:
            multiply(step + 1)
        for group in range(BLOCK // 2 // GROUP):
            add_ramped(step, group)

    loc_rates = rates // epoch_count

    def send(side, back):
        back = back.astype(jnp.bfloat16)
        rows_here = quarter // loc_rows
        for row in range(rows_here):
            for rate in range(rates):
                dest = (side * rows_here + row) * epoch_count + rate // loc_rates
                out_ref[dest, rate % loc_rates] = back[
                    rate * width : (rate + 1) * width, row * loc_rows : (row + 1) * loc_rows
                ]

    inverse_parts(sums, even_table, odd_table, slice(0, quarter), quarter, send)


def inverse_parts(left, even_table, odd_table, at, quarter, send):
    half = 2 * quarter
    far = slice(quarter + at.start, quarter + at.stop)

    def product(first, depth, right):
        return jnp.dot(left[:, first : first + depth], right, preferred_element_type=jnp.float32)

    zero = product(0, quarter, even_table[:quarter, at])
    two = product(quarter, quarter, even_table[quarter:, at])
    for position, even, span in ((0, zero + two, at), (1, zero - two, far)):
        odd = product(half, half, odd_table[:, span])
        send(position, even + odd)
        send(position + 2, even - odd)


def column_stage(rate_vectors, epoch_times, spectra, even_table, odd_table, epoch_count):
    devices, loc_epochs, width, loc_rows = spectra.shape
    half, quarter = even_table.shape
    length = 2 * half
    epochs, rates = epoch_times.shape[0], rate_vectors.shape[0]
    out = (devices, rates // epoch_count, width, loc_rows)
    scalars = pl.BlockSpec(memory_space=pltpu.SMEM)
    return pl.pallas_call(
        functools.partial(column_kernel, epoch_count),
        in_specs=[scalars, scalars, IN_VMEM, IN_VMEM, IN_VMEM],
        out_specs=IN_VMEM,
        out_shape=pltpu.VMEM(out, jnp.bfloat16),
        scratch_shapes=[
            pltpu.VMEM((rates * epochs, half), jnp.float32),
            pltpu.VMEM((rates * epochs, half), jnp.float32),
            pltpu.VMEM((4, rates * epochs, width, GROUP), jnp.float32),
            pltpu.VMEM((2, epochs * width, quarter), jnp.bfloat16),
            pltpu.VMEM((epochs * width, half), jnp.bfloat16),
            pltpu.VMEM((2, epochs * width, BLOCK), jnp.float32),
            pltpu.VMEM((rates * width, length), jnp.bfloat16),
        ],
        compiler_params=pltpu.CompilerParams(vmem_limit_bytes=40 * MIB),
        cost_estimate=cost(
            2 * (even_table.size + odd_table.size) * (epochs + rates) * width,
            3 * half * half + 4 * spectra.size,
        ),
        name="column_stage",
    )(
        rate_vectors,
        epoch_times,
        *(in_space(part, pltpu.VMEM) for part in (spectra, even_table, odd_table)),
    )


def image_kernel(back, even_table, odd_table, out_hbm, left, staged, out_sems):
    quarter = even_table.shape[1]
    _, width, rows = back.shape
    cols = width // 2
    per_group = GROUP // cols
    for group in range(back.shape[0] // per_group):
        members = [back[group * per_group + place] for place in range(per_group)]
        if cols % 16 != 0 or rows % 128 != 0:
            members = [member.astype(jnp.float32) for member in members]
        parts = [member[:cols] for member in members] + [member[cols:] for member in members]
        whole = jnp.concatenate(parts, axis=0)
        left[:, group * 2 * GROUP : (group + 1) * 2 * GROUP] = whole.T.astype(jnp.bfloat16)
    out_copies = []
    for block in range(quarter // IMAGE_BLOCK):

        def send(side, pixels):
            start = side * quarter + block * IMAGE_BLOCK
            at = slice(start, start + IMAGE_BLOCK)
            staged[:, at] = pixels
            out_copies.append(
                pltpu.make_async_copy(
                    staged.at[:, at], out_hbm.at[0, :, at], out_sems.at[4 * block + side]
                )
            )
            out_copies[-1].start()

        at = slice(block * IMAGE_BLOCK, (block + 1) * IMAGE_BLOCK)
        inverse_parts(left, even_table, odd_table, at, quarter, send)
    wait_copies(out_copies)


def image_rows(back, even_table, odd_table):
    rows = back.shape[2]
    half, quarter = even_table.shape
    length = 2 * half
    return pl.pallas_call(
        image_kernel,
        in_specs=[IN_VMEM, IN_VMEM, IN_VMEM],
        out_specs=HBM,
        out_shape=jax.ShapeDtypeStruct((1, rows, length), jnp.float32),
        scratch_shapes=[
            pltpu.VMEM((rows, length), jnp.bfloat16),
            pltpu.VMEM((rows, length), jnp.float32),
            pltpu.SemaphoreType.DMA((length // IMAGE_BLOCK,)),
        ],
        compiler_params=pltpu.CompilerParams(vmem_limit_bytes=40 * MIB),
        cost_estimate=cost(
            2 * rows * (even_table.size + odd_table.size), 3 * half * half + 6 * rows * length
        ),
        name="image_rows",
    )(*(in_space(part, pltpu.VMEM) for part in (back, even_table, odd_table)))


def local(images, rate_vectors, epoch_times):
    _, loc_rows, length = images.shape
    epoch_count = lax.axis_size("epoch")
    devices = lax.axis_size("row") * epoch_count
    even_table, odd_table = [jnp.asarray(part) for part in packed_tables(length)]

    def exchange(values):
        return lax.all_to_all(values, ("row", "epoch"), 0, 0, tiled=True)

    spectra = exchange(row_transform(images, even_table, odd_table, devices))
    back = exchange(
        column_stage(rate_vectors, epoch_times, spectra, even_table, odd_table, epoch_count)
    )
    return image_rows(
        back.reshape(devices, length // devices, loc_rows), even_table, odd_table
    )


def solution(mesh):
    in_specs = (P(("group", "epoch"), "row", None), P(), P())
    out_specs = P(("group", "epoch"), "row", None)
    return jax.shard_map(local, mesh=mesh, in_specs=in_specs, out_specs=out_specs, check_vma=False)
```

```python
import functools
import math

import jax
import jax.numpy as jnp
import ml_dtypes
import numpy as np
from jax import lax
from jax.experimental import pallas as pl
from jax.experimental.pallas import tpu as pltpu
from jax.sharding import PartitionSpec as P

SUBPIX = 16
GROUP = 128
BLOCK = 512
IMAGE_BLOCK = 512
ROW_CHUNK = 32
PIECES = 4
MIB = 1024 * 1024
CONTRACT_LAST = (((1,), (1,)), ((), ()))
HBM = pl.BlockSpec(memory_space=pltpu.HBM)
IN_VMEM = pl.BlockSpec(memory_space=pltpu.VMEM)


def packed_freqs(index, half):
    count = half // 4
    kind = index >> (count.bit_length() - 1)
    return 4 * (index & (count - 1)) + 2 * (kind & 1) + (kind >> 1)


def packed_tables(length):
    half, quarter = length // 2, length // 4
    freqs = packed_freqs(np.arange(half, dtype=np.int32), half)
    positions = np.arange(half, dtype=np.int32)
    turns = freqs[:, None] * positions[None, :] % length
    angles = turns.astype(np.float32) * np.float32(2.0 * math.pi / length)
    factor = np.float32(1.0 / math.sqrt(length))
    cosine = np.cos(angles) * factor
    sine = np.sin(angles) * factor
    sine[0] = np.where(positions % 2 == 0, factor, -factor)
    groups = np.stack([cosine.reshape(-1, GROUP, half), sine.reshape(-1, GROUP, half)], axis=1)
    table = groups.reshape(length, half).astype(ml_dtypes.bfloat16)
    return np.ascontiguousarray(table[:half, :quarter]), table[half:]


def cost(flops, bytes_accessed):
    return pl.CostEstimate(flops=flops, bytes_accessed=bytes_accessed, transcendentals=0)


def in_space(array, space):
    return pltpu.with_memory_space_constraint(array, space)


def wait_copies(copies):
    for copy in copies:
        copy.wait()


def fold(quarters):
    first, second, third, fourth = quarters
    near, far = first + third, second + fourth
    return near + far, near - far, first - third, second - fourth


def row_kernel(
    images_hbm,
    even_hbm,
    odd_hbm,
    out_ref,
    images,
    even_table,
    odd_table,
    folded,
    image_sems,
    table_sems,
):
    loc_epochs, loc_rows, length = images.shape
    half, quarter = length // 2, length // 4
    devices, _, width, _ = out_ref.shape
    cols = width // 2
    steps = length // BLOCK
    per_step = devices // steps
    per_group = GROUP // cols
    def copies(source, target, sems, pieces):
        rows = source.shape[0] // pieces
        spans = [pl.ds(piece * rows, rows) for piece in range(pieces)]
        return [
            pltpu.make_async_copy(source.at[span], target.at[span], sems.at[piece])
            for piece, span in enumerate(spans)
        ]

    pieces = max(1, min(PIECES, loc_rows // 16))
    image_copies = [
        copies(images_hbm.at[loc], images.at[loc], image_sems.at[loc], pieces)
        for loc in range(loc_epochs)
    ]
    even_copies = copies(even_hbm, even_table, table_sems.at[0], PIECES)
    odd_copies = copies(odd_hbm.at[:, :quarter], odd_table, table_sems.at[1], 2)
    halfway = PIECES // 2
    table_copies = [even_copies[:halfway], even_copies[halfway:], odd_copies[:1], odd_copies[1:]]
    for copy in sum(image_copies, []) + table_copies[0]:
        copy.start()
    for loc in range(loc_epochs):
        wait_copies(image_copies[loc])
        if loc == 0:
            for copy in sum(table_copies[1:], []):
                copy.start()
        at = slice(loc * loc_rows, (loc + 1) * loc_rows)
        folds = fold([images[loc, :, part * quarter : (part + 1) * quarter] for part in range(4)])
        for part in range(4):
            folded[part, at] = folds[part]
    for step in range(steps):
        wait_copies(table_copies[step])
        at = slice(step % (steps // 2) * BLOCK, (step % (steps // 2) + 1) * BLOCK)
        left = (even_table if step < steps // 2 else odd_table)[at]
        sources = [step] if step < steps // 2 else [2, 3]
        terms = [
            lax.dot_general(
                left, folded[source], CONTRACT_LAST, preferred_element_type=jnp.float32
            )
            for source in sources
        ]
        for dest in range(per_step):
            start = dest // per_group * 2 * GROUP + dest % per_group * cols
            cosine, sine = [slice(first, first + cols) for first in (start, start + GROUP)]
            parts = [terms[0][cosine], terms[0][sine]]
            if step == 2:
                parts = [parts[0] - terms[1][sine], parts[1] + terms[1][cosine]]
            if step == 3:
                parts = [parts[0] + terms[1][sine], parts[1] - terms[1][cosine]]
            block = jnp.concatenate(parts, axis=0).astype(jnp.bfloat16)
            for loc in range(loc_epochs):
                out_ref[step * per_step + dest, loc] = block[:, loc * loc_rows : (loc + 1) * loc_rows]


def row_transform(images, even_table, odd_table, devices):
    loc_epochs, loc_rows, length = images.shape
    half, quarter = length // 2, length // 4
    rows = loc_epochs * loc_rows
    steps = length // BLOCK
    out = (devices, loc_epochs, length // devices, loc_rows)
    return pl.pallas_call(
        row_kernel,
        in_specs=[HBM, HBM, HBM],
        out_specs=IN_VMEM,
        out_shape=pltpu.VMEM(out, jnp.bfloat16),
        scratch_shapes=[
            pltpu.VMEM(images.shape, jnp.bfloat16),
            pltpu.VMEM(even_table.shape, jnp.bfloat16),
            pltpu.VMEM(even_table.shape, jnp.bfloat16),
            pltpu.VMEM((4, rows, quarter), jnp.bfloat16),
            pltpu.SemaphoreType.DMA((loc_epochs, PIECES)),
            pltpu.SemaphoreType.DMA((2, PIECES)),
        ],
        compiler_params=pltpu.CompilerParams(vmem_limit_bytes=40 * MIB),
        cost_estimate=cost(
            2 * rows * (even_table.size + odd_table.size), 3 * half * half + 4 * rows * length
        ),
        name="row_transform",
    )(*(in_space(part, pltpu.HBM) for part in (images, even_table, odd_table)))


def cos_sin(turns, whole):
    quarter, eighth = whole // 4, whole // 8
    shifted = (turns + eighth) & (whole - 1)
    quadrant = shifted >> (quarter.bit_length() - 1)
    angle = ((shifted & (quarter - 1)) - eighth).astype(jnp.float32) * (2.0 * math.pi / whole)
    square = angle * angle
    sine, cosine = 1.0 / 362880.0, 1.0 / 40320.0
    for divisor in (-5040.0, 120.0, -6.0, 1.0):
        sine = sine * square + 1.0 / divisor
    for divisor in (-720.0, 24.0, -2.0, 1.0):
        cosine = cosine * square + 1.0 / divisor
    sine = sine * angle
    odd = (quadrant & 1) == 1
    first, second = jnp.where(odd, sine, cosine), jnp.where(odd, cosine, sine)
    return (
        jnp.where(((quadrant + 1) & 2) == 2, -first, first),
        jnp.where(quadrant >= 2, -second, second),
    )


def spread_pairs(scalars, lanes):
    pair = lax.broadcasted_iota(jnp.int32, (len(scalars), lanes), 0)
    values = jnp.zeros((len(scalars), lanes), jnp.int32)
    for index, scalar in enumerate(scalars):
        values = jnp.where(pair == index, scalar, values)
    return values


def row_factors(shift_y, half):
    shifts = spread_pairs(shift_y, half)
    freqs = packed_freqs(lax.broadcasted_iota(jnp.int32, shifts.shape, 1), half)
    cosine, sine = cos_sin((freqs - half) * shifts, SUBPIX * 2 * half)
    return jnp.where(freqs == 0, 1.0, 2.0 * cosine), jnp.where(freqs == 0, 0.0, 2.0 * sine)


def column_factors(shift_y, shift_x, scale, device, cols, half):
    shifts_y, shifts_x = spread_pairs(shift_y, GROUP), spread_pairs(shift_x, GROUP)
    lane = lax.broadcasted_iota(jnp.int32, shifts_x.shape, 1)
    freqs = packed_freqs(device * cols + (lane & (cols - 1)), half)
    is_sine = (lane & cols) > 0
    paired = freqs == 0
    zero_col = paired & jnp.logical_not(is_sine)
    cosine, sine = cos_sin(shifts_x * (freqs - half), SUBPIX * 2 * half)
    ramp_cos = jnp.where(paired, scale, 2.0 * scale * cosine)
    ramp_sin = jnp.where(paired, 0.0, 2.0 * scale * sine)
    ramp_sin = jnp.where(is_sine, ramp_sin, -ramp_sin)
    cos_x, cos_y, cos_xy = [
        cos_sin(shifts, 2 * SUBPIX)[0] for shifts in (shifts_x, shifts_y, shifts_x + shifts_y)
    ]
    main = jnp.where(zero_col, cos_y, cos_xy)
    lead = jnp.where(zero_col, 1.0, cos_x)
    return jnp.concatenate(
        [main * ramp_cos, main * ramp_sin, lead * ramp_cos, lead * ramp_sin], axis=0
    )


def column_kernel(
    epoch_count,
    rate_smem,
    time_smem,
    received,
    even_table,
    odd_table,
    out_ref,
    rows_cos,
    rows_sin,
    spread,
    even_fold,
    odd_fold,
    products,
    sums,
):
    devices, loc_epochs, width, loc_rows = received.shape
    row_count = devices // epoch_count
    epochs = epoch_count * loc_epochs
    rates = rate_smem.shape[0]
    pairs = rates * epochs
    cols = width // 2
    half, quarter = even_table.shape
    length = 2 * half
    steps = length // BLOCK
    device = lax.axis_index("row") * epoch_count + lax.axis_index("epoch")
    period = SUBPIX * length
    shift_y, shift_x = [
        [
            rate_smem[rate, axis] * time_smem[epoch] & (period - 1)
            for rate in range(rates)
            for epoch in range(epochs)
        ]
        for axis in range(2)
    ]
    per_tile = max(1, GROUP // loc_rows)
    tile_rows = per_tile * loc_rows
    for tile in range(row_count // 4 // per_tile):
        at_lane = slice(tile * tile_rows, (tile + 1) * tile_rows)
        far_lane = slice(quarter + at_lane.start, quarter + at_lane.stop)
        for core in range(epoch_count):
            for loc in range(loc_epochs):
                quarters = []
                for side in range(4):
                    first = side * row_count // 4 + tile * per_tile
                    parts = [
                        received[(first + part) * epoch_count + core, loc] for part in range(per_tile)
                    ]
                    quarters.append(parts[0] if per_tile == 1 else jnp.concatenate(parts, axis=1))
                at_row = (core * loc_epochs + loc) * width
                at = slice(at_row, at_row + width)
                folds = fold(quarters)
                even_fold[0, at, at_lane], even_fold[1, at, at_lane] = folds[:2]
                odd_fold[at, at_lane], odd_fold[at, far_lane] = folds[2:]

    def multiply(step):
        at = slice(step % (steps // 2) * BLOCK, (step % (steps // 2) + 1) * BLOCK)
        if step < steps // 2:
            left, right = even_fold[4 * step // steps], even_table[at]
        else:
            left, right = odd_fold[...], odd_table[at]
        products[step % 2] = lax.dot_general(
            left, right, CONTRACT_LAST, preferred_element_type=jnp.float32
        )

    multiply(0)
    rows_cos[...], rows_sin[...] = row_factors(shift_y, half)
    factors = column_factors(shift_y, shift_x, 1.0 / math.sqrt(epochs), device, cols, half).T
    for kind in range(4):
        for pair in range(pairs):
            at = kind * pairs + pair
            spread[kind, pair] = jnp.broadcast_to(factors[:width, at : at + 1], (width, GROUP))

    chunk = min(ROW_CHUNK, cols)

    def add_ramped(step, group):
        tile = (step * BLOCK // 2 // GROUP + group) * GROUP
        at_even = group * 2 * GROUP
        at_odd = at_even + GROUP
        for start in range(0, cols, chunk):
            real = slice(start, start + chunk)
            imag = slice(cols + start, cols + start + chunk)
            totals = [[[0.0, 0.0], [0.0, 0.0]] for _ in range(rates)]
            leads = [[0.0, 0.0] for _ in range(rates)]
            for epoch in range(epochs):
                loaded = []
                for part in (real, imag):
                    at = slice(epoch * width + part.start, epoch * width + part.stop)
                    loaded.append(
                        [
                            products[step % 2, at, first : first + GROUP]
                            for first in (at_even, at_odd)
                        ]
                    )
                for rate in range(rates):
                    pair = rate * epochs + epoch
                    cos_row = rows_cos[pair : pair + 1, tile : tile + GROUP]
                    sin_row = rows_sin[pair : pair + 1, tile : tile + GROUP]
                    turned = [
                        (cos_row * even + sin_row * odd, cos_row * odd - sin_row * even)
                        for even, odd in loaded
                    ]
                    straight = [spread[0, pair, part] for part in (real, imag)]
                    crossed = [spread[1, pair, part] for part in (real, imag)]
                    for part in range(2):
                        for which in range(2):
                            totals[rate][part][which] += (
                                straight[part] * turned[part][which]
                                + crossed[1 - part] * turned[1 - part][which]
                            )
                        if step == 0 and group == 0:
                            own, other = (real, imag) if part == 0 else (imag, real)
                            leads[rate][part] += (
                                spread[2, pair, own] * loaded[part][0]
                                + spread[3, pair, other] * loaded[1 - part][0]
                            )
            for rate in range(rates):
                for part, rows in enumerate((real, imag)):
                    even_sum, odd_sum = totals[rate][part]
                    if step == 0 and group == 0:
                        first = lax.broadcasted_iota(jnp.int32, even_sum.shape, 1) == 0
                        even_sum = jnp.where(first, leads[rate][part], even_sum)
                    at = slice(rate * width + rows.start, rate * width + rows.stop)
                    for values, lane in ((even_sum, at_even), (odd_sum, at_odd)):
                        lane = step * BLOCK + lane
                        sums[at, lane : lane + GROUP] = values.astype(jnp.bfloat16)

    for step in range(steps):
        if step + 1 < steps:
            multiply(step + 1)
        for group in range(BLOCK // 2 // GROUP):
            add_ramped(step, group)

    loc_rates = rates // epoch_count

    def send(side, back):
        back = back.astype(jnp.bfloat16)
        rows_here = quarter // loc_rows
        for row in range(rows_here):
            for rate in range(rates):
                dest = (side * rows_here + row) * epoch_count + rate // loc_rates
                out_ref[dest, rate % loc_rates] = back[
                    rate * width : (rate + 1) * width, row * loc_rows : (row + 1) * loc_rows
                ]

    inverse_parts(sums, even_table, odd_table, slice(0, quarter), quarter, send)


def inverse_parts(left, even_table, odd_table, at, quarter, send):
    half = 2 * quarter
    far = slice(quarter + at.start, quarter + at.stop)

    def product(first, depth, right):
        return jnp.dot(left[:, first : first + depth], right, preferred_element_type=jnp.float32)

    zero = product(0, quarter, even_table[:quarter, at])
    two = product(quarter, quarter, even_table[quarter:, at])
    for position, even, span in ((0, zero + two, at), (1, zero - two, far)):
        odd = product(half, half, odd_table[:, span])
        send(position, even + odd)
        send(position + 2, even - odd)


def column_stage(rate_vectors, epoch_times, spectra, even_table, odd_table, epoch_count):
    devices, loc_epochs, width, loc_rows = spectra.shape
    half, quarter = even_table.shape
    length = 2 * half
    epochs, rates = epoch_times.shape[0], rate_vectors.shape[0]
    out = (devices, rates // epoch_count, width, loc_rows)
    scalars = pl.BlockSpec(memory_space=pltpu.SMEM)
    return pl.pallas_call(
        functools.partial(column_kernel, epoch_count),
        in_specs=[scalars, scalars, IN_VMEM, IN_VMEM, IN_VMEM],
        out_specs=IN_VMEM,
        out_shape=pltpu.VMEM(out, jnp.bfloat16),
        scratch_shapes=[
            pltpu.VMEM((rates * epochs, half), jnp.float32),
            pltpu.VMEM((rates * epochs, half), jnp.float32),
            pltpu.VMEM((4, rates * epochs, width, GROUP), jnp.float32),
            pltpu.VMEM((2, epochs * width, quarter), jnp.bfloat16),
            pltpu.VMEM((epochs * width, half), jnp.bfloat16),
            pltpu.VMEM((2, epochs * width, BLOCK), jnp.float32),
            pltpu.VMEM((rates * width, length), jnp.bfloat16),
        ],
        compiler_params=pltpu.CompilerParams(vmem_limit_bytes=40 * MIB),
        cost_estimate=cost(
            2 * (even_table.size + odd_table.size) * (epochs + rates) * width,
            3 * half * half + 4 * spectra.size,
        ),
        name="column_stage",
    )(
        rate_vectors,
        epoch_times,
        *(in_space(part, pltpu.VMEM) for part in (spectra, even_table, odd_table)),
    )


def image_kernel(back, even_table, odd_table, out_hbm, left, staged, out_sems):
    quarter = even_table.shape[1]
    _, width, rows = back.shape
    cols = width // 2
    per_group = GROUP // cols
    for group in range(back.shape[0] // per_group):
        members = [back[group * per_group + place] for place in range(per_group)]
        if cols % 16 != 0 or rows % 128 != 0:
            members = [member.astype(jnp.float32) for member in members]
        parts = [member[:cols] for member in members] + [member[cols:] for member in members]
        whole = jnp.concatenate(parts, axis=0)
        left[:, group * 2 * GROUP : (group + 1) * 2 * GROUP] = whole.T.astype(jnp.bfloat16)
    out_copies = []
    for block in range(quarter // IMAGE_BLOCK):

        def send(side, pixels):
            start = side * quarter + block * IMAGE_BLOCK
            at = slice(start, start + IMAGE_BLOCK)
            staged[:, at] = pixels
            out_copies.append(
                pltpu.make_async_copy(
                    staged.at[:, at], out_hbm.at[0, :, at], out_sems.at[4 * block + side]
                )
            )
            out_copies[-1].start()

        at = slice(block * IMAGE_BLOCK, (block + 1) * IMAGE_BLOCK)
        inverse_parts(left, even_table, odd_table, at, quarter, send)
    wait_copies(out_copies)


def image_rows(back, even_table, odd_table):
    rows = back.shape[2]
    half, quarter = even_table.shape
    length = 2 * half
    return pl.pallas_call(
        image_kernel,
        in_specs=[IN_VMEM, IN_VMEM, IN_VMEM],
        out_specs=HBM,
        out_shape=jax.ShapeDtypeStruct((1, rows, length), jnp.float32),
        scratch_shapes=[
            pltpu.VMEM((rows, length), jnp.bfloat16),
            pltpu.VMEM((rows, length), jnp.float32),
            pltpu.SemaphoreType.DMA((length // IMAGE_BLOCK,)),
        ],
        compiler_params=pltpu.CompilerParams(vmem_limit_bytes=40 * MIB),
        cost_estimate=cost(
            2 * rows * (even_table.size + odd_table.size), 3 * half * half + 6 * rows * length
        ),
        name="image_rows",
    )(*(in_space(part, pltpu.VMEM) for part in (back, even_table, odd_table)))


def local(images, rate_vectors, epoch_times):
    _, loc_rows, length = images.shape
    epoch_count = lax.axis_size("epoch")
    devices = lax.axis_size("row") * epoch_count
    even_table, odd_table = [jnp.asarray(part) for part in packed_tables(length)]

    def exchange(values):
        return lax.all_to_all(values, ("row", "epoch"), 0, 0, tiled=True)

    spectra = exchange(row_transform(images, even_table, odd_table, devices))
    back = exchange(
        column_stage(rate_vectors, epoch_times, spectra, even_table, odd_table, epoch_count)
    )
    return image_rows(
        back.reshape(devices, length // devices, loc_rows), even_table, odd_table
    )


def solution(mesh):
    in_specs = (P(("group", "epoch"), "row", None), P(), P())
    out_specs = P(("group", "epoch"), "row", None)
    return jax.shard_map(local, mesh=mesh, in_specs=in_specs, out_specs=out_specs, check_vma=False)
```

```python
import functools
import math

import jax
import jax.numpy as jnp
import ml_dtypes
import numpy as np
from jax import lax
from jax.experimental import pallas as pl
from jax.experimental.pallas import tpu as pltpu
from jax.sharding import PartitionSpec as P

SUBPIX = 16
GROUP = 128
BLOCK = 512
IMAGE_BLOCK = 512
ROW_CHUNK = 16
PIECES = 4
MIB = 1024 * 1024
CONTRACT_LAST = (((1,), (1,)), ((), ()))
HBM = pl.BlockSpec(memory_space=pltpu.HBM)
IN_VMEM = pl.BlockSpec(memory_space=pltpu.VMEM)


def packed_freqs(index, half):
    count = half // 4
    kind = index >> (count.bit_length() - 1)
    return 4 * (index & (count - 1)) + 2 * (kind & 1) + (kind >> 1)


def packed_tables(length):
    half, quarter = length // 2, length // 4
    freqs = packed_freqs(np.arange(half, dtype=np.int32), half)
    positions = np.arange(half, dtype=np.int32)
    turns = freqs[:, None] * positions[None, :] % length
    angles = turns.astype(np.float32) * np.float32(2.0 * math.pi / length)
    factor = np.float32(1.0 / math.sqrt(length))
    cosine = np.cos(angles) * factor
    sine = np.sin(angles) * factor
    sine[0] = np.where(positions % 2 == 0, factor, -factor)
    groups = np.stack([cosine.reshape(-1, GROUP, half), sine.reshape(-1, GROUP, half)], axis=1)
    table = groups.reshape(length, half).astype(ml_dtypes.bfloat16)
    return np.ascontiguousarray(table[:half, :quarter]), table[half:]


def cost(flops, bytes_accessed):
    return pl.CostEstimate(flops=flops, bytes_accessed=bytes_accessed, transcendentals=0)


def in_space(array, space):
    return pltpu.with_memory_space_constraint(array, space)


def wait_copies(copies):
    for copy in copies:
        copy.wait()


def fold(quarters):
    first, second, third, fourth = quarters
    near, far = first + third, second + fourth
    return near + far, near - far, first - third, second - fourth


def row_kernel(
    images_hbm,
    even_hbm,
    odd_hbm,
    out_ref,
    images,
    even_table,
    odd_table,
    folded,
    image_sems,
    table_sems,
):
    loc_epochs, loc_rows, length = images.shape
    half, quarter = length // 2, length // 4
    devices, _, width, _ = out_ref.shape
    cols = width // 2
    steps = length // BLOCK
    per_step = devices // steps
    per_group = GROUP // cols
    def copies(source, target, sems, pieces):
        rows = source.shape[0] // pieces
        spans = [pl.ds(piece * rows, rows) for piece in range(pieces)]
        return [
            pltpu.make_async_copy(source.at[span], target.at[span], sems.at[piece])
            for piece, span in enumerate(spans)
        ]

    pieces = max(1, min(PIECES, loc_rows // 16))
    image_copies = [
        copies(images_hbm.at[loc], images.at[loc], image_sems.at[loc], pieces)
        for loc in range(loc_epochs)
    ]
    even_copies = copies(even_hbm, even_table, table_sems.at[0], PIECES)
    odd_copies = copies(odd_hbm.at[:, :quarter], odd_table, table_sems.at[1], 2)
    halfway = PIECES // 2
    table_copies = [even_copies[:halfway], even_copies[halfway:], odd_copies[:1], odd_copies[1:]]
    for copy in sum(image_copies, []) + table_copies[0]:
        copy.start()
    for loc in range(loc_epochs):
        wait_copies(image_copies[loc])
        if loc == 0:
            for copy in sum(table_copies[1:], []):
                copy.start()
        at = slice(loc * loc_rows, (loc + 1) * loc_rows)
        folds = fold([images[loc, :, part * quarter : (part + 1) * quarter] for part in range(4)])
        for part in range(4):
            folded[part, at] = folds[part]
    for step in range(steps):
        wait_copies(table_copies[step])
        at = slice(step % (steps // 2) * BLOCK, (step % (steps // 2) + 1) * BLOCK)
        left = (even_table if step < steps // 2 else odd_table)[at]
        sources = [step] if step < steps // 2 else [2, 3]
        terms = [
            lax.dot_general(
                left, folded[source], CONTRACT_LAST, preferred_element_type=jnp.float32
            )
            for source in sources
        ]
        for dest in range(per_step):
            start = dest // per_group * 2 * GROUP + dest % per_group * cols
            cosine, sine = [slice(first, first + cols) for first in (start, start + GROUP)]
            parts = [terms[0][cosine], terms[0][sine]]
            if step == 2:
                parts = [parts[0] - terms[1][sine], parts[1] + terms[1][cosine]]
            if step == 3:
                parts = [parts[0] + terms[1][sine], parts[1] - terms[1][cosine]]
            block = jnp.concatenate(parts, axis=0).astype(jnp.bfloat16)
            for loc in range(loc_epochs):
                out_ref[step * per_step + dest, loc] = block[:, loc * loc_rows : (loc + 1) * loc_rows]


def row_transform(images, even_table, odd_table, devices):
    loc_epochs, loc_rows, length = images.shape
    half, quarter = length // 2, length // 4
    rows = loc_epochs * loc_rows
    steps = length // BLOCK
    out = (devices, loc_epochs, length // devices, loc_rows)
    return pl.pallas_call(
        row_kernel,
        in_specs=[HBM, HBM, HBM],
        out_specs=IN_VMEM,
        out_shape=pltpu.VMEM(out, jnp.bfloat16),
        scratch_shapes=[
            pltpu.VMEM(images.shape, jnp.bfloat16),
            pltpu.VMEM(even_table.shape, jnp.bfloat16),
            pltpu.VMEM(even_table.shape, jnp.bfloat16),
            pltpu.VMEM((4, rows, quarter), jnp.bfloat16),
            pltpu.SemaphoreType.DMA((loc_epochs, PIECES)),
            pltpu.SemaphoreType.DMA((2, PIECES)),
        ],
        compiler_params=pltpu.CompilerParams(vmem_limit_bytes=40 * MIB),
        cost_estimate=cost(
            2 * rows * (even_table.size + odd_table.size), 3 * half * half + 4 * rows * length
        ),
        name="row_transform",
    )(*(in_space(part, pltpu.HBM) for part in (images, even_table, odd_table)))


def cos_sin(turns, whole):
    quarter, eighth = whole // 4, whole // 8
    shifted = (turns + eighth) & (whole - 1)
    quadrant = shifted >> (quarter.bit_length() - 1)
    angle = ((shifted & (quarter - 1)) - eighth).astype(jnp.float32) * (2.0 * math.pi / whole)
    square = angle * angle
    sine, cosine = 1.0 / 362880.0, 1.0 / 40320.0
    for divisor in (-5040.0, 120.0, -6.0, 1.0):
        sine = sine * square + 1.0 / divisor
    for divisor in (-720.0, 24.0, -2.0, 1.0):
        cosine = cosine * square + 1.0 / divisor
    sine = sine * angle
    odd = (quadrant & 1) == 1
    first, second = jnp.where(odd, sine, cosine), jnp.where(odd, cosine, sine)
    return (
        jnp.where(((quadrant + 1) & 2) == 2, -first, first),
        jnp.where(quadrant >= 2, -second, second),
    )


def spread_pairs(scalars, lanes):
    pair = lax.broadcasted_iota(jnp.int32, (len(scalars), lanes), 0)
    values = jnp.zeros((len(scalars), lanes), jnp.int32)
    for index, scalar in enumerate(scalars):
        values = jnp.where(pair == index, scalar, values)
    return values


def row_factors(shift_y, half):
    shifts = spread_pairs(shift_y, half)
    freqs = packed_freqs(lax.broadcasted_iota(jnp.int32, shifts.shape, 1), half)
    cosine, sine = cos_sin((freqs - half) * shifts, SUBPIX * 2 * half)
    return jnp.where(freqs == 0, 1.0, 2.0 * cosine), jnp.where(freqs == 0, 0.0, 2.0 * sine)


def column_factors(shift_y, shift_x, scale, device, cols, half):
    shifts_y, shifts_x = spread_pairs(shift_y, GROUP), spread_pairs(shift_x, GROUP)
    lane = lax.broadcasted_iota(jnp.int32, shifts_x.shape, 1)
    freqs = packed_freqs(device * cols + (lane & (cols - 1)), half)
    is_sine = (lane & cols) > 0
    paired = freqs == 0
    zero_col = paired & jnp.logical_not(is_sine)
    cosine, sine = cos_sin(shifts_x * (freqs - half), SUBPIX * 2 * half)
    ramp_cos = jnp.where(paired, scale, 2.0 * scale * cosine)
    ramp_sin = jnp.where(paired, 0.0, 2.0 * scale * sine)
    ramp_sin = jnp.where(is_sine, ramp_sin, -ramp_sin)
    cos_x, cos_y, cos_xy = [
        cos_sin(shifts, 2 * SUBPIX)[0] for shifts in (shifts_x, shifts_y, shifts_x + shifts_y)
    ]
    main = jnp.where(zero_col, cos_y, cos_xy)
    lead = jnp.where(zero_col, 1.0, cos_x)
    return jnp.concatenate(
        [main * ramp_cos, main * ramp_sin, lead * ramp_cos, lead * ramp_sin], axis=0
    )


def column_kernel(
    epoch_count,
    rate_smem,
    time_smem,
    received,
    even_table,
    odd_table,
    out_ref,
    rows_cos,
    rows_sin,
    spread,
    even_fold,
    odd_fold,
    products,
    sums,
):
    devices, loc_epochs, width, loc_rows = received.shape
    row_count = devices // epoch_count
    epochs = epoch_count * loc_epochs
    rates = rate_smem.shape[0]
    pairs = rates * epochs
    cols = width // 2
    half, quarter = even_table.shape
    length = 2 * half
    steps = length // BLOCK
    device = lax.axis_index("row") * epoch_count + lax.axis_index("epoch")
    period = SUBPIX * length
    shift_y, shift_x = [
        [
            rate_smem[rate, axis] * time_smem[epoch] & (period - 1)
            for rate in range(rates)
            for epoch in range(epochs)
        ]
        for axis in range(2)
    ]
    per_tile = max(1, GROUP // loc_rows)
    tile_rows = per_tile * loc_rows
    for tile in range(row_count // 4 // per_tile):
        at_lane = slice(tile * tile_rows, (tile + 1) * tile_rows)
        far_lane = slice(quarter + at_lane.start, quarter + at_lane.stop)
        for core in range(epoch_count):
            for loc in range(loc_epochs):
                quarters = []
                for side in range(4):
                    first = side * row_count // 4 + tile * per_tile
                    parts = [
                        received[(first + part) * epoch_count + core, loc] for part in range(per_tile)
                    ]
                    quarters.append(parts[0] if per_tile == 1 else jnp.concatenate(parts, axis=1))
                at_row = (core * loc_epochs + loc) * width
                at = slice(at_row, at_row + width)
                folds = fold(quarters)
                even_fold[0, at, at_lane], even_fold[1, at, at_lane] = folds[:2]
                odd_fold[at, at_lane], odd_fold[at, far_lane] = folds[2:]

    def multiply(step):
        at = slice(step % (steps // 2) * BLOCK, (step % (steps // 2) + 1) * BLOCK)
        if step < steps // 2:
            left, right = even_fold[4 * step // steps], even_table[at]
        else:
            left, right = odd_fold[...], odd_table[at]
        products[step % 2] = lax.dot_general(
            left, right, CONTRACT_LAST, preferred_element_type=jnp.float32
        )

    multiply(0)
    rows_cos[...], rows_sin[...] = row_factors(shift_y, half)
    factors = column_factors(shift_y, shift_x, 1.0 / math.sqrt(epochs), device, cols, half).T
    for kind in range(4):
        for pair in range(pairs):
            at = kind * pairs + pair
            spread[kind, pair] = jnp.broadcast_to(factors[:width, at : at + 1], (width, GROUP))

    chunk = min(ROW_CHUNK, cols)

    def add_ramped(step, group):
        tile = (step * BLOCK // 2 // GROUP + group) * GROUP
        at_even = group * 2 * GROUP
        at_odd = at_even + GROUP
        for start in range(0, cols, chunk):
            real = slice(start, start + chunk)
            imag = slice(cols + start, cols + start + chunk)
            totals = [[[0.0, 0.0], [0.0, 0.0]] for _ in range(rates)]
            leads = [[0.0, 0.0] for _ in range(rates)]
            for epoch in range(epochs):
                loaded = []
                for part in (real, imag):
                    at = slice(epoch * width + part.start, epoch * width + part.stop)
                    loaded.append(
                        [
                            products[step % 2, at, first : first + GROUP]
                            for first in (at_even, at_odd)
                        ]
                    )
                for rate in range(rates):
                    pair = rate * epochs + epoch
                    cos_row = rows_cos[pair : pair + 1, tile : tile + GROUP]
                    sin_row = rows_sin[pair : pair + 1, tile : tile + GROUP]
                    turned = [
                        (cos_row * even + sin_row * odd, cos_row * odd - sin_row * even)
                        for even, odd in loaded
                    ]
                    straight = [spread[0, pair, part] for part in (real, imag)]
                    crossed = [spread[1, pair, part] for part in (real, imag)]
                    for part in range(2):
                        for which in range(2):
                            totals[rate][part][which] += (
                                straight[part] * turned[part][which]
                                + crossed[1 - part] * turned[1 - part][which]
                            )
                        if step == 0 and group == 0:
                            own, other = (real, imag) if part == 0 else (imag, real)
                            leads[rate][part] += (
                                spread[2, pair, own] * loaded[part][0]
                                + spread[3, pair, other] * loaded[1 - part][0]
                            )
            for rate in range(rates):
                for part, rows in enumerate((real, imag)):
                    even_sum, odd_sum = totals[rate][part]
                    if step == 0 and group == 0:
                        first = lax.broadcasted_iota(jnp.int32, even_sum.shape, 1) == 0
                        even_sum = jnp.where(first, leads[rate][part], even_sum)
                    at = slice(rate * width + rows.start, rate * width + rows.stop)
                    for values, lane in ((even_sum, at_even), (odd_sum, at_odd)):
                        lane = step * BLOCK + lane
                        sums[at, lane : lane + GROUP] = values.astype(jnp.bfloat16)

    for step in range(steps):
        if step + 1 < steps:
            multiply(step + 1)
        for group in range(BLOCK // 2 // GROUP):
            add_ramped(step, group)

    loc_rates = rates // epoch_count

    def send(side, back):
        back = back.astype(jnp.bfloat16)
        rows_here = quarter // loc_rows
        for row in range(rows_here):
            for rate in range(rates):
                dest = (side * rows_here + row) * epoch_count + rate // loc_rates
                out_ref[dest, rate % loc_rates] = back[
                    rate * width : (rate + 1) * width, row * loc_rows : (row + 1) * loc_rows
                ]

    inverse_parts(sums, even_table, odd_table, slice(0, quarter), quarter, send)


def inverse_parts(left, even_table, odd_table, at, quarter, send):
    half = 2 * quarter
    far = slice(quarter + at.start, quarter + at.stop)

    def product(first, depth, right):
        return jnp.dot(left[:, first : first + depth], right, preferred_element_type=jnp.float32)

    zero = product(0, quarter, even_table[:quarter, at])
    two = product(quarter, quarter, even_table[quarter:, at])
    for position, even, span in ((0, zero + two, at), (1, zero - two, far)):
        odd = product(half, half, odd_table[:, span])
        send(position, even + odd)
        send(position + 2, even - odd)


def column_stage(rate_vectors, epoch_times, spectra, even_table, odd_table, epoch_count):
    devices, loc_epochs, width, loc_rows = spectra.shape
    half, quarter = even_table.shape
    length = 2 * half
    epochs, rates = epoch_times.shape[0], rate_vectors.shape[0]
    out = (devices, rates // epoch_count, width, loc_rows)
    scalars = pl.BlockSpec(memory_space=pltpu.SMEM)
    return pl.pallas_call(
        functools.partial(column_kernel, epoch_count),
        in_specs=[scalars, scalars, IN_VMEM, IN_VMEM, IN_VMEM],
        out_specs=IN_VMEM,
        out_shape=pltpu.VMEM(out, jnp.bfloat16),
        scratch_shapes=[
            pltpu.VMEM((rates * epochs, half), jnp.float32),
            pltpu.VMEM((rates * epochs, half), jnp.float32),
            pltpu.VMEM((4, rates * epochs, width, GROUP), jnp.float32),
            pltpu.VMEM((2, epochs * width, quarter), jnp.bfloat16),
            pltpu.VMEM((epochs * width, half), jnp.bfloat16),
            pltpu.VMEM((2, epochs * width, BLOCK), jnp.float32),
            pltpu.VMEM((rates * width, length), jnp.bfloat16),
        ],
        compiler_params=pltpu.CompilerParams(vmem_limit_bytes=40 * MIB),
        cost_estimate=cost(
            2 * (even_table.size + odd_table.size) * (epochs + rates) * width,
            3 * half * half + 4 * spectra.size,
        ),
        name="column_stage",
    )(
        rate_vectors,
        epoch_times,
        *(in_space(part, pltpu.VMEM) for part in (spectra, even_table, odd_table)),
    )


def image_kernel(back, even_table, odd_table, out_hbm, left, staged, out_sems):
    quarter = even_table.shape[1]
    _, width, rows = back.shape
    cols = width // 2
    per_group = GROUP // cols
    for group in range(back.shape[0] // per_group):
        members = [back[group * per_group + place] for place in range(per_group)]
        if cols % 16 != 0 or rows % 128 != 0:
            members = [member.astype(jnp.float32) for member in members]
        parts = [member[:cols] for member in members] + [member[cols:] for member in members]
        whole = jnp.concatenate(parts, axis=0)
        left[:, group * 2 * GROUP : (group + 1) * 2 * GROUP] = whole.T.astype(jnp.bfloat16)
    out_copies = []
    for block in range(quarter // IMAGE_BLOCK):

        def send(side, pixels):
            start = side * quarter + block * IMAGE_BLOCK
            at = slice(start, start + IMAGE_BLOCK)
            staged[:, at] = pixels
            out_copies.append(
                pltpu.make_async_copy(
                    staged.at[:, at], out_hbm.at[0, :, at], out_sems.at[4 * block + side]
                )
            )
            out_copies[-1].start()

        at = slice(block * IMAGE_BLOCK, (block + 1) * IMAGE_BLOCK)
        inverse_parts(left, even_table, odd_table, at, quarter, send)
    wait_copies(out_copies)


def image_rows(back, even_table, odd_table):
    rows = back.shape[2]
    half, quarter = even_table.shape
    length = 2 * half
    return pl.pallas_call(
        image_kernel,
        in_specs=[IN_VMEM, IN_VMEM, IN_VMEM],
        out_specs=HBM,
        out_shape=jax.ShapeDtypeStruct((1, rows, length), jnp.float32),
        scratch_shapes=[
            pltpu.VMEM((rows, length), jnp.bfloat16),
            pltpu.VMEM((rows, length), jnp.float32),
            pltpu.SemaphoreType.DMA((length // IMAGE_BLOCK,)),
        ],
        compiler_params=pltpu.CompilerParams(vmem_limit_bytes=40 * MIB),
        cost_estimate=cost(
            2 * rows * (even_table.size + odd_table.size), 3 * half * half + 6 * rows * length
        ),
        name="image_rows",
    )(*(in_space(part, pltpu.VMEM) for part in (back, even_table, odd_table)))


def local(images, rate_vectors, epoch_times):
    _, loc_rows, length = images.shape
    epoch_count = lax.axis_size("epoch")
    devices = lax.axis_size("row") * epoch_count
    even_table, odd_table = [jnp.asarray(part) for part in packed_tables(length)]

    def exchange(values):
        blocks = values.reshape(devices, -1, loc_rows)
        received = lax.all_to_all(blocks, ("row", "epoch"), 0, 0, tiled=True)
        return received.reshape(values.shape)

    spectra = exchange(row_transform(images, even_table, odd_table, devices))
    back = exchange(
        column_stage(rate_vectors, epoch_times, spectra, even_table, odd_table, epoch_count)
    )
    return image_rows(
        back.reshape(devices, length // devices, loc_rows), even_table, odd_table
    )


def solution(mesh):
    in_specs = (P(("group", "epoch"), "row", None), P(), P())
    out_specs = P(("group", "epoch"), "row", None)
    return jax.shard_map(local, mesh=mesh, in_specs=in_specs, out_specs=out_specs, check_vma=False)
```

```python
import functools
import math

import jax
import jax.numpy as jnp
import ml_dtypes
import numpy as np
from jax import lax
from jax.experimental import pallas as pl
from jax.experimental.pallas import tpu as pltpu
from jax.sharding import PartitionSpec as P

SUBPIX = 16
GROUP = 128
BLOCK = 512
IMAGE_BLOCK = 512
ROW_CHUNK = 16
PIECES = 4
MIB = 1024 * 1024
CONTRACT_LAST = (((1,), (1,)), ((), ()))
HBM = pl.BlockSpec(memory_space=pltpu.HBM)
IN_VMEM = pl.BlockSpec(memory_space=pltpu.VMEM)


def packed_freqs(index, half):
    count = half // 4
    kind = index >> (count.bit_length() - 1)
    return 4 * (index & (count - 1)) + 2 * (kind & 1) + (kind >> 1)


def packed_tables(length):
    half, quarter = length // 2, length // 4
    freqs = packed_freqs(np.arange(half, dtype=np.int32), half)
    positions = np.arange(half, dtype=np.int32)
    turns = freqs[:, None] * positions[None, :] % length
    angles = turns.astype(np.float32) * np.float32(2.0 * math.pi / length)
    factor = np.float32(1.0 / math.sqrt(length))
    cosine = np.cos(angles) * factor
    sine = np.sin(angles) * factor
    sine[0] = np.where(positions % 2 == 0, factor, -factor)
    groups = np.stack([cosine.reshape(-1, GROUP, half), sine.reshape(-1, GROUP, half)], axis=1)
    table = groups.reshape(length, half).astype(ml_dtypes.bfloat16)
    return np.ascontiguousarray(table[:half, :quarter]), table[half:]


def cost(flops, bytes_accessed):
    return pl.CostEstimate(flops=flops, bytes_accessed=bytes_accessed, transcendentals=0)


def in_space(array, space):
    return pltpu.with_memory_space_constraint(array, space)


def wait_copies(copies):
    for copy in copies:
        copy.wait()


def fold(quarters):
    first, second, third, fourth = quarters
    near, far = first + third, second + fourth
    return near + far, near - far, first - third, second - fourth


def row_kernel(
    images_hbm,
    even_hbm,
    odd_hbm,
    out_ref,
    images,
    even_table,
    odd_table,
    folded,
    image_sems,
    table_sems,
):
    loc_epochs, loc_rows, length = images.shape
    half, quarter = length // 2, length // 4
    devices, _, width, _ = out_ref.shape
    cols = width // 2
    steps = length // BLOCK
    per_step = devices // steps
    per_group = GROUP // cols
    def copies(source, target, sems, pieces):
        rows = source.shape[0] // pieces
        spans = [pl.ds(piece * rows, rows) for piece in range(pieces)]
        return [
            pltpu.make_async_copy(source.at[span], target.at[span], sems.at[piece])
            for piece, span in enumerate(spans)
        ]

    pieces = max(1, min(PIECES, loc_rows // 16))
    image_copies = [
        copies(images_hbm.at[loc], images.at[loc], image_sems.at[loc], pieces)
        for loc in range(loc_epochs)
    ]
    even_copies = copies(even_hbm, even_table, table_sems.at[0], PIECES)
    odd_copies = copies(odd_hbm.at[:, :quarter], odd_table, table_sems.at[1], 2)
    halfway = PIECES // 2
    table_copies = [even_copies[:halfway], even_copies[halfway:], odd_copies[:1], odd_copies[1:]]
    for copy in sum(image_copies, []) + table_copies[0]:
        copy.start()
    for loc in range(loc_epochs):
        wait_copies(image_copies[loc])
        if loc == 0:
            for copy in sum(table_copies[1:], []):
                copy.start()
        at = slice(loc * loc_rows, (loc + 1) * loc_rows)
        folds = fold([images[loc, :, part * quarter : (part + 1) * quarter] for part in range(4)])
        for part in range(4):
            folded[part, at] = folds[part]
    for step in range(steps):
        wait_copies(table_copies[step])
        at = slice(step % (steps // 2) * BLOCK, (step % (steps // 2) + 1) * BLOCK)
        left = (even_table if step < steps // 2 else odd_table)[at]
        sources = [step] if step < steps // 2 else [2, 3]
        terms = [
            lax.dot_general(
                left, folded[source], CONTRACT_LAST, preferred_element_type=jnp.float32
            )
            for source in sources
        ]
        for dest in range(per_step):
            start = dest // per_group * 2 * GROUP + dest % per_group * cols
            cosine, sine = [slice(first, first + cols) for first in (start, start + GROUP)]
            parts = [terms[0][cosine], terms[0][sine]]
            if step == 2:
                parts = [parts[0] - terms[1][sine], parts[1] + terms[1][cosine]]
            if step == 3:
                parts = [parts[0] + terms[1][sine], parts[1] - terms[1][cosine]]
            block = jnp.concatenate(parts, axis=0).astype(jnp.bfloat16)
            for loc in range(loc_epochs):
                out_ref[step * per_step + dest, loc] = block[:, loc * loc_rows : (loc + 1) * loc_rows]


def row_transform(images, even_table, odd_table, devices):
    loc_epochs, loc_rows, length = images.shape
    half, quarter = length // 2, length // 4
    rows = loc_epochs * loc_rows
    steps = length // BLOCK
    out = (devices, loc_epochs, length // devices, loc_rows)
    return pl.pallas_call(
        row_kernel,
        in_specs=[HBM, HBM, HBM],
        out_specs=IN_VMEM,
        out_shape=pltpu.VMEM(out, jnp.bfloat16),
        scratch_shapes=[
            pltpu.VMEM(images.shape, jnp.bfloat16),
            pltpu.VMEM(even_table.shape, jnp.bfloat16),
            pltpu.VMEM(even_table.shape, jnp.bfloat16),
            pltpu.VMEM((4, rows, quarter), jnp.bfloat16),
            pltpu.SemaphoreType.DMA((loc_epochs, PIECES)),
            pltpu.SemaphoreType.DMA((2, PIECES)),
        ],
        compiler_params=pltpu.CompilerParams(vmem_limit_bytes=40 * MIB),
        cost_estimate=cost(
            2 * rows * (even_table.size + odd_table.size), 3 * half * half + 4 * rows * length
        ),
        name="row_transform",
    )(*(in_space(part, pltpu.HBM) for part in (images, even_table, odd_table)))


def cos_sin(turns, whole):
    quarter, eighth = whole // 4, whole // 8
    shifted = (turns + eighth) & (whole - 1)
    quadrant = shifted >> (quarter.bit_length() - 1)
    angle = ((shifted & (quarter - 1)) - eighth).astype(jnp.float32) * (2.0 * math.pi / whole)
    square = angle * angle
    sine, cosine = 1.0 / 362880.0, 1.0 / 40320.0
    for divisor in (-5040.0, 120.0, -6.0, 1.0):
        sine = sine * square + 1.0 / divisor
    for divisor in (-720.0, 24.0, -2.0, 1.0):
        cosine = cosine * square + 1.0 / divisor
    sine = sine * angle
    odd = (quadrant & 1) == 1
    first, second = jnp.where(odd, sine, cosine), jnp.where(odd, cosine, sine)
    return (
        jnp.where(((quadrant + 1) & 2) == 2, -first, first),
        jnp.where(quadrant >= 2, -second, second),
    )


def spread_pairs(scalars, lanes):
    pair = lax.broadcasted_iota(jnp.int32, (len(scalars), lanes), 0)
    values = jnp.zeros((len(scalars), lanes), jnp.int32)
    for index, scalar in enumerate(scalars):
        values = jnp.where(pair == index, scalar, values)
    return values


def row_factors(shift_y, half):
    shifts = spread_pairs(shift_y, half)
    freqs = packed_freqs(lax.broadcasted_iota(jnp.int32, shifts.shape, 1), half)
    cosine, sine = cos_sin((freqs - half) * shifts, SUBPIX * 2 * half)
    return jnp.where(freqs == 0, 1.0, 2.0 * cosine), jnp.where(freqs == 0, 0.0, 2.0 * sine)


def column_factors(shift_y, shift_x, scale, device, cols, half):
    shifts_y, shifts_x = spread_pairs(shift_y, GROUP), spread_pairs(shift_x, GROUP)
    lane = lax.broadcasted_iota(jnp.int32, shifts_x.shape, 1)
    freqs = packed_freqs(device * cols + (lane & (cols - 1)), half)
    is_sine = (lane & cols) > 0
    paired = freqs == 0
    zero_col = paired & jnp.logical_not(is_sine)
    cosine, sine = cos_sin(shifts_x * (freqs - half), SUBPIX * 2 * half)
    ramp_cos = jnp.where(paired, scale, 2.0 * scale * cosine)
    ramp_sin = jnp.where(paired, 0.0, 2.0 * scale * sine)
    ramp_sin = jnp.where(is_sine, ramp_sin, -ramp_sin)
    cos_x, cos_y, cos_xy = [
        cos_sin(shifts, 2 * SUBPIX)[0] for shifts in (shifts_x, shifts_y, shifts_x + shifts_y)
    ]
    main = jnp.where(zero_col, cos_y, cos_xy)
    lead = jnp.where(zero_col, 1.0, cos_x)
    return jnp.concatenate(
        [main * ramp_cos, main * ramp_sin, lead * ramp_cos, lead * ramp_sin], axis=0
    )


def column_kernel(
    epoch_count,
    rate_smem,
    time_smem,
    received,
    even_table,
    odd_table,
    out_ref,
    rows_cos,
    rows_sin,
    spread,
    columns,
    even_fold,
    odd_fold,
    products,
    sums,
):
    devices, loc_epochs, width, loc_rows = received.shape
    row_count = devices // epoch_count
    epochs = epoch_count * loc_epochs
    rates = rate_smem.shape[0]
    pairs = rates * epochs
    cols = width // 2
    half, quarter = even_table.shape
    length = 2 * half
    steps = length // BLOCK
    device = lax.axis_index("row") * epoch_count + lax.axis_index("epoch")
    period = SUBPIX * length
    shift_y, shift_x = [
        [
            rate_smem[rate, axis] * time_smem[epoch] & (period - 1)
            for rate in range(rates)
            for epoch in range(epochs)
        ]
        for axis in range(2)
    ]
    per_tile = max(1, GROUP // loc_rows)
    tile_rows = per_tile * loc_rows
    for tile in range(row_count // 4 // per_tile):
        at_lane = slice(tile * tile_rows, (tile + 1) * tile_rows)
        far_lane = slice(quarter + at_lane.start, quarter + at_lane.stop)
        for core in range(epoch_count):
            for loc in range(loc_epochs):
                quarters = []
                for side in range(4):
                    first = side * row_count // 4 + tile * per_tile
                    parts = [
                        received[(first + part) * epoch_count + core, loc] for part in range(per_tile)
                    ]
                    quarters.append(parts[0] if per_tile == 1 else jnp.concatenate(parts, axis=1))
                at_row = (core * loc_epochs + loc) * width
                at = slice(at_row, at_row + width)
                folds = fold(quarters)
                even_fold[0, at, at_lane], even_fold[1, at, at_lane] = folds[:2]
                odd_fold[at, at_lane], odd_fold[at, far_lane] = folds[2:]

    def multiply(step):
        at = slice(step % (steps // 2) * BLOCK, (step % (steps // 2) + 1) * BLOCK)
        if step < steps // 2:
            left, right = even_fold[4 * step // steps], even_table[at]
        else:
            left, right = odd_fold[...], odd_table[at]
        products[step % 2] = lax.dot_general(
            left, right, CONTRACT_LAST, preferred_element_type=jnp.float32
        )

    multiply(0)
    rows_cos[...], rows_sin[...] = row_factors(shift_y, half)
    factors = column_factors(shift_y, shift_x, 1.0 / math.sqrt(epochs), device, cols, half).T
    columns[...] = factors
    for kind in range(2):
        for pair in range(pairs):
            at = kind * pairs + pair
            spread[kind, pair] = jnp.broadcast_to(factors[:width, at : at + 1], (width, GROUP))

    chunk = min(ROW_CHUNK, cols)

    def add_ramped(step, group):
        tile = (step * BLOCK // 2 // GROUP + group) * GROUP
        at_even = group * 2 * GROUP
        at_odd = at_even + GROUP
        for start in range(0, cols, chunk):
            real = slice(start, start + chunk)
            imag = slice(cols + start, cols + start + chunk)
            totals = [[[0.0, 0.0], [0.0, 0.0]] for _ in range(rates)]
            leads = [[0.0, 0.0] for _ in range(rates)]
            for epoch in range(epochs):
                loaded = []
                for part in (real, imag):
                    at = slice(epoch * width + part.start, epoch * width + part.stop)
                    loaded.append(
                        [
                            products[step % 2, at, first : first + GROUP]
                            for first in (at_even, at_odd)
                        ]
                    )
                for rate in range(rates):
                    pair = rate * epochs + epoch
                    cos_row = rows_cos[pair : pair + 1, tile : tile + GROUP]
                    sin_row = rows_sin[pair : pair + 1, tile : tile + GROUP]
                    turned = [
                        (cos_row * even + sin_row * odd, cos_row * odd - sin_row * even)
                        for even, odd in loaded
                    ]
                    straight = [spread[0, pair, part] for part in (real, imag)]
                    crossed = [spread[1, pair, part] for part in (real, imag)]
                    for part in range(2):
                        for which in range(2):
                            totals[rate][part][which] += (
                                straight[part] * turned[part][which]
                                + crossed[1 - part] * turned[1 - part][which]
                            )
                        if step == 0 and group == 0:
                            own, other = (real, imag) if part == 0 else (imag, real)
                            at_own = 2 * pairs + pair
                            at_other = 3 * pairs + pair
                            leads[rate][part] += (
                                columns[own, at_own : at_own + 1] * loaded[part][0][:, :1]
                                + columns[other, at_other : at_other + 1] * loaded[1 - part][0][:, :1]
                            )
            for rate in range(rates):
                for part, rows in enumerate((real, imag)):
                    even_sum, odd_sum = totals[rate][part]
                    if step == 0 and group == 0:
                        first = lax.broadcasted_iota(jnp.int32, even_sum.shape, 1) == 0
                        even_sum = jnp.where(first, leads[rate][part], even_sum)
                    at = slice(rate * width + rows.start, rate * width + rows.stop)
                    for values, lane in ((even_sum, at_even), (odd_sum, at_odd)):
                        lane = step * BLOCK + lane
                        sums[at, lane : lane + GROUP] = values.astype(jnp.bfloat16)

    for step in range(steps):
        if step + 1 < steps:
            multiply(step + 1)
        for group in range(BLOCK // 2 // GROUP):
            add_ramped(step, group)

    loc_rates = rates // epoch_count

    def send(side, back):
        back = back.astype(jnp.bfloat16)
        rows_here = quarter // loc_rows
        for row in range(rows_here):
            for rate in range(rates):
                dest = (side * rows_here + row) * epoch_count + rate // loc_rates
                out_ref[dest, rate % loc_rates] = back[
                    rate * width : (rate + 1) * width, row * loc_rows : (row + 1) * loc_rows
                ]

    inverse_parts(sums, even_table, odd_table, slice(0, quarter), quarter, send)


def inverse_parts(left, even_table, odd_table, at, quarter, send):
    half = 2 * quarter
    far = slice(quarter + at.start, quarter + at.stop)

    def product(first, depth, right):
        return jnp.dot(left[:, first : first + depth], right, preferred_element_type=jnp.float32)

    zero = product(0, quarter, even_table[:quarter, at])
    two = product(quarter, quarter, even_table[quarter:, at])
    for position, even, span in ((0, zero + two, at), (1, zero - two, far)):
        odd = product(half, half, odd_table[:, span])
        send(position, even + odd)
        send(position + 2, even - odd)


def column_stage(rate_vectors, epoch_times, spectra, even_table, odd_table, epoch_count):
    devices, loc_epochs, width, loc_rows = spectra.shape
    half, quarter = even_table.shape
    length = 2 * half
    epochs, rates = epoch_times.shape[0], rate_vectors.shape[0]
    out = (devices, rates // epoch_count, width, loc_rows)
    scalars = pl.BlockSpec(memory_space=pltpu.SMEM)
    return pl.pallas_call(
        functools.partial(column_kernel, epoch_count),
        in_specs=[scalars, scalars, IN_VMEM, IN_VMEM, IN_VMEM],
        out_specs=IN_VMEM,
        out_shape=pltpu.VMEM(out, jnp.bfloat16),
        scratch_shapes=[
            pltpu.VMEM((rates * epochs, half), jnp.float32),
            pltpu.VMEM((rates * epochs, half), jnp.float32),
            pltpu.VMEM((2, rates * epochs, width, GROUP), jnp.float32),
            pltpu.VMEM((GROUP, 4 * rates * epochs), jnp.float32),
            pltpu.VMEM((2, epochs * width, quarter), jnp.bfloat16),
            pltpu.VMEM((epochs * width, half), jnp.bfloat16),
            pltpu.VMEM((2, epochs * width, BLOCK), jnp.float32),
            pltpu.VMEM((rates * width, length), jnp.bfloat16),
        ],
        compiler_params=pltpu.CompilerParams(vmem_limit_bytes=40 * MIB),
        cost_estimate=cost(
            2 * (even_table.size + odd_table.size) * (epochs + rates) * width,
            3 * half * half + 4 * spectra.size,
        ),
        name="column_stage",
    )(
        rate_vectors,
        epoch_times,
        *(in_space(part, pltpu.VMEM) for part in (spectra, even_table, odd_table)),
    )


def image_kernel(back, even_table, odd_table, out_hbm, left, staged, out_sems):
    quarter = even_table.shape[1]
    _, width, rows = back.shape
    cols = width // 2
    per_group = GROUP // cols
    for group in range(back.shape[0] // per_group):
        members = [back[group * per_group + place] for place in range(per_group)]
        if cols % 16 != 0 or rows % 128 != 0:
            members = [member.astype(jnp.float32) for member in members]
        parts = [member[:cols] for member in members] + [member[cols:] for member in members]
        whole = jnp.concatenate(parts, axis=0)
        left[:, group * 2 * GROUP : (group + 1) * 2 * GROUP] = whole.T.astype(jnp.bfloat16)
    out_copies = []
    for block in range(quarter // IMAGE_BLOCK):

        def send(side, pixels):
            start = side * quarter + block * IMAGE_BLOCK
            at = slice(start, start + IMAGE_BLOCK)
            staged[:, at] = pixels
            out_copies.append(
                pltpu.make_async_copy(
                    staged.at[:, at], out_hbm.at[0, :, at], out_sems.at[4 * block + side]
                )
            )
            out_copies[-1].start()

        at = slice(block * IMAGE_BLOCK, (block + 1) * IMAGE_BLOCK)
        inverse_parts(left, even_table, odd_table, at, quarter, send)
    wait_copies(out_copies)


def image_rows(back, even_table, odd_table):
    rows = back.shape[2]
    half, quarter = even_table.shape
    length = 2 * half
    return pl.pallas_call(
        image_kernel,
        in_specs=[IN_VMEM, IN_VMEM, IN_VMEM],
        out_specs=HBM,
        out_shape=jax.ShapeDtypeStruct((1, rows, length), jnp.float32),
        scratch_shapes=[
            pltpu.VMEM((rows, length), jnp.bfloat16),
            pltpu.VMEM((rows, length), jnp.float32),
            pltpu.SemaphoreType.DMA((length // IMAGE_BLOCK,)),
        ],
        compiler_params=pltpu.CompilerParams(vmem_limit_bytes=40 * MIB),
        cost_estimate=cost(
            2 * rows * (even_table.size + odd_table.size), 3 * half * half + 6 * rows * length
        ),
        name="image_rows",
    )(*(in_space(part, pltpu.VMEM) for part in (back, even_table, odd_table)))


def local(images, rate_vectors, epoch_times):
    _, loc_rows, length = images.shape
    epoch_count = lax.axis_size("epoch")
    devices = lax.axis_size("row") * epoch_count
    even_table, odd_table = [jnp.asarray(part) for part in packed_tables(length)]

    def exchange(values):
        return lax.all_to_all(values, ("row", "epoch"), 0, 0, tiled=True)

    spectra = exchange(row_transform(images, even_table, odd_table, devices))
    back = exchange(
        column_stage(rate_vectors, epoch_times, spectra, even_table, odd_table, epoch_count)
    )
    return image_rows(
        back.reshape(devices, length // devices, loc_rows), even_table, odd_table
    )


def solution(mesh):
    in_specs = (P(("group", "epoch"), "row", None), P(), P())
    out_specs = P(("group", "epoch"), "row", None)
    return jax.shard_map(local, mesh=mesh, in_specs=in_specs, out_specs=out_specs, check_vma=False)
```

```python
import functools
import math

import jax
import jax.numpy as jnp
import ml_dtypes
import numpy as np
from jax import lax
from jax.experimental import pallas as pl
from jax.experimental.pallas import tpu as pltpu
from jax.sharding import PartitionSpec as P

SUBPIX = 16
GROUP = 128
BLOCK = 512
IMAGE_BLOCK = 512
ROW_CHUNK = 16
PIECES = 8
MIB = 1024 * 1024
CONTRACT_LAST = (((1,), (1,)), ((), ()))
HBM = pl.BlockSpec(memory_space=pltpu.HBM)
IN_VMEM = pl.BlockSpec(memory_space=pltpu.VMEM)


def packed_freqs(index, half):
    count = half // 4
    kind = index >> (count.bit_length() - 1)
    return 4 * (index & (count - 1)) + 2 * (kind & 1) + (kind >> 1)


def packed_tables(length):
    half, quarter = length // 2, length // 4
    freqs = packed_freqs(np.arange(half, dtype=np.int32), half)
    positions = np.arange(half, dtype=np.int32)
    turns = freqs[:, None] * positions[None, :] % length
    angles = turns.astype(np.float32) * np.float32(2.0 * math.pi / length)
    factor = np.float32(1.0 / math.sqrt(length))
    cosine = np.cos(angles) * factor
    sine = np.sin(angles) * factor
    sine[0] = np.where(positions % 2 == 0, factor, -factor)
    groups = np.stack([cosine.reshape(-1, GROUP, half), sine.reshape(-1, GROUP, half)], axis=1)
    table = groups.reshape(length, half).astype(ml_dtypes.bfloat16)
    return np.ascontiguousarray(table[:half, :quarter]), table[half:]


def cost(flops, bytes_accessed):
    return pl.CostEstimate(flops=flops, bytes_accessed=bytes_accessed, transcendentals=0)


def in_space(array, space):
    return pltpu.with_memory_space_constraint(array, space)


def wait_copies(copies):
    for copy in copies:
        copy.wait()


def fold(quarters):
    first, second, third, fourth = quarters
    near, far = first + third, second + fourth
    return near + far, near - far, first - third, second - fourth


def row_kernel(
    images_hbm,
    even_hbm,
    odd_hbm,
    out_ref,
    images,
    even_table,
    odd_table,
    folded,
    image_sems,
    table_sems,
):
    loc_epochs, loc_rows, length = images.shape
    half, quarter = length // 2, length // 4
    devices, _, width, _ = out_ref.shape
    cols = width // 2
    steps = length // BLOCK
    per_step = devices // steps
    per_group = GROUP // cols
    def copies(source, target, sems, pieces):
        rows = source.shape[0] // pieces
        spans = [pl.ds(piece * rows, rows) for piece in range(pieces)]
        return [
            pltpu.make_async_copy(source.at[span], target.at[span], sems.at[piece])
            for piece, span in enumerate(spans)
        ]

    pieces = max(1, min(PIECES, loc_rows // 16))
    image_copies = [
        copies(images_hbm.at[loc], images.at[loc], image_sems.at[loc], pieces)
        for loc in range(loc_epochs)
    ]
    even_copies = copies(even_hbm, even_table, table_sems.at[0], PIECES)
    odd_copies = copies(odd_hbm.at[:, :quarter], odd_table, table_sems.at[1], 2)
    halfway = PIECES // 2
    table_copies = [even_copies[:halfway], even_copies[halfway:], odd_copies[:1], odd_copies[1:]]
    for copy in sum(image_copies, []) + even_copies:
        copy.start()
    for loc in range(loc_epochs):
        wait_copies(image_copies[loc])
        if loc == loc_epochs - 1:
            for copy in odd_copies:
                copy.start()
        at = slice(loc * loc_rows, (loc + 1) * loc_rows)
        folds = fold([images[loc, :, part * quarter : (part + 1) * quarter] for part in range(4)])
        for part in range(4):
            folded[part, at] = folds[part]
    for step in range(steps):
        wait_copies(table_copies[step])
        at = slice(step % (steps // 2) * BLOCK, (step % (steps // 2) + 1) * BLOCK)
        left = (even_table if step < steps // 2 else odd_table)[at]
        sources = [step] if step < steps // 2 else [2, 3]
        terms = [
            lax.dot_general(
                left, folded[source], CONTRACT_LAST, preferred_element_type=jnp.float32
            )
            for source in sources
        ]
        for dest in range(per_step):
            start = dest // per_group * 2 * GROUP + dest % per_group * cols
            cosine, sine = [slice(first, first + cols) for first in (start, start + GROUP)]
            parts = [terms[0][cosine], terms[0][sine]]
            if step == 2:
                parts = [parts[0] - terms[1][sine], parts[1] + terms[1][cosine]]
            if step == 3:
                parts = [parts[0] + terms[1][sine], parts[1] - terms[1][cosine]]
            block = jnp.concatenate(parts, axis=0).astype(jnp.bfloat16)
            for loc in range(loc_epochs):
                out_ref[step * per_step + dest, loc] = block[:, loc * loc_rows : (loc + 1) * loc_rows]


def row_transform(images, even_table, odd_table, devices):
    loc_epochs, loc_rows, length = images.shape
    half, quarter = length // 2, length // 4
    rows = loc_epochs * loc_rows
    steps = length // BLOCK
    out = (devices, loc_epochs, length // devices, loc_rows)
    return pl.pallas_call(
        row_kernel,
        in_specs=[HBM, HBM, HBM],
        out_specs=IN_VMEM,
        out_shape=pltpu.VMEM(out, jnp.bfloat16),
        scratch_shapes=[
            pltpu.VMEM(images.shape, jnp.bfloat16),
            pltpu.VMEM(even_table.shape, jnp.bfloat16),
            pltpu.VMEM(even_table.shape, jnp.bfloat16),
            pltpu.VMEM((4, rows, quarter), jnp.bfloat16),
            pltpu.SemaphoreType.DMA((loc_epochs, PIECES)),
            pltpu.SemaphoreType.DMA((2, PIECES)),
        ],
        compiler_params=pltpu.CompilerParams(vmem_limit_bytes=40 * MIB),
        cost_estimate=cost(
            2 * rows * (even_table.size + odd_table.size), 3 * half * half + 4 * rows * length
        ),
        name="row_transform",
    )(*(in_space(part, pltpu.HBM) for part in (images, even_table, odd_table)))


def cos_sin(turns, whole):
    quarter, eighth = whole // 4, whole // 8
    shifted = (turns + eighth) & (whole - 1)
    quadrant = shifted >> (quarter.bit_length() - 1)
    angle = ((shifted & (quarter - 1)) - eighth).astype(jnp.float32) * (2.0 * math.pi / whole)
    square = angle * angle
    sine, cosine = 1.0 / 362880.0, 1.0 / 40320.0
    for divisor in (-5040.0, 120.0, -6.0, 1.0):
        sine = sine * square + 1.0 / divisor
    for divisor in (-720.0, 24.0, -2.0, 1.0):
        cosine = cosine * square + 1.0 / divisor
    sine = sine * angle
    odd = (quadrant & 1) == 1
    first, second = jnp.where(odd, sine, cosine), jnp.where(odd, cosine, sine)
    return (
        jnp.where(((quadrant + 1) & 2) == 2, -first, first),
        jnp.where(quadrant >= 2, -second, second),
    )


def spread_pairs(scalars, lanes):
    pair = lax.broadcasted_iota(jnp.int32, (len(scalars), lanes), 0)
    values = jnp.zeros((len(scalars), lanes), jnp.int32)
    for index, scalar in enumerate(scalars):
        values = jnp.where(pair == index, scalar, values)
    return values


def row_factors(shift_y, half):
    shifts = spread_pairs(shift_y, half)
    freqs = packed_freqs(lax.broadcasted_iota(jnp.int32, shifts.shape, 1), half)
    cosine, sine = cos_sin((freqs - half) * shifts, SUBPIX * 2 * half)
    return jnp.where(freqs == 0, 1.0, 2.0 * cosine), jnp.where(freqs == 0, 0.0, 2.0 * sine)


def column_factors(shift_y, shift_x, scale, device, cols, half):
    shifts_y, shifts_x = spread_pairs(shift_y, GROUP), spread_pairs(shift_x, GROUP)
    lane = lax.broadcasted_iota(jnp.int32, shifts_x.shape, 1)
    freqs = packed_freqs(device * cols + (lane & (cols - 1)), half)
    is_sine = (lane & cols) > 0
    paired = freqs == 0
    zero_col = paired & jnp.logical_not(is_sine)
    cosine, sine = cos_sin(shifts_x * (freqs - half), SUBPIX * 2 * half)
    ramp_cos = jnp.where(paired, scale, 2.0 * scale * cosine)
    ramp_sin = jnp.where(paired, 0.0, 2.0 * scale * sine)
    ramp_sin = jnp.where(is_sine, ramp_sin, -ramp_sin)
    cos_x, cos_y, cos_xy = [
        cos_sin(shifts, 2 * SUBPIX)[0] for shifts in (shifts_x, shifts_y, shifts_x + shifts_y)
    ]
    main = jnp.where(zero_col, cos_y, cos_xy)
    lead = jnp.where(zero_col, 1.0, cos_x)
    return jnp.concatenate(
        [main * ramp_cos, main * ramp_sin, lead * ramp_cos, lead * ramp_sin], axis=0
    )


def column_kernel(
    epoch_count,
    rate_smem,
    time_smem,
    received,
    even_table,
    odd_table,
    out_ref,
    rows_cos,
    rows_sin,
    spread,
    even_fold,
    odd_fold,
    products,
    sums,
):
    devices, loc_epochs, width, loc_rows = received.shape
    row_count = devices // epoch_count
    epochs = epoch_count * loc_epochs
    rates = rate_smem.shape[0]
    pairs = rates * epochs
    cols = width // 2
    half, quarter = even_table.shape
    length = 2 * half
    steps = length // BLOCK
    device = lax.axis_index("row") * epoch_count + lax.axis_index("epoch")
    period = SUBPIX * length
    shift_y, shift_x = [
        [
            rate_smem[rate, axis] * time_smem[epoch] & (period - 1)
            for rate in range(rates)
            for epoch in range(epochs)
        ]
        for axis in range(2)
    ]
    per_tile = max(1, GROUP // loc_rows)
    tile_rows = per_tile * loc_rows
    for tile in range(row_count // 4 // per_tile):
        at_lane = slice(tile * tile_rows, (tile + 1) * tile_rows)
        far_lane = slice(quarter + at_lane.start, quarter + at_lane.stop)
        for core in range(epoch_count):
            for loc in range(loc_epochs):
                quarters = []
                for side in range(4):
                    first = side * row_count // 4 + tile * per_tile
                    parts = [
                        received[(first + part) * epoch_count + core, loc] for part in range(per_tile)
                    ]
                    quarters.append(parts[0] if per_tile == 1 else jnp.concatenate(parts, axis=1))
                at_row = (core * loc_epochs + loc) * width
                at = slice(at_row, at_row + width)
                folds = fold(quarters)
                even_fold[0, at, at_lane], even_fold[1, at, at_lane] = folds[:2]
                odd_fold[at, at_lane], odd_fold[at, far_lane] = folds[2:]

    def multiply(step):
        at = slice(step % (steps // 2) * BLOCK, (step % (steps // 2) + 1) * BLOCK)
        if step < steps // 2:
            left, right = even_fold[4 * step // steps], even_table[at]
        else:
            left, right = odd_fold[...], odd_table[at]
        products[step % 2] = lax.dot_general(
            left, right, CONTRACT_LAST, preferred_element_type=jnp.float32
        )

    multiply(0)
    rows_cos[...], rows_sin[...] = row_factors(shift_y, half)
    factors = column_factors(shift_y, shift_x, 1.0 / math.sqrt(epochs), device, cols, half).T
    for kind in range(4):
        for pair in range(pairs):
            at = kind * pairs + pair
            spread[kind, pair] = jnp.broadcast_to(factors[:width, at : at + 1], (width, GROUP))

    chunk = min(ROW_CHUNK, cols)

    def add_ramped(step, group):
        tile = (step * BLOCK // 2 // GROUP + group) * GROUP
        at_even = group * 2 * GROUP
        at_odd = at_even + GROUP
        for start in range(0, cols, chunk):
            real = slice(start, start + chunk)
            imag = slice(cols + start, cols + start + chunk)
            totals = [[[0.0, 0.0], [0.0, 0.0]] for _ in range(rates)]
            leads = [[0.0, 0.0] for _ in range(rates)]
            for epoch in range(epochs):
                loaded = []
                for part in (real, imag):
                    at = slice(epoch * width + part.start, epoch * width + part.stop)
                    loaded.append(
                        [
                            products[step % 2, at, first : first + GROUP]
                            for first in (at_even, at_odd)
                        ]
                    )
                for rate in range(rates):
                    pair = rate * epochs + epoch
                    cos_row = rows_cos[pair : pair + 1, tile : tile + GROUP]
                    sin_row = rows_sin[pair : pair + 1, tile : tile + GROUP]
                    turned = [
                        (cos_row * even + sin_row * odd, cos_row * odd - sin_row * even)
                        for even, odd in loaded
                    ]
                    straight = [spread[0, pair, part] for part in (real, imag)]
                    crossed = [spread[1, pair, part] for part in (real, imag)]
                    for part in range(2):
                        for which in range(2):
                            totals[rate][part][which] += (
                                straight[part] * turned[part][which]
                                + crossed[1 - part] * turned[1 - part][which]
                            )
                        if step == 0 and group == 0:
                            own, other = (real, imag) if part == 0 else (imag, real)
                            leads[rate][part] += (
                                spread[2, pair, own] * loaded[part][0]
                                + spread[3, pair, other] * loaded[1 - part][0]
                            )
            for rate in range(rates):
                for part, rows in enumerate((real, imag)):
                    even_sum, odd_sum = totals[rate][part]
                    if step == 0 and group == 0:
                        first = lax.broadcasted_iota(jnp.int32, even_sum.shape, 1) == 0
                        even_sum = jnp.where(first, leads[rate][part], even_sum)
                    at = slice(rate * width + rows.start, rate * width + rows.stop)
                    for values, lane in ((even_sum, at_even), (odd_sum, at_odd)):
                        lane = step * BLOCK + lane
                        sums[at, lane : lane + GROUP] = values.astype(jnp.bfloat16)

    for step in range(steps):
        if step + 1 < steps:
            multiply(step + 1)
        for group in range(BLOCK // 2 // GROUP):
            add_ramped(step, group)

    loc_rates = rates // epoch_count

    def send(side, back):
        back = back.astype(jnp.bfloat16)
        rows_here = quarter // loc_rows
        for row in range(rows_here):
            for rate in range(rates):
                dest = (side * rows_here + row) * epoch_count + rate // loc_rates
                out_ref[dest, rate % loc_rates] = back[
                    rate * width : (rate + 1) * width, row * loc_rows : (row + 1) * loc_rows
                ]

    inverse_parts(sums, even_table, odd_table, slice(0, quarter), quarter, send)


def inverse_parts(left, even_table, odd_table, at, quarter, send):
    half = 2 * quarter
    far = slice(quarter + at.start, quarter + at.stop)

    def product(first, depth, right):
        return jnp.dot(left[:, first : first + depth], right, preferred_element_type=jnp.float32)

    zero = product(0, quarter, even_table[:quarter, at])
    two = product(quarter, quarter, even_table[quarter:, at])
    for position, even, span in ((0, zero + two, at), (1, zero - two, far)):
        odd = product(half, half, odd_table[:, span])
        send(position, even + odd)
        send(position + 2, even - odd)


def column_stage(rate_vectors, epoch_times, spectra, even_table, odd_table, epoch_count):
    devices, loc_epochs, width, loc_rows = spectra.shape
    half, quarter = even_table.shape
    length = 2 * half
    epochs, rates = epoch_times.shape[0], rate_vectors.shape[0]
    out = (devices, rates // epoch_count, width, loc_rows)
    scalars = pl.BlockSpec(memory_space=pltpu.SMEM)
    return pl.pallas_call(
        functools.partial(column_kernel, epoch_count),
        in_specs=[scalars, scalars, IN_VMEM, IN_VMEM, IN_VMEM],
        out_specs=IN_VMEM,
        out_shape=pltpu.VMEM(out, jnp.bfloat16),
        scratch_shapes=[
            pltpu.VMEM((rates * epochs, half), jnp.float32),
            pltpu.VMEM((rates * epochs, half), jnp.float32),
            pltpu.VMEM((4, rates * epochs, width, GROUP), jnp.float32),
            pltpu.VMEM((2, epochs * width, quarter), jnp.bfloat16),
            pltpu.VMEM((epochs * width, half), jnp.bfloat16),
            pltpu.VMEM((2, epochs * width, BLOCK), jnp.float32),
            pltpu.VMEM((rates * width, length), jnp.bfloat16),
        ],
        compiler_params=pltpu.CompilerParams(vmem_limit_bytes=40 * MIB),
        cost_estimate=cost(
            2 * (even_table.size + odd_table.size) * (epochs + rates) * width,
            3 * half * half + 4 * spectra.size,
        ),
        name="column_stage",
    )(
        rate_vectors,
        epoch_times,
        *(in_space(part, pltpu.VMEM) for part in (spectra, even_table, odd_table)),
    )


def image_kernel(back, even_table, odd_table, out_hbm, left, staged, out_sems):
    quarter = even_table.shape[1]
    _, width, rows = back.shape
    cols = width // 2
    per_group = GROUP // cols
    for group in range(back.shape[0] // per_group):
        members = [back[group * per_group + place] for place in range(per_group)]
        if cols % 16 != 0 or rows % 128 != 0:
            members = [member.astype(jnp.float32) for member in members]
        parts = [member[:cols] for member in members] + [member[cols:] for member in members]
        whole = jnp.concatenate(parts, axis=0)
        left[:, group * 2 * GROUP : (group + 1) * 2 * GROUP] = whole.T.astype(jnp.bfloat16)
    out_copies = []
    for block in range(quarter // IMAGE_BLOCK):

        def send(side, pixels):
            start = side * quarter + block * IMAGE_BLOCK
            at = slice(start, start + IMAGE_BLOCK)
            staged[:, at] = pixels
            out_copies.append(
                pltpu.make_async_copy(
                    staged.at[:, at], out_hbm.at[0, :, at], out_sems.at[4 * block + side]
                )
            )
            out_copies[-1].start()

        at = slice(block * IMAGE_BLOCK, (block + 1) * IMAGE_BLOCK)
        inverse_parts(left, even_table, odd_table, at, quarter, send)
    wait_copies(out_copies)


def image_rows(back, even_table, odd_table):
    rows = back.shape[2]
    half, quarter = even_table.shape
    length = 2 * half
    return pl.pallas_call(
        image_kernel,
        in_specs=[IN_VMEM, IN_VMEM, IN_VMEM],
        out_specs=HBM,
        out_shape=jax.ShapeDtypeStruct((1, rows, length), jnp.float32),
        scratch_shapes=[
            pltpu.VMEM((rows, length), jnp.bfloat16),
            pltpu.VMEM((rows, length), jnp.float32),
            pltpu.SemaphoreType.DMA((length // IMAGE_BLOCK,)),
        ],
        compiler_params=pltpu.CompilerParams(vmem_limit_bytes=40 * MIB),
        cost_estimate=cost(
            2 * rows * (even_table.size + odd_table.size), 3 * half * half + 6 * rows * length
        ),
        name="image_rows",
    )(*(in_space(part, pltpu.VMEM) for part in (back, even_table, odd_table)))


def local(images, rate_vectors, epoch_times):
    _, loc_rows, length = images.shape
    epoch_count = lax.axis_size("epoch")
    devices = lax.axis_size("row") * epoch_count
    even_table, odd_table = [jnp.asarray(part) for part in packed_tables(length)]

    def exchange(values):
        return lax.all_to_all(values, ("row", "epoch"), 0, 0, tiled=True)

    spectra = exchange(row_transform(images, even_table, odd_table, devices))
    back = exchange(
        column_stage(rate_vectors, epoch_times, spectra, even_table, odd_table, epoch_count)
    )
    return image_rows(
        back.reshape(devices, length // devices, loc_rows), even_table, odd_table
    )


def solution(mesh):
    in_specs = (P(("group", "epoch"), "row", None), P(), P())
    out_specs = P(("group", "epoch"), "row", None)
    return jax.shard_map(local, mesh=mesh, in_specs=in_specs, out_specs=out_specs, check_vma=False)
```
